32 devices in a mesh: groups: 2 (over y), tiles: 4 (over z), folds: 2 (over x), sub: 2 (over core).
Axes of the slice: x: 2, y: 2, z: 4, core: 2. Of those that a mesh axis runs over, the one named last changes fastest.
Arguments:
- features: bfloat16 [2, 32, 16, 16, 1024], P('folds', ('groups', 'tiles', 'sub')), parts along dimension 1, may hold values from -6 to 6
- conv_first: bfloat16 [2, 3, 3, 3, 64, 32], P('folds'), may hold values from -0.15625 to 0.15625
- gain_first: float32 [2, 32], P('folds'), may hold values from 0.1 to 1.9
- shift_first: float32 [2, 32], P('folds'), may hold values from -3 to 3
- conv_second: bfloat16 [2, 3, 3, 3, 32, 32], P('folds'), may hold values from -0.21875 to 0.21875
- gain_second: float32 [2, 32], P('folds'), may hold values from 0.1 to 1.9
- shift_second: float32 [2, 32], P('folds'), may hold values from -3 to 3
- head_weight: bfloat16 [2, 32, 16], P('folds'), may hold values from -1 to 1
- head_bias: float32 [2, 16], P('folds'), may hold values from -4 to 4
- corners: int32 [32, 3], P(('groups', 'tiles', 'sub')), parts along dimension 0, may hold values from 0 to 48, as said below
- counts: int32 [8, 2], P('groups'), parts along dimension 0, may hold values from 0 to 2, as said below
Outputs:
- logits: float32 [128, 40, 640], P(('groups', 'tiles'), ('folds', 'sub')), parts along dimension 0
The draws below stay inside these ranges and needn't reach their ends.
There are 2 independent parts, one for each index of `groups`. The reference program is written for one: setup_inputs(seed, part) draws one part's arguments, and reference() takes and returns one part's arrays. A program takes and returns all parts, laid end to end along the dimension named above; an argument that names none is the same for every part. Nothing has to cross between parts.
Inputs may be any that keep to these rules, and one draw needn't show every extreme that they name: `corners`: for slot n = (t * 2 + s) * 2 + j, the z coordinate lies in [t * 16, (t + 1) * 16) and equals (3) * 16 in the last slab; x lies in [0, 24] and y in [0, 24]. counts[t, s] + counts[t xor (2), s] <= 2 for every t and s; some entry equals 2.
All inputs are finite; a program needn't handle non-finite values.
Results may differ from the reference program's by a relative error of at most 0.01.
Values may be sent and summed in bfloat16 or wider, within the bound.
No kernel may reach another device: no remote copies, remote signals or barrier semaphores. Data moves between devices by JAX's collectives and lax.ppermute only.
A program may use at most 128 MiB of HBM per device.

```python
import jax
import jax.numpy as jnp
from jax import lax

CIN = 64
CH = 32
CLASSES = 16
WE = 16
CAP = 2
TZ = 16
VX = 40
VY = 40
FOLDS = 2
TILES = 4
HALVES = 2
WINDOWS = 16
VZ = 64


def draw_counts(key, part):
    subkeys = jax.random.split(jax.random.fold_in(key, 17), 5)
    half_tiles = TILES // 2
    grid_shape = (half_tiles, HALVES)
    totals = jax.random.randint(subkeys[0], grid_shape, CAP // 2, CAP + 1)
    lower_part = jax.random.randint(subkeys[1], grid_shape, 0, totals + 1)
    chosen_tile = jax.random.randint(subkeys[2], (), 0, half_tiles)
    chosen_half = jax.random.randint(subkeys[3], (), 0, HALVES)
    upper_side = jax.random.randint(subkeys[4], (), 0, 2)
    marked = (jnp.arange(half_tiles)[:, None] == chosen_tile) & (jnp.arange(HALVES)[None, :] == chosen_half)
    totals = jnp.where(marked, CAP, totals)
    lower_part = jnp.where(marked, CAP * (1 - upper_side), lower_part)
    return jnp.concatenate([lower_part, totals - lower_part], axis=0).astype(jnp.int32)


def draw_corners(key, part):
    subkeys = jax.random.split(jax.random.fold_in(key, 29), 3)
    total_windows = TILES * HALVES * CAP
    owner_tile = jnp.arange(total_windows) // (HALVES * CAP)
    offsets = jax.random.randint(subkeys[0], (total_windows,), 0, TZ)
    offsets = jnp.where(owner_tile == TILES - 1, 0, offsets)
    depth = owner_tile * TZ + offsets
    across = jax.random.randint(subkeys[1], (total_windows,), 0, VX - WE + 1)
    along = jax.random.randint(subkeys[2], (total_windows,), 0, VY - WE + 1)
    return jnp.stack([depth, across, along], axis=1).astype(jnp.int32)


def block_scale(rng, extent, shards, smallest, largest):
    factor_of, own = 1.0, jax.random.fold_in(rng, 6)
    for axis_at, blocks in shards:
        steps = jnp.exp(jax.random.uniform(jax.random.fold_in(own, axis_at), (blocks,), jnp.float32, smallest / len(shards), largest / len(shards)))
        factor_of = factor_of * jnp.repeat(steps, extent[axis_at] // blocks).reshape([-1 if axis == axis_at else 1 for axis in range(len(extent))])
    return factor_of


def gaussian(rng, extent, scale, bound, cuts=(), kind=jnp.bfloat16):
    array = jax.random.normal(rng, extent, jnp.float32) * scale
    if len(cuts) > 0:
        array = block_scale(rng, extent, cuts, -0.22, 0.18) * array
    return jnp.clip(array, min=-bound, max=bound).astype(kind)


def setup_inputs(seed: int = 0, part: int = 0) -> dict:
    splits = jax.random.split(jax.random.key(seed), 12)
    part_splits = jax.random.split(jax.random.fold_in(splits[11], part), 12)
    return {
        "features": gaussian(part_splits[0], (FOLDS, WINDOWS, WE, WE, WE * CIN), 1.0, 6.0, ((0, 2), (1, 8))),
        "conv_first": gaussian(splits[1], (FOLDS, 3, 3, 3, CIN, CH), (27 * CIN) ** -0.5, 0.15625, ((0, 2),)),
        "gain_first": jnp.clip(1.0 + 0.18 * jax.random.normal(splits[2], (FOLDS, CH), jnp.float32), 0.1, 1.9),
        "shift_first": gaussian(splits[3], (FOLDS, CH), 0.5, 3.0, ((0, 2),), jnp.float32),
        "conv_second": gaussian(splits[4], (FOLDS, 3, 3, 3, CH, CH), (27 * CH) ** -0.5, 0.21875, ((0, 2),)),
        "gain_second": jnp.clip(1.0 + 0.18 * jax.random.normal(splits[5], (FOLDS, CH), jnp.float32), 0.1, 1.9),
        "shift_second": gaussian(splits[6], (FOLDS, CH), 0.5, 3.0, ((0, 2),), jnp.float32),
        "head_weight": gaussian(splits[7], (FOLDS, CH, CLASSES), CH ** -0.5, 1.0, ((0, 2),)),
        "head_bias": gaussian(splits[8], (FOLDS, CLASSES), 1.0, 4.0, ((0, 2),), jnp.float32),
        "corners": draw_corners(jax.random.fold_in(jax.random.fold_in(splits[11], part), 71), part),
        "counts": draw_counts(jax.random.fold_in(jax.random.fold_in(splits[11], part), 71), part),
    }


epsilon = 1e-05
leak_slope = 0.01

def gauss_table():
    coords = jnp.arange(WE, dtype=jnp.float32)
    center = (WE - 1) / 2.0
    spread = WE / 4.0
    profile = jnp.exp(-(coords - center) ** 2 / (2.0 * spread * spread))
    return profile[:, None, None] * profile[None, :, None] * profile[None, None, :]

def convolve(inputs, kernel):
    return lax.conv_general_dilated(inputs, kernel, (1, 1, 1), 'SAME', dimension_numbers=('NDHWC', 'DHWIO', 'NDHWC'), preferred_element_type=jnp.float32)

def normalize(hidden, gain_vec, shift_vec):
    mean_value = lax.optimization_barrier(jnp.mean(hidden, axis=(1, 2, 3), keepdims=True))
    variance = lax.optimization_barrier(jnp.mean((hidden - mean_value) ** 2, axis=(1, 2, 3), keepdims=True))
    scaled = (hidden - mean_value) * lax.rsqrt(variance + epsilon) * gain_vec + shift_vec
    return jnp.where(scaled >= 0, scaled, leak_slope * scaled).astype(jnp.bfloat16)

def decode(windows, kernel_one, gain_one, shift_one, kernel_two, gain_two, shift_two, head_kernel, head_shift):
    count = windows.shape[0]
    inputs = windows.reshape(count, WE, WE, WE, CIN)
    normed_first = normalize(convolve(inputs, kernel_one), gain_one, shift_one)
    normed_second = normalize(convolve(normed_first, kernel_two), gain_two, shift_two)
    head = jnp.einsum('nzxyc,ck->nzxyk', normed_second.astype(jnp.float32), head_kernel.astype(jnp.float32))
    weighted = ((head + head_shift) * gauss_table()[None, :, :, :, None]).astype(jnp.bfloat16)
    return weighted.reshape(count, WE, WE, WE * CLASSES)

def reference(features, conv_first, gain_first, shift_first, conv_second, gain_second, shift_second, head_weight, head_bias, corners, counts):
    volume = jnp.zeros((VZ + WE, VX, VY * CLASSES), jnp.float32)
    live_mask = (jnp.arange(CAP, dtype=jnp.int32)[None, None, :] < counts[:, :, None]).reshape(-1).astype(jnp.float32)
    for fold_index in range(FOLDS):
        weighted = decode(features[fold_index], conv_first[fold_index], gain_first[fold_index], shift_first[fold_index], conv_second[fold_index], gain_second[fold_index], shift_second[fold_index], head_weight[fold_index], head_bias[fold_index])

        def add_one(slot_index, total):
            window_piece = weighted[slot_index].astype(jnp.float32) * live_mask[slot_index]
            corner_start = (corners[slot_index, 0].astype(jnp.int32), corners[slot_index, 1].astype(jnp.int32), (corners[slot_index, 2] * CLASSES).astype(jnp.int32))
            current = lax.dynamic_slice(total, corner_start, window_piece.shape)
            return lax.dynamic_update_slice(total, current + window_piece, corner_start)
        volume = lax.fori_loop(0, WINDOWS, add_one, volume)
    return volume[:VZ]
```

```python
import functools

import jax
import jax.numpy as jnp
from jax import lax
from jax.experimental import pallas as pl
from jax.experimental.pallas import tpu as pltpu
from jax.sharding import PartitionSpec as P

TZ = 16
VX = 40
VY = 40

epsilon = 1e-05
leak_slope = 0.01
half = 8
far = 1 << 20
bf16 = jnp.bfloat16
f32 = jnp.float32
vmem_bytes = 48 << 20


def iota(shape, dim):
    return lax.broadcasted_iota(jnp.int32, shape, dim)


def split_index(index, width):
    whole = jnp.floor((index.astype(f32) + 0.5) * (1.0 / width)).astype(jnp.int32)
    return whole, index - whole * width


def tile_matrix(width, lanes):
    return (iota((width, lanes), 1) % width == iota((width, lanes), 0)).astype(bf16)


def tiled_row(ref, lanes):
    width = ref.shape[1]
    row = jnp.concatenate([ref[...], jnp.zeros((1, lanes - width), f32)], axis=1)
    row = jnp.broadcast_to(row, (8, lanes))
    reach = width
    while reach < lanes:
        row = row + pltpu.roll(row, reach, 1)
        reach *= 2
    return row[0:1]


def build_band(taps_ref, band_ref, lead, group):
    out_width = taps_ref.shape[1]
    lanes = half * out_width
    in_width = taps_ref.shape[0] // 27
    spread = tile_matrix(out_width, lanes)
    place = iota((in_width, lanes), 1) // out_width
    for dz in range(3):
        for dx in range(3):
            base = (dz * 3 + dx) * 3 * in_width
            tiled = jnp.dot(
                taps_ref[base : base + 3 * in_width], spread, preferred_element_type=f32
            )
            for yi in range(group):
                block = jnp.zeros((in_width, lanes), f32)
                for dy in range(3):
                    yo = yi - lead - dy
                    if 0 <= yo < half:
                        block = jnp.where(
                            place == yo, tiled[dy * in_width : (dy + 1) * in_width], block
                        )
                at = (dz * group + yi) * in_width
                band_ref[dx, at : at + in_width, :] = block.astype(bf16)


def convolve(pad_ref, band_ref, hidden_ref, edge, step):
    rows, lanes = hidden_ref.shape[0], band_ref.shape[2]
    depth = band_ref.shape[1] // 3
    across = iota((rows, lanes), 0) % edge
    for side in range(2):
        parts = []
        for dx in range(3):
            total = None
            for dz in range(3):
                part = jnp.dot(
                    pad_ref[dz * edge : dz * edge + rows, side * step : side * step + depth],
                    band_ref[dx, dz * depth : (dz + 1) * depth, :],
                    preferred_element_type=f32,
                )
                total = part if total is None else total + part
            parts.append(total)
        before = jnp.where(across == 0, 0.0, pltpu.roll(parts[0], 1, 0))
        after = jnp.where(across == edge - 1, 0.0, pltpu.roll(parts[2], rows - 1, 0))
        hidden_ref[:, side * lanes : (side + 1) * lanes] = parts[1] + before + after


def channel_mean(values, width, voxels):
    lanes = values.shape[1] // 2
    row = jnp.sum(values, axis=0, keepdims=True)
    row = jnp.broadcast_to(row[:, :lanes] + row[:, lanes:], (8, lanes))
    reach = width
    while reach < lanes:
        row = row + pltpu.roll(row, reach, 1)
        reach *= 2
    return row[0:1] * (1.0 / voxels)


def normalize(hidden, gain, shift, width, voxels):
    mean_value = channel_mean(hidden, width, voxels)
    centered = hidden - jnp.concatenate([mean_value, mean_value], axis=1)
    variance = channel_mean(centered * centered, width, voxels)
    factor = lax.rsqrt(variance + epsilon) * gain
    scaled = centered * jnp.concatenate([factor, factor], axis=1) + jnp.concatenate(
        [shift, shift], axis=1
    )
    return jnp.maximum(scaled, leak_slope * scaled).astype(bf16)


def section_kernel(
    sizes,
    corners_ref,
    counts_ref,
    features_ref,
    taps_one_ref,
    gain_one_ref,
    shift_one_ref,
    taps_two_ref,
    gain_two_ref,
    shift_two_ref,
    head_ref,
    bias_ref,
    *rest,
):
    slots, edge, chunk, peers = sizes
    out_refs = rest[:peers]
    pad_one, pad_two, band_one, band_two, hidden, sems = rest[peers:]
    width = taps_one_ref.shape[1]
    in_width = taps_one_ref.shape[0] // 27
    classes = head_ref.shape[1]
    area = edge * edge
    stride = area + edge
    voxels = float(area * edge)
    margin = 128
    data = edge * in_width

    copies = []
    for slot in range(slots):
        copy = pltpu.make_async_copy(
            features_ref.at[slot],
            pad_one.at[pl.ds(edge + slot * stride, area), pl.ds(margin, data)],
            sems.at[slot],
        )
        copy.start()
        copies.append(copy)
    for pad in (pad_one, pad_two):
        inner = pad.shape[1] - 2 * margin
        for slot in range(slots + 1):
            pad[slot * stride : slot * stride + edge, :] = jnp.zeros((edge, pad.shape[1]), bf16)
        pad[:, :margin] = jnp.zeros((pad.shape[0], margin), bf16)
        pad[:, margin + inner :] = jnp.zeros((pad.shape[0], margin), bf16)

    group_one = half + 2 * (margin // in_width)
    group_two = half + 2 * (margin // width)
    build_band(taps_one_ref, band_one, margin // in_width - 1, group_one)
    build_band(taps_two_ref, band_two, margin // width - 1, group_two)
    lanes = half * width
    gain_one, shift_one = tiled_row(gain_one_ref, lanes), tiled_row(shift_one_ref, lanes)
    gain_two, shift_two = tiled_row(gain_two_ref, lanes), tiled_row(shift_two_ref, lanes)

    logit_lanes = half * classes
    head_row = jnp.dot(
        head_ref[...], tile_matrix(classes, logit_lanes), preferred_element_type=f32
    )
    head_block = jnp.where(
        iota((lanes, logit_lanes), 0) // width == iota((lanes, logit_lanes), 1) // classes,
        jnp.concatenate([head_row] * half, axis=0),
        0.0,
    ).astype(bf16)
    bias = tiled_row(bias_ref, 2 * logit_lanes)

    center, spread = (edge - 1) / 2.0, edge / 4.0

    def profile(offset):
        return jnp.exp(-((offset.astype(f32) - center) ** 2) / (2.0 * spread * spread))

    row_at = iota((area, 2 * logit_lanes), 0)
    lane_at = iota((1, 2 * logit_lanes), 1)
    gauss = profile(row_at // edge) * profile(row_at % edge) * profile(lane_at // classes)

    place_z, place_x = split_index(iota((edge * chunk, area), 0), chunk)
    source = iota((edge * chunk, area), 1)
    offset = jnp.where(place_z == source // edge, source % edge - place_x, far)
    tile_index = lax.axis_index("tiles")
    sub_index = lax.axis_index("sub")
    position = lax.axis_index("folds") * lax.axis_size("sub") + sub_index
    live_count = counts_ref[tile_index, sub_index]

    for copy in copies:
        copy.wait()
    convolve(pad_one, band_one, hidden, edge, half * in_width)
    for slot in range(slots):
        at = slot * stride
        pad_two[at + edge : at + edge + area, margin : margin + 2 * lanes] = normalize(
            hidden[at : at + area, :], gain_one, shift_one, width, voxels
        )
    convolve(pad_two, band_two, hidden, edge, half * width)
    for slot in range(slots):
        at = slot * stride
        normed = normalize(hidden[at : at + area, :], gain_two, shift_two, width, voxels)
        logits = jnp.concatenate(
            [
                jnp.dot(normed[:, :lanes], head_block, preferred_element_type=f32),
                jnp.dot(normed[:, lanes:], head_block, preferred_element_type=f32),
            ],
            axis=1,
        )
        weighted = ((logits + bias) * gauss).astype(bf16)
        for peer in range(peers):
            shift = (position ^ peer) * chunk - corners_ref[slot, 1]
            shift = jnp.where(slot < live_count, shift, 2 * far)
            select = (offset == shift).astype(f32).astype(bf16)
            out_refs[peer][slot * edge * chunk : (slot + 1) * edge * chunk, :] = jnp.dot(
                select, weighted, preferred_element_type=f32
            ).astype(bf16)


def gather_kernel(sizes, own_corners_ref, other_corners_ref, *rest):
    slots, edge, chunk, peers, classes = sizes
    piece_refs = rest[:peers]
    own_ref, spill_ref, total = rest[peers:]
    rows = edge * chunk
    held = TZ * edge
    width = edge * classes
    tile_index = lax.axis_index("tiles")

    high_z, high_x = iota((held, rows), 0) // edge, iota((held, rows), 0) % edge
    low_z, low_x = split_index(iota((rows, rows), 0), chunk)
    from_z, from_x = split_index(iota((held, rows), 1), chunk)
    upper = jnp.where(high_x == from_x, high_z - from_z, far)
    lower = jnp.where(low_x == from_x[:rows], low_z + TZ - from_z[:rows], far)
    offset = jnp.concatenate([upper, lower], axis=0)

    total[...] = jnp.zeros(total.shape, f32)
    for parity, corners_ref in enumerate((own_corners_ref, other_corners_ref)):
        for slot in range(slots):
            depth = corners_ref[slot, 0] - tile_index * TZ
            start = corners_ref[slot, 2] * classes
            select = (offset == depth).astype(f32).astype(bf16)
            piece = None
            for peer in range(parity, peers, 2):
                part = jnp.dot(
                    select,
                    piece_refs[peer][slot * rows : (slot + 1) * rows, :],
                    preferred_element_type=f32,
                )
                piece = part if piece is None else piece + part
            piece = jnp.concatenate([piece, jnp.zeros((held + rows, 128), f32)], axis=1)
            piece = pltpu.roll(piece, start % 128, 1)
            lane_at = pl.multiple_of((start // 128) * 128, 128)
            total[:, pl.ds(lane_at, width + 128)] += piece
    own = total[:held, : VY * classes].reshape(TZ, edge, VY * classes)
    own_ref[...] = own[:, :chunk, :]
    spill_ref[...] = total[held:, : VY * classes].astype(bf16)


def join_kernel(own_ref, arrived_ref, out_ref):
    depth, chunk, lanes = own_ref.shape
    rows = arrived_ref.shape[0]
    edge = 16
    at_z, at_x = iota((depth * edge, rows), 0) // edge, iota((depth * edge, rows), 0) % edge
    from_z, from_x = split_index(iota((depth * edge, rows), 1), chunk)
    select = ((at_z == from_z) & (at_x == from_x)).astype(f32).astype(bf16)
    arrived = jnp.dot(select, arrived_ref[...], preferred_element_type=f32)
    out_ref[...] = own_ref[...] + arrived.reshape(depth, edge, lanes)[:, :chunk, :]


vmem = pl.BlockSpec(memory_space=pltpu.VMEM)
smem = pl.BlockSpec(memory_space=pltpu.SMEM)
limits = pltpu.CompilerParams(vmem_limit_bytes=vmem_bytes)


def on_device(
    features,
    conv_first,
    gain_first,
    shift_first,
    conv_second,
    gain_second,
    shift_second,
    head_weight,
    head_bias,
    corners,
    counts,
):
    _, slots, edge, _, data = features.shape
    in_width, width = conv_first.shape[-2:]
    classes = head_bias.shape[1]
    peers = lax.axis_size("folds") * lax.axis_size("sub")
    chunk = VX // peers
    area = edge * edge
    padded_rows = slots * (area + edge) + edge
    margin = 128

    subs = lax.axis_size("sub")
    other_corners = lax.ppermute(corners, "sub", [(i, i ^ 1) for i in range(subs)])

    pieces = pl.pallas_call(
        functools.partial(section_kernel, (slots, edge, chunk, peers)),
        out_shape=[jax.ShapeDtypeStruct((slots * edge * chunk, edge * classes), bf16)] * peers,
        in_specs=[smem, smem, pl.BlockSpec(memory_space=pl.ANY)] + [vmem] * 8,
        out_specs=[vmem] * peers,
        scratch_shapes=[
            pltpu.VMEM((padded_rows, data + 2 * margin), bf16),
            pltpu.VMEM((padded_rows, edge * width + 2 * margin), bf16),
            pltpu.VMEM((3, 3 * (half * in_width + 2 * margin), half * width), bf16),
            pltpu.VMEM((3, 3 * (half * width + 2 * margin), half * width), bf16),
            pltpu.VMEM((padded_rows - 2 * edge, edge * width), f32),
            pltpu.SemaphoreType.DMA((slots,)),
        ],
        compiler_params=limits,
        name="section",
    )(
        corners,
        counts,
        features.reshape(slots, area, data),
        conv_first.reshape(27 * in_width, width),
        gain_first,
        shift_first,
        conv_second.reshape(27 * width, width),
        gain_second,
        shift_second,
        head_weight[0],
        head_bias,
    )
    arrived = [pieces[0]]
    for peer in range(1, peers):
        pairs = [(i, i ^ peer) for i in range(peers)]
        arrived.append(lax.ppermute(pieces[peer], ("folds", "sub"), pairs))

    own, spill = pl.pallas_call(
        functools.partial(gather_kernel, (slots, edge, chunk, peers, classes)),
        out_shape=[
            jax.ShapeDtypeStruct((TZ, chunk, VY * classes), f32),
            jax.ShapeDtypeStruct((edge * chunk, VY * classes), bf16),
        ],
        in_specs=[smem, smem] + [vmem] * peers,
        out_specs=[vmem, vmem],
        scratch_shapes=[
            pltpu.VMEM((TZ * edge + edge * chunk, VY * classes + 128), f32),
        ],
        compiler_params=limits,
        name="gather",
    )(corners, other_corners, *arrived)

    tiles = lax.axis_size("tiles")
    from_below = lax.ppermute(spill, "tiles", [(i, i + 1) for i in range(tiles - 1)])
    return pl.pallas_call(
        join_kernel,
        out_shape=jax.ShapeDtypeStruct((TZ, chunk, VY * classes), f32),
        in_specs=[vmem, vmem],
        out_specs=vmem,
        compiler_params=limits,
        name="join",
    )(own, from_below)


def solution(mesh):
    placed = (
        P("folds", ("groups", "tiles", "sub"), None, None, None),
        P("folds", None, None, None, None, None),
        P("folds", None),
        P("folds", None),
        P("folds", None, None, None, None, None),
        P("folds", None),
        P("folds", None),
        P("folds", None, None),
        P("folds", None),
        P(("groups", "tiles", "sub"), None),
        P("groups", None),
    )
    return jax.shard_map(
        on_device,
        mesh=mesh,
        in_specs=placed,
        out_specs=P(("groups", "tiles"), ("folds", "sub"), None),
        check_vma=False,
    )
```

```python
import functools

import jax
import jax.numpy as jnp
from jax import lax
from jax.experimental import pallas as pl
from jax.experimental.pallas import tpu as pltpu
from jax.sharding import PartitionSpec as P

TZ = 16
VX = 40
VY = 40

epsilon = 1e-05
leak_slope = 0.01
half = 8
far = 1 << 20
bf16 = jnp.bfloat16
f32 = jnp.float32
vmem_bytes = 48 << 20


def iota(shape, dim):
    return lax.broadcasted_iota(jnp.int32, shape, dim)


def tile_matrix(width, lanes):
    return (iota((width, lanes), 1) % width == iota((width, lanes), 0)).astype(bf16)


def tiled_row(ref, lanes):
    width = ref.shape[1]
    row = jnp.concatenate([ref[...], jnp.zeros((1, lanes - width), f32)], axis=1)
    row = jnp.broadcast_to(row, (8, lanes))
    reach = width
    while reach < lanes:
        row = row + pltpu.roll(row, reach, 1)
        reach *= 2
    return row[0:1]


def spread_taps(taps_ref, at, in_width, out_width, spread, swapped):
    if swapped:
        return [
            lax.dot_general(
                taps_ref[(at + dy) * out_width : (at + dy + 1) * out_width],
                spread,
                (((0,), (0,)), ((), ())),
                preferred_element_type=f32,
            )
            for dy in range(3)
        ]
    return [
        jnp.dot(
            taps_ref[(at + dy) * in_width : (at + dy + 1) * in_width],
            spread,
            preferred_element_type=f32,
        )
        for dy in range(3)
    ]


def build_band(taps_ref, band_ref, lead, group, in_width, out_width, swapped):
    lanes = half * out_width
    spread = tile_matrix(out_width, lanes)
    place = iota((in_width, lanes), 1) // out_width
    for dz in range(3):
        for dx in range(3):
            tiled = spread_taps(taps_ref, (dz * 3 + dx) * 3, in_width, out_width, spread, swapped)
            for yi in range(group):
                block = jnp.zeros((in_width, lanes), f32)
                for dy in range(3):
                    yo = yi - lead - dy
                    if 0 <= yo < half:
                        block = jnp.where(place == yo, tiled[dy], block)
                at = (dz * group + yi) * in_width
                band_ref[dx, at : at + in_width, :] = block.astype(bf16)


def convolve(pad_ref, band_ref, hidden_ref, edge, step):
    rows, lanes = hidden_ref.shape[0], band_ref.shape[2]
    depth = band_ref.shape[1] // 3
    across = iota((rows, lanes), 0) % edge
    for side in range(2):
        parts = []
        for dx in range(3):
            total = None
            for dz in range(3):
                part = jnp.dot(
                    pad_ref[dz * edge : dz * edge + rows, side * step : side * step + depth],
                    band_ref[dx, dz * depth : (dz + 1) * depth, :],
                    preferred_element_type=f32,
                )
                total = part if total is None else total + part
            parts.append(total)
        before = jnp.where(across == 0, 0.0, pltpu.roll(parts[0], 1, 0))
        after = jnp.where(across == edge - 1, 0.0, pltpu.roll(parts[2], rows - 1, 0))
        hidden_ref[:, side * lanes : (side + 1) * lanes] = parts[1] + before + after


def channel_mean(values, width, voxels):
    lanes = values.shape[1] // 2
    row = jnp.sum(values, axis=0, keepdims=True)
    row = jnp.broadcast_to(row[:, :lanes] + row[:, lanes:], (8, lanes))
    reach = width
    while reach < lanes:
        row = row + pltpu.roll(row, reach, 1)
        reach *= 2
    return row[0:1] * (1.0 / voxels)


def normalize(hidden, gain, shift, width, voxels):
    mean_value = channel_mean(hidden, width, voxels)
    centered = hidden - jnp.concatenate([mean_value, mean_value], axis=1)
    variance = channel_mean(centered * centered, width, voxels)
    factor = lax.rsqrt(variance + epsilon) * gain
    scaled = centered * jnp.concatenate([factor, factor], axis=1) + jnp.concatenate(
        [shift, shift], axis=1
    )
    return jnp.maximum(scaled, leak_slope * scaled).astype(bf16)


def section_kernel(
    sizes,
    corners_hbm,
    counts_hbm,
    features_ref,
    taps_one_hbm,
    gain_one_hbm,
    shift_one_hbm,
    taps_two_hbm,
    gain_two_hbm,
    shift_two_hbm,
    head_hbm,
    bias_hbm,
    *rest,
):
    slots, edge, chunk, peers = sizes
    out_refs = rest[:peers]
    (
        pad_one,
        pad_two,
        band_one,
        band_two,
        hidden,
        corners_ref,
        counts_ref,
        taps_one_ref,
        gain_one_ref,
        shift_one_ref,
        taps_two_ref,
        gain_two_ref,
        shift_two_ref,
        head_ref,
        bias_ref,
        sems,
        small_sems,
    ) = rest[peers:]
    in_width = taps_one_ref.shape[1]
    classes, width = head_ref.shape
    area = edge * edge
    stride = area + edge
    voxels = float(area * edge)
    margin = 128
    data = edge * in_width

    small = []
    for at, (source, target) in enumerate(
        (
            (taps_one_hbm, taps_one_ref),
            (taps_two_hbm, taps_two_ref),
            (gain_one_hbm, gain_one_ref),
            (shift_one_hbm, shift_one_ref),
            (gain_two_hbm, gain_two_ref),
            (shift_two_hbm, shift_two_ref),
            (head_hbm, head_ref),
            (bias_hbm, bias_ref),
            (corners_hbm, corners_ref),
            (counts_hbm, counts_ref),
        )
    ):
        copy = pltpu.make_async_copy(source, target, small_sems.at[at])
        copy.start()
        small.append(copy)
    copies = []
    for slot in range(slots):
        copy = pltpu.make_async_copy(
            features_ref.at[slot],
            pad_one.at[pl.ds(edge + slot * stride, area), pl.ds(margin, data)],
            sems.at[slot],
        )
        copy.start()
        copies.append(copy)
    for pad in (pad_one, pad_two):
        inner = pad.shape[1] - 2 * margin
        for slot in range(slots + 1):
            pad[slot * stride : slot * stride + edge, :] = jnp.zeros((edge, pad.shape[1]), bf16)
        pad[:, :margin] = jnp.zeros((pad.shape[0], margin), bf16)
        pad[:, margin + inner :] = jnp.zeros((pad.shape[0], margin), bf16)

    logit_lanes = half * classes
    center, spread = (edge - 1) / 2.0, edge / 4.0

    def profile(offset):
        return jnp.exp(-((offset.astype(f32) - center) ** 2) / (2.0 * spread * spread))

    row_at = iota((area, 2 * logit_lanes), 0)
    lane_at = iota((1, 2 * logit_lanes), 1)
    gauss = profile(row_at // edge) * profile(row_at % edge) * profile(lane_at // classes)

    row = iota((chunk * edge, area), 0)
    source = iota((chunk * edge, area), 1)
    turn = (row % edge - source // edge) & (edge - 1)
    code = turn + edge * (source % edge - row // edge)
    tile_index = lax.axis_index("tiles")
    sub_index = lax.axis_index("sub")
    position = lax.axis_index("folds") * lax.axis_size("sub") + sub_index

    for copy in small:
        copy.wait()
    group_one = half + 2 * (margin // in_width)
    group_two = half + 2 * (margin // width)
    build_band(taps_one_ref, band_one, margin // in_width - 1, group_one, in_width, width, True)
    build_band(taps_two_ref, band_two, margin // width - 1, group_two, width, width, False)
    lanes = half * width
    gain_one, shift_one = tiled_row(gain_one_ref, lanes), tiled_row(shift_one_ref, lanes)
    gain_two, shift_two = tiled_row(gain_two_ref, lanes), tiled_row(shift_two_ref, lanes)

    head_row = lax.dot_general(
        head_ref[...],
        tile_matrix(classes, logit_lanes),
        (((0,), (0,)), ((), ())),
        preferred_element_type=f32,
    )
    head_block = jnp.where(
        iota((lanes, logit_lanes), 0) // width == iota((lanes, logit_lanes), 1) // classes,
        jnp.concatenate([head_row] * half, axis=0),
        0.0,
    ).astype(bf16)
    bias = tiled_row(bias_ref, 2 * logit_lanes)
    live_count = counts_ref[sub_index, tile_index]

    mark = iota((edge, 2 * logit_lanes), 0)
    notes = jnp.zeros((edge, 2 * logit_lanes), f32)
    for slot in range(slots):
        depth = corners_ref[slot, 0] - tile_index * TZ
        notes = jnp.where(mark == 2 * slot, depth.astype(f32), notes)
        notes = jnp.where(mark == 2 * slot + 1, corners_ref[slot, 2].astype(f32), notes)
    out_refs[1][slots * edge * chunk :, :] = notes.astype(bf16)

    for copy in copies:
        copy.wait()
    convolve(pad_one, band_one, hidden, edge, half * in_width)
    for slot in range(slots):
        at = slot * stride
        pad_two[at + edge : at + edge + area, margin : margin + 2 * lanes] = normalize(
            hidden[at : at + area, :], gain_one, shift_one, width, voxels
        )
    convolve(pad_two, band_two, hidden, edge, half * width)
    for slot in range(slots):
        at = slot * stride
        normed = normalize(hidden[at : at + area, :], gain_two, shift_two, width, voxels)
        logits = jnp.concatenate(
            [
                jnp.dot(normed[:, :lanes], head_block, preferred_element_type=f32),
                jnp.dot(normed[:, lanes:], head_block, preferred_element_type=f32),
            ],
            axis=1,
        )
        weighted = (logits + bias) * gauss
        lane_shift = (corners_ref[slot, 2] * classes) % (2 * logit_lanes)
        weighted = pltpu.roll(weighted, lane_shift, 1).astype(bf16)
        depth = corners_ref[slot, 0] - tile_index * TZ
        for peer in range(peers):
            wanted = depth + edge * ((position ^ peer) * chunk - corners_ref[slot, 1])
            wanted = jnp.where(slot < live_count, wanted, far)
            select = (code == wanted).astype(f32).astype(bf16)
            out_refs[peer][slot * edge * chunk : (slot + 1) * edge * chunk, :] = jnp.dot(
                select, weighted, preferred_element_type=f32
            ).astype(bf16)


def gather_kernel(sizes, corners_ref, *rest):
    slots, edge, chunk, peers, classes = sizes
    piece_refs = rest[:peers]
    own_ref, spill_ref = rest[peers:]
    rows = edge * chunk
    lanes = edge * classes
    tile_index = lax.axis_index("tiles")
    blocks = -(-VY * classes // lanes)

    notes = piece_refs[1][slots * rows :, :].astype(f32)
    depth_at = iota((edge, lanes), 0)
    lane_at = iota((edge, lanes), 1)
    masks = []
    for parity in range(2):
        for slot in range(slots):
            if parity == 0:
                depth = corners_ref[slot, 0] - tile_index * TZ
                start = corners_ref[slot, 2] * classes
            else:
                depth = notes[2 * slot : 2 * slot + 1].astype(jnp.int32)
                start = notes[2 * slot + 1 : 2 * slot + 2].astype(jnp.int32) * classes
            keep = depth_at >= depth
            inside = []
            for block in range(blocks):
                lane = lane_at + block * lanes
                inside.append((lane >= start) & (lane < start + lanes))
            masks.append((keep, inside))

    for across in range(chunk):
        own = [jnp.zeros((edge, lanes), f32) for _ in range(blocks)]
        spill = [jnp.zeros((edge, lanes), f32) for _ in range(blocks)]
        for parity in range(2):
            for slot in range(slots):
                at = slot * rows + across * edge
                piece = None
                for peer in range(parity, peers, 2):
                    part = piece_refs[peer][at : at + edge, :].astype(f32)
                    piece = part if piece is None else piece + part
                keep, inside = masks[parity * slots + slot]
                upper = jnp.where(keep, piece, 0.0)
                lower = jnp.where(keep, 0.0, piece)
                for block in range(blocks):
                    own[block] = own[block] + jnp.where(inside[block], upper, 0.0)
                    spill[block] = spill[block] + jnp.where(inside[block], lower, 0.0)
        own = jnp.concatenate(own, axis=1)[:, : VY * classes]
        spill = jnp.concatenate(spill, axis=1)[:, : VY * classes]
        own_ref[across] = own
        spill_ref[across] = spill.astype(bf16)


def join_kernel(own_ref, arrived_ref, out_ref):
    has_below = (lax.axis_index("tiles") > 0).astype(f32)
    out_ref[...] = own_ref[...] + arrived_ref[...].astype(f32) * has_below


vmem = pl.BlockSpec(memory_space=pltpu.VMEM)
smem = pl.BlockSpec(memory_space=pltpu.SMEM)
hbm = pl.BlockSpec(memory_space=pltpu.HBM)
limits = pltpu.CompilerParams(vmem_limit_bytes=vmem_bytes)
ample = pltpu.CompilerParams(vmem_limit_bytes=60000000)


def on_device(
    features,
    conv_first,
    gain_first,
    shift_first,
    conv_second,
    gain_second,
    shift_second,
    head_weight,
    head_bias,
    corners,
    counts,
):
    _, slots, edge, _, data = features.shape
    in_width, width = conv_first.shape[-2:]
    classes = head_bias.shape[1]
    peers = lax.axis_size("folds") * lax.axis_size("sub")
    chunk = VX // peers
    area = edge * edge
    padded_rows = slots * (area + edge) + edge
    margin = 128

    lanes = edge * classes
    piece = slots * edge * chunk
    rows = [piece + edge if peer == 1 else piece for peer in range(peers)]
    pieces = pl.pallas_call(
        functools.partial(section_kernel, (slots, edge, chunk, peers)),
        out_shape=[jax.ShapeDtypeStruct((count, lanes), bf16) for count in rows],
        in_specs=[hbm] * 11,
        out_specs=[vmem] * peers,
        scratch_shapes=[
            pltpu.VMEM((padded_rows, data + 2 * margin), bf16),
            pltpu.VMEM((padded_rows, edge * width + 2 * margin), bf16),
            pltpu.VMEM((3, 3 * (half * in_width + 2 * margin), half * width), bf16),
            pltpu.VMEM((3, 3 * (half * width + 2 * margin), half * width), bf16),
            pltpu.VMEM((padded_rows - 2 * edge, edge * width), f32),
            pltpu.SMEM(corners.shape, jnp.int32),
            pltpu.SMEM(counts.shape[::-1], jnp.int32),
            pltpu.VMEM((27 * width, in_width), bf16),
            pltpu.VMEM((1, width), f32),
            pltpu.VMEM((1, width), f32),
            pltpu.VMEM((27 * width, width), bf16),
            pltpu.VMEM((1, width), f32),
            pltpu.VMEM((1, width), f32),
            pltpu.VMEM((classes, width), bf16),
            pltpu.VMEM((1, classes), f32),
            pltpu.SemaphoreType.DMA((slots,)),
            pltpu.SemaphoreType.DMA((10,)),
        ],
        compiler_params=ample,
        name="section",
    )(
        corners,
        counts.T,
        features.reshape(slots, area, data),
        jnp.swapaxes(conv_first, 4, 5).reshape(27 * width, in_width),
        gain_first,
        shift_first,
        conv_second.reshape(27 * width, width),
        gain_second,
        shift_second,
        head_weight[0].T,
        head_bias,
    )
    arrived = [pieces[0]]
    for peer in range(1, peers):
        pairs = [(i, i ^ peer) for i in range(peers)]
        arrived.append(lax.ppermute(pieces[peer], ("folds", "sub"), pairs))

    own, spill = pl.pallas_call(
        functools.partial(gather_kernel, (slots, edge, chunk, peers, classes)),
        out_shape=[
            jax.ShapeDtypeStruct((chunk, TZ, VY * classes), f32),
            jax.ShapeDtypeStruct((chunk, edge, VY * classes), bf16),
        ],
        in_specs=[smem] + [vmem] * peers,
        out_specs=[vmem, vmem],
        compiler_params=limits,
        name="gather",
    )(corners, *arrived)

    tiles = lax.axis_size("tiles")
    from_below = lax.ppermute(spill, "tiles", [(i, (i + 1) % tiles) for i in range(tiles)])
    joined = pl.pallas_call(
        join_kernel,
        out_shape=jax.ShapeDtypeStruct((chunk, TZ, VY * classes), f32),
        in_specs=[vmem, vmem],
        out_specs=vmem,
        compiler_params=limits,
        name="join",
    )(own, from_below)
    return jnp.transpose(joined, (1, 0, 2))


def solution(mesh):
    placed = (
        P("folds", ("groups", "tiles", "sub"), None, None, None),
        P("folds", None, None, None, None, None),
        P("folds", None),
        P("folds", None),
        P("folds", None, None, None, None, None),
        P("folds", None),
        P("folds", None),
        P("folds", None, None),
        P("folds", None),
        P(("groups", "tiles", "sub"), None),
        P("groups", None),
    )
    return jax.shard_map(
        on_device,
        mesh=mesh,
        in_specs=placed,
        out_specs=P(("groups", "tiles"), ("folds", "sub"), None),
        check_vma=False,
    )
```

```python
import functools

import jax
import jax.numpy as jnp
from jax import lax
from jax.experimental import pallas as pl
from jax.experimental.pallas import tpu as pltpu
from jax.sharding import PartitionSpec as P

TZ = 16
VX = 40
VY = 40

epsilon = 1e-05
leak_slope = 0.01
far = 1 << 20
bf16 = jnp.bfloat16
f32 = jnp.float32
vmem_bytes = 48 << 20


def iota(shape, dim):
    return lax.broadcasted_iota(jnp.int32, shape, dim)


def tile_matrix(width, lanes):
    return (iota((width, lanes), 1) % width == iota((width, lanes), 0)).astype(bf16)


def tiled_row(ref, lanes):
    width = ref.shape[1]
    row = jnp.concatenate([ref[...], jnp.zeros((1, lanes - width), f32)], axis=1)
    row = jnp.broadcast_to(row, (8, lanes))
    reach = width
    while reach < lanes:
        row = row + pltpu.roll(row, reach, 1)
        reach *= 2
    return row[0:1]


def lane_bands(parts, places):
    total = None
    for place, part in enumerate(parts):
        if part is not None:
            held = part if total is None else jnp.where(places == place, part, total)
            first = place if total is None else first
            total = held
    if total is None:
        return None
    if any(part is None for part in parts):
        empty = None
        for place, part in enumerate(parts):
            if part is None:
                here = places == place
                empty = here if empty is None else empty | here
        total = jnp.where(empty, 0.0, total)
    return total


def build_first(taps_ref, band_ref, in_width, width):
    spread = tile_matrix(width, 128)
    places = iota((in_width, 128), 1) // width
    zero = jnp.zeros((in_width, 128), bf16)
    orders = (((1, 0), (2, None)), ((0, 1), (None, 2)))
    for dz in range(3):
        tiled = {}
        for dx in range(3):
            for dy in range(3):
                at = ((dz * 3 + dx) * 3 + dy) * width
                tiled[dx, dy] = lax.dot_general(
                    taps_ref[at : at + width],
                    spread,
                    (((0,), (0,)), ((), ())),
                    preferred_element_type=f32,
                )
        for variant in range(2):
            for yi in range(4):
                for side in range(2):
                    parts = []
                    for dx in orders[variant][side]:
                        for yo in range(2):
                            parts.append(None if dx is None else tiled.get((dx, yi - yo)))
                    block = lane_bands(parts, places)
                    band_ref[
                        variant,
                        dz,
                        yi * in_width : (yi + 1) * in_width,
                        side * 128 : (side + 1) * 128,
                    ] = zero if block is None else block.astype(bf16)


def build_second(taps_ref, band_ref, width):
    spread = tile_matrix(width, 128)
    places = iota((width, 128), 1) // width
    zero = jnp.zeros((width, 128), bf16)
    for dz in range(3):
        at = dz * 9 * width
        tiled = jnp.dot(taps_ref[at : at + 9 * width], spread, preferred_element_type=f32)
        for dx in range(3):
            taps = {
                dy: tiled[(dx * 3 + dy) * width : (dx * 3 + dy + 1) * width] for dy in range(3)
            }
            for yi in range(8):
                block = lane_bands([taps.get(yi - yo) for yo in range(4)], places)
                band_ref[dz, yi * width : (yi + 1) * width, dx * 128 : (dx + 1) * 128] = (
                    zero if block is None else block.astype(bf16)
                )


def banded(pad_ref, lane, area, edge, bands):
    total = None
    for dz in range(3):
        part = jnp.dot(
            pad_ref[dz * edge : dz * edge + area, lane : lane + 256],
            bands(dz),
            preferred_element_type=f32,
        )
        total = part if total is None else total + part
    return total


def join_across(before, here, after, across, edge):
    rows = here.shape[0]
    before = jnp.where(across == 0, 0.0, pltpu.roll(before, 1, 0))
    after = jnp.where(across == edge - 1, 0.0, pltpu.roll(after, rows - 1, 0))
    return here + before + after


def channel_mean(values, width, voxels):
    row = jnp.sum(values, axis=0, keepdims=True)
    folded = row[:, :128]
    for at in range(128, row.shape[1], 128):
        folded = folded + row[:, at : at + 128]
    folded = jnp.broadcast_to(folded, (8, 128))
    reach = width
    while reach < 128:
        folded = folded + pltpu.roll(folded, reach, 1)
        reach *= 2
    return folded[0:1] * (1.0 / voxels)


def repeated(row, lanes):
    return jnp.concatenate([row] * (lanes // 128), axis=1)


def normalize(hidden, gain, shift, width, voxels, valid):
    lanes = hidden.shape[1]
    centered = hidden - repeated(channel_mean(hidden, width, voxels), lanes)
    if valid is not None:
        centered = jnp.where(valid, centered, 0.0)
    variance = channel_mean(centered * centered, width, voxels)
    factor = lax.rsqrt(variance + epsilon) * gain
    scaled = centered * repeated(factor, lanes) + repeated(shift, lanes)
    scaled = jnp.maximum(scaled, leak_slope * scaled)
    if valid is not None:
        scaled = jnp.where(valid, scaled, 0.0)
    return scaled.astype(bf16)


def section_kernel(
    sizes,
    corners_hbm,
    counts_hbm,
    features_ref,
    taps_one_hbm,
    gain_one_hbm,
    shift_one_hbm,
    taps_two_hbm,
    gain_two_hbm,
    shift_two_hbm,
    head_hbm,
    bias_hbm,
    *rest,
):
    slot, edge, chunk, peers = sizes
    out_refs = rest[:peers]
    (
        pad_one,
        pad_two,
        band_one,
        band_two,
        hidden,
        corners_ref,
        counts_ref,
        taps_one_ref,
        gain_one_ref,
        shift_one_ref,
        taps_two_ref,
        gain_two_ref,
        shift_two_ref,
        head_ref,
        bias_ref,
        sems,
    ) = rest[peers:]
    in_width = taps_one_ref.shape[1]
    classes, width = head_ref.shape
    area = edge * edge
    voxels = float(area * edge)
    data = edge * in_width
    lanes = edge * classes

    copies = []
    for at, (source, target) in enumerate(
        (
            (taps_one_hbm, taps_one_ref),
            (taps_two_hbm, taps_two_ref),
            (gain_one_hbm, gain_one_ref),
            (shift_one_hbm, shift_one_ref),
            (gain_two_hbm, gain_two_ref),
            (shift_two_hbm, shift_two_ref),
            (head_hbm, head_ref),
            (bias_hbm, bias_ref),
            (corners_hbm, corners_ref),
            (counts_hbm, counts_ref),
            (features_ref.at[slot], pad_one.at[pl.ds(edge, area), pl.ds(128, data)]),
        )
    ):
        copy = pltpu.make_async_copy(source, target, sems.at[at])
        copy.start()
        copies.append(copy)
    for pad in (pad_one, pad_two):
        pad[:edge, :] = jnp.zeros((edge, pad.shape[1]), bf16)
        pad[edge + area :, :] = jnp.zeros((edge, pad.shape[1]), bf16)
    pad_one[:, :128] = jnp.zeros((pad_one.shape[0], 128), bf16)
    pad_one[:, 128 + data :] = jnp.zeros((pad_one.shape[0], 128), bf16)

    center, spread = (edge - 1) / 2.0, edge / 4.0

    def profile(offset):
        return jnp.exp(-((offset.astype(f32) - center) ** 2) / (2.0 * spread * spread))

    row_at = iota((area, lanes), 0)
    lane_at = iota((1, lanes), 1)
    gauss = profile(row_at // edge) * profile(row_at % edge) * profile(lane_at // classes)

    row = iota((chunk * edge, area), 0)
    source = iota((chunk * edge, area), 1)
    turn = (row % edge - source // edge) & (edge - 1)
    code = turn + edge * (source % edge - row // edge)
    across = iota((area, 128), 0) % edge
    tile_index = lax.axis_index("tiles")
    sub_index = lax.axis_index("sub")
    position = lax.axis_index("folds") * lax.axis_size("sub") + sub_index

    for copy in copies[:-1]:
        copy.wait()
    build_first(taps_one_ref, band_one, in_width, width)
    build_second(taps_two_ref, band_two, width)
    gain_one, shift_one = tiled_row(gain_one_ref, 128), tiled_row(shift_one_ref, 128)
    gain_two, shift_two = tiled_row(gain_two_ref, 128), tiled_row(shift_two_ref, 128)

    half = edge // 2
    head_row = lax.dot_general(
        head_ref[...],
        tile_matrix(classes, half * classes),
        (((0,), (0,)), ((), ())),
        preferred_element_type=f32,
    )
    block = (half * width, half * classes)
    head_block = jnp.where(
        iota(block, 0) // width == iota(block, 1) // classes,
        jnp.concatenate([head_row] * half, axis=0),
        0.0,
    ).astype(bf16)
    bias = tiled_row(bias_ref, lanes)

    depth = corners_ref[slot, 0] - tile_index * TZ
    lane_start = corners_ref[slot, 2] * classes
    mark = iota((edge, lanes), 0)
    notes = jnp.where(mark == 0, depth.astype(f32), 0.0)
    notes = jnp.where(mark == 1, corners_ref[slot, 2].astype(f32), notes).astype(bf16)
    for peer in range(2):
        out_refs[peer][edge * chunk :, :] = notes

    copies[-1].wait()
    low = iota((area, 128), 1) < 64
    for pair in range(edge // 4 + 1):
        even = banded(pad_one, 256 * pair, area, edge, lambda dz: band_one[0, dz])
        if pair < edge // 4:
            odd = banded(pad_one, 256 * pair + 128, area, edge, lambda dz: band_one[1, dz])
            here = jnp.where(low, even[:, :128], odd[:, :128])
            before = jnp.where(low, odd[:, :128], even[:, :128])
            after = even[:, 128:] + odd[:, 128:]
        else:
            here = jnp.where(low, even[:, :128], 0.0)
            before = jnp.where(low, 0.0, even[:, :128])
            after = even[:, 128:]
        before = pltpu.roll(before, 64, 1)
        hidden[:, pair * 128 : (pair + 1) * 128] = join_across(before, here, after, across, edge)
    wide = hidden.shape[1]
    spot = iota((area, wide), 1)
    valid = (spot >= width) & (spot < (edge + 1) * width)
    first = jnp.where(valid, hidden[...], 0.0)
    pad_two[edge : edge + area, :] = normalize(first, gain_one, shift_one, width, voxels, valid)

    for quad in range(edge // 4):
        three = banded(pad_two, 128 * quad, area, edge, lambda dz: band_two[dz])
        hidden[:, quad * 128 : (quad + 1) * 128] = join_across(
            three[:, :128], three[:, 128:256], three[:, 256:], across, edge
        )
    normed = normalize(hidden[:, : edge * width], gain_two, shift_two, width, voxels, None)
    logits = jnp.concatenate(
        [
            jnp.dot(normed[:, : half * width], head_block, preferred_element_type=f32),
            jnp.dot(normed[:, half * width :], head_block, preferred_element_type=f32),
        ],
        axis=1,
    )
    weighted = (logits + bias) * gauss
    weighted = pltpu.roll(weighted, lane_start % lanes, 1).astype(bf16)
    alive = slot < counts_ref[sub_index, tile_index]
    for peer in range(peers):
        wanted = depth + edge * ((position ^ peer) * chunk - corners_ref[slot, 1])
        wanted = jnp.where(alive, wanted, far)
        select = (code == wanted).astype(f32).astype(bf16)
        out_refs[peer][: edge * chunk, :] = jnp.dot(
            select, weighted, preferred_element_type=f32
        ).astype(bf16)


def gather_kernel(sizes, *rest):
    slots, edge, chunk, peers, classes = sizes
    out_ref = rest[-1]
    rows = edge * chunk
    lanes = edge * classes
    blocks = -(-VY * classes // lanes)
    depth_at = iota((edge, lanes), 0)
    lane_at = iota((edge, lanes), 1)

    groups = []
    for slot in range(slots):
        for below in range(2):
            refs = rest[(slot * 2 + below) * peers : (slot * 2 + below + 1) * peers]
            for parity in range(2):
                notes = refs[parity][rows:, :].astype(f32).astype(jnp.int32)
                keep = depth_at < notes[0:1] if below else depth_at >= notes[0:1]
                start = notes[1:2] * classes
                inside = []
                for block in range(blocks):
                    lane = lane_at + block * lanes
                    inside.append((lane >= start) & (lane < start + lanes))
                groups.append((refs[parity::2], keep, inside))

    for across in range(chunk):
        total = [jnp.zeros((edge, lanes), f32) for _ in range(blocks)]
        for refs, keep, inside in groups:
            piece = None
            for ref in refs:
                part = ref[across * edge : (across + 1) * edge, :].astype(f32)
                piece = part if piece is None else piece + part
            piece = jnp.where(keep, piece, 0.0)
            for block in range(blocks):
                total[block] = total[block] + jnp.where(inside[block], piece, 0.0)
        out_ref[across] = jnp.concatenate(total, axis=1)[:, : VY * classes]


vmem = pl.BlockSpec(memory_space=pltpu.VMEM)
hbm = pl.BlockSpec(memory_space=pltpu.HBM)
limits = pltpu.CompilerParams(vmem_limit_bytes=vmem_bytes)
ample = pltpu.CompilerParams(vmem_limit_bytes=60000000)


def on_device(
    features,
    conv_first,
    gain_first,
    shift_first,
    conv_second,
    gain_second,
    shift_second,
    head_weight,
    head_bias,
    corners,
    counts,
):
    _, slots, edge, _, data = features.shape
    in_width, width = conv_first.shape[-2:]
    classes = head_bias.shape[1]
    peers = lax.axis_size("folds") * lax.axis_size("sub")
    tiles = lax.axis_size("tiles")
    chunk = VX // peers
    area = edge * edge
    lanes = edge * classes
    piece = edge * chunk
    rows = [piece + edge if peer < 2 else piece for peer in range(peers)]
    operands = (
        corners,
        counts.T,
        features.reshape(slots, area, data),
        jnp.swapaxes(conv_first, 4, 5).reshape(27 * width, in_width),
        gain_first,
        shift_first,
        conv_second.reshape(27 * width, width),
        gain_second,
        shift_second,
        head_weight[0].T,
        head_bias,
    )
    received = []
    for slot in range(slots):
        pieces = pl.pallas_call(
            functools.partial(section_kernel, (slot, edge, chunk, peers)),
            out_shape=[jax.ShapeDtypeStruct((count, lanes), bf16) for count in rows],
            in_specs=[hbm] * 11,
            out_specs=[vmem] * peers,
            scratch_shapes=[
                pltpu.VMEM((area + 2 * edge, data + 256), bf16),
                pltpu.VMEM((area + 2 * edge, edge * width + 128), bf16),
                pltpu.VMEM((2, 3, 256, 256), bf16),
                pltpu.VMEM((3, 256, 384), bf16),
                pltpu.VMEM((area, edge * width + 128), f32),
                pltpu.SMEM(corners.shape, jnp.int32),
                pltpu.SMEM(counts.shape[::-1], jnp.int32),
                pltpu.VMEM((27 * width, in_width), bf16),
                pltpu.VMEM((1, width), f32),
                pltpu.VMEM((1, width), f32),
                pltpu.VMEM((27 * width, width), bf16),
                pltpu.VMEM((1, width), f32),
                pltpu.VMEM((1, width), f32),
                pltpu.VMEM((classes, width), bf16),
                pltpu.VMEM((1, classes), f32),
                pltpu.SemaphoreType.DMA((11,)),
            ],
            compiler_params=ample,
            cost_estimate=pl.CostEstimate(
                flops=6000000000, bytes_accessed=3000000, transcendentals=0
            ),
            name=f"section_{slot}",
        )(*operands)
        own, below = [], []
        for peer in range(peers):
            pairs = [(i, i ^ peer) for i in range(peers)]
            onward = [
                (tile * peers + i, (tile + 1) * peers + (i ^ peer))
                for tile in range(tiles - 1)
                for i in range(peers)
            ]
            own.append(
                lax.ppermute(pieces[peer], ("folds", "sub"), pairs) if peer else pieces[peer]
            )
            below.append(lax.ppermute(pieces[peer], ("tiles", "folds", "sub"), onward))
        received += own + below

    joined = pl.pallas_call(
        functools.partial(gather_kernel, (slots, edge, chunk, peers, classes)),
        out_shape=jax.ShapeDtypeStruct((chunk, TZ, VY * classes), f32),
        in_specs=[vmem] * len(received),
        out_specs=vmem,
        compiler_params=limits,
        name="gather",
    )(*received)
    return jnp.transpose(joined, (1, 0, 2))


def solution(mesh):
    placed = (
        P("folds", ("groups", "tiles", "sub"), None, None, None),
        P("folds", None, None, None, None, None),
        P("folds", None),
        P("folds", None),
        P("folds", None, None, None, None, None),
        P("folds", None),
        P("folds", None),
        P("folds", None, None),
        P("folds", None),
        P(("groups", "tiles", "sub"), None),
        P("groups", None),
    )
    return jax.shard_map(
        on_device,
        mesh=mesh,
        in_specs=placed,
        out_specs=P(("groups", "tiles"), ("folds", "sub"), None),
        check_vma=False,
    )
```

```python
import functools

import jax
import jax.numpy as jnp
from jax import lax
from jax.experimental import pallas as pl
from jax.experimental.pallas import tpu as pltpu
from jax.sharding import PartitionSpec as P

TZ = 16
VX = 40
VY = 40

epsilon = 1e-05
leak_slope = 0.01
far = 1 << 20
bf16 = jnp.bfloat16
f32 = jnp.float32
vmem_bytes = 48 << 20


def iota(shape, dim):
    return lax.broadcasted_iota(jnp.int32, shape, dim)


def tile_matrix(width, lanes):
    return (iota((width, lanes), 1) % width == iota((width, lanes), 0)).astype(bf16)


def tiled_row(ref, lanes):
    width = ref.shape[1]
    row = jnp.concatenate([ref[...], jnp.zeros((1, lanes - width), f32)], axis=1)
    row = jnp.broadcast_to(row, (8, lanes))
    reach = width
    while reach < lanes:
        row = row + pltpu.roll(row, reach, 1)
        reach *= 2
    return row[0:1]


def lane_bands(parts, places):
    total = None
    for place, part in enumerate(parts):
        if part is not None:
            total = part if total is None else jnp.where(places == place, part, total)
    if total is None:
        return None
    if any(part is None for part in parts):
        empty = None
        for place, part in enumerate(parts):
            if part is None:
                here = places == place
                empty = here if empty is None else empty | here
        total = jnp.where(empty, 0.0, total)
    return total


def build_first(taps_ref, band_ref, in_width, width):
    spread = tile_matrix(width, 128)
    places = iota((in_width, 128), 1) // width
    zero = jnp.zeros((in_width, 128), bf16)
    orders = (((1, 0), (2, None)), ((0, 1), (None, 2)))
    for dz in range(3):
        tiled = {}
        for dx in range(3):
            for dy in range(3):
                at = ((dz * 3 + dx) * 3 + dy) * width
                tiled[dx, dy] = lax.dot_general(
                    taps_ref[at : at + width],
                    spread,
                    (((0,), (0,)), ((), ())),
                    preferred_element_type=f32,
                )
        for variant in range(2):
            for yi in range(4):
                for side in range(2):
                    parts = []
                    for dx in orders[variant][side]:
                        for yo in range(2):
                            parts.append(None if dx is None else tiled.get((dx, yi - yo)))
                    block = lane_bands(parts, places)
                    band_ref[
                        variant,
                        dz,
                        yi * in_width : (yi + 1) * in_width,
                        side * 128 : (side + 1) * 128,
                    ] = zero if block is None else block.astype(bf16)


def build_second(taps_ref, band_ref, width):
    spread = tile_matrix(width, 128)
    places = iota((width, 128), 1) // width
    zero = jnp.zeros((width, 128), bf16)
    for dz in range(3):
        at = dz * 9 * width
        tiled = jnp.dot(taps_ref[at : at + 9 * width], spread, preferred_element_type=f32)
        for dx in range(3):
            taps = {
                dy: tiled[(dx * 3 + dy) * width : (dx * 3 + dy + 1) * width] for dy in range(3)
            }
            for yi in range(8):
                block = lane_bands([taps.get(yi - yo) for yo in range(4)], places)
                band_ref[dz, yi * width : (yi + 1) * width, dx * 128 : (dx + 1) * 128] = (
                    zero if block is None else block.astype(bf16)
                )


def banded(pad_ref, lane, count, edge, bands):
    total = None
    for dz in range(3):
        part = jnp.dot(
            pad_ref[dz * edge : dz * edge + count, lane : lane + 256],
            bands(dz),
            preferred_element_type=f32,
        )
        total = part if total is None else total + part
    return total


def join_across(before, here, after, across, edge):
    rows = here.shape[0]
    before = jnp.where(across == 0, 0.0, pltpu.roll(before, 1, 0))
    after = jnp.where(across == edge - 1, 0.0, pltpu.roll(after, rows - 1, 0))
    return here + before + after


def channel_mean(blocks, width, voxels):
    folded = None
    for block in blocks:
        row = jnp.sum(block, axis=0, keepdims=True)
        folded = row if folded is None else folded + row
    folded = jnp.broadcast_to(folded, (8, 128))
    reach = width
    while reach < 128:
        folded = folded + pltpu.roll(folded, reach, 1)
        reach *= 2
    return folded[0:1] * (1.0 / voxels)


def normalize(blocks, masks, gain, shift, width, voxels):
    mean_value = channel_mean(blocks, width, voxels)
    centered = []
    for block, mask in zip(blocks, masks):
        moved = block - mean_value
        centered.append(moved if mask is None else jnp.where(mask, moved, 0.0))
    variance = channel_mean([moved * moved for moved in centered], width, voxels)
    factor = lax.rsqrt(variance + epsilon) * gain
    results = []
    for moved, mask in zip(centered, masks):
        scaled = moved * factor + shift
        scaled = jnp.maximum(scaled, leak_slope * scaled)
        results.append((scaled if mask is None else jnp.where(mask, scaled, 0.0)).astype(bf16))
    return results


def section_kernel(
    sizes,
    corners_hbm,
    counts_hbm,
    features_ref,
    taps_one_hbm,
    gain_one_hbm,
    shift_one_hbm,
    taps_two_hbm,
    gain_two_hbm,
    shift_two_hbm,
    head_hbm,
    bias_hbm,
    *rest,
):
    slots, edge, chunk, peers = sizes
    out_refs = rest[:peers]
    (
        pad_one,
        pad_two,
        band_one,
        band_two,
        hidden,
        corners_ref,
        counts_ref,
        taps_one_ref,
        gain_one_ref,
        shift_one_ref,
        taps_two_ref,
        gain_two_ref,
        shift_two_ref,
        head_ref,
        bias_ref,
        sems,
    ) = rest[peers:]
    in_width = taps_one_ref.shape[1]
    classes, width = head_ref.shape
    area = edge * edge
    stride = area + edge
    count = hidden.shape[0]
    voxels = float(area * edge)
    data = edge * in_width
    lanes = edge * classes

    copies = []
    for at, (source, target) in enumerate(
        [
            (taps_one_hbm, taps_one_ref),
            (taps_two_hbm, taps_two_ref),
            (gain_one_hbm, gain_one_ref),
            (shift_one_hbm, shift_one_ref),
            (gain_two_hbm, gain_two_ref),
            (shift_two_hbm, shift_two_ref),
            (head_hbm, head_ref),
            (bias_hbm, bias_ref),
            (corners_hbm, corners_ref),
            (counts_hbm, counts_ref),
        ]
        + [
            (
                features_ref.at[slot],
                pad_one.at[pl.ds(edge + slot * stride, area), pl.ds(128, data)],
            )
            for slot in range(slots)
        ]
    ):
        copy = pltpu.make_async_copy(source, target, sems.at[at])
        copy.start()
        copies.append(copy)
    for pad in (pad_one, pad_two):
        for slot in range(slots + 1):
            pad[slot * stride : slot * stride + edge, :] = jnp.zeros((edge, pad.shape[1]), bf16)
    pad_one[:, :128] = jnp.zeros((pad_one.shape[0], 128), bf16)
    pad_one[:, 128 + data :] = jnp.zeros((pad_one.shape[0], 128), bf16)

    center, spread = (edge - 1) / 2.0, edge / 4.0

    def profile(offset):
        return jnp.exp(-((offset.astype(f32) - center) ** 2) / (2.0 * spread * spread))

    row_at = iota((area, 128), 0)
    lane_at = iota((1, lanes), 1)
    gauss = profile(row_at // edge) * profile(row_at % edge)
    gauss = jnp.concatenate([gauss] * (lanes // 128), axis=1) * profile(lane_at // classes)

    row = iota((chunk * edge, area), 0)
    source = iota((chunk * edge, area), 1)
    turn = (row % edge - source // edge) & (edge - 1)
    code = turn + edge * (source % edge - row // edge)
    across = iota((count, 128), 0) % edge
    tile_index = lax.axis_index("tiles")
    sub_index = lax.axis_index("sub")
    position = lax.axis_index("folds") * lax.axis_size("sub") + sub_index

    for copy in copies[:-slots]:
        copy.wait()
    build_first(taps_one_ref, band_one, in_width, width)
    build_second(taps_two_ref, band_two, width)
    gain_one, shift_one = tiled_row(gain_one_ref, 128), tiled_row(shift_one_ref, 128)
    gain_two, shift_two = tiled_row(gain_two_ref, 128), tiled_row(shift_two_ref, 128)

    half = edge // 2
    head_row = lax.dot_general(
        head_ref[...],
        tile_matrix(classes, half * classes),
        (((0,), (0,)), ((), ())),
        preferred_element_type=f32,
    )
    block = (half * width, half * classes)
    head_block = jnp.where(
        iota(block, 0) // width == iota(block, 1) // classes,
        jnp.concatenate([head_row] * half, axis=0),
        0.0,
    ).astype(bf16)
    bias = tiled_row(bias_ref, lanes)

    mark = iota((edge, lanes), 0)
    notes = jnp.zeros((edge, lanes), f32)
    for slot in range(slots):
        depth = corners_ref[slot, 0] - tile_index * TZ
        notes = jnp.where(mark == 2 * slot, depth.astype(f32), notes)
        notes = jnp.where(mark == 2 * slot + 1, corners_ref[slot, 2].astype(f32), notes)
    out_refs[1][slots * edge * chunk :, :] = notes.astype(bf16)

    for copy in copies[-slots:]:
        copy.wait()
    low = iota((count, 128), 1) < 64
    spot = iota((area, 128), 1)
    pairs = edge // 4 + 1
    for pair in range(pairs):
        even = banded(pad_one, 256 * pair, count, edge, lambda dz: band_one[0, dz])
        if pair < pairs - 1:
            odd = banded(pad_one, 256 * pair + 128, count, edge, lambda dz: band_one[1, dz])
            here = jnp.where(low, even[:, :128], odd[:, :128])
            before = jnp.where(low, odd[:, :128], even[:, :128])
            after = even[:, 128:] + odd[:, 128:]
        else:
            here = jnp.where(low, even[:, :128], 0.0)
            before = jnp.where(low, 0.0, even[:, :128])
            after = even[:, 128:]
        before = pltpu.roll(before, 64, 1)
        hidden[:, pair * 128 : (pair + 1) * 128] = join_across(before, here, after, across, edge)
    masks = [None] * pairs
    masks[0] = spot >= width
    masks[-1] = spot < width
    for slot in range(slots):
        at = slot * stride
        blocks = [hidden[at : at + area, pair * 128 : (pair + 1) * 128] for pair in range(pairs)]
        blocks[0] = jnp.where(masks[0], blocks[0], 0.0)
        blocks[-1] = jnp.where(masks[-1], blocks[-1], 0.0)
        normed = normalize(blocks, masks, gain_one, shift_one, width, voxels)
        for pair in range(pairs):
            pad_two[at + edge : at + edge + area, pair * 128 : (pair + 1) * 128] = normed[pair]

    quads = edge // 4
    for quad in range(quads):
        three = banded(pad_two, 128 * quad, count, edge, lambda dz: band_two[dz])
        hidden[:, quad * 128 : (quad + 1) * 128] = join_across(
            three[:, :128], three[:, 128:256], three[:, 256:], across, edge
        )
    for slot in range(slots):
        at = slot * stride
        blocks = [hidden[at : at + area, quad * 128 : (quad + 1) * 128] for quad in range(quads)]
        normed = normalize(blocks, [None] * quads, gain_two, shift_two, width, voxels)
        logits = jnp.concatenate(
            [
                jnp.dot(
                    jnp.concatenate(normed[side : side + quads // 2], axis=1),
                    head_block,
                    preferred_element_type=f32,
                )
                for side in (0, quads // 2)
            ],
            axis=1,
        )
        weighted = (logits + bias) * gauss
        lane_start = corners_ref[slot, 2] * classes
        weighted = pltpu.roll(weighted, lane_start % lanes, 1).astype(bf16)
        depth = corners_ref[slot, 0] - tile_index * TZ
        alive = slot < counts_ref[sub_index, tile_index]
        for peer in range(peers):
            wanted = depth + edge * ((position ^ peer) * chunk - corners_ref[slot, 1])
            wanted = jnp.where(alive, wanted, far)
            select = (code == wanted).astype(f32).astype(bf16)
            out_refs[peer][slot * edge * chunk : (slot + 1) * edge * chunk, :] = jnp.dot(
                select, weighted, preferred_element_type=f32
            ).astype(bf16)


def gather_kernel(sizes, corners_ref, *rest):
    slots, edge, chunk, peers, classes = sizes
    piece_refs = rest[:peers]
    own_ref, spill_ref = rest[peers:]
    rows = edge * chunk
    lanes = edge * classes
    tile_index = lax.axis_index("tiles")
    blocks = -(-VY * classes // lanes)

    notes = piece_refs[1][slots * rows :, :].astype(f32)
    depth_at = iota((edge, lanes), 0)
    lane_at = iota((edge, lanes), 1)
    masks = []
    for parity in range(2):
        for slot in range(slots):
            if parity == 0:
                depth = corners_ref[slot, 0] - tile_index * TZ
                start = corners_ref[slot, 2] * classes
            else:
                depth = notes[2 * slot : 2 * slot + 1].astype(jnp.int32)
                start = notes[2 * slot + 1 : 2 * slot + 2].astype(jnp.int32) * classes
            keep = depth_at >= depth
            inside = []
            for block in range(blocks):
                lane = lane_at + block * lanes
                inside.append((lane >= start) & (lane < start + lanes))
            masks.append((keep, inside))

    for across in range(chunk):
        own = [jnp.zeros((edge, lanes), f32) for _ in range(blocks)]
        spill = [jnp.zeros((edge, lanes), f32) for _ in range(blocks)]
        for parity in range(2):
            for slot in range(slots):
                at = slot * rows + across * edge
                piece = None
                for peer in range(parity, peers, 2):
                    part = piece_refs[peer][at : at + edge, :].astype(f32)
                    piece = part if piece is None else piece + part
                keep, inside = masks[parity * slots + slot]
                upper = jnp.where(keep, piece, 0.0)
                lower = jnp.where(keep, 0.0, piece)
                for block in range(blocks):
                    own[block] = own[block] + jnp.where(inside[block], upper, 0.0)
                    spill[block] = spill[block] + jnp.where(inside[block], lower, 0.0)
        own = jnp.concatenate(own, axis=1)[:, : VY * classes]
        spill = jnp.concatenate(spill, axis=1)[:, : VY * classes]
        own_ref[across] = own
        spill_ref[across] = spill.astype(bf16)


def join_kernel(own_ref, even_ref, odd_ref, out_ref):
    tile_index = lax.axis_index("tiles")
    from_even = (tile_index % 2 == 1).astype(f32)
    from_odd = ((tile_index % 2 == 0) & (tile_index > 0)).astype(f32)
    out_ref[...] = (
        own_ref[...]
        + even_ref[...].astype(f32) * from_even
        + odd_ref[...].astype(f32) * from_odd
    )


vmem = pl.BlockSpec(memory_space=pltpu.VMEM)
smem = pl.BlockSpec(memory_space=pltpu.SMEM)
hbm = pl.BlockSpec(memory_space=pltpu.HBM)
limits = pltpu.CompilerParams(vmem_limit_bytes=vmem_bytes)
ample = pltpu.CompilerParams(vmem_limit_bytes=60000000)


def on_device(
    features,
    conv_first,
    gain_first,
    shift_first,
    conv_second,
    gain_second,
    shift_second,
    head_weight,
    head_bias,
    corners,
    counts,
):
    _, slots, edge, _, data = features.shape
    in_width, width = conv_first.shape[-2:]
    classes = head_bias.shape[1]
    peers = lax.axis_size("folds") * lax.axis_size("sub")
    tiles = lax.axis_size("tiles")
    chunk = VX // peers
    area = edge * edge
    lanes = edge * classes
    piece = slots * edge * chunk
    padded = slots * (area + edge) + edge
    rows = [piece + edge if peer == 1 else piece for peer in range(peers)]
    pieces = pl.pallas_call(
        functools.partial(section_kernel, (slots, edge, chunk, peers)),
        out_shape=[pltpu.VMEM((count, lanes), bf16) for count in rows],
        in_specs=[hbm] * 11,
        out_specs=[vmem] * peers,
        scratch_shapes=[
            pltpu.VMEM((padded, data + 256), bf16),
            pltpu.VMEM((padded, edge * width + 128), bf16),
            pltpu.VMEM((2, 3, 256, 256), bf16),
            pltpu.VMEM((3, 256, 384), bf16),
            pltpu.VMEM((padded - 2 * edge, edge * width + 128), f32),
            pltpu.SMEM(corners.shape, jnp.int32),
            pltpu.SMEM(counts.shape[::-1], jnp.int32),
            pltpu.VMEM((27 * width, in_width), bf16),
            pltpu.VMEM((1, width), f32),
            pltpu.VMEM((1, width), f32),
            pltpu.VMEM((27 * width, width), bf16),
            pltpu.VMEM((1, width), f32),
            pltpu.VMEM((1, width), f32),
            pltpu.VMEM((classes, width), bf16),
            pltpu.VMEM((1, classes), f32),
            pltpu.SemaphoreType.DMA((10 + slots,)),
        ],
        compiler_params=ample,
        name="section",
    )(
        corners,
        counts.T,
        features.reshape(slots, area, data),
        jnp.swapaxes(conv_first, 4, 5).reshape(27 * width, in_width),
        gain_first,
        shift_first,
        conv_second.reshape(27 * width, width),
        gain_second,
        shift_second,
        head_weight[0].T,
        head_bias,
    )
    arrived = [pieces[0]]
    for peer in range(1, peers):
        pairs = [(i, i ^ peer) for i in range(peers)]
        arrived.append(lax.ppermute(pieces[peer], ("folds", "sub"), pairs))

    own, spill = pl.pallas_call(
        functools.partial(gather_kernel, (slots, edge, chunk, peers, classes)),
        out_shape=[
            jax.ShapeDtypeStruct((chunk, TZ, VY * classes), f32),
            jax.ShapeDtypeStruct((chunk, edge, VY * classes), bf16),
        ],
        in_specs=[smem] + [vmem] * peers,
        out_specs=[vmem, vmem],
        compiler_params=limits,
        name="gather",
    )(corners, *arrived)

    even = [(i, i ^ 1) for i in range(tiles)]
    odd = [(0, 0), (tiles - 1, tiles - 1)] + [
        (i, i + 1 if i % 2 else i - 1) for i in range(1, tiles - 1)
    ]
    joined = pl.pallas_call(
        join_kernel,
        out_shape=jax.ShapeDtypeStruct((chunk, TZ, VY * classes), f32),
        in_specs=[vmem, vmem, vmem],
        out_specs=vmem,
        compiler_params=limits,
        name="join",
    )(own, lax.ppermute(spill, "tiles", even), lax.ppermute(spill, "tiles", odd))
    return jnp.transpose(joined, (1, 0, 2))


def solution(mesh):
    placed = (
        P("folds", ("groups", "tiles", "sub"), None, None, None),
        P("folds", None, None, None, None, None),
        P("folds", None),
        P("folds", None),
        P("folds", None, None, None, None, None),
        P("folds", None),
        P("folds", None),
        P("folds", None, None),
        P("folds", None),
        P(("groups", "tiles", "sub"), None),
        P("groups", None),
    )
    return jax.shard_map(
        on_device,
        mesh=mesh,
        in_specs=placed,
        out_specs=P(("groups", "tiles"), ("folds", "sub"), None),
        check_vma=False,
    )
```

```python
import functools

import jax
import jax.numpy as jnp
from jax import lax
from jax.experimental import pallas as pl
from jax.experimental.pallas import tpu as pltpu
from jax.sharding import PartitionSpec as P

TZ = 16
VX = 40
VY = 40

epsilon = 1e-05
leak_slope = 0.01
far = 1 << 20
bf16 = jnp.bfloat16
f32 = jnp.float32
vmem_bytes = 48 << 20


def iota(shape, dim):
    return lax.broadcasted_iota(jnp.int32, shape, dim)


def tile_matrix(width, lanes):
    return (iota((width, lanes), 1) % width == iota((width, lanes), 0)).astype(bf16)


def tiled_row(ref, lanes):
    width = ref.shape[1]
    row = jnp.concatenate([ref[...], jnp.zeros((1, lanes - width), f32)], axis=1)
    row = jnp.broadcast_to(row, (8, lanes))
    reach = width
    while reach < lanes:
        row = row + pltpu.roll(row, reach, 1)
        reach *= 2
    return row[0:1]


def lane_bands(parts, places):
    total = None
    for place, part in enumerate(parts):
        if part is not None:
            total = part if total is None else jnp.where(places == place, part, total)
    if total is None:
        return None
    if any(part is None for part in parts):
        empty = None
        for place, part in enumerate(parts):
            if part is None:
                here = places == place
                empty = here if empty is None else empty | here
        total = jnp.where(empty, 0.0, total)
    return total


def build_first(taps_ref, band_ref, in_width, width):
    spread = tile_matrix(width, 128)
    places = iota((in_width, 128), 1) // width
    zero = jnp.zeros((in_width, 128), bf16)
    orders = (((1, 0), (2, None)), ((0, 1), (None, 2)))
    for dz in range(3):
        tiled = {}
        for dx in range(3):
            for dy in range(3):
                at = ((dz * 3 + dx) * 3 + dy) * width
                tiled[dx, dy] = lax.dot_general(
                    taps_ref[at : at + width],
                    spread,
                    (((0,), (0,)), ((), ())),
                    preferred_element_type=f32,
                )
        for variant in range(2):
            for yi in range(4):
                for side in range(2):
                    parts = []
                    for dx in orders[variant][side]:
                        for yo in range(2):
                            parts.append(None if dx is None else tiled.get((dx, yi - yo)))
                    block = lane_bands(parts, places)
                    band_ref[
                        variant,
                        dz,
                        yi * in_width : (yi + 1) * in_width,
                        side * 128 : (side + 1) * 128,
                    ] = zero if block is None else block.astype(bf16)


def build_second(taps_ref, band_ref, width):
    spread = tile_matrix(width, 128)
    places = iota((width, 128), 1) // width
    zero = jnp.zeros((width, 128), bf16)
    for dz in range(3):
        at = dz * 9 * width
        tiled = jnp.dot(taps_ref[at : at + 9 * width], spread, preferred_element_type=f32)
        for dx in range(3):
            taps = {
                dy: tiled[(dx * 3 + dy) * width : (dx * 3 + dy + 1) * width] for dy in range(3)
            }
            for yi in range(8):
                block = lane_bands([taps.get(yi - yo) for yo in range(4)], places)
                band_ref[dz, yi * width : (yi + 1) * width, dx * 128 : (dx + 1) * 128] = (
                    zero if block is None else block.astype(bf16)
                )


def banded(pad_ref, lane, count, edge, bands):
    total = None
    for dz in range(3):
        part = jnp.dot(
            pad_ref[dz * edge : dz * edge + count, lane : lane + 256],
            bands(dz),
            preferred_element_type=f32,
        )
        total = part if total is None else total + part
    return total


def join_across(before, here, after, across, edge):
    rows = here.shape[0]
    before = jnp.where(across == 0, 0.0, pltpu.roll(before, 1, 0))
    after = jnp.where(across == edge - 1, 0.0, pltpu.roll(after, rows - 1, 0))
    return here + before + after


def channel_mean(blocks, width, voxels):
    folded = None
    for block in blocks:
        row = jnp.sum(block, axis=0, keepdims=True)
        folded = row if folded is None else folded + row
    folded = jnp.broadcast_to(folded, (8, 128))
    reach = width
    while reach < 128:
        folded = folded + pltpu.roll(folded, reach, 1)
        reach *= 2
    return folded[0:1] * (1.0 / voxels)


def normalize(blocks, masks, gain, shift, width, voxels):
    mean_value = channel_mean(blocks, width, voxels)
    centered = []
    for block, mask in zip(blocks, masks):
        moved = block - mean_value
        centered.append(moved if mask is None else jnp.where(mask, moved, 0.0))
    variance = channel_mean([moved * moved for moved in centered], width, voxels)
    factor = lax.rsqrt(variance + epsilon) * gain
    results = []
    for moved, mask in zip(centered, masks):
        scaled = moved * factor + shift
        scaled = jnp.maximum(scaled, leak_slope * scaled)
        results.append((scaled if mask is None else jnp.where(mask, scaled, 0.0)).astype(bf16))
    return results


def section_kernel(
    sizes,
    corners_hbm,
    counts_hbm,
    features_ref,
    taps_one_hbm,
    gain_one_hbm,
    shift_one_hbm,
    taps_two_hbm,
    gain_two_hbm,
    shift_two_hbm,
    head_hbm,
    bias_hbm,
    *rest,
):
    slots, edge, chunk, peers = sizes
    out_refs = rest[:peers]
    (
        pad_one,
        pad_two,
        band_one,
        band_two,
        hidden,
        corners_ref,
        counts_ref,
        taps_one_ref,
        gain_one_ref,
        shift_one_ref,
        taps_two_ref,
        gain_two_ref,
        shift_two_ref,
        head_ref,
        bias_ref,
        sems,
    ) = rest[peers:]
    in_width = taps_one_ref.shape[1]
    classes, width = head_ref.shape
    area = edge * edge
    stride = area + edge
    count = hidden.shape[0]
    voxels = float(area * edge)
    data = edge * in_width
    lanes = edge * classes

    copies = []
    for at, (source, target) in enumerate(
        [
            (taps_one_hbm, taps_one_ref),
            (taps_two_hbm, taps_two_ref),
            (gain_one_hbm, gain_one_ref),
            (shift_one_hbm, shift_one_ref),
            (gain_two_hbm, gain_two_ref),
            (shift_two_hbm, shift_two_ref),
            (head_hbm, head_ref),
            (bias_hbm, bias_ref),
            (corners_hbm, corners_ref),
            (counts_hbm, counts_ref),
        ]
        + [
            (
                features_ref.at[slot],
                pad_one.at[pl.ds(edge + slot * stride, area), pl.ds(128, data)],
            )
            for slot in range(slots)
        ]
    ):
        copy = pltpu.make_async_copy(source, target, sems.at[at])
        copy.start()
        copies.append(copy)
    for pad in (pad_one, pad_two):
        for slot in range(slots + 1):
            pad[slot * stride : slot * stride + edge, :] = jnp.zeros((edge, pad.shape[1]), bf16)
    pad_one[:, :128] = jnp.zeros((pad_one.shape[0], 128), bf16)
    pad_one[:, 128 + data :] = jnp.zeros((pad_one.shape[0], 128), bf16)

    center, spread = (edge - 1) / 2.0, edge / 4.0

    def profile(offset):
        return jnp.exp(-((offset.astype(f32) - center) ** 2) / (2.0 * spread * spread))

    row_at = iota((area, 128), 0)
    lane_at = iota((1, lanes), 1)
    gauss = profile(row_at // edge) * profile(row_at % edge)
    gauss = jnp.concatenate([gauss] * (lanes // 128), axis=1) * profile(lane_at // classes)

    row = iota((chunk * edge, area), 0)
    source = iota((chunk * edge, area), 1)
    turn = (row % edge - source // edge) & (edge - 1)
    code = turn + edge * (source % edge - row // edge)
    across = iota((count, 128), 0) % edge
    tile_index = lax.axis_index("tiles")
    sub_index = lax.axis_index("sub")
    position = lax.axis_index("folds") * lax.axis_size("sub") + sub_index

    for copy in copies[:-slots]:
        copy.wait()
    build_first(taps_one_ref, band_one, in_width, width)
    build_second(taps_two_ref, band_two, width)
    gain_one, shift_one = tiled_row(gain_one_ref, 128), tiled_row(shift_one_ref, 128)
    gain_two, shift_two = tiled_row(gain_two_ref, 128), tiled_row(shift_two_ref, 128)

    half = edge // 2
    head_row = lax.dot_general(
        head_ref[...],
        tile_matrix(classes, half * classes),
        (((0,), (0,)), ((), ())),
        preferred_element_type=f32,
    )
    block = (half * width, half * classes)
    head_block = jnp.where(
        iota(block, 0) // width == iota(block, 1) // classes,
        jnp.concatenate([head_row] * half, axis=0),
        0.0,
    ).astype(bf16)
    bias = tiled_row(bias_ref, lanes)

    mark = iota((edge, lanes), 0)
    notes = jnp.zeros((edge, lanes), f32)
    for slot in range(slots):
        depth = corners_ref[slot, 0] - tile_index * TZ
        notes = jnp.where(mark == 2 * slot, depth.astype(f32), notes)
        notes = jnp.where(mark == 2 * slot + 1, corners_ref[slot, 2].astype(f32), notes)
    out_refs[1][slots * edge * chunk :, :] = notes.astype(bf16)

    for copy in copies[-slots:]:
        copy.wait()
    low = iota((count, 128), 1) < 64
    spot = iota((area, 128), 1)
    pairs = edge // 4 + 1
    for pair in range(pairs):
        even = banded(pad_one, 256 * pair, count, edge, lambda dz: band_one[0, dz])
        if pair < pairs - 1:
            odd = banded(pad_one, 256 * pair + 128, count, edge, lambda dz: band_one[1, dz])
            here = jnp.where(low, even[:, :128], odd[:, :128])
            before = jnp.where(low, odd[:, :128], even[:, :128])
            after = even[:, 128:] + odd[:, 128:]
        else:
            here = jnp.where(low, even[:, :128], 0.0)
            before = jnp.where(low, 0.0, even[:, :128])
            after = even[:, 128:]
        before = pltpu.roll(before, 64, 1)
        hidden[:, pair * 128 : (pair + 1) * 128] = join_across(before, here, after, across, edge)
    masks = [None] * pairs
    masks[0] = spot >= width
    masks[-1] = spot < width
    for slot in range(slots):
        at = slot * stride
        blocks = [hidden[at : at + area, pair * 128 : (pair + 1) * 128] for pair in range(pairs)]
        blocks[0] = jnp.where(masks[0], blocks[0], 0.0)
        blocks[-1] = jnp.where(masks[-1], blocks[-1], 0.0)
        normed = normalize(blocks, masks, gain_one, shift_one, width, voxels)
        for pair in range(pairs):
            pad_two[at + edge : at + edge + area, pair * 128 : (pair + 1) * 128] = normed[pair]

    quads = edge // 4
    for quad in range(quads):
        three = banded(pad_two, 128 * quad, count, edge, lambda dz: band_two[dz])
        hidden[:, quad * 128 : (quad + 1) * 128] = join_across(
            three[:, :128], three[:, 128:256], three[:, 256:], across, edge
        )
    for slot in range(slots):
        at = slot * stride
        blocks = [hidden[at : at + area, quad * 128 : (quad + 1) * 128] for quad in range(quads)]
        normed = normalize(blocks, [None] * quads, gain_two, shift_two, width, voxels)
        logits = jnp.concatenate(
            [
                jnp.dot(
                    jnp.concatenate(normed[side : side + quads // 2], axis=1),
                    head_block,
                    preferred_element_type=f32,
                )
                for side in (0, quads // 2)
            ],
            axis=1,
        )
        weighted = (logits + bias) * gauss
        lane_start = corners_ref[slot, 2] * classes
        weighted = pltpu.roll(weighted, lane_start % lanes, 1).astype(bf16)
        depth = corners_ref[slot, 0] - tile_index * TZ
        alive = slot < counts_ref[sub_index, tile_index]
        for peer in range(peers):
            wanted = depth + edge * ((position ^ peer) * chunk - corners_ref[slot, 1])
            wanted = jnp.where(alive, wanted, far)
            select = (code == wanted).astype(f32).astype(bf16)
            out_refs[peer][slot * edge * chunk : (slot + 1) * edge * chunk, :] = jnp.dot(
                select, weighted, preferred_element_type=f32
            ).astype(bf16)


def gather_kernel(sizes, spilled, corners_ref, *rest):
    slots, edge, chunk, peers, classes = sizes
    piece_refs = rest[:peers]
    out_ref = rest[peers]
    rows = edge * chunk
    lanes = edge * classes
    tile_index = lax.axis_index("tiles")
    blocks = -(-VY * classes // lanes)

    notes = piece_refs[1][slots * rows :, :].astype(f32).astype(jnp.int32)
    depth_at = iota((edge, lanes), 0)
    lane_at = iota((edge, lanes), 1)
    groups = []
    for parity in range(2):
        for slot in range(slots):
            if parity == 0:
                depth = corners_ref[slot, 0] - tile_index * TZ
                start = corners_ref[slot, 2] * classes
            else:
                depth = notes[2 * slot : 2 * slot + 1]
                start = notes[2 * slot + 1 : 2 * slot + 2] * classes
            keep = depth_at < depth if spilled else depth_at >= depth
            inside = []
            for block in range(blocks):
                lane = lane_at + block * lanes
                inside.append(keep & (lane >= start) & (lane < start + lanes))
            groups.append((parity, slot, inside))

    for across in range(chunk):
        total = [jnp.zeros((edge, lanes), f32) for _ in range(blocks)]
        for parity, slot, inside in groups:
            at = slot * rows + across * edge
            piece = None
            for peer in range(parity, peers, 2):
                part = piece_refs[peer][at : at + edge, :].astype(f32)
                piece = part if piece is None else piece + part
            for block in range(blocks):
                total[block] = total[block] + jnp.where(inside[block], piece, 0.0)
        out_ref[across] = jnp.concatenate(total, axis=1)[:, : VY * classes].astype(out_ref.dtype)


def join_kernel(own_ref, odd_ref, even_ref, out_ref):
    tile_index = lax.axis_index("tiles")
    from_even = (tile_index % 2 == 1).astype(f32)
    from_odd = ((tile_index % 2 == 0) & (tile_index > 0)).astype(f32)
    out_ref[...] = (
        own_ref[...]
        + even_ref[...].astype(f32) * from_even
        + odd_ref[...].astype(f32) * from_odd
    )


vmem = pl.BlockSpec(memory_space=pltpu.VMEM)
smem = pl.BlockSpec(memory_space=pltpu.SMEM)
hbm = pl.BlockSpec(memory_space=pltpu.HBM)
limits = pltpu.CompilerParams(vmem_limit_bytes=vmem_bytes)
ample = pltpu.CompilerParams(vmem_limit_bytes=60000000)


def on_device(
    features,
    conv_first,
    gain_first,
    shift_first,
    conv_second,
    gain_second,
    shift_second,
    head_weight,
    head_bias,
    corners,
    counts,
):
    _, slots, edge, _, data = features.shape
    in_width, width = conv_first.shape[-2:]
    classes = head_bias.shape[1]
    peers = lax.axis_size("folds") * lax.axis_size("sub")
    tiles = lax.axis_size("tiles")
    chunk = VX // peers
    area = edge * edge
    lanes = edge * classes
    piece = slots * edge * chunk
    padded = slots * (area + edge) + edge
    rows = [piece + edge if peer == 1 else piece for peer in range(peers)]
    pieces = pl.pallas_call(
        functools.partial(section_kernel, (slots, edge, chunk, peers)),
        out_shape=[pltpu.VMEM((count, lanes), bf16) for count in rows],
        in_specs=[hbm] * 11,
        out_specs=[vmem] * peers,
        scratch_shapes=[
            pltpu.VMEM((padded, data + 256), bf16),
            pltpu.VMEM((padded, edge * width + 128), bf16),
            pltpu.VMEM((2, 3, 256, 256), bf16),
            pltpu.VMEM((3, 256, 384), bf16),
            pltpu.VMEM((padded - 2 * edge, edge * width + 128), f32),
            pltpu.SMEM(corners.shape, jnp.int32),
            pltpu.SMEM(counts.shape[::-1], jnp.int32),
            pltpu.VMEM((27 * width, in_width), bf16),
            pltpu.VMEM((1, width), f32),
            pltpu.VMEM((1, width), f32),
            pltpu.VMEM((27 * width, width), bf16),
            pltpu.VMEM((1, width), f32),
            pltpu.VMEM((1, width), f32),
            pltpu.VMEM((classes, width), bf16),
            pltpu.VMEM((1, classes), f32),
            pltpu.SemaphoreType.DMA((10 + slots,)),
        ],
        compiler_params=ample,
        name="section",
    )(
        corners,
        counts.T,
        features.reshape(slots, area, data),
        jnp.swapaxes(conv_first, 4, 5).reshape(27 * width, in_width),
        gain_first,
        shift_first,
        conv_second.reshape(27 * width, width),
        gain_second,
        shift_second,
        head_weight[0].T,
        head_bias,
    )
    arrived = [pieces[0]] + [None] * (peers - 1)
    for peer in [*range(2, peers), 1]:
        pairs = [(i, i ^ peer) for i in range(peers)]
        arrived[peer] = lax.ppermute(pieces[peer], ("folds", "sub"), pairs)

    own, spill = (
        pl.pallas_call(
            functools.partial(gather_kernel, (slots, edge, chunk, peers, classes), spilled),
            out_shape=pltpu.VMEM((chunk, TZ, VY * classes), kind),
            in_specs=[smem] + [vmem] * peers,
            out_specs=vmem,
            compiler_params=limits,
            cost_estimate=pl.CostEstimate(
                flops=500000000, bytes_accessed=2000000, transcendentals=0
            ),
            name=name,
        )(corners, *arrived)
        for spilled, kind, name in ((False, f32, "own"), (True, bf16, "spill"))
    )

    even = [(i, i ^ 1) for i in range(tiles)]
    odd = [(0, 0), (tiles - 1, tiles - 1)] + [
        (i, i + 1 if i % 2 else i - 1) for i in range(1, tiles - 1)
    ]
    from_odd = lax.ppermute(spill, "tiles", odd)
    from_even = lax.ppermute(spill, "tiles", even)
    joined = pl.pallas_call(
        join_kernel,
        out_shape=jax.ShapeDtypeStruct((chunk, TZ, VY * classes), f32),
        in_specs=[vmem, vmem, vmem],
        out_specs=vmem,
        compiler_params=limits,
        name="join",
    )(own, from_odd, from_even)
    return jnp.transpose(joined, (1, 0, 2))


def solution(mesh):
    placed = (
        P("folds", ("groups", "tiles", "sub"), None, None, None),
        P("folds", None, None, None, None, None),
        P("folds", None),
        P("folds", None),
        P("folds", None, None, None, None, None),
        P("folds", None),
        P("folds", None),
        P("folds", None, None),
        P("folds", None),
        P(("groups", "tiles", "sub"), None),
        P("groups", None),
    )
    return jax.shard_map(
        on_device,
        mesh=mesh,
        in_specs=placed,
        out_specs=P(("groups", "tiles"), ("folds", "sub"), None),
        check_vma=False,
    )
```

```python
import functools

import jax
import jax.numpy as jnp
from jax import lax
from jax.experimental import pallas as pl
from jax.experimental.pallas import tpu as pltpu
from jax.sharding import PartitionSpec as P

TZ = 16
VX = 40
VY = 40

epsilon = 1e-05
leak_slope = 0.01
far = 1 << 20
bf16 = jnp.bfloat16
f32 = jnp.float32
vmem_bytes = 48 << 20


def iota(shape, dim):
    return lax.broadcasted_iota(jnp.int32, shape, dim)


def tile_matrix(width, lanes):
    return (iota((width, lanes), 1) % width == iota((width, lanes), 0)).astype(bf16)


def tiled_row(ref, lanes):
    width = ref.shape[1]
    row = jnp.concatenate([ref[...], jnp.zeros((1, lanes - width), f32)], axis=1)
    row = jnp.broadcast_to(row, (8, lanes))
    reach = width
    while reach < lanes:
        row = row + pltpu.roll(row, reach, 1)
        reach *= 2
    return row[0:1]


def lane_bands(parts, places):
    total = None
    for place, part in enumerate(parts):
        if part is not None:
            total = part if total is None else jnp.where(places == place, part, total)
    if total is None:
        return None
    if any(part is None for part in parts):
        empty = None
        for place, part in enumerate(parts):
            if part is None:
                here = places == place
                empty = here if empty is None else empty | here
        total = jnp.where(empty, 0.0, total)
    return total


def build_first(taps_ref, band_ref, in_width, width):
    spread = tile_matrix(width, 128)
    places = iota((in_width, 128), 1) // width
    zero = jnp.zeros((in_width, 128), bf16)
    orders = (((1, 0), (2, None)), ((0, 1), (None, 2)))
    for dz in range(3):
        tiled = {}
        for dx in range(3):
            for dy in range(3):
                at = ((dz * 3 + dx) * 3 + dy) * width
                tiled[dx, dy] = lax.dot_general(
                    taps_ref[at : at + width],
                    spread,
                    (((0,), (0,)), ((), ())),
                    preferred_element_type=f32,
                )
        for variant in range(2):
            for yi in range(4):
                for side in range(2):
                    parts = []
                    for dx in orders[variant][side]:
                        for yo in range(2):
                            parts.append(None if dx is None else tiled.get((dx, yi - yo)))
                    block = lane_bands(parts, places)
                    band_ref[
                        variant,
                        dz,
                        yi * in_width : (yi + 1) * in_width,
                        side * 128 : (side + 1) * 128,
                    ] = zero if block is None else block.astype(bf16)


def build_second(taps_ref, band_ref, width):
    spread = tile_matrix(width, 128)
    places = iota((width, 128), 1) // width
    zero = jnp.zeros((width, 128), bf16)
    for dz in range(3):
        at = dz * 9 * width
        tiled = jnp.dot(taps_ref[at : at + 9 * width], spread, preferred_element_type=f32)
        for dx in range(3):
            taps = {
                dy: tiled[(dx * 3 + dy) * width : (dx * 3 + dy + 1) * width] for dy in range(3)
            }
            for yi in range(8):
                block = lane_bands([taps.get(yi - yo) for yo in range(4)], places)
                band_ref[dz, yi * width : (yi + 1) * width, dx * 128 : (dx + 1) * 128] = (
                    zero if block is None else block.astype(bf16)
                )


def banded(pad_ref, lane, count, edge, bands):
    total = None
    for dz in range(3):
        part = jnp.dot(
            pad_ref[dz * edge : dz * edge + count, lane : lane + 256],
            bands(dz),
            preferred_element_type=f32,
        )
        total = part if total is None else total + part
    return total


def join_across(before, here, after, across, edge):
    rows = here.shape[0]
    before = jnp.where(across == 0, 0.0, pltpu.roll(before, 1, 0))
    after = jnp.where(across == edge - 1, 0.0, pltpu.roll(after, rows - 1, 0))
    return here + before + after


def channel_mean(blocks, width, voxels):
    folded = None
    for block in blocks:
        row = jnp.sum(block, axis=0, keepdims=True)
        folded = row if folded is None else folded + row
    folded = jnp.broadcast_to(folded, (8, 128))
    reach = width
    while reach < 128:
        folded = folded + pltpu.roll(folded, reach, 1)
        reach *= 2
    return folded[0:1] * (1.0 / voxels)


def normalize(blocks, masks, gain, shift, width, voxels):
    mean_value = channel_mean(blocks, width, voxels)
    centered = []
    for block, mask in zip(blocks, masks):
        moved = block - mean_value
        centered.append(moved if mask is None else jnp.where(mask, moved, 0.0))
    variance = channel_mean([moved * moved for moved in centered], width, voxels)
    factor = lax.rsqrt(variance + epsilon) * gain
    results = []
    for moved, mask in zip(centered, masks):
        scaled = moved * factor + shift
        scaled = jnp.maximum(scaled, leak_slope * scaled)
        results.append((scaled if mask is None else jnp.where(mask, scaled, 0.0)).astype(bf16))
    return results


def section_kernel(
    sizes,
    corners_hbm,
    counts_hbm,
    features_ref,
    taps_one_hbm,
    gain_one_hbm,
    shift_one_hbm,
    taps_two_hbm,
    gain_two_hbm,
    shift_two_hbm,
    head_hbm,
    bias_hbm,
    *rest,
):
    slots, edge, chunk, parts = sizes
    out_refs = rest[: len(parts)]
    (
        pad_one,
        pad_two,
        band_one,
        band_two,
        hidden,
        corners_ref,
        counts_ref,
        taps_one_ref,
        gain_one_ref,
        shift_one_ref,
        taps_two_ref,
        gain_two_ref,
        shift_two_ref,
        head_ref,
        bias_ref,
        sems,
    ) = rest[len(parts) :]
    in_width = taps_one_ref.shape[1]
    classes, width = head_ref.shape
    area = edge * edge
    stride = area + edge
    count = hidden.shape[0]
    voxels = float(area * edge)
    data = edge * in_width
    lanes = edge * classes

    copies = []
    for at, (source, target) in enumerate(
        [
            (taps_one_hbm, taps_one_ref),
            (taps_two_hbm, taps_two_ref),
            (gain_one_hbm, gain_one_ref),
            (shift_one_hbm, shift_one_ref),
            (gain_two_hbm, gain_two_ref),
            (shift_two_hbm, shift_two_ref),
            (head_hbm, head_ref),
            (bias_hbm, bias_ref),
            (corners_hbm, corners_ref),
            (counts_hbm, counts_ref),
        ]
        + [
            (
                features_ref.at[slot],
                pad_one.at[pl.ds(edge + slot * stride, area), pl.ds(128, data)],
            )
            for slot in range(slots)
        ]
    ):
        copy = pltpu.make_async_copy(source, target, sems.at[at])
        copy.start()
        copies.append(copy)
    for pad in (pad_one, pad_two):
        for slot in range(slots + 1):
            pad[slot * stride : slot * stride + edge, :] = jnp.zeros((edge, pad.shape[1]), bf16)
    pad_one[:, :128] = jnp.zeros((pad_one.shape[0], 128), bf16)
    pad_one[:, 128 + data :] = jnp.zeros((pad_one.shape[0], 128), bf16)

    center, spread = (edge - 1) / 2.0, edge / 4.0

    def profile(offset):
        return jnp.exp(-((offset.astype(f32) - center) ** 2) / (2.0 * spread * spread))

    row_at = iota((area, 128), 0)
    lane_at = iota((1, lanes), 1)
    gauss = profile(row_at // edge) * profile(row_at % edge)
    gauss = jnp.concatenate([gauss] * (lanes // 128), axis=1) * profile(lane_at // classes)

    row = iota((chunk * edge, area), 0)
    source = iota((chunk * edge, area), 1)
    turn = (row % edge - source // edge) & (edge - 1)
    code = turn + edge * (source % edge - row // edge)
    across = iota((count, 128), 0) % edge
    tile_index = lax.axis_index("tiles")
    sub_index = lax.axis_index("sub")
    position = lax.axis_index("folds") * lax.axis_size("sub") + sub_index

    for copy in copies[:-slots]:
        copy.wait()
    build_first(taps_one_ref, band_one, in_width, width)
    build_second(taps_two_ref, band_two, width)
    gain_one, shift_one = tiled_row(gain_one_ref, 128), tiled_row(shift_one_ref, 128)
    gain_two, shift_two = tiled_row(gain_two_ref, 128), tiled_row(shift_two_ref, 128)

    half = edge // 2
    head_row = lax.dot_general(
        head_ref[...],
        tile_matrix(classes, half * classes),
        (((0,), (0,)), ((), ())),
        preferred_element_type=f32,
    )
    block = (half * width, half * classes)
    head_block = jnp.where(
        iota(block, 0) // width == iota(block, 1) // classes,
        jnp.concatenate([head_row] * half, axis=0),
        0.0,
    ).astype(bf16)
    bias = tiled_row(bias_ref, lanes)

    mark = iota((edge, lanes), 0)
    notes = jnp.zeros((edge, lanes), f32)
    for slot in range(slots):
        depth = corners_ref[slot, 0] - tile_index * TZ
        notes = jnp.where(mark == 2 * slot, depth.astype(f32), notes)
        notes = jnp.where(mark == 2 * slot + 1, corners_ref[slot, 2].astype(f32), notes)
    for (peer, _, _), out_ref in zip(parts, out_refs):
        if peer == 1:
            out_ref[slots * edge * chunk :, :] = notes.astype(bf16)

    for copy in copies[-slots:]:
        copy.wait()
    low = iota((count, 128), 1) < 64
    spot = iota((area, 128), 1)
    pairs = edge // 4 + 1
    for pair in range(pairs):
        even = banded(pad_one, 256 * pair, count, edge, lambda dz: band_one[0, dz])
        if pair < pairs - 1:
            odd = banded(pad_one, 256 * pair + 128, count, edge, lambda dz: band_one[1, dz])
            here = jnp.where(low, even[:, :128], odd[:, :128])
            before = jnp.where(low, odd[:, :128], even[:, :128])
            after = even[:, 128:] + odd[:, 128:]
        else:
            here = jnp.where(low, even[:, :128], 0.0)
            before = jnp.where(low, 0.0, even[:, :128])
            after = even[:, 128:]
        before = pltpu.roll(before, 64, 1)
        hidden[:, pair * 128 : (pair + 1) * 128] = join_across(before, here, after, across, edge)
    masks = [None] * pairs
    masks[0] = spot >= width
    masks[-1] = spot < width
    for slot in range(slots):
        at = slot * stride
        blocks = [hidden[at : at + area, pair * 128 : (pair + 1) * 128] for pair in range(pairs)]
        blocks[0] = jnp.where(masks[0], blocks[0], 0.0)
        blocks[-1] = jnp.where(masks[-1], blocks[-1], 0.0)
        normed = normalize(blocks, masks, gain_one, shift_one, width, voxels)
        for pair in range(pairs):
            pad_two[at + edge : at + edge + area, pair * 128 : (pair + 1) * 128] = normed[pair]

    quads = edge // 4
    for quad in range(quads):
        three = banded(pad_two, 128 * quad, count, edge, lambda dz: band_two[dz])
        hidden[:, quad * 128 : (quad + 1) * 128] = join_across(
            three[:, :128], three[:, 128:256], three[:, 256:], across, edge
        )
    for slot in range(slots):
        at = slot * stride
        blocks = [hidden[at : at + area, quad * 128 : (quad + 1) * 128] for quad in range(quads)]
        normed = normalize(blocks, [None] * quads, gain_two, shift_two, width, voxels)
        logits = jnp.concatenate(
            [
                jnp.dot(
                    jnp.concatenate(normed[side : side + quads // 2], axis=1),
                    head_block,
                    preferred_element_type=f32,
                )
                for side in (0, quads // 2)
            ],
            axis=1,
        )
        weighted = (logits + bias) * gauss
        lane_start = corners_ref[slot, 2] * classes
        weighted = pltpu.roll(weighted, lane_start % lanes, 1).astype(bf16)
        depth = corners_ref[slot, 0] - tile_index * TZ
        alive = slot < counts_ref[sub_index, tile_index]
        for (peer, low_row, high_row), out_ref in zip(parts, out_refs):
            wanted = depth + edge * ((position ^ peer) * chunk - corners_ref[slot, 1])
            wanted = jnp.where(alive, wanted, far)
            select = (code[low_row * edge : high_row * edge] == wanted).astype(f32).astype(bf16)
            size = (high_row - low_row) * edge
            out_ref[slot * size : (slot + 1) * size, :] = jnp.dot(
                select, weighted, preferred_element_type=f32
            ).astype(bf16)


def gather_kernel(sizes, spilled, corners_ref, *rest):
    slots, edge, chunk, parts, first, last, classes = sizes
    part_refs = rest[: len(parts)]
    out_ref = rest[len(parts)]
    lanes = edge * classes
    tile_index = lax.axis_index("tiles")
    blocks = -(-VY * classes // lanes)

    for (peer, _, _), part_ref in zip(parts, part_refs):
        if peer == 1:
            notes = part_ref[slots * edge * chunk :, :].astype(f32).astype(jnp.int32)
    depth_at = iota((edge, lanes), 0)
    lane_at = iota((edge, lanes), 1)
    groups = []
    for parity in range(2):
        for slot in range(slots):
            if parity == 0:
                depth = corners_ref[slot, 0] - tile_index * TZ
                start = corners_ref[slot, 2] * classes
            else:
                depth = notes[2 * slot : 2 * slot + 1]
                start = notes[2 * slot + 1 : 2 * slot + 2] * classes
            keep = depth_at < depth if spilled else depth_at >= depth
            inside = []
            for block in range(blocks):
                lane = lane_at + block * lanes
                inside.append(keep & (lane >= start) & (lane < start + lanes))
            groups.append((parity, slot, inside))

    for across in range(first, last):
        total = [jnp.zeros((edge, lanes), f32) for _ in range(blocks)]
        for parity, slot, inside in groups:
            piece = None
            for (peer, low_row, high_row), part_ref in zip(parts, part_refs):
                if peer % 2 == parity and low_row <= across < high_row:
                    at = (slot * (high_row - low_row) + across - low_row) * edge
                    part = part_ref[at : at + edge, :].astype(f32)
                    piece = part if piece is None else piece + part
            for block in range(blocks):
                total[block] = total[block] + jnp.where(inside[block], piece, 0.0)
        total = jnp.concatenate(total, axis=1)[:, : VY * classes]
        out_ref[across - first] = total.astype(out_ref.dtype)


def join_kernel(halves, own_ref, *rest):
    out_ref = rest[-1]
    for (low_row, high_row), arrived_ref in zip(halves, rest):
        out_ref[low_row:high_row] = own_ref[low_row:high_row] + arrived_ref[...].astype(f32)


vmem = pl.BlockSpec(memory_space=pltpu.VMEM)
smem = pl.BlockSpec(memory_space=pltpu.SMEM)
hbm = pl.BlockSpec(memory_space=pltpu.HBM)
limits = pltpu.CompilerParams(vmem_limit_bytes=vmem_bytes)
ample = pltpu.CompilerParams(vmem_limit_bytes=60000000)


def on_device(
    features,
    conv_first,
    gain_first,
    shift_first,
    conv_second,
    gain_second,
    shift_second,
    head_weight,
    head_bias,
    corners,
    counts,
):
    _, slots, edge, _, data = features.shape
    in_width, width = conv_first.shape[-2:]
    classes = head_bias.shape[1]
    peers = lax.axis_size("folds") * lax.axis_size("sub")
    tiles = lax.axis_size("tiles")
    chunk = VX // peers
    area = edge * edge
    lanes = edge * classes
    padded = slots * (area + edge) + edge
    middle = chunk // 2
    halves = ((0, middle), (middle, chunk))
    parts = [(0, 0, chunk), (1, 0, chunk)]
    for low_row, high_row in halves:
        parts += [(peer, low_row, high_row) for peer in range(2, peers)]
    rows = [
        slots * edge * (high_row - low_row) + (edge if peer == 1 else 0)
        for peer, low_row, high_row in parts
    ]
    pieces = pl.pallas_call(
        functools.partial(section_kernel, (slots, edge, chunk, parts)),
        out_shape=[pltpu.VMEM((count, lanes), bf16) for count in rows],
        in_specs=[hbm] * 11,
        out_specs=[vmem] * len(parts),
        scratch_shapes=[
            pltpu.VMEM((padded, data + 256), bf16),
            pltpu.VMEM((padded, edge * width + 128), bf16),
            pltpu.VMEM((2, 3, 256, 256), bf16),
            pltpu.VMEM((3, 256, 384), bf16),
            pltpu.VMEM((padded - 2 * edge, edge * width + 128), f32),
            pltpu.SMEM(corners.shape, jnp.int32),
            pltpu.SMEM(counts.shape[::-1], jnp.int32),
            pltpu.VMEM((27 * width, in_width), bf16),
            pltpu.VMEM((1, width), f32),
            pltpu.VMEM((1, width), f32),
            pltpu.VMEM((27 * width, width), bf16),
            pltpu.VMEM((1, width), f32),
            pltpu.VMEM((1, width), f32),
            pltpu.VMEM((classes, width), bf16),
            pltpu.VMEM((1, classes), f32),
            pltpu.SemaphoreType.DMA((10 + slots,)),
        ],
        compiler_params=ample,
        name="section",
    )(
        corners,
        counts.T,
        features.reshape(slots, area, data),
        jnp.swapaxes(conv_first, 4, 5).reshape(27 * width, in_width),
        gain_first,
        shift_first,
        conv_second.reshape(27 * width, width),
        gain_second,
        shift_second,
        head_weight[0].T,
        head_bias,
    )
    arrived = []
    for (peer, _, _), piece in zip(parts, pieces):
        pairs = [(i, i ^ peer) for i in range(peers)]
        arrived.append(lax.ppermute(piece, ("folds", "sub"), pairs) if peer else piece)

    def gather(first, last, spilled, kind, name):
        chosen = [
            (part, piece)
            for part, piece in zip(parts, arrived)
            if part[1] < last and first < part[2]
        ]
        return pl.pallas_call(
            functools.partial(
                gather_kernel,
                (slots, edge, chunk, [part for part, _ in chosen], first, last, classes),
                spilled,
            ),
            out_shape=pltpu.VMEM((last - first, TZ, VY * classes), kind),
            in_specs=[smem] + [vmem] * len(chosen),
            out_specs=vmem,
            compiler_params=limits,
            cost_estimate=pl.CostEstimate(
                flops=500000000, bytes_accessed=2000000, transcendentals=0
            ),
            name=name,
        )(corners, *[piece for _, piece in chosen])

    onward = [(tile, tile + 1) for tile in range(tiles - 1)]
    from_below = [
        lax.ppermute(gather(first, last, True, bf16, f"spill_{first}"), "tiles", onward)
        for first, last in halves
    ]
    own = gather(0, chunk, False, f32, "own")
    joined = pl.pallas_call(
        functools.partial(join_kernel, halves),
        out_shape=jax.ShapeDtypeStruct((chunk, TZ, VY * classes), f32),
        in_specs=[vmem] * (1 + len(halves)),
        out_specs=vmem,
        compiler_params=limits,
        name="join",
    )(own, *from_below)
    return jnp.transpose(joined, (1, 0, 2))


def solution(mesh):
    placed = (
        P("folds", ("groups", "tiles", "sub"), None, None, None),
        P("folds", None, None, None, None, None),
        P("folds", None),
        P("folds", None),
        P("folds", None, None, None, None, None),
        P("folds", None),
        P("folds", None),
        P("folds", None, None),
        P("folds", None),
        P(("groups", "tiles", "sub"), None),
        P("groups", None),
    )
    return jax.shard_map(
        on_device,
        mesh=mesh,
        in_specs=placed,
        out_specs=P(("groups", "tiles"), ("folds", "sub"), None),
        check_vma=False,
    )
```

```python
import functools

import jax
import jax.numpy as jnp
from jax import lax
from jax.experimental import pallas as pl
from jax.experimental.pallas import tpu as pltpu
from jax.sharding import PartitionSpec as P

TZ = 16
VX = 40
VY = 40

epsilon = 1e-05
leak_slope = 0.01
far = 1 << 20
bf16 = jnp.bfloat16
f32 = jnp.float32
vmem_bytes = 48 << 20


def iota(shape, dim):
    return lax.broadcasted_iota(jnp.int32, shape, dim)


def tile_matrix(width, lanes):
    return (iota((width, lanes), 1) % width == iota((width, lanes), 0)).astype(bf16)


def tiled_row(ref, lanes):
    width = ref.shape[1]
    row = jnp.concatenate([ref[...], jnp.zeros((1, lanes - width), f32)], axis=1)
    row = jnp.broadcast_to(row, (8, lanes))
    reach = width
    while reach < lanes:
        row = row + pltpu.roll(row, reach, 1)
        reach *= 2
    return row[0:1]


def lane_bands(parts, places):
    total = None
    for place, part in enumerate(parts):
        if part is not None:
            total = part if total is None else jnp.where(places == place, part, total)
    if total is None:
        return None
    if any(part is None for part in parts):
        empty = None
        for place, part in enumerate(parts):
            if part is None:
                here = places == place
                empty = here if empty is None else empty | here
        total = jnp.where(empty, 0.0, total)
    return total


def build_first(taps_ref, band_ref, in_width, width):
    spread = tile_matrix(width, 128)
    places = iota((in_width, 128), 1) // width
    zero = jnp.zeros((in_width, 128), bf16)
    orders = (((1, 0), (2, None)), ((0, 1), (None, 2)))
    for dz in range(3):
        tiled = {}
        for dx in range(3):
            for dy in range(3):
                at = ((dz * 3 + dx) * 3 + dy) * width
                tiled[dx, dy] = lax.dot_general(
                    taps_ref[at : at + width],
                    spread,
                    (((0,), (0,)), ((), ())),
                    preferred_element_type=f32,
                )
        for variant in range(2):
            for yi in range(4):
                for side in range(2):
                    parts = []
                    for dx in orders[variant][side]:
                        for yo in range(2):
                            parts.append(None if dx is None else tiled.get((dx, yi - yo)))
                    block = lane_bands(parts, places)
                    band_ref[
                        variant,
                        dz,
                        yi * in_width : (yi + 1) * in_width,
                        side * 128 : (side + 1) * 128,
                    ] = zero if block is None else block.astype(bf16)


def build_second(taps_ref, band_ref, width):
    spread = tile_matrix(width, 128)
    places = iota((width, 128), 1) // width
    zero = jnp.zeros((width, 128), bf16)
    for dz in range(3):
        at = dz * 9 * width
        tiled = jnp.dot(taps_ref[at : at + 9 * width], spread, preferred_element_type=f32)
        for dx in range(3):
            taps = {
                dy: tiled[(dx * 3 + dy) * width : (dx * 3 + dy + 1) * width] for dy in range(3)
            }
            for yi in range(8):
                block = lane_bands([taps.get(yi - yo) for yo in range(4)], places)
                band_ref[dz, yi * width : (yi + 1) * width, dx * 128 : (dx + 1) * 128] = (
                    zero if block is None else block.astype(bf16)
                )


def banded(pad_ref, lane, count, edge, bands):
    total = None
    for dz in range(3):
        part = jnp.dot(
            pad_ref[dz * edge : dz * edge + count, lane : lane + 256],
            bands(dz),
            preferred_element_type=f32,
        )
        total = part if total is None else total + part
    return total


def join_across(before, here, after, across, edge):
    rows = here.shape[0]
    before = jnp.where(across == 0, 0.0, pltpu.roll(before, 1, 0))
    after = jnp.where(across == edge - 1, 0.0, pltpu.roll(after, rows - 1, 0))
    return here + before + after


def channel_mean(blocks, width, voxels):
    folded = None
    for block in blocks:
        row = jnp.sum(block, axis=0, keepdims=True)
        folded = row if folded is None else folded + row
    folded = jnp.broadcast_to(folded, (8, 128))
    reach = width
    while reach < 128:
        folded = folded + pltpu.roll(folded, reach, 1)
        reach *= 2
    return folded[0:1] * (1.0 / voxels)


def normalize(blocks, masks, gain, shift, width, voxels):
    mean_value = channel_mean(blocks, width, voxels)
    centered = []
    for block, mask in zip(blocks, masks):
        moved = block - mean_value
        centered.append(moved if mask is None else jnp.where(mask, moved, 0.0))
    variance = channel_mean([moved * moved for moved in centered], width, voxels)
    factor = lax.rsqrt(variance + epsilon) * gain
    results = []
    for moved, mask in zip(centered, masks):
        scaled = moved * factor + shift
        scaled = jnp.maximum(scaled, leak_slope * scaled)
        results.append((scaled if mask is None else jnp.where(mask, scaled, 0.0)).astype(bf16))
    return results


def section_kernel(
    sizes,
    corners_hbm,
    counts_hbm,
    features_ref,
    taps_one_hbm,
    gain_one_hbm,
    shift_one_hbm,
    taps_two_hbm,
    gain_two_hbm,
    shift_two_hbm,
    head_hbm,
    bias_hbm,
    *rest,
):
    slots, edge, chunk, parts = sizes
    out_refs = rest[: len(parts)]
    (
        pad_one,
        pad_two,
        band_one,
        band_two,
        hidden,
        corners_ref,
        counts_ref,
        taps_one_ref,
        gain_one_ref,
        shift_one_ref,
        taps_two_ref,
        gain_two_ref,
        shift_two_ref,
        head_ref,
        bias_ref,
        sems,
    ) = rest[len(parts) :]
    in_width = taps_one_ref.shape[1]
    classes, width = head_ref.shape
    area = edge * edge
    stride = area + edge
    count = hidden.shape[0]
    voxels = float(area * edge)
    data = edge * in_width
    lanes = edge * classes

    copies = []
    for at, (source, target) in enumerate(
        [
            (taps_one_hbm, taps_one_ref),
            (taps_two_hbm, taps_two_ref),
            (gain_one_hbm, gain_one_ref),
            (shift_one_hbm, shift_one_ref),
            (gain_two_hbm, gain_two_ref),
            (shift_two_hbm, shift_two_ref),
            (head_hbm, head_ref),
            (bias_hbm, bias_ref),
            (corners_hbm, corners_ref),
            (counts_hbm, counts_ref),
        ]
        + [
            (
                features_ref.at[slot],
                pad_one.at[pl.ds(edge + slot * stride, area), pl.ds(128, data)],
            )
            for slot in range(slots)
        ]
    ):
        copy = pltpu.make_async_copy(source, target, sems.at[at])
        copy.start()
        copies.append(copy)
    for pad in (pad_one, pad_two):
        for slot in range(slots + 1):
            pad[slot * stride : slot * stride + edge, :] = jnp.zeros((edge, pad.shape[1]), bf16)
    pad_one[:, :128] = jnp.zeros((pad_one.shape[0], 128), bf16)
    pad_one[:, 128 + data :] = jnp.zeros((pad_one.shape[0], 128), bf16)

    center, spread = (edge - 1) / 2.0, edge / 4.0

    def profile(offset):
        return jnp.exp(-((offset.astype(f32) - center) ** 2) / (2.0 * spread * spread))

    row_at = iota((area, 128), 0)
    lane_at = iota((1, lanes), 1)
    gauss = profile(row_at // edge) * profile(row_at % edge)
    gauss = jnp.concatenate([gauss] * (lanes // 128), axis=1) * profile(lane_at // classes)

    row = iota((chunk * edge, area), 0)
    source = iota((chunk * edge, area), 1)
    turn = (row % edge - source // edge) & (edge - 1)
    code = turn + edge * (source % edge - row // edge)
    across = iota((count, 128), 0) % edge
    tile_index = lax.axis_index("tiles")
    sub_index = lax.axis_index("sub")
    position = lax.axis_index("folds") * lax.axis_size("sub") + sub_index

    for copy in copies[:-slots]:
        copy.wait()
    build_first(taps_one_ref, band_one, in_width, width)
    build_second(taps_two_ref, band_two, width)
    gain_one, shift_one = tiled_row(gain_one_ref, 128), tiled_row(shift_one_ref, 128)
    gain_two, shift_two = tiled_row(gain_two_ref, 128), tiled_row(shift_two_ref, 128)

    half = edge // 2
    head_row = lax.dot_general(
        head_ref[...],
        tile_matrix(classes, half * classes),
        (((0,), (0,)), ((), ())),
        preferred_element_type=f32,
    )
    block = (half * width, half * classes)
    head_block = jnp.where(
        iota(block, 0) // width == iota(block, 1) // classes,
        jnp.concatenate([head_row] * half, axis=0),
        0.0,
    ).astype(bf16)
    bias = tiled_row(bias_ref, lanes)

    mark = iota((edge, lanes), 0)
    notes = jnp.zeros((edge, lanes), f32)
    for slot in range(slots):
        depth = corners_ref[slot, 0] - tile_index * TZ
        notes = jnp.where(mark == 2 * slot, depth.astype(f32), notes)
        notes = jnp.where(mark == 2 * slot + 1, corners_ref[slot, 2].astype(f32), notes)
    for (peer, _, _), out_ref in zip(parts, out_refs):
        if peer == 1:
            out_ref[slots * edge * chunk :, :] = notes.astype(bf16)

    for copy in copies[-slots:]:
        copy.wait()
    low = iota((count, 128), 1) < 64
    spot = iota((area, 128), 1)
    pairs = edge // 4 + 1
    for pair in range(pairs):
        even = banded(pad_one, 256 * pair, count, edge, lambda dz: band_one[0, dz])
        if pair < pairs - 1:
            odd = banded(pad_one, 256 * pair + 128, count, edge, lambda dz: band_one[1, dz])
            here = jnp.where(low, even[:, :128], odd[:, :128])
            before = jnp.where(low, odd[:, :128], even[:, :128])
            after = even[:, 128:] + odd[:, 128:]
        else:
            here = jnp.where(low, even[:, :128], 0.0)
            before = jnp.where(low, 0.0, even[:, :128])
            after = even[:, 128:]
        before = pltpu.roll(before, 64, 1)
        hidden[:, pair * 128 : (pair + 1) * 128] = join_across(before, here, after, across, edge)
    masks = [None] * pairs
    masks[0] = spot >= width
    masks[-1] = spot < width
    for slot in range(slots):
        at = slot * stride
        blocks = [hidden[at : at + area, pair * 128 : (pair + 1) * 128] for pair in range(pairs)]
        blocks[0] = jnp.where(masks[0], blocks[0], 0.0)
        blocks[-1] = jnp.where(masks[-1], blocks[-1], 0.0)
        normed = normalize(blocks, masks, gain_one, shift_one, width, voxels)
        for pair in range(pairs):
            pad_two[at + edge : at + edge + area, pair * 128 : (pair + 1) * 128] = normed[pair]

    quads = edge // 4
    for quad in range(quads):
        three = banded(pad_two, 128 * quad, count, edge, lambda dz: band_two[dz])
        hidden[:, quad * 128 : (quad + 1) * 128] = join_across(
            three[:, :128], three[:, 128:256], three[:, 256:], across, edge
        )
    for slot in range(slots):
        at = slot * stride
        blocks = [hidden[at : at + area, quad * 128 : (quad + 1) * 128] for quad in range(quads)]
        normed = normalize(blocks, [None] * quads, gain_two, shift_two, width, voxels)
        logits = jnp.concatenate(
            [
                jnp.dot(
                    jnp.concatenate(normed[side : side + quads // 2], axis=1),
                    head_block,
                    preferred_element_type=f32,
                )
                for side in (0, quads // 2)
            ],
            axis=1,
        )
        weighted = (logits + bias) * gauss
        lane_start = corners_ref[slot, 2] * classes
        weighted = pltpu.roll(weighted, lane_start % lanes, 1).astype(bf16)
        depth = corners_ref[slot, 0] - tile_index * TZ
        alive = slot < counts_ref[sub_index, tile_index]
        for (peer, low_row, high_row), out_ref in zip(parts, out_refs):
            wanted = depth + edge * ((position ^ peer) * chunk - corners_ref[slot, 1])
            wanted = jnp.where(alive, wanted, far)
            select = (code[low_row * edge : high_row * edge] == wanted).astype(f32).astype(bf16)
            size = (high_row - low_row) * edge
            out_ref[slot * size : (slot + 1) * size, :] = jnp.dot(
                select, weighted, preferred_element_type=f32
            ).astype(bf16)


def gather_kernel(sizes, spilled, corners_ref, *rest):
    slots, edge, chunk, parts, first, last, classes = sizes
    part_refs = rest[: len(parts)]
    out_ref = rest[len(parts)]
    lanes = edge * classes
    tile_index = lax.axis_index("tiles")
    blocks = -(-VY * classes // lanes)

    for (peer, _, _), part_ref in zip(parts, part_refs):
        if peer == 1:
            notes = part_ref[slots * edge * chunk :, :].astype(f32).astype(jnp.int32)
    depth_at = iota((edge, lanes), 0)
    lane_at = iota((edge, lanes), 1)
    groups = []
    for parity in range(2):
        for slot in range(slots):
            if parity == 0:
                depth = corners_ref[slot, 0] - tile_index * TZ
                start = corners_ref[slot, 2] * classes
            else:
                depth = notes[2 * slot : 2 * slot + 1]
                start = notes[2 * slot + 1 : 2 * slot + 2] * classes
            keep = depth_at < depth if spilled else depth_at >= depth
            inside = []
            for block in range(blocks):
                lane = lane_at + block * lanes
                inside.append(keep & (lane >= start) & (lane < start + lanes))
            groups.append((parity, slot, inside))

    for across in range(first, last):
        total = [jnp.zeros((edge, lanes), f32) for _ in range(blocks)]
        for parity, slot, inside in groups:
            piece = None
            for (peer, low_row, high_row), part_ref in zip(parts, part_refs):
                if peer % 2 == parity and low_row <= across < high_row:
                    at = (slot * (high_row - low_row) + across - low_row) * edge
                    part = part_ref[at : at + edge, :].astype(f32)
                    piece = part if piece is None else piece + part
            for block in range(blocks):
                total[block] = total[block] + jnp.where(inside[block], piece, 0.0)
        total = jnp.concatenate(total, axis=1)[:, : VY * classes]
        out_ref[across - first] = total.astype(out_ref.dtype)


def join_kernel(halves, own_ref, *rest):
    out_ref = rest[-1]
    tile_index = lax.axis_index("tiles")
    from_even = (tile_index % 2 == 1).astype(f32)
    from_odd = ((tile_index % 2 == 0) & (tile_index > 0)).astype(f32)
    for at, (low_row, high_row) in enumerate(halves):
        even_ref, odd_ref = rest[2 * at : 2 * at + 2]
        out_ref[low_row:high_row] = (
            own_ref[low_row:high_row]
            + even_ref[...].astype(f32) * from_even
            + odd_ref[...].astype(f32) * from_odd
        )


vmem = pl.BlockSpec(memory_space=pltpu.VMEM)
smem = pl.BlockSpec(memory_space=pltpu.SMEM)
hbm = pl.BlockSpec(memory_space=pltpu.HBM)
limits = pltpu.CompilerParams(vmem_limit_bytes=vmem_bytes)
ample = pltpu.CompilerParams(vmem_limit_bytes=60000000)


def on_device(
    features,
    conv_first,
    gain_first,
    shift_first,
    conv_second,
    gain_second,
    shift_second,
    head_weight,
    head_bias,
    corners,
    counts,
):
    _, slots, edge, _, data = features.shape
    in_width, width = conv_first.shape[-2:]
    classes = head_bias.shape[1]
    peers = lax.axis_size("folds") * lax.axis_size("sub")
    tiles = lax.axis_size("tiles")
    chunk = VX // peers
    area = edge * edge
    lanes = edge * classes
    padded = slots * (area + edge) + edge
    middle = chunk // 2
    halves = ((0, middle), (middle, chunk))
    parts = [(0, 0, chunk), (1, 0, chunk)]
    for low_row, high_row in halves:
        parts += [(peer, low_row, high_row) for peer in range(2, peers)]
    rows = [
        slots * edge * (high_row - low_row) + (edge if peer == 1 else 0)
        for peer, low_row, high_row in parts
    ]
    pieces = pl.pallas_call(
        functools.partial(section_kernel, (slots, edge, chunk, parts)),
        out_shape=[pltpu.VMEM((count, lanes), bf16) for count in rows],
        in_specs=[hbm] * 11,
        out_specs=[vmem] * len(parts),
        scratch_shapes=[
            pltpu.VMEM((padded, data + 256), bf16),
            pltpu.VMEM((padded, edge * width + 128), bf16),
            pltpu.VMEM((2, 3, 256, 256), bf16),
            pltpu.VMEM((3, 256, 384), bf16),
            pltpu.VMEM((padded - 2 * edge, edge * width + 128), f32),
            pltpu.SMEM(corners.shape, jnp.int32),
            pltpu.SMEM(counts.shape[::-1], jnp.int32),
            pltpu.VMEM((27 * width, in_width), bf16),
            pltpu.VMEM((1, width), f32),
            pltpu.VMEM((1, width), f32),
            pltpu.VMEM((27 * width, width), bf16),
            pltpu.VMEM((1, width), f32),
            pltpu.VMEM((1, width), f32),
            pltpu.VMEM((classes, width), bf16),
            pltpu.VMEM((1, classes), f32),
            pltpu.SemaphoreType.DMA((10 + slots,)),
        ],
        compiler_params=ample,
        name="section",
    )(
        corners,
        counts.T,
        features.reshape(slots, area, data),
        jnp.swapaxes(conv_first, 4, 5).reshape(27 * width, in_width),
        gain_first,
        shift_first,
        conv_second.reshape(27 * width, width),
        gain_second,
        shift_second,
        head_weight[0].T,
        head_bias,
    )
    arrived = []
    for (peer, _, _), piece in zip(parts, pieces):
        pairs = [(i, i ^ peer) for i in range(peers)]
        arrived.append(lax.ppermute(piece, ("folds", "sub"), pairs) if peer else piece)

    def gather(first, last, spilled, kind, name):
        chosen = [
            (part, piece)
            for part, piece in zip(parts, arrived)
            if part[1] < last and first < part[2]
        ]
        return pl.pallas_call(
            functools.partial(
                gather_kernel,
                (slots, edge, chunk, [part for part, _ in chosen], first, last, classes),
                spilled,
            ),
            out_shape=pltpu.VMEM((last - first, TZ, VY * classes), kind),
            in_specs=[smem] + [vmem] * len(chosen),
            out_specs=vmem,
            compiler_params=limits,
            cost_estimate=pl.CostEstimate(
                flops=500000000, bytes_accessed=2000000, transcendentals=0
            ),
            name=name,
        )(corners, *[piece for _, piece in chosen])

    even = [(tile, tile ^ 1) for tile in range(tiles)]
    odd = []
    for tile in range(tiles):
        for i in range(peers):
            if 0 < tile < tiles - 1:
                target = (tile + 1 if tile % 2 else tile - 1) * peers + i
            else:
                target = tile * peers + (i ^ 1)
            odd.append((tile * peers + i, target))
    from_below = []
    for first, last in halves:
        spill = gather(first, last, True, bf16, f"spill_{first}")
        from_below.append(lax.ppermute(spill, "tiles", even))
        from_below.append(lax.ppermute(spill, ("tiles", "folds", "sub"), odd))
    own = gather(0, chunk, False, f32, "own")
    joined = pl.pallas_call(
        functools.partial(join_kernel, halves),
        out_shape=jax.ShapeDtypeStruct((chunk, TZ, VY * classes), f32),
        in_specs=[vmem] * (1 + 2 * len(halves)),
        out_specs=vmem,
        compiler_params=limits,
        name="join",
    )(own, *from_below)
    return jnp.transpose(joined, (1, 0, 2))


def solution(mesh):
    placed = (
        P("folds", ("groups", "tiles", "sub"), None, None, None),
        P("folds", None, None, None, None, None),
        P("folds", None),
        P("folds", None),
        P("folds", None, None, None, None, None),
        P("folds", None),
        P("folds", None),
        P("folds", None, None),
        P("folds", None),
        P(("groups", "tiles", "sub"), None),
        P("groups", None),
    )
    return jax.shard_map(
        on_device,
        mesh=mesh,
        in_specs=placed,
        out_specs=P(("groups", "tiles"), ("folds", "sub"), None),
        check_vma=False,
    )
```

```python
import functools

import jax
import jax.numpy as jnp
from jax import lax
from jax.experimental import pallas as pl
from jax.experimental.pallas import tpu as pltpu
from jax.sharding import PartitionSpec as P

TZ = 16
VX = 40
VY = 40

epsilon = 1e-05
leak_slope = 0.01
far = 1 << 20
bf16 = jnp.bfloat16
f32 = jnp.float32
vmem_bytes = 24 << 20


def iota(shape, dim):
    return lax.broadcasted_iota(jnp.int32, shape, dim)


def tile_matrix(width, lanes):
    return (iota((width, lanes), 1) % width == iota((width, lanes), 0)).astype(bf16)


def tiled_row(ref, lanes):
    width = ref.shape[1]
    row = jnp.concatenate([ref[...], jnp.zeros((1, lanes - width), f32)], axis=1)
    row = jnp.broadcast_to(row, (8, lanes))
    reach = width
    while reach < lanes:
        row = row + pltpu.roll(row, reach, 1)
        reach *= 2
    return row[0:1]


def lane_bands(parts, places):
    total = None
    for place, part in enumerate(parts):
        if part is not None:
            total = part if total is None else jnp.where(places == place, part, total)
    if total is None:
        return None
    if any(part is None for part in parts):
        empty = None
        for place, part in enumerate(parts):
            if part is None:
                here = places == place
                empty = here if empty is None else empty | here
        total = jnp.where(empty, 0.0, total)
    return total


def build_first(taps_ref, band_ref, in_width, width):
    spread = tile_matrix(width, 128)
    places = iota((in_width, 128), 1) // width
    zero = jnp.zeros((in_width, 128), bf16)
    orders = (((1, 0), (2, None)), ((0, 1), (None, 2)))
    for dz in range(3):
        tiled = {}
        for dx in range(3):
            for dy in range(3):
                at = ((dz * 3 + dx) * 3 + dy) * width
                tiled[dx, dy] = lax.dot_general(
                    taps_ref[at : at + width],
                    spread,
                    (((0,), (0,)), ((), ())),
                    preferred_element_type=f32,
                )
        for variant in range(2):
            for yi in range(4):
                for side in range(2):
                    parts = []
                    for dx in orders[variant][side]:
                        for yo in range(2):
                            parts.append(None if dx is None else tiled.get((dx, yi - yo)))
                    block = lane_bands(parts, places)
                    band_ref[
                        variant,
                        dz,
                        yi * in_width : (yi + 1) * in_width,
                        side * 128 : (side + 1) * 128,
                    ] = zero if block is None else block.astype(bf16)


def build_second(taps_ref, band_ref, width):
    spread = tile_matrix(width, 128)
    places = iota((width, 128), 1) // width
    zero = jnp.zeros((width, 128), bf16)
    for dz in range(3):
        at = dz * 9 * width
        tiled = jnp.dot(taps_ref[at : at + 9 * width], spread, preferred_element_type=f32)
        for dx in range(3):
            taps = {
                dy: tiled[(dx * 3 + dy) * width : (dx * 3 + dy + 1) * width] for dy in range(3)
            }
            for yi in range(8):
                block = lane_bands([taps.get(yi - yo) for yo in range(4)], places)
                band_ref[dz, yi * width : (yi + 1) * width, dx * 128 : (dx + 1) * 128] = (
                    zero if block is None else block.astype(bf16)
                )


def banded(pad_ref, lane, count, edge, bands):
    total = None
    for dz in range(3):
        part = jnp.dot(
            pad_ref[dz * edge : dz * edge + count, lane : lane + 256],
            bands(dz),
            preferred_element_type=f32,
        )
        total = part if total is None else total + part
    return total


def join_across(before, here, after, across, edge):
    rows = here.shape[0]
    before = jnp.where(across == 0, 0.0, pltpu.roll(before, 1, 0))
    after = jnp.where(across == edge - 1, 0.0, pltpu.roll(after, rows - 1, 0))
    return here + before + after


def channel_mean(blocks, width, voxels):
    folded = None
    for block in blocks:
        row = jnp.sum(block, axis=0, keepdims=True)
        folded = row if folded is None else folded + row
    folded = jnp.broadcast_to(folded, (8, 128))
    reach = width
    while reach < 128:
        folded = folded + pltpu.roll(folded, reach, 1)
        reach *= 2
    return folded[0:1] * (1.0 / voxels)


def normalize(blocks, masks, gain, shift, width, voxels):
    mean_value = channel_mean(blocks, width, voxels)
    centered = []
    for block, mask in zip(blocks, masks):
        moved = block - mean_value
        centered.append(moved if mask is None else jnp.where(mask, moved, 0.0))
    variance = channel_mean([moved * moved for moved in centered], width, voxels)
    factor = lax.rsqrt(variance + epsilon) * gain
    results = []
    for moved, mask in zip(centered, masks):
        scaled = moved * factor + shift
        scaled = jnp.maximum(scaled, leak_slope * scaled)
        results.append((scaled if mask is None else jnp.where(mask, scaled, 0.0)).astype(bf16))
    return results


def fetch(pairs, sems):
    copies = []
    for at, (source, target) in enumerate(pairs):
        copy = pltpu.make_async_copy(source, target, sems.at[at])
        copy.start()
        copies.append(copy)
    return copies


def clear_edges(pad, edge, margin):
    rows, lanes = pad.shape
    pad[:edge, :] = jnp.zeros((edge, lanes), bf16)
    pad[rows - edge :, :] = jnp.zeros((edge, lanes), bf16)
    if margin:
        pad[:, :margin] = jnp.zeros((rows, margin), bf16)
        pad[:, lanes - margin :] = jnp.zeros((rows, margin), bf16)


def window_logits(pad_one, pad_two, hidden, band_one, band_two, rows_ref, head_ref, gauss_ref):
    area, lanes = gauss_ref.shape
    edge = pad_two.shape[0] - area
    edge = edge // 2
    width = (hidden.shape[1] - 128) // edge
    voxels = float(area * edge)
    across = iota((area, 128), 0) % edge
    spot = iota((area, 128), 1)
    low = spot < 64
    gain_one, shift_one = rows_ref[0:1, :128], rows_ref[1:2, :128]
    gain_two, shift_two = rows_ref[2:3, :128], rows_ref[3:4, :128]
    pairs = edge // 4 + 1
    for pair in range(pairs):
        even = banded(pad_one, 256 * pair, area, edge, lambda dz: band_one[0, dz])
        if pair < pairs - 1:
            odd = banded(pad_one, 256 * pair + 128, area, edge, lambda dz: band_one[1, dz])
            here = jnp.where(low, even[:, :128], odd[:, :128])
            before = jnp.where(low, odd[:, :128], even[:, :128])
            after = even[:, 128:] + odd[:, 128:]
        else:
            here = jnp.where(low, even[:, :128], 0.0)
            before = jnp.where(low, 0.0, even[:, :128])
            after = even[:, 128:]
        before = pltpu.roll(before, 64, 1)
        hidden[:, pair * 128 : (pair + 1) * 128] = join_across(before, here, after, across, edge)
    masks = [None] * pairs
    masks[0] = spot >= width
    masks[-1] = spot < width
    blocks = [hidden[:, pair * 128 : (pair + 1) * 128] for pair in range(pairs)]
    blocks[0] = jnp.where(masks[0], blocks[0], 0.0)
    blocks[-1] = jnp.where(masks[-1], blocks[-1], 0.0)
    normed = normalize(blocks, masks, gain_one, shift_one, width, voxels)
    for pair in range(pairs):
        pad_two[edge : edge + area, pair * 128 : (pair + 1) * 128] = normed[pair]

    quads = edge // 4
    for quad in range(quads):
        three = banded(pad_two, 128 * quad, area, edge, lambda dz: band_two[dz])
        hidden[:, quad * 128 : (quad + 1) * 128] = join_across(
            three[:, :128], three[:, 128:256], three[:, 256:], across, edge
        )
    blocks = [hidden[:, quad * 128 : (quad + 1) * 128] for quad in range(quads)]
    normed = normalize(blocks, [None] * quads, gain_two, shift_two, width, voxels)
    logits = jnp.concatenate(
        [
            jnp.dot(
                jnp.concatenate(normed[side : side + quads // 2], axis=1),
                head_ref[...],
                preferred_element_type=f32,
            )
            for side in (0, quads // 2)
        ],
        axis=1,
    )
    return (logits + rows_ref[4:5, :]) * gauss_ref[...]


def place(weighted, slot, pieces, corners_ref, counts_ref, code_ref, chunk, edge):
    tile_index = lax.axis_index("tiles")
    sub_index = lax.axis_index("sub")
    position = lax.axis_index("folds") * lax.axis_size("sub") + sub_index
    depth = corners_ref[slot, 0] - tile_index * TZ
    alive = slot < counts_ref[sub_index, tile_index]
    selects = []
    for peer, low_row, high_row, _, _ in pieces:
        wanted = depth + edge * ((position ^ peer) * chunk - corners_ref[slot, 1])
        wanted = jnp.where(alive, wanted, far)
        code = code_ref[low_row * edge : high_row * edge, :]
        selects.append((code == wanted).astype(f32).astype(bf16))
    placed = jnp.dot(jnp.concatenate(selects, axis=0), weighted, preferred_element_type=f32)
    placed = placed.astype(bf16)
    start = 0
    for _, low_row, high_row, out_ref, at in pieces:
        size = (high_row - low_row) * edge
        out_ref[at : at + size, :] = placed[start : start + size]
        start += size


def turned(weighted, slot, corners_ref, lanes, classes):
    return pltpu.roll(weighted, (corners_ref[slot, 2] * classes) % lanes, 1).astype(bf16)


def first_kernel(
    sizes,
    corners_hbm,
    counts_hbm,
    features_ref,
    taps_one_hbm,
    gain_one_hbm,
    shift_one_hbm,
    taps_two_hbm,
    gain_two_hbm,
    shift_two_hbm,
    head_hbm,
    bias_hbm,
    *rest,
):
    slots, edge, chunk, parts = sizes
    out_refs = rest[: len(parts)]
    (
        weighted_ref,
        band_one,
        band_two,
        rows_ref,
        head_block_ref,
        gauss_ref,
        code_ref,
        next_ref,
        pad_one,
        pad_two,
        hidden,
        corners_ref,
        counts_ref,
        taps_one_ref,
        gain_one_ref,
        shift_one_ref,
        taps_two_ref,
        gain_two_ref,
        shift_two_ref,
        head_ref,
        bias_ref,
        sems,
    ) = rest[len(parts) :]
    in_width = taps_one_ref.shape[1]
    classes, width = head_ref.shape
    area = edge * edge
    data = edge * in_width
    lanes = edge * classes
    inner = (pl.ds(edge, area), pl.ds(128, data))
    copies = fetch(
        [
            (taps_one_hbm, taps_one_ref),
            (features_ref.at[0], pad_one.at[inner]),
            (taps_two_hbm, taps_two_ref),
            (gain_one_hbm, gain_one_ref),
            (shift_one_hbm, shift_one_ref),
            (gain_two_hbm, gain_two_ref),
            (shift_two_hbm, shift_two_ref),
            (head_hbm, head_ref),
            (bias_hbm, bias_ref),
            (corners_hbm, corners_ref),
            (counts_hbm, counts_ref),
        ]
        + [
            (features_ref.at[slot], next_ref.at[(slot - 1,) + inner])
            for slot in range(1, slots)
        ],
        sems,
    )
    clear_edges(pad_one, edge, 128)
    clear_edges(pad_two, edge, 0)
    for slot in range(1, slots):
        clear_edges(next_ref.at[slot - 1], edge, 128)

    center, spread = (edge - 1) / 2.0, edge / 4.0

    def profile(offset):
        return jnp.exp(-((offset.astype(f32) - center) ** 2) / (2.0 * spread * spread))

    row_at = iota((area, 128), 0)
    lane_at = iota((1, lanes), 1)
    gauss = profile(row_at // edge) * profile(row_at % edge)
    gauss = jnp.concatenate([gauss] * (lanes // 128), axis=1) * profile(lane_at // classes)
    gauss_ref[...] = gauss
    row = iota((chunk * edge, area), 0)
    source = iota((chunk * edge, area), 1)
    turn = (row % edge - source // edge) & (edge - 1)
    code_ref[...] = turn + edge * (source % edge - row // edge)

    copies[0].wait()
    build_first(taps_one_ref, band_one, in_width, width)
    for copy in copies[1:11]:
        copy.wait()
    build_second(taps_two_ref, band_two, width)
    rows_ref[0:1, :128] = tiled_row(gain_one_ref, 128)
    rows_ref[1:2, :128] = tiled_row(shift_one_ref, 128)
    rows_ref[2:3, :128] = tiled_row(gain_two_ref, 128)
    rows_ref[3:4, :128] = tiled_row(shift_two_ref, 128)
    rows_ref[4:5, :] = tiled_row(bias_ref, lanes)
    half = edge // 2
    head_row = lax.dot_general(
        head_ref[...],
        tile_matrix(classes, half * classes),
        (((0,), (0,)), ((), ())),
        preferred_element_type=f32,
    )
    block = (half * width, half * classes)
    head_block_ref[...] = jnp.where(
        iota(block, 0) // width == iota(block, 1) // classes,
        jnp.concatenate([head_row] * half, axis=0),
        0.0,
    ).astype(bf16)

    weighted = window_logits(
        pad_one, pad_two, hidden, band_one, band_two, rows_ref, head_block_ref, gauss_ref
    )
    weighted = turned(weighted, 0, corners_ref, lanes, classes)
    weighted_ref[...] = weighted
    place(
        weighted,
        0,
        [(part[0], part[1], part[2], ref, 0) for part, ref in zip(parts, out_refs)],
        corners_ref,
        counts_ref,
        code_ref,
        chunk,
        edge,
    )
    for copy in copies[11:]:
        copy.wait()


def next_kernel(
    sizes,
    corners_hbm,
    counts_hbm,
    band_one,
    band_two,
    rows_ref,
    head_block_ref,
    gauss_ref,
    code_ref,
    next_ref,
    *rest,
):
    slots, edge, chunk, classes, parts = sizes
    weighted_refs = rest[:1]
    out_refs = rest[1 : 1 + len(parts)]
    pad_two, hidden, corners_ref, counts_ref, sems = rest[1 + len(parts) :]
    lanes = edge * classes
    copies = fetch([(corners_hbm, corners_ref), (counts_hbm, counts_ref)], sems)
    clear_edges(pad_two, edge, 0)
    for copy in copies:
        copy.wait()
    mark = iota((edge, lanes), 0)
    notes = jnp.zeros((edge, lanes), f32)
    for slot in range(slots):
        depth = corners_ref[slot, 0] - lax.axis_index("tiles") * TZ
        notes = jnp.where(mark == 2 * slot, depth.astype(f32), notes)
        notes = jnp.where(mark == 2 * slot + 1, corners_ref[slot, 2].astype(f32), notes)
    for slot in range(slots):
        if slot == 0:
            weighted = weighted_refs[0][...]
        else:
            weighted = window_logits(
                next_ref.at[slot - 1],
                pad_two,
                hidden,
                band_one,
                band_two,
                rows_ref,
                head_block_ref,
                gauss_ref,
            )
            weighted = turned(weighted, slot, corners_ref, lanes, classes)
        pieces = []
        for (peer, low_row, high_row, first), out_ref in zip(parts, out_refs):
            if slot >= first:
                at = (slot - first) * (high_row - low_row) * edge
                pieces.append((peer, low_row, high_row, out_ref, at))
        place(weighted, slot, pieces, corners_ref, counts_ref, code_ref, chunk, edge)
    for (peer, _, _, _), out_ref in zip(parts, out_refs):
        if peer < 2:
            out_ref[slots * edge * chunk :, :] = notes.astype(bf16)


def gather_kernel(sizes, spilled, *rest):
    slots, edge, chunk, parts, first, last, classes = sizes
    part_refs = rest[: len(parts)]
    out_ref = rest[len(parts)]
    lanes = edge * classes
    blocks = -(-VY * classes // lanes)

    depth_at = iota((edge, lanes), 0)
    lane_at = iota((edge, lanes), 1)
    groups = []
    for (peer, _, _, _, _), part_ref in zip(parts, part_refs):
        if peer >= 2:
            continue
        notes = part_ref[slots * edge * chunk :, :].astype(f32).astype(jnp.int32)
        for slot in range(slots):
            depth = notes[2 * slot : 2 * slot + 1]
            start = notes[2 * slot + 1 : 2 * slot + 2] * classes
            keep = depth_at < depth if spilled else depth_at >= depth
            inside = []
            for block in range(blocks):
                lane = lane_at + block * lanes
                inside.append(keep & (lane >= start) & (lane < start + lanes))
            groups.append((peer, slot, inside))

    for across in range(first, last):
        total = [jnp.zeros((edge, lanes), f32) for _ in range(blocks)]
        for parity, slot, inside in groups:
            piece = None
            for (peer, low_row, high_row, low_slot, high_slot), part_ref in zip(parts, part_refs):
                if (
                    peer % 2 == parity
                    and low_row <= across < high_row
                    and low_slot <= slot < high_slot
                ):
                    at = ((slot - low_slot) * (high_row - low_row) + across - low_row) * edge
                    part = part_ref[at : at + edge, :].astype(f32)
                    piece = part if piece is None else piece + part
            for block in range(blocks):
                total[block] = total[block] + jnp.where(inside[block], piece, 0.0)
        total = jnp.concatenate(total, axis=1)[:, : VY * classes]
        out_ref[across - first] = total.astype(out_ref.dtype)


def join_kernel(halves, own_ref, *rest):
    out_ref = rest[-1]
    tile_index = lax.axis_index("tiles")
    from_even = (tile_index % 2 == 1).astype(f32)
    from_odd = ((tile_index % 2 == 0) & (tile_index > 0)).astype(f32)
    for at, (low_row, high_row) in enumerate(halves):
        even_ref, odd_ref = rest[2 * at : 2 * at + 2]
        out_ref[low_row:high_row] = (
            own_ref[low_row:high_row]
            + even_ref[...].astype(f32) * from_even
            + odd_ref[...].astype(f32) * from_odd
        )


vmem = pl.BlockSpec(memory_space=pltpu.VMEM)
hbm = pl.BlockSpec(memory_space=pltpu.HBM)
limits = pltpu.CompilerParams(vmem_limit_bytes=vmem_bytes)
ample = pltpu.CompilerParams(vmem_limit_bytes=58000000)


def on_device(
    features,
    conv_first,
    gain_first,
    shift_first,
    conv_second,
    gain_second,
    shift_second,
    head_weight,
    head_bias,
    corners,
    counts,
):
    _, slots, edge, _, data = features.shape
    in_width, width = conv_first.shape[-2:]
    classes = head_bias.shape[1]
    peers = lax.axis_size("folds") * lax.axis_size("sub")
    tiles = lax.axis_size("tiles")
    chunk = VX // peers
    area = edge * edge
    lanes = edge * classes
    middle = chunk // 2
    halves = ((0, middle), (middle, chunk))
    far_peers = range(2, peers)
    first_parts = [(peer, 0, chunk) for peer in far_peers]
    next_parts = [(0, 0, chunk, 0), (1, 0, chunk, 0)]
    for low_row, high_row in halves:
        next_parts += [(peer, low_row, high_row, 1) for peer in far_peers]

    small = [
        pltpu.SMEM(corners.shape, jnp.int32),
        pltpu.SMEM(counts.shape[::-1], jnp.int32),
    ]
    pad_one = (area + 2 * edge, data + 256)
    pad_two = pltpu.VMEM((area + 2 * edge, edge * width + 128), bf16)
    hidden = pltpu.VMEM((area, edge * width + 128), f32)
    work = pl.CostEstimate(flops=5000000000, bytes_accessed=3000000, transcendentals=0)
    outs = [pltpu.VMEM((chunk * edge, lanes), bf16) for _ in first_parts] + [
        pltpu.VMEM((area, lanes), bf16),
        pltpu.VMEM((2, 3, 256, 256), bf16),
        pltpu.VMEM((3, 256, 384), bf16),
        pltpu.VMEM((8, lanes), f32),
        pltpu.VMEM((edge // 2 * width, edge // 2 * classes), bf16),
        pltpu.VMEM((area, lanes), f32),
        pltpu.VMEM((chunk * edge, area), jnp.int32),
        pltpu.VMEM((slots - 1,) + pad_one, bf16),
    ]
    *first_pieces, weighted, band_one, band_two, rows, head_block, gauss, code, following = (
        pl.pallas_call(
            functools.partial(first_kernel, (slots, edge, chunk, first_parts)),
            out_shape=outs,
            in_specs=[hbm] * 11,
            out_specs=[vmem] * len(outs),
            scratch_shapes=[pltpu.VMEM(pad_one, bf16), pad_two, hidden]
            + small
            + [
                pltpu.VMEM((27 * width, in_width), bf16),
                pltpu.VMEM((1, width), f32),
                pltpu.VMEM((1, width), f32),
                pltpu.VMEM((27 * width, width), bf16),
                pltpu.VMEM((1, width), f32),
                pltpu.VMEM((1, width), f32),
                pltpu.VMEM((classes, width), bf16),
                pltpu.VMEM((1, classes), f32),
                pltpu.SemaphoreType.DMA((10 + slots,)),
            ],
            compiler_params=ample,
            cost_estimate=work,
            name="first_slot",
        )(
            corners,
            counts.T,
            features.reshape(slots, area, data),
            jnp.swapaxes(conv_first, 4, 5).reshape(27 * width, in_width),
            gain_first,
            shift_first,
            conv_second.reshape(27 * width, width),
            gain_second,
            shift_second,
            head_weight[0].T,
            head_bias,
        )
    )
    next_pieces = pl.pallas_call(
        functools.partial(next_kernel, (slots, edge, chunk, classes, next_parts)),
        out_shape=[
            pltpu.VMEM(
                (
                    (slots - first) * edge * (high_row - low_row) + (edge if peer < 2 else 0),
                    lanes,
                ),
                bf16,
            )
            for peer, low_row, high_row, first in next_parts
        ],
        in_specs=[hbm] * 2 + [vmem] * 8,
        out_specs=[vmem] * len(next_parts),
        scratch_shapes=[pad_two, hidden] + small + [pltpu.SemaphoreType.DMA((2,))],
        compiler_params=limits,
        cost_estimate=work,
        name="next_slots",
    )(corners, counts.T, band_one, band_two, rows, head_block, gauss, code, following, weighted)

    def exchange(peer, piece):
        pairs = [(i, i ^ peer) for i in range(peers)]
        return lax.ppermute(piece, ("folds", "sub"), pairs) if peer else piece

    early = [exchange(part[0], piece) for part, piece in zip(first_parts, first_pieces)]
    early, next_pieces = lax.optimization_barrier((early, next_pieces))
    late = [exchange(part[0], piece) for part, piece in zip(next_parts, next_pieces)]
    parts = [part + (0, 1) for part in first_parts] + [part + (slots,) for part in next_parts]
    arrived = early + late

    def gather(first, last, spilled, kind, name):
        chosen = [
            (part, piece)
            for part, piece in zip(parts, arrived)
            if part[1] < last and first < part[2]
        ]
        return pl.pallas_call(
            functools.partial(
                gather_kernel,
                (slots, edge, chunk, [part for part, _ in chosen], first, last, classes),
                spilled,
            ),
            out_shape=pltpu.VMEM((last - first, TZ, VY * classes), kind),
            in_specs=[vmem] * len(chosen),
            out_specs=vmem,
            compiler_params=limits,
            cost_estimate=pl.CostEstimate(
                flops=500000000, bytes_accessed=2000000, transcendentals=0
            ),
            name=name,
        )(*[piece for _, piece in chosen])

    even = [(tile, tile ^ 1) for tile in range(tiles)]
    odd = []
    for tile in range(tiles):
        for i in range(peers):
            if 0 < tile < tiles - 1:
                target = (tile + 1 if tile % 2 else tile - 1) * peers + i
            else:
                target = tile * peers + (i ^ 1)
            odd.append((tile * peers + i, target))
    from_below = []
    for first, last in halves:
        spill = gather(first, last, True, bf16, f"spill_{first}")
        from_below.append(lax.ppermute(spill, "tiles", even))
        from_below.append(lax.ppermute(spill, ("tiles", "folds", "sub"), odd))
    own = gather(0, chunk, False, f32, "own")
    joined = pl.pallas_call(
        functools.partial(join_kernel, halves),
        out_shape=jax.ShapeDtypeStruct((chunk, TZ, VY * classes), f32),
        in_specs=[vmem] * (1 + 2 * len(halves)),
        out_specs=vmem,
        compiler_params=limits,
        name="join",
    )(own, *from_below)
    return jnp.transpose(joined, (1, 0, 2))


def solution(mesh):
    placed = (
        P("folds", ("groups", "tiles", "sub"), None, None, None),
        P("folds", None, None, None, None, None),
        P("folds", None),
        P("folds", None),
        P("folds", None, None, None, None, None),
        P("folds", None),
        P("folds", None),
        P("folds", None, None),
        P("folds", None),
        P(("groups", "tiles", "sub"), None),
        P("groups", None),
    )
    return jax.shard_map(
        on_device,
        mesh=mesh,
        in_specs=placed,
        out_specs=P(("groups", "tiles"), ("folds", "sub"), None),
        check_vma=False,
    )
```

```python
import functools

import jax
import jax.numpy as jnp
from jax import lax
from jax.experimental import pallas as pl
from jax.experimental.pallas import tpu as pltpu
from jax.sharding import PartitionSpec as P

TZ = 16
VX = 40
VY = 40

epsilon = 1e-05
leak_slope = 0.01
far = 1 << 20
bf16 = jnp.bfloat16
f32 = jnp.float32
vmem_bytes = 48 << 20


def iota(shape, dim):
    return lax.broadcasted_iota(jnp.int32, shape, dim)


def tile_matrix(width, lanes):
    return (iota((width, lanes), 1) % width == iota((width, lanes), 0)).astype(bf16)


def tiled_row(ref, lanes):
    width = ref.shape[1]
    row = jnp.concatenate([ref[...], jnp.zeros((1, lanes - width), f32)], axis=1)
    row = jnp.broadcast_to(row, (8, lanes))
    reach = width
    while reach < lanes:
        row = row + pltpu.roll(row, reach, 1)
        reach *= 2
    return row[0:1]


def lane_bands(parts, places):
    total = None
    for place, part in enumerate(parts):
        if part is not None:
            total = part if total is None else jnp.where(places == place, part, total)
    if total is None:
        return None
    if any(part is None for part in parts):
        empty = None
        for place, part in enumerate(parts):
            if part is None:
                here = places == place
                empty = here if empty is None else empty | here
        total = jnp.where(empty, 0.0, total)
    return total


def build_first(taps_ref, band_ref, in_width, width):
    spread = tile_matrix(width, 128)
    places = iota((in_width, 128), 1) // width
    zero = jnp.zeros((in_width, 128), bf16)
    orders = (((1, 0), (2, None)), ((0, 1), (None, 2)))
    for dz in range(3):
        tiled = {}
        for dx in range(3):
            for dy in range(3):
                at = ((dz * 3 + dx) * 3 + dy) * width
                tiled[dx, dy] = lax.dot_general(
                    taps_ref[at : at + width],
                    spread,
                    (((0,), (0,)), ((), ())),
                    preferred_element_type=f32,
                )
        for variant in range(2):
            for yi in range(4):
                for side in range(2):
                    parts = []
                    for dx in orders[variant][side]:
                        for yo in range(2):
                            parts.append(None if dx is None else tiled.get((dx, yi - yo)))
                    block = lane_bands(parts, places)
                    band_ref[
                        variant,
                        dz,
                        yi * in_width : (yi + 1) * in_width,
                        side * 128 : (side + 1) * 128,
                    ] = zero if block is None else block.astype(bf16)


def build_second(taps_ref, band_ref, width):
    spread = tile_matrix(width, 128)
    places = iota((width, 128), 1) // width
    zero = jnp.zeros((width, 128), bf16)
    for dz in range(3):
        at = dz * 9 * width
        tiled = jnp.dot(taps_ref[at : at + 9 * width], spread, preferred_element_type=f32)
        for dx in range(3):
            taps = {
                dy: tiled[(dx * 3 + dy) * width : (dx * 3 + dy + 1) * width] for dy in range(3)
            }
            for yi in range(8):
                block = lane_bands([taps.get(yi - yo) for yo in range(4)], places)
                band_ref[dz, yi * width : (yi + 1) * width, dx * 128 : (dx + 1) * 128] = (
                    zero if block is None else block.astype(bf16)
                )


def banded(pad_ref, lane, count, edge, bands):
    total = None
    for dz in range(3):
        part = jnp.dot(
            pad_ref[dz * edge : dz * edge + count, lane : lane + 256],
            bands(dz),
            preferred_element_type=f32,
        )
        total = part if total is None else total + part
    return total


def join_across(before, here, after, across, edge):
    rows = here.shape[0]
    before = jnp.where(across == 0, 0.0, pltpu.roll(before, 1, 0))
    after = jnp.where(across == edge - 1, 0.0, pltpu.roll(after, rows - 1, 0))
    return here + before + after


def channel_mean(blocks, width, voxels):
    folded = None
    for block in blocks:
        row = jnp.sum(block, axis=0, keepdims=True)
        folded = row if folded is None else folded + row
    folded = jnp.broadcast_to(folded, (8, 128))
    reach = width
    while reach < 128:
        folded = folded + pltpu.roll(folded, reach, 1)
        reach *= 2
    return folded[0:1] * (1.0 / voxels)


def normalize(blocks, masks, gain, shift, width, voxels):
    mean_value = channel_mean(blocks, width, voxels)
    centered = []
    for block, mask in zip(blocks, masks):
        moved = block - mean_value
        centered.append(moved if mask is None else jnp.where(mask, moved, 0.0))
    variance = channel_mean([moved * moved for moved in centered], width, voxels)
    factor = lax.rsqrt(variance + epsilon) * gain
    results = []
    for moved, mask in zip(centered, masks):
        scaled = moved * factor + shift
        scaled = jnp.maximum(scaled, leak_slope * scaled)
        results.append((scaled if mask is None else jnp.where(mask, scaled, 0.0)).astype(bf16))
    return results


def section_kernel(
    sizes,
    corners_hbm,
    counts_hbm,
    features_ref,
    taps_one_hbm,
    gain_one_hbm,
    shift_one_hbm,
    taps_two_hbm,
    gain_two_hbm,
    shift_two_hbm,
    head_hbm,
    bias_hbm,
    *rest,
):
    slots, edge, chunk, parts = sizes
    out_refs = rest[: len(parts)]
    (
        pad_one,
        pad_two,
        band_one,
        band_two,
        hidden,
        corners_ref,
        counts_ref,
        taps_one_ref,
        gain_one_ref,
        shift_one_ref,
        taps_two_ref,
        gain_two_ref,
        shift_two_ref,
        head_ref,
        bias_ref,
        sems,
    ) = rest[len(parts) :]
    in_width = taps_one_ref.shape[1]
    classes, width = head_ref.shape
    area = edge * edge
    stride = area + edge
    count = hidden.shape[0]
    voxels = float(area * edge)
    data = edge * in_width
    lanes = edge * classes

    copies = []
    for at, (source, target) in enumerate(
        [
            (taps_one_hbm, taps_one_ref),
            (taps_two_hbm, taps_two_ref),
            (gain_one_hbm, gain_one_ref),
            (shift_one_hbm, shift_one_ref),
            (gain_two_hbm, gain_two_ref),
            (shift_two_hbm, shift_two_ref),
            (head_hbm, head_ref),
            (bias_hbm, bias_ref),
            (corners_hbm, corners_ref),
            (counts_hbm, counts_ref),
        ]
        + [
            (
                features_ref.at[slot],
                pad_one.at[pl.ds(edge + slot * stride, area), pl.ds(128, data)],
            )
            for slot in range(slots)
        ]
    ):
        copy = pltpu.make_async_copy(source, target, sems.at[at])
        copy.start()
        copies.append(copy)
    for pad in (pad_one, pad_two):
        for slot in range(slots + 1):
            pad[slot * stride : slot * stride + edge, :] = jnp.zeros((edge, pad.shape[1]), bf16)
    pad_one[:, :128] = jnp.zeros((pad_one.shape[0], 128), bf16)
    pad_one[:, 128 + data :] = jnp.zeros((pad_one.shape[0], 128), bf16)

    center, spread = (edge - 1) / 2.0, edge / 4.0

    def profile(offset):
        return jnp.exp(-((offset.astype(f32) - center) ** 2) / (2.0 * spread * spread))

    row_at = iota((area, 128), 0)
    lane_at = iota((1, lanes), 1)
    gauss = profile(row_at // edge) * profile(row_at % edge)
    gauss = jnp.concatenate([gauss] * (lanes // 128), axis=1) * profile(lane_at // classes)

    row = iota((chunk * edge, area), 0)
    source = iota((chunk * edge, area), 1)
    turn = (row % edge - source // edge) & (edge - 1)
    code = turn + edge * (source % edge - row // edge)
    across = iota((count, 128), 0) % edge
    tile_index = lax.axis_index("tiles")
    sub_index = lax.axis_index("sub")
    position = lax.axis_index("folds") * lax.axis_size("sub") + sub_index

    for copy in copies[:-slots]:
        copy.wait()
    build_first(taps_one_ref, band_one, in_width, width)
    build_second(taps_two_ref, band_two, width)
    gain_one, shift_one = tiled_row(gain_one_ref, 128), tiled_row(shift_one_ref, 128)
    gain_two, shift_two = tiled_row(gain_two_ref, 128), tiled_row(shift_two_ref, 128)

    half = edge // 2
    head_row = lax.dot_general(
        head_ref[...],
        tile_matrix(classes, half * classes),
        (((0,), (0,)), ((), ())),
        preferred_element_type=f32,
    )
    block = (half * width, half * classes)
    head_block = jnp.where(
        iota(block, 0) // width == iota(block, 1) // classes,
        jnp.concatenate([head_row] * half, axis=0),
        0.0,
    ).astype(bf16)
    bias = tiled_row(bias_ref, lanes)

    mark = iota((edge, lanes), 0)
    notes = jnp.zeros((edge, lanes), f32)
    for slot in range(slots):
        depth = corners_ref[slot, 0] - tile_index * TZ
        notes = jnp.where(mark == 2 * slot, depth.astype(f32), notes)
        notes = jnp.where(mark == 2 * slot + 1, corners_ref[slot, 2].astype(f32), notes)
    for (peer, _, _), out_ref in zip(parts, out_refs):
        if peer < 2:
            out_ref[slots * edge * chunk :, :] = notes.astype(bf16)

    for copy in copies[-slots:]:
        copy.wait()
    low = iota((count, 128), 1) < 64
    spot = iota((area, 128), 1)
    pairs = edge // 4 + 1
    for pair in range(pairs):
        even = banded(pad_one, 256 * pair, count, edge, lambda dz: band_one[0, dz])
        if pair < pairs - 1:
            odd = banded(pad_one, 256 * pair + 128, count, edge, lambda dz: band_one[1, dz])
            here = jnp.where(low, even[:, :128], odd[:, :128])
            before = jnp.where(low, odd[:, :128], even[:, :128])
            after = even[:, 128:] + odd[:, 128:]
        else:
            here = jnp.where(low, even[:, :128], 0.0)
            before = jnp.where(low, 0.0, even[:, :128])
            after = even[:, 128:]
        before = pltpu.roll(before, 64, 1)
        hidden[:, pair * 128 : (pair + 1) * 128] = join_across(before, here, after, across, edge)
    masks = [None] * pairs
    masks[0] = spot >= width
    masks[-1] = spot < width
    for slot in range(slots):
        at = slot * stride
        blocks = [hidden[at : at + area, pair * 128 : (pair + 1) * 128] for pair in range(pairs)]
        blocks[0] = jnp.where(masks[0], blocks[0], 0.0)
        blocks[-1] = jnp.where(masks[-1], blocks[-1], 0.0)
        normed = normalize(blocks, masks, gain_one, shift_one, width, voxels)
        for pair in range(pairs):
            pad_two[at + edge : at + edge + area, pair * 128 : (pair + 1) * 128] = normed[pair]

    quads = edge // 4
    for quad in range(quads):
        three = banded(pad_two, 128 * quad, count, edge, lambda dz: band_two[dz])
        hidden[:, quad * 128 : (quad + 1) * 128] = join_across(
            three[:, :128], three[:, 128:256], three[:, 256:], across, edge
        )
    for slot in range(slots):
        at = slot * stride
        blocks = [hidden[at : at + area, quad * 128 : (quad + 1) * 128] for quad in range(quads)]
        normed = normalize(blocks, [None] * quads, gain_two, shift_two, width, voxels)
        logits = jnp.concatenate(
            [
                jnp.dot(
                    jnp.concatenate(normed[side : side + quads // 2], axis=1),
                    head_block,
                    preferred_element_type=f32,
                )
                for side in (0, quads // 2)
            ],
            axis=1,
        )
        weighted = (logits + bias) * gauss
        lane_start = corners_ref[slot, 2] * classes
        weighted = pltpu.roll(weighted, lane_start % lanes, 1).astype(bf16)
        depth = corners_ref[slot, 0] - tile_index * TZ
        alive = slot < counts_ref[sub_index, tile_index]
        for (peer, low_row, high_row), out_ref in zip(parts, out_refs):
            wanted = depth + edge * ((position ^ peer) * chunk - corners_ref[slot, 1])
            wanted = jnp.where(alive, wanted, far)
            select = (code[low_row * edge : high_row * edge] == wanted).astype(f32).astype(bf16)
            size = (high_row - low_row) * edge
            out_ref[slot * size : (slot + 1) * size, :] = jnp.dot(
                select, weighted, preferred_element_type=f32
            ).astype(bf16)


def gather_kernel(sizes, spilled, *rest):
    slots, edge, chunk, parts, first, last, classes = sizes
    part_refs = rest[: len(parts)]
    out_ref = rest[len(parts)]
    lanes = edge * classes
    blocks = -(-VY * classes // lanes)

    depth_at = iota((edge, lanes), 0)
    lane_at = iota((edge, lanes), 1)
    groups = []
    for (peer, _, _), part_ref in zip(parts, part_refs):
        if peer >= 2:
            continue
        notes = part_ref[slots * edge * chunk :, :].astype(f32).astype(jnp.int32)
        for slot in range(slots):
            depth = notes[2 * slot : 2 * slot + 1]
            start = notes[2 * slot + 1 : 2 * slot + 2] * classes
            keep = depth_at < depth if spilled else depth_at >= depth
            inside = []
            for block in range(blocks):
                lane = lane_at + block * lanes
                inside.append(keep & (lane >= start) & (lane < start + lanes))
            groups.append((peer, slot, inside))

    for across in range(first, last):
        total = [jnp.zeros((edge, lanes), f32) for _ in range(blocks)]
        for parity, slot, inside in groups:
            piece = None
            for (peer, low_row, high_row), part_ref in zip(parts, part_refs):
                if peer % 2 == parity and low_row <= across < high_row:
                    at = (slot * (high_row - low_row) + across - low_row) * edge
                    part = part_ref[at : at + edge, :].astype(f32)
                    piece = part if piece is None else piece + part
            for block in range(blocks):
                total[block] = total[block] + jnp.where(inside[block], piece, 0.0)
        total = jnp.concatenate(total, axis=1)[:, : VY * classes]
        out_ref[across - first] = total.astype(out_ref.dtype)


def join_kernel(halves, own_ref, *rest):
    out_ref, total, sems = rest[-3:]
    tile_index = lax.axis_index("tiles")
    from_even = (tile_index % 2 == 1).astype(f32)
    from_odd = ((tile_index % 2 == 0) & (tile_index > 0)).astype(f32)
    copies = []
    for at, (low_row, high_row) in enumerate(halves):
        even_ref, odd_ref = rest[2 * at : 2 * at + 2]
        for row in range(low_row, high_row):
            total[row] = (
                own_ref[row]
                + even_ref[row - low_row].astype(f32) * from_even
                + odd_ref[row - low_row].astype(f32) * from_odd
            )
            copy = pltpu.make_async_copy(total.at[row], out_ref.at[row], sems.at[row])
            copy.start()
            copies.append(copy)
    for copy in copies:
        copy.wait()


vmem = pl.BlockSpec(memory_space=pltpu.VMEM)
hbm = pl.BlockSpec(memory_space=pltpu.HBM)
limits = pltpu.CompilerParams(vmem_limit_bytes=vmem_bytes)
ample = pltpu.CompilerParams(vmem_limit_bytes=60000000)


def on_device(
    features,
    conv_first,
    gain_first,
    shift_first,
    conv_second,
    gain_second,
    shift_second,
    head_weight,
    head_bias,
    corners,
    counts,
):
    _, slots, edge, _, data = features.shape
    in_width, width = conv_first.shape[-2:]
    classes = head_bias.shape[1]
    peers = lax.axis_size("folds") * lax.axis_size("sub")
    tiles = lax.axis_size("tiles")
    chunk = VX // peers
    area = edge * edge
    lanes = edge * classes
    padded = slots * (area + edge) + edge
    middle = chunk // 2
    halves = ((0, middle), (middle, chunk))
    parts = [(0, 0, chunk), (1, 0, chunk)]
    for low_row, high_row in halves:
        parts += [(peer, low_row, high_row) for peer in range(2, peers)]
    rows = [
        slots * edge * (high_row - low_row) + (edge if peer < 2 else 0)
        for peer, low_row, high_row in parts
    ]
    pieces = pl.pallas_call(
        functools.partial(section_kernel, (slots, edge, chunk, parts)),
        out_shape=[pltpu.VMEM((count, lanes), bf16) for count in rows],
        in_specs=[hbm] * 11,
        out_specs=[vmem] * len(parts),
        scratch_shapes=[
            pltpu.VMEM((padded, data + 256), bf16),
            pltpu.VMEM((padded, edge * width + 128), bf16),
            pltpu.VMEM((2, 3, 256, 256), bf16),
            pltpu.VMEM((3, 256, 384), bf16),
            pltpu.VMEM((padded - 2 * edge, edge * width + 128), f32),
            pltpu.SMEM(corners.shape, jnp.int32),
            pltpu.SMEM(counts.shape[::-1], jnp.int32),
            pltpu.VMEM((27 * width, in_width), bf16),
            pltpu.VMEM((1, width), f32),
            pltpu.VMEM((1, width), f32),
            pltpu.VMEM((27 * width, width), bf16),
            pltpu.VMEM((1, width), f32),
            pltpu.VMEM((1, width), f32),
            pltpu.VMEM((classes, width), bf16),
            pltpu.VMEM((1, classes), f32),
            pltpu.SemaphoreType.DMA((10 + slots,)),
        ],
        compiler_params=ample,
        name="section",
    )(
        corners,
        counts.T,
        features.reshape(slots, area, data),
        jnp.swapaxes(conv_first, 4, 5).reshape(27 * width, in_width),
        gain_first,
        shift_first,
        conv_second.reshape(27 * width, width),
        gain_second,
        shift_second,
        head_weight[0].T,
        head_bias,
    )
    arrived = []
    for (peer, _, _), piece in zip(parts, pieces):
        pairs = [(i, i ^ peer) for i in range(peers)]
        arrived.append(lax.ppermute(piece, ("folds", "sub"), pairs) if peer else piece)

    def gather(first, last, spilled, kind, name):
        chosen = [
            (part, piece)
            for part, piece in zip(parts, arrived)
            if part[1] < last and first < part[2]
        ]
        return pl.pallas_call(
            functools.partial(
                gather_kernel,
                (slots, edge, chunk, [part for part, _ in chosen], first, last, classes),
                spilled,
            ),
            out_shape=pltpu.VMEM((last - first, TZ, VY * classes), kind),
            in_specs=[vmem] * len(chosen),
            out_specs=vmem,
            compiler_params=limits,
            cost_estimate=pl.CostEstimate(
                flops=500000000, bytes_accessed=2000000, transcendentals=0
            ),
            name=name,
        )(*[piece for _, piece in chosen])

    even = [(tile, tile ^ 1) for tile in range(tiles)]
    odd = []
    for tile in range(tiles):
        for i in range(peers):
            if 0 < tile < tiles - 1:
                target = (tile + 1 if tile % 2 else tile - 1) * peers + i
            else:
                target = tile * peers + (i ^ 1)
            odd.append((tile * peers + i, target))
    from_below = []
    for first, last in halves:
        spill = gather(first, last, True, bf16, f"spill_{first}")
        from_below.append(lax.ppermute(spill, "tiles", even))
        from_below.append(lax.ppermute(spill, ("tiles", "folds", "sub"), odd))
    own = gather(0, chunk, False, f32, "own")
    joined = pl.pallas_call(
        functools.partial(join_kernel, halves),
        out_shape=jax.ShapeDtypeStruct((chunk, TZ, VY * classes), f32),
        in_specs=[vmem] * (1 + 2 * len(halves)),
        out_specs=hbm,
        scratch_shapes=[
            pltpu.VMEM((chunk, TZ, VY * classes), f32),
            pltpu.SemaphoreType.DMA((chunk,)),
        ],
        compiler_params=limits,
        name="join",
    )(own, *from_below)
    return jnp.transpose(joined, (1, 0, 2))


def solution(mesh):
    placed = (
        P("folds", ("groups", "tiles", "sub"), None, None, None),
        P("folds", None, None, None, None, None),
        P("folds", None),
        P("folds", None),
        P("folds", None, None, None, None, None),
        P("folds", None),
        P("folds", None),
        P("folds", None, None),
        P("folds", None),
        P(("groups", "tiles", "sub"), None),
        P("groups", None),
    )
    return jax.shard_map(
        on_device,
        mesh=mesh,
        in_specs=placed,
        out_specs=P(("groups", "tiles"), ("folds", "sub"), None),
        check_vma=False,
    )
```

```python
import functools

import jax
import jax.numpy as jnp
from jax import lax
from jax.experimental import pallas as pl
from jax.experimental.pallas import tpu as pltpu
from jax.sharding import PartitionSpec as P

TZ = 16
VX = 40
VY = 40

epsilon = 1e-05
leak_slope = 0.01
far = 1 << 20
bf16 = jnp.bfloat16
f32 = jnp.float32
vmem_bytes = 48 << 20


def iota(shape, dim):
    return lax.broadcasted_iota(jnp.int32, shape, dim)


def tile_matrix(width, lanes):
    return (iota((width, lanes), 1) % width == iota((width, lanes), 0)).astype(bf16)


def tiled_row(ref, lanes):
    width = ref.shape[1]
    row = jnp.concatenate([ref[...], jnp.zeros((1, lanes - width), f32)], axis=1)
    row = jnp.broadcast_to(row, (8, lanes))
    reach = width
    while reach < lanes:
        row = row + pltpu.roll(row, reach, 1)
        reach *= 2
    return row[0:1]


def lane_bands(parts, places):
    total = None
    for place, part in enumerate(parts):
        if part is not None:
            total = part if total is None else jnp.where(places == place, part, total)
    if total is None:
        return None
    if any(part is None for part in parts):
        empty = None
        for place, part in enumerate(parts):
            if part is None:
                here = places == place
                empty = here if empty is None else empty | here
        total = jnp.where(empty, 0.0, total)
    return total


def build_first(taps_ref, band_ref, in_width, width):
    spread = tile_matrix(width, 128)
    places = iota((in_width, 128), 1) // width
    zero = jnp.zeros((in_width, 128), bf16)
    orders = (((1, 0), (2, None)), ((0, 1), (None, 2)))
    for dz in range(3):
        tiled = {}
        for dx in range(3):
            for dy in range(3):
                at = ((dz * 3 + dx) * 3 + dy) * width
                tiled[dx, dy] = lax.dot_general(
                    taps_ref[at : at + width],
                    spread,
                    (((0,), (0,)), ((), ())),
                    preferred_element_type=f32,
                )
        for variant in range(2):
            for yi in range(4):
                for side in range(2):
                    parts = []
                    for dx in orders[variant][side]:
                        for yo in range(2):
                            parts.append(None if dx is None else tiled.get((dx, yi - yo)))
                    block = lane_bands(parts, places)
                    band_ref[
                        variant,
                        dz,
                        yi * in_width : (yi + 1) * in_width,
                        side * 128 : (side + 1) * 128,
                    ] = zero if block is None else block.astype(bf16)


def build_second(taps_ref, band_ref, width):
    spread = tile_matrix(width, 128)
    places = iota((width, 128), 1) // width
    zero = jnp.zeros((width, 128), bf16)
    for dz in range(3):
        at = dz * 9 * width
        tiled = jnp.dot(taps_ref[at : at + 9 * width], spread, preferred_element_type=f32)
        for dx in range(3):
            taps = {
                dy: tiled[(dx * 3 + dy) * width : (dx * 3 + dy + 1) * width] for dy in range(3)
            }
            for yi in range(8):
                block = lane_bands([taps.get(yi - yo) for yo in range(4)], places)
                band_ref[dz, yi * width : (yi + 1) * width, dx * 128 : (dx + 1) * 128] = (
                    zero if block is None else block.astype(bf16)
                )


def banded(pad_ref, lane, count, edge, bands):
    total = None
    for dz in range(3):
        part = jnp.dot(
            pad_ref[dz * edge : dz * edge + count, lane : lane + 256],
            bands(dz),
            preferred_element_type=f32,
        )
        total = part if total is None else total + part
    return total


def join_across(before, here, after, across, edge):
    rows = here.shape[0]
    before = jnp.where(across == 0, 0.0, pltpu.roll(before, 1, 0))
    after = jnp.where(across == edge - 1, 0.0, pltpu.roll(after, rows - 1, 0))
    return here + before + after


def channel_mean(blocks, width, voxels):
    folded = None
    for block in blocks:
        row = jnp.sum(block, axis=0, keepdims=True)
        folded = row if folded is None else folded + row
    folded = jnp.broadcast_to(folded, (8, 128))
    reach = width
    while reach < 128:
        folded = folded + pltpu.roll(folded, reach, 1)
        reach *= 2
    return folded[0:1] * (1.0 / voxels)


def normalize(blocks, masks, gain, shift, width, voxels):
    mean_value = channel_mean(blocks, width, voxels)
    centered = []
    for block, mask in zip(blocks, masks):
        moved = block - mean_value
        centered.append(moved if mask is None else jnp.where(mask, moved, 0.0))
    variance = channel_mean([moved * moved for moved in centered], width, voxels)
    factor = lax.rsqrt(variance + epsilon) * gain
    results = []
    for moved, mask in zip(centered, masks):
        scaled = moved * factor + shift
        scaled = jnp.maximum(scaled, leak_slope * scaled)
        results.append((scaled if mask is None else jnp.where(mask, scaled, 0.0)).astype(bf16))
    return results


def section_kernel(
    sizes,
    corners_hbm,
    counts_hbm,
    features_ref,
    taps_one_hbm,
    gain_one_hbm,
    shift_one_hbm,
    taps_two_hbm,
    gain_two_hbm,
    shift_two_hbm,
    head_hbm,
    bias_hbm,
    *rest,
):
    slots, edge, chunk, parts = sizes
    out_refs = rest[: len(parts)]
    (
        pad_one,
        pad_two,
        band_one,
        band_two,
        hidden,
        corners_ref,
        counts_ref,
        taps_one_ref,
        gain_one_ref,
        shift_one_ref,
        taps_two_ref,
        gain_two_ref,
        shift_two_ref,
        head_ref,
        bias_ref,
        sems,
    ) = rest[len(parts) :]
    in_width = taps_one_ref.shape[1]
    classes, width = head_ref.shape
    area = edge * edge
    stride = area + edge
    count = hidden.shape[0]
    voxels = float(area * edge)
    data = edge * in_width
    lanes = edge * classes

    copies = []
    for at, (source, target) in enumerate(
        [
            (taps_one_hbm, taps_one_ref),
            (taps_two_hbm, taps_two_ref),
            (gain_one_hbm, gain_one_ref),
            (shift_one_hbm, shift_one_ref),
            (gain_two_hbm, gain_two_ref),
            (shift_two_hbm, shift_two_ref),
            (head_hbm, head_ref),
            (bias_hbm, bias_ref),
            (corners_hbm, corners_ref),
            (counts_hbm, counts_ref),
        ]
        + [
            (
                features_ref.at[slot],
                pad_one.at[pl.ds(edge + slot * stride, area), pl.ds(128, data)],
            )
            for slot in range(slots)
        ]
    ):
        copy = pltpu.make_async_copy(source, target, sems.at[at])
        copy.start()
        copies.append(copy)
    for pad in (pad_one, pad_two):
        for slot in range(slots + 1):
            pad[slot * stride : slot * stride + edge, :] = jnp.zeros((edge, pad.shape[1]), bf16)
    pad_one[:, :128] = jnp.zeros((pad_one.shape[0], 128), bf16)
    pad_one[:, 128 + data :] = jnp.zeros((pad_one.shape[0], 128), bf16)

    center, spread = (edge - 1) / 2.0, edge / 4.0

    def profile(offset):
        return jnp.exp(-((offset.astype(f32) - center) ** 2) / (2.0 * spread * spread))

    row_at = iota((area, 128), 0)
    lane_at = iota((1, lanes), 1)
    gauss = profile(row_at // edge) * profile(row_at % edge)
    gauss = jnp.concatenate([gauss] * (lanes // 128), axis=1) * profile(lane_at // classes)

    row = iota((chunk * edge, area), 0)
    source = iota((chunk * edge, area), 1)
    turn = (row % edge - source // edge) & (edge - 1)
    code = turn + edge * (source % edge - row // edge)
    across = iota((count, 128), 0) % edge
    tile_index = lax.axis_index("tiles")
    sub_index = lax.axis_index("sub")
    position = lax.axis_index("folds") * lax.axis_size("sub") + sub_index

    for copy in copies[:-slots]:
        copy.wait()
    build_first(taps_one_ref, band_one, in_width, width)
    build_second(taps_two_ref, band_two, width)
    gain_one, shift_one = tiled_row(gain_one_ref, 128), tiled_row(shift_one_ref, 128)
    gain_two, shift_two = tiled_row(gain_two_ref, 128), tiled_row(shift_two_ref, 128)

    half = edge // 2
    head_row = lax.dot_general(
        head_ref[...],
        tile_matrix(classes, half * classes),
        (((0,), (0,)), ((), ())),
        preferred_element_type=f32,
    )
    block = (half * width, half * classes)
    head_block = jnp.where(
        iota(block, 0) // width == iota(block, 1) // classes,
        jnp.concatenate([head_row] * half, axis=0),
        0.0,
    ).astype(bf16)
    bias = tiled_row(bias_ref, lanes)

    mark = iota((edge, lanes), 0)
    notes = jnp.zeros((edge, lanes), f32)
    for slot in range(slots):
        depth = corners_ref[slot, 0] - tile_index * TZ
        notes = jnp.where(mark == 2 * slot, depth.astype(f32), notes)
        notes = jnp.where(mark == 2 * slot + 1, corners_ref[slot, 2].astype(f32), notes)
    for (_, low_row, high_row, noted), out_ref in zip(parts, out_refs):
        if noted:
            out_ref[slots * edge * (high_row - low_row) :, :] = notes.astype(bf16)

    for copy in copies[-slots:]:
        copy.wait()
    low = iota((count, 128), 1) < 64
    spot = iota((area, 128), 1)
    pairs = edge // 4 + 1
    for pair in range(pairs):
        even = banded(pad_one, 256 * pair, count, edge, lambda dz: band_one[0, dz])
        if pair < pairs - 1:
            odd = banded(pad_one, 256 * pair + 128, count, edge, lambda dz: band_one[1, dz])
            here = jnp.where(low, even[:, :128], odd[:, :128])
            before = jnp.where(low, odd[:, :128], even[:, :128])
            after = even[:, 128:] + odd[:, 128:]
        else:
            here = jnp.where(low, even[:, :128], 0.0)
            before = jnp.where(low, 0.0, even[:, :128])
            after = even[:, 128:]
        before = pltpu.roll(before, 64, 1)
        hidden[:, pair * 128 : (pair + 1) * 128] = join_across(before, here, after, across, edge)
    masks = [None] * pairs
    masks[0] = spot >= width
    masks[-1] = spot < width
    for slot in range(slots):
        at = slot * stride
        blocks = [hidden[at : at + area, pair * 128 : (pair + 1) * 128] for pair in range(pairs)]
        blocks[0] = jnp.where(masks[0], blocks[0], 0.0)
        blocks[-1] = jnp.where(masks[-1], blocks[-1], 0.0)
        normed = normalize(blocks, masks, gain_one, shift_one, width, voxels)
        for pair in range(pairs):
            pad_two[at + edge : at + edge + area, pair * 128 : (pair + 1) * 128] = normed[pair]

    quads = edge // 4
    for quad in range(quads):
        three = banded(pad_two, 128 * quad, count, edge, lambda dz: band_two[dz])
        hidden[:, quad * 128 : (quad + 1) * 128] = join_across(
            three[:, :128], three[:, 128:256], three[:, 256:], across, edge
        )
    for slot in range(slots):
        at = slot * stride
        blocks = [hidden[at : at + area, quad * 128 : (quad + 1) * 128] for quad in range(quads)]
        normed = normalize(blocks, [None] * quads, gain_two, shift_two, width, voxels)
        logits = jnp.concatenate(
            [
                jnp.dot(
                    jnp.concatenate(normed[side : side + quads // 2], axis=1),
                    head_block,
                    preferred_element_type=f32,
                )
                for side in (0, quads // 2)
            ],
            axis=1,
        )
        weighted = (logits + bias) * gauss
        lane_start = corners_ref[slot, 2] * classes
        weighted = pltpu.roll(weighted, lane_start % lanes, 1).astype(bf16)
        depth = corners_ref[slot, 0] - tile_index * TZ
        alive = slot < counts_ref[sub_index, tile_index]
        for (peer, low_row, high_row, _), out_ref in zip(parts, out_refs):
            wanted = depth + edge * ((position ^ peer) * chunk - corners_ref[slot, 1])
            wanted = jnp.where(alive, wanted, far)
            select = (code[low_row * edge : high_row * edge] == wanted).astype(f32).astype(bf16)
            size = (high_row - low_row) * edge
            out_ref[slot * size : (slot + 1) * size, :] = jnp.dot(
                select, weighted, preferred_element_type=f32
            ).astype(bf16)


def gather_kernel(sizes, spilled, *rest):
    slots, edge, chunk, parts, first, last, classes = sizes
    part_refs = rest[: len(parts)]
    out_ref = rest[len(parts)]
    lanes = edge * classes
    blocks = -(-VY * classes // lanes)

    depth_at = iota((edge, lanes), 0)
    lane_at = iota((edge, lanes), 1)
    groups = []
    for (peer, low_row, high_row, noted), part_ref in zip(parts, part_refs):
        if not noted or any(group[0] == peer % 2 for group in groups):
            continue
        notes = part_ref[slots * edge * (high_row - low_row) :, :].astype(f32).astype(jnp.int32)
        for slot in range(slots):
            depth = notes[2 * slot : 2 * slot + 1]
            start = notes[2 * slot + 1 : 2 * slot + 2] * classes
            keep = depth_at < depth if spilled else depth_at >= depth
            inside = []
            for block in range(blocks):
                lane = lane_at + block * lanes
                inside.append(keep & (lane >= start) & (lane < start + lanes))
            groups.append((peer % 2, slot, inside))

    for across in range(first, last):
        total = [jnp.zeros((edge, lanes), f32) for _ in range(blocks)]
        for parity, slot, inside in groups:
            piece = None
            for (peer, low_row, high_row, _), part_ref in zip(parts, part_refs):
                if peer % 2 == parity and low_row <= across < high_row:
                    at = (slot * (high_row - low_row) + across - low_row) * edge
                    part = part_ref[at : at + edge, :].astype(f32)
                    piece = part if piece is None else piece + part
            for block in range(blocks):
                total[block] = total[block] + jnp.where(inside[block], piece, 0.0)
        total = jnp.concatenate(total, axis=1)[:, : VY * classes]
        out_ref[across - first] = total.astype(out_ref.dtype)


def join_kernel(halves, own_ref, *rest):
    out_ref, total, sems = rest[-3:]
    tile_index = lax.axis_index("tiles")
    from_even = (tile_index % 2 == 1).astype(f32)
    from_odd = ((tile_index % 2 == 0) & (tile_index > 0)).astype(f32)
    copies = []
    for at, (low_row, high_row) in enumerate(halves):
        even_ref, odd_ref = rest[2 * at : 2 * at + 2]
        for row in range(low_row, high_row):
            total[row] = (
                own_ref[row]
                + even_ref[row - low_row].astype(f32) * from_even
                + odd_ref[row - low_row].astype(f32) * from_odd
            )
            copy = pltpu.make_async_copy(total.at[row], out_ref.at[row], sems.at[row])
            copy.start()
            copies.append(copy)
    for copy in copies:
        copy.wait()


vmem = pl.BlockSpec(memory_space=pltpu.VMEM)
hbm = pl.BlockSpec(memory_space=pltpu.HBM)
limits = pltpu.CompilerParams(vmem_limit_bytes=vmem_bytes)
ample = pltpu.CompilerParams(vmem_limit_bytes=60000000)


def on_device(
    features,
    conv_first,
    gain_first,
    shift_first,
    conv_second,
    gain_second,
    shift_second,
    head_weight,
    head_bias,
    corners,
    counts,
):
    _, slots, edge, _, data = features.shape
    in_width, width = conv_first.shape[-2:]
    classes = head_bias.shape[1]
    peers = lax.axis_size("folds") * lax.axis_size("sub")
    tiles = lax.axis_size("tiles")
    chunk = VX // peers
    area = edge * edge
    lanes = edge * classes
    padded = slots * (area + edge) + edge
    middle = chunk // 2
    halves = ((0, middle), (middle, chunk))
    parts = [(0, 0, chunk, True)]
    for low_row, high_row in halves:
        parts += [
            (peer, low_row, high_row, peer == peers - 1)
            for peer in [*range(2, peers), 1]
        ]
    rows = [
        slots * edge * (high_row - low_row) + (edge if noted else 0)
        for _, low_row, high_row, noted in parts
    ]
    pieces = pl.pallas_call(
        functools.partial(section_kernel, (slots, edge, chunk, parts)),
        out_shape=[pltpu.VMEM((count, lanes), bf16) for count in rows],
        in_specs=[hbm] * 11,
        out_specs=[vmem] * len(parts),
        scratch_shapes=[
            pltpu.VMEM((padded, data + 256), bf16),
            pltpu.VMEM((padded, edge * width + 128), bf16),
            pltpu.VMEM((2, 3, 256, 256), bf16),
            pltpu.VMEM((3, 256, 384), bf16),
            pltpu.VMEM((padded - 2 * edge, edge * width + 128), f32),
            pltpu.SMEM(corners.shape, jnp.int32),
            pltpu.SMEM(counts.shape[::-1], jnp.int32),
            pltpu.VMEM((27 * width, in_width), bf16),
            pltpu.VMEM((1, width), f32),
            pltpu.VMEM((1, width), f32),
            pltpu.VMEM((27 * width, width), bf16),
            pltpu.VMEM((1, width), f32),
            pltpu.VMEM((1, width), f32),
            pltpu.VMEM((classes, width), bf16),
            pltpu.VMEM((1, classes), f32),
            pltpu.SemaphoreType.DMA((10 + slots,)),
        ],
        compiler_params=ample,
        name="section",
    )(
        corners,
        counts.T,
        features.reshape(slots, area, data),
        jnp.swapaxes(conv_first, 4, 5).reshape(27 * width, in_width),
        gain_first,
        shift_first,
        conv_second.reshape(27 * width, width),
        gain_second,
        shift_second,
        head_weight[0].T,
        head_bias,
    )
    arrived = []
    for (peer, _, _, _), piece in zip(parts, pieces):
        pairs = [(i, i ^ peer) for i in range(peers)]
        arrived.append(lax.ppermute(piece, ("folds", "sub"), pairs) if peer else piece)

    def gather(first, last, spilled, kind, name):
        chosen = [
            (part, piece)
            for part, piece in zip(parts, arrived)
            if part[1] < last and first < part[2]
        ]
        return pl.pallas_call(
            functools.partial(
                gather_kernel,
                (slots, edge, chunk, [part for part, _ in chosen], first, last, classes),
                spilled,
            ),
            out_shape=pltpu.VMEM((last - first, TZ, VY * classes), kind),
            in_specs=[vmem] * len(chosen),
            out_specs=vmem,
            compiler_params=limits,
            cost_estimate=pl.CostEstimate(
                flops=500000000, bytes_accessed=2000000, transcendentals=0
            ),
            name=name,
        )(*[piece for _, piece in chosen])

    even = [(tile, tile ^ 1) for tile in range(tiles)]
    odd = []
    for tile in range(tiles):
        for i in range(peers):
            if 0 < tile < tiles - 1:
                target = (tile + 1 if tile % 2 else tile - 1) * peers + i
            else:
                target = tile * peers + (i ^ 1)
            odd.append((tile * peers + i, target))
    from_below = []
    for first, last in halves:
        spill = gather(first, last, True, bf16, f"spill_{first}")
        from_below.append(lax.ppermute(spill, "tiles", even))
        from_below.append(lax.ppermute(spill, ("tiles", "folds", "sub"), odd))
    own = gather(0, chunk, False, f32, "own")
    joined = pl.pallas_call(
        functools.partial(join_kernel, halves),
        out_shape=jax.ShapeDtypeStruct((chunk, TZ, VY * classes), f32),
        in_specs=[vmem] * (1 + 2 * len(halves)),
        out_specs=hbm,
        scratch_shapes=[
            pltpu.VMEM((chunk, TZ, VY * classes), f32),
            pltpu.SemaphoreType.DMA((chunk,)),
        ],
        compiler_params=limits,
        name="join",
    )(own, *from_below)
    return jnp.transpose(joined, (1, 0, 2))


def solution(mesh):
    placed = (
        P("folds", ("groups", "tiles", "sub"), None, None, None),
        P("folds", None, None, None, None, None),
        P("folds", None),
        P("folds", None),
        P("folds", None, None, None, None, None),
        P("folds", None),
        P("folds", None),
        P("folds", None, None),
        P("folds", None),
        P(("groups", "tiles", "sub"), None),
        P("groups", None),
    )
    return jax.shard_map(
        on_device,
        mesh=mesh,
        in_specs=placed,
        out_specs=P(("groups", "tiles"), ("folds", "sub"), None),
        check_vma=False,
    )
```

```python
import functools

import jax
import jax.numpy as jnp
from jax import lax
from jax.experimental import pallas as pl
from jax.experimental.pallas import tpu as pltpu
from jax.sharding import PartitionSpec as P

TZ = 16
VX = 40
VY = 40

epsilon = 1e-05
leak_slope = 0.01
far = 1 << 20
bf16 = jnp.bfloat16
f32 = jnp.float32
vmem_bytes = 48 << 20


def iota(shape, dim):
    return lax.broadcasted_iota(jnp.int32, shape, dim)


def tile_matrix(width, lanes):
    return (iota((width, lanes), 1) % width == iota((width, lanes), 0)).astype(bf16)


def tiled_row(ref, lanes):
    width = ref.shape[1]
    row = jnp.concatenate([ref[...], jnp.zeros((1, lanes - width), f32)], axis=1)
    row = jnp.broadcast_to(row, (8, lanes))
    reach = width
    while reach < lanes:
        row = row + pltpu.roll(row, reach, 1)
        reach *= 2
    return row[0:1]


def lane_bands(parts, places):
    total = None
    for place, part in enumerate(parts):
        if part is not None:
            total = part if total is None else jnp.where(places == place, part, total)
    if total is None:
        return None
    if any(part is None for part in parts):
        empty = None
        for place, part in enumerate(parts):
            if part is None:
                here = places == place
                empty = here if empty is None else empty | here
        total = jnp.where(empty, 0.0, total)
    return total


def build_first(taps_ref, band_ref, in_width, width):
    spread = tile_matrix(width, 128)
    places = iota((in_width, 128), 1) // width
    zero = jnp.zeros((in_width, 128), bf16)
    orders = (((1, 0), (2, None)), ((0, 1), (None, 2)))
    for dz in range(3):
        tiled = {}
        for dx in range(3):
            for dy in range(3):
                at = ((dz * 3 + dx) * 3 + dy) * width
                tiled[dx, dy] = lax.dot_general(
                    taps_ref[at : at + width],
                    spread,
                    (((0,), (0,)), ((), ())),
                    preferred_element_type=f32,
                )
        for variant in range(2):
            for yi in range(4):
                for side in range(2):
                    parts = []
                    for dx in orders[variant][side]:
                        for yo in range(2):
                            parts.append(None if dx is None else tiled.get((dx, yi - yo)))
                    block = lane_bands(parts, places)
                    at = dz * 256 + yi * in_width
                    band_ref[variant, at : at + in_width, side * 128 : (side + 1) * 128] = zero if block is None else block.astype(bf16)


def build_second(taps_ref, band_ref, width):
    spread = tile_matrix(width, 128)
    places = iota((width, 128), 1) // width
    zero = jnp.zeros((width, 128), bf16)
    for dz in range(3):
        at = dz * 9 * width
        tiled = jnp.dot(taps_ref[at : at + 9 * width], spread, preferred_element_type=f32)
        for dx in range(3):
            taps = {
                dy: tiled[(dx * 3 + dy) * width : (dx * 3 + dy + 1) * width] for dy in range(3)
            }
            for yi in range(8):
                block = lane_bands([taps.get(yi - yo) for yo in range(4)], places)
                at = dz * 256 + yi * width
                band_ref[at : at + width, dx * 128 : (dx + 1) * 128] = (
                    zero if block is None else block.astype(bf16)
                )


def banded(pad_ref, lane, count, edge, band):
    view = [pad_ref[dz * edge : dz * edge + count, lane : lane + 256] for dz in range(3)]
    return jnp.dot(jnp.concatenate(view, axis=1), band, preferred_element_type=f32)


def join_across(before, here, after, across, edge):
    rows = here.shape[0]
    before = jnp.where(across == 0, 0.0, pltpu.roll(before, 1, 0))
    after = jnp.where(across == edge - 1, 0.0, pltpu.roll(after, rows - 1, 0))
    return here + before + after


def channel_mean(blocks, width, voxels):
    folded = None
    for block in blocks:
        row = jnp.sum(block, axis=0, keepdims=True)
        folded = row if folded is None else folded + row
    folded = jnp.broadcast_to(folded, (8, 128))
    reach = width
    while reach < 128:
        folded = folded + pltpu.roll(folded, reach, 1)
        reach *= 2
    return folded[0:1] * (1.0 / voxels)


def normalize(blocks, masks, gain, shift, width, voxels):
    mean_value = channel_mean(blocks, width, voxels)
    centered = []
    for block, mask in zip(blocks, masks):
        moved = block - mean_value
        centered.append(moved if mask is None else jnp.where(mask, moved, 0.0))
    variance = channel_mean([moved * moved for moved in centered], width, voxels)
    factor = lax.rsqrt(variance + epsilon) * gain
    results = []
    for moved, mask in zip(centered, masks):
        scaled = moved * factor + shift
        scaled = jnp.maximum(scaled, leak_slope * scaled)
        results.append((scaled if mask is None else jnp.where(mask, scaled, 0.0)).astype(bf16))
    return results


def section_kernel(
    sizes,
    corners_hbm,
    counts_hbm,
    features_ref,
    taps_one_hbm,
    gain_one_hbm,
    shift_one_hbm,
    taps_two_hbm,
    gain_two_hbm,
    shift_two_hbm,
    head_hbm,
    bias_hbm,
    *rest,
):
    slots, edge, chunk, parts = sizes
    out_refs = rest[: len(parts)]
    (
        pad_one,
        pad_two,
        band_one,
        band_two,
        hidden,
        corners_ref,
        counts_ref,
        taps_one_ref,
        gain_one_ref,
        shift_one_ref,
        taps_two_ref,
        gain_two_ref,
        shift_two_ref,
        head_ref,
        bias_ref,
        sems,
    ) = rest[len(parts) :]
    in_width = taps_one_ref.shape[1]
    classes, width = head_ref.shape
    area = edge * edge
    stride = area + edge
    count = hidden.shape[0]
    voxels = float(area * edge)
    data = edge * in_width
    lanes = edge * classes

    copies = []
    for at, (source, target) in enumerate(
        [
            (taps_one_hbm, taps_one_ref),
            (taps_two_hbm, taps_two_ref),
            (gain_one_hbm, gain_one_ref),
            (shift_one_hbm, shift_one_ref),
            (gain_two_hbm, gain_two_ref),
            (shift_two_hbm, shift_two_ref),
            (head_hbm, head_ref),
            (bias_hbm, bias_ref),
            (corners_hbm, corners_ref),
            (counts_hbm, counts_ref),
        ]
        + [
            (
                features_ref.at[slot],
                pad_one.at[pl.ds(edge + slot * stride, area), pl.ds(128, data)],
            )
            for slot in range(slots)
        ]
    ):
        copy = pltpu.make_async_copy(source, target, sems.at[at])
        copy.start()
        copies.append(copy)
    for pad in (pad_one, pad_two):
        for slot in range(slots + 1):
            pad[slot * stride : slot * stride + edge, :] = jnp.zeros((edge, pad.shape[1]), bf16)
    pad_one[:, :128] = jnp.zeros((pad_one.shape[0], 128), bf16)
    pad_one[:, 128 + data :] = jnp.zeros((pad_one.shape[0], 128), bf16)

    center, spread = (edge - 1) / 2.0, edge / 4.0

    def profile(offset):
        return jnp.exp(-((offset.astype(f32) - center) ** 2) / (2.0 * spread * spread))

    row_at = iota((area, 128), 0)
    lane_at = iota((1, lanes), 1)
    gauss = profile(row_at // edge) * profile(row_at % edge)
    gauss = jnp.concatenate([gauss] * (lanes // 128), axis=1) * profile(lane_at // classes)

    row = iota((chunk * edge, area), 0)
    source = iota((chunk * edge, area), 1)
    turn = (row % edge - source // edge) & (edge - 1)
    code = turn + edge * (source % edge - row // edge)
    across = iota((count, 128), 0) % edge
    tile_index = lax.axis_index("tiles")
    sub_index = lax.axis_index("sub")
    position = lax.axis_index("folds") * lax.axis_size("sub") + sub_index

    for copy in copies[:-slots]:
        copy.wait()
    build_first(taps_one_ref, band_one, in_width, width)
    build_second(taps_two_ref, band_two, width)
    gain_one, shift_one = tiled_row(gain_one_ref, 128), tiled_row(shift_one_ref, 128)
    gain_two, shift_two = tiled_row(gain_two_ref, 128), tiled_row(shift_two_ref, 128)

    half = edge // 2
    head_row = lax.dot_general(
        head_ref[...],
        tile_matrix(classes, half * classes),
        (((0,), (0,)), ((), ())),
        preferred_element_type=f32,
    )
    block = (half * width, half * classes)
    head_block = jnp.where(
        iota(block, 0) // width == iota(block, 1) // classes,
        jnp.concatenate([head_row] * half, axis=0),
        0.0,
    ).astype(bf16)
    bias = tiled_row(bias_ref, lanes)

    mark = iota((edge, lanes), 0)
    notes = jnp.zeros((edge, lanes), f32)
    for slot in range(slots):
        depth = corners_ref[slot, 0] - tile_index * TZ
        notes = jnp.where(mark == 2 * slot, depth.astype(f32), notes)
        notes = jnp.where(mark == 2 * slot + 1, corners_ref[slot, 2].astype(f32), notes)
    for (_, low_row, high_row, noted), out_ref in zip(parts, out_refs):
        if noted:
            out_ref[slots * edge * (high_row - low_row) :, :] = notes.astype(bf16)

    for copy in copies[-slots:]:
        copy.wait()
    low = iota((count, 128), 1) < 64
    spot = iota((area, 128), 1)
    pairs = edge // 4 + 1
    for pair in range(pairs):
        even = banded(pad_one, 256 * pair, count, edge, band_one[0])
        if pair < pairs - 1:
            odd = banded(pad_one, 256 * pair + 128, count, edge, band_one[1])
            here = jnp.where(low, even[:, :128], odd[:, :128])
            before = jnp.where(low, odd[:, :128], even[:, :128])
            after = even[:, 128:] + odd[:, 128:]
        else:
            here = jnp.where(low, even[:, :128], 0.0)
            before = jnp.where(low, 0.0, even[:, :128])
            after = even[:, 128:]
        before = pltpu.roll(before, 64, 1)
        hidden[:, pair * 128 : (pair + 1) * 128] = join_across(before, here, after, across, edge)
    masks = [None] * pairs
    masks[0] = spot >= width
    masks[-1] = spot < width
    for slot in range(slots):
        at = slot * stride
        blocks = [hidden[at : at + area, pair * 128 : (pair + 1) * 128] for pair in range(pairs)]
        blocks[0] = jnp.where(masks[0], blocks[0], 0.0)
        blocks[-1] = jnp.where(masks[-1], blocks[-1], 0.0)
        normed = normalize(blocks, masks, gain_one, shift_one, width, voxels)
        for pair in range(pairs):
            pad_two[at + edge : at + edge + area, pair * 128 : (pair + 1) * 128] = normed[pair]

    quads = edge // 4
    for quad in range(quads):
        three = banded(pad_two, 128 * quad, count, edge, band_two[...])
        hidden[:, quad * 128 : (quad + 1) * 128] = join_across(
            three[:, :128], three[:, 128:256], three[:, 256:], across, edge
        )
    for slot in range(slots):
        at = slot * stride
        blocks = [hidden[at : at + area, quad * 128 : (quad + 1) * 128] for quad in range(quads)]
        normed = normalize(blocks, [None] * quads, gain_two, shift_two, width, voxels)
        logits = jnp.concatenate(
            [
                jnp.dot(
                    jnp.concatenate(normed[side : side + quads // 2], axis=1),
                    head_block,
                    preferred_element_type=f32,
                )
                for side in (0, quads // 2)
            ],
            axis=1,
        )
        weighted = (logits + bias) * gauss
        lane_start = corners_ref[slot, 2] * classes
        weighted = pltpu.roll(weighted, lane_start % lanes, 1).astype(bf16)
        depth = corners_ref[slot, 0] - tile_index * TZ
        alive = slot < counts_ref[sub_index, tile_index]
        for (peer, low_row, high_row, _), out_ref in zip(parts, out_refs):
            wanted = depth + edge * ((position ^ peer) * chunk - corners_ref[slot, 1])
            wanted = jnp.where(alive, wanted, far)
            select = (code[low_row * edge : high_row * edge] == wanted).astype(f32).astype(bf16)
            size = (high_row - low_row) * edge
            out_ref[slot * size : (slot + 1) * size, :] = jnp.dot(
                select, weighted, preferred_element_type=f32
            ).astype(bf16)


def gather_kernel(sizes, spilled, *rest):
    slots, edge, chunk, parts, first, last, classes = sizes
    part_refs = rest[: len(parts)]
    out_ref = rest[len(parts)]
    lanes = edge * classes
    blocks = -(-VY * classes // lanes)

    depth_at = iota((edge, lanes), 0)
    lane_at = iota((edge, lanes), 1)
    groups = []
    for (peer, low_row, high_row, noted), part_ref in zip(parts, part_refs):
        if not noted or any(group[0] == peer % 2 for group in groups):
            continue
        notes = part_ref[slots * edge * (high_row - low_row) :, :].astype(f32).astype(jnp.int32)
        for slot in range(slots):
            depth = notes[2 * slot : 2 * slot + 1]
            start = notes[2 * slot + 1 : 2 * slot + 2] * classes
            keep = depth_at < depth if spilled else depth_at >= depth
            inside = []
            for block in range(blocks):
                lane = lane_at + block * lanes
                inside.append(keep & (lane >= start) & (lane < start + lanes))
            groups.append((peer % 2, slot, inside))

    for across in range(first, last):
        total = [jnp.zeros((edge, lanes), f32) for _ in range(blocks)]
        for parity, slot, inside in groups:
            piece = None
            for (peer, low_row, high_row, _), part_ref in zip(parts, part_refs):
                if peer % 2 == parity and low_row <= across < high_row:
                    at = (slot * (high_row - low_row) + across - low_row) * edge
                    part = part_ref[at : at + edge, :].astype(f32)
                    piece = part if piece is None else piece + part
            for block in range(blocks):
                total[block] = total[block] + jnp.where(inside[block], piece, 0.0)
        total = jnp.concatenate(total, axis=1)[:, : VY * classes]
        out_ref[across - first] = total.astype(out_ref.dtype)


def join_kernel(halves, own_ref, *rest):
    out_ref, total, sems = rest[-3:]
    tile_index = lax.axis_index("tiles")
    from_even = (tile_index % 2 == 1).astype(f32)
    from_odd = ((tile_index % 2 == 0) & (tile_index > 0)).astype(f32)
    copies = []
    for at, (low_row, high_row) in enumerate(halves):
        even_ref, odd_ref = rest[2 * at : 2 * at + 2]
        for row in range(low_row, high_row):
            total[row] = (
                own_ref[row]
                + even_ref[row - low_row].astype(f32) * from_even
                + odd_ref[row - low_row].astype(f32) * from_odd
            )
            copy = pltpu.make_async_copy(total.at[row], out_ref.at[row], sems.at[row])
            copy.start()
            copies.append(copy)
    for copy in copies:
        copy.wait()


vmem = pl.BlockSpec(memory_space=pltpu.VMEM)
hbm = pl.BlockSpec(memory_space=pltpu.HBM)
limits = pltpu.CompilerParams(vmem_limit_bytes=vmem_bytes)
ample = pltpu.CompilerParams(vmem_limit_bytes=60000000)


def on_device(
    features,
    conv_first,
    gain_first,
    shift_first,
    conv_second,
    gain_second,
    shift_second,
    head_weight,
    head_bias,
    corners,
    counts,
):
    _, slots, edge, _, data = features.shape
    in_width, width = conv_first.shape[-2:]
    classes = head_bias.shape[1]
    peers = lax.axis_size("folds") * lax.axis_size("sub")
    tiles = lax.axis_size("tiles")
    chunk = VX // peers
    area = edge * edge
    lanes = edge * classes
    padded = slots * (area + edge) + edge
    middle = chunk // 2
    halves = ((0, middle), (middle, chunk))
    parts = [(0, 0, chunk, True)]
    for low_row, high_row in halves:
        parts += [
            (peer, low_row, high_row, peer == peers - 1)
            for peer in [*range(2, peers), 1]
        ]
    rows = [
        slots * edge * (high_row - low_row) + (edge if noted else 0)
        for _, low_row, high_row, noted in parts
    ]
    pieces = pl.pallas_call(
        functools.partial(section_kernel, (slots, edge, chunk, parts)),
        out_shape=[pltpu.VMEM((count, lanes), bf16) for count in rows],
        in_specs=[hbm] * 11,
        out_specs=[vmem] * len(parts),
        scratch_shapes=[
            pltpu.VMEM((padded, data + 256), bf16),
            pltpu.VMEM((padded, edge * width + 128), bf16),
            pltpu.VMEM((2, 768, 256), bf16),
            pltpu.VMEM((768, 384), bf16),
            pltpu.VMEM((padded - 2 * edge, edge * width + 128), f32),
            pltpu.SMEM(corners.shape, jnp.int32),
            pltpu.SMEM(counts.shape[::-1], jnp.int32),
            pltpu.VMEM((27 * width, in_width), bf16),
            pltpu.VMEM((1, width), f32),
            pltpu.VMEM((1, width), f32),
            pltpu.VMEM((27 * width, width), bf16),
            pltpu.VMEM((1, width), f32),
            pltpu.VMEM((1, width), f32),
            pltpu.VMEM((classes, width), bf16),
            pltpu.VMEM((1, classes), f32),
            pltpu.SemaphoreType.DMA((10 + slots,)),
        ],
        compiler_params=ample,
        name="section",
    )(
        corners,
        counts.T,
        features.reshape(slots, area, data),
        jnp.swapaxes(conv_first, 4, 5).reshape(27 * width, in_width),
        gain_first,
        shift_first,
        conv_second.reshape(27 * width, width),
        gain_second,
        shift_second,
        head_weight[0].T,
        head_bias,
    )
    arrived = []
    for (peer, _, _, _), piece in zip(parts, pieces):
        pairs = [(i, i ^ peer) for i in range(peers)]
        arrived.append(lax.ppermute(piece, ("folds", "sub"), pairs) if peer else piece)

    def gather(first, last, spilled, kind, name):
        chosen = [
            (part, piece)
            for part, piece in zip(parts, arrived)
            if part[1] < last and first < part[2]
        ]
        return pl.pallas_call(
            functools.partial(
                gather_kernel,
                (slots, edge, chunk, [part for part, _ in chosen], first, last, classes),
                spilled,
            ),
            out_shape=pltpu.VMEM((last - first, TZ, VY * classes), kind),
            in_specs=[vmem] * len(chosen),
            out_specs=vmem,
            compiler_params=limits,
            cost_estimate=pl.CostEstimate(
                flops=500000000, bytes_accessed=2000000, transcendentals=0
            ),
            name=name,
        )(*[piece for _, piece in chosen])

    even = [(tile, tile ^ 1) for tile in range(tiles)]
    odd = []
    for tile in range(tiles):
        for i in range(peers):
            if 0 < tile < tiles - 1:
                target = (tile + 1 if tile % 2 else tile - 1) * peers + i
            else:
                target = tile * peers + (i ^ 1)
            odd.append((tile * peers + i, target))
    from_below = []
    for first, last in halves:
        spill = gather(first, last, True, bf16, f"spill_{first}")
        from_below.append(lax.ppermute(spill, "tiles", even))
        from_below.append(lax.ppermute(spill, ("tiles", "folds", "sub"), odd))
    own = gather(0, chunk, False, f32, "own")
    joined = pl.pallas_call(
        functools.partial(join_kernel, halves),
        out_shape=jax.ShapeDtypeStruct((chunk, TZ, VY * classes), f32),
        in_specs=[vmem] * (1 + 2 * len(halves)),
        out_specs=hbm,
        scratch_shapes=[
            pltpu.VMEM((chunk, TZ, VY * classes), f32),
            pltpu.SemaphoreType.DMA((chunk,)),
        ],
        compiler_params=limits,
        name="join",
    )(own, *from_below)
    return jnp.transpose(joined, (1, 0, 2))


def solution(mesh):
    placed = (
        P("folds", ("groups", "tiles", "sub"), None, None, None),
        P("folds", None, None, None, None, None),
        P("folds", None),
        P("folds", None),
        P("folds", None, None, None, None, None),
        P("folds", None),
        P("folds", None),
        P("folds", None, None),
        P("folds", None),
        P(("groups", "tiles", "sub"), None),
        P("groups", None),
    )
    return jax.shard_map(
        on_device,
        mesh=mesh,
        in_specs=placed,
        out_specs=P(("groups", "tiles"), ("folds", "sub"), None),
        check_vma=False,
    )
```

```python
import functools

import jax
import jax.numpy as jnp
from jax import lax
from jax.experimental import pallas as pl
from jax.experimental.pallas import tpu as pltpu
from jax.sharding import PartitionSpec as P

TZ = 16
VX = 40
VY = 40

epsilon = 1e-05
leak_slope = 0.01
far = 1 << 20
bf16 = jnp.bfloat16
f32 = jnp.float32
vmem_bytes = 48 << 20


def iota(shape, dim):
    return lax.broadcasted_iota(jnp.int32, shape, dim)


def tile_matrix(width, lanes):
    return (iota((width, lanes), 1) % width == iota((width, lanes), 0)).astype(bf16)


def tiled_row(ref, lanes):
    width = ref.shape[1]
    row = jnp.concatenate([ref[...], jnp.zeros((1, lanes - width), f32)], axis=1)
    row = jnp.broadcast_to(row, (8, lanes))
    reach = width
    while reach < lanes:
        row = row + pltpu.roll(row, reach, 1)
        reach *= 2
    return row[0:1]


def lane_bands(parts, places):
    total = None
    for place, part in enumerate(parts):
        if part is not None:
            total = part if total is None else jnp.where(places == place, part, total)
    if total is None:
        return None
    if any(part is None for part in parts):
        empty = None
        for place, part in enumerate(parts):
            if part is None:
                here = places == place
                empty = here if empty is None else empty | here
        total = jnp.where(empty, 0.0, total)
    return total


def build_first(taps_ref, band_ref, in_width, width):
    spread = tile_matrix(width, 128)
    places = iota((in_width, 128), 1) // width
    zero = jnp.zeros((in_width, 128), bf16)
    orders = (((1, 0), (2, None)), ((0, 1), (None, 2)))
    for dz in range(3):
        tiled = {}
        for dx in range(3):
            for dy in range(3):
                at = ((dz * 3 + dx) * 3 + dy) * width
                tiled[dx, dy] = lax.dot_general(
                    taps_ref[at : at + width],
                    spread,
                    (((0,), (0,)), ((), ())),
                    preferred_element_type=f32,
                )
        for variant in range(2):
            for yi in range(4):
                for side in range(2):
                    parts = []
                    for dx in orders[variant][side]:
                        for yo in range(2):
                            parts.append(None if dx is None else tiled.get((dx, yi - yo)))
                    block = lane_bands(parts, places)
                    at = dz * 256 + yi * in_width
                    band_ref[variant, at : at + in_width, side * 128 : (side + 1) * 128] = zero if block is None else block.astype(bf16)


def build_second(taps_ref, band_ref, width, dz):
    spread = tile_matrix(width, 128)
    places = iota((width, 128), 1) // width
    zero = jnp.zeros((width, 128), bf16)
    at = dz * 9 * width
    tiled = jnp.dot(taps_ref[at : at + 9 * width], spread, preferred_element_type=f32)
    for dx in range(3):
        taps = {dy: tiled[(dx * 3 + dy) * width : (dx * 3 + dy + 1) * width] for dy in range(3)}
        for yi in range(8):
            block = lane_bands([taps.get(yi - yo) for yo in range(4)], places)
            at = dz * 256 + yi * width
            band_ref[at : at + width, dx * 128 : (dx + 1) * 128] = (
                zero if block is None else block.astype(bf16)
            )


def banded(pad_ref, lane, count, edge, band):
    view = [pad_ref[dz * edge : dz * edge + count, lane : lane + 256] for dz in range(3)]
    return jnp.dot(jnp.concatenate(view, axis=1), band, preferred_element_type=f32)


def join_across(before, here, after, across, edge):
    rows = here.shape[0]
    before = jnp.where(across == 0, 0.0, pltpu.roll(before, 1, 0))
    after = jnp.where(across == edge - 1, 0.0, pltpu.roll(after, rows - 1, 0))
    return here + before + after


def folded(row, width):
    row = jnp.broadcast_to(row, (8, 128))
    reach = width
    while reach < 128:
        row = row + pltpu.roll(row, reach, 1)
        reach *= 2
    return row[0:1]


class Norm:
    def __init__(self, width, rows, voxels):
        self.width, self.rows, self.voxels = width, rows, voxels
        self.base = None
        self.first = self.second = 0.0

    def take(self, block, mask, held):
        kept = block if mask is None else jnp.where(mask, block, 0.0)
        if self.base is None:
            total = folded(jnp.sum(kept, axis=0, keepdims=True), self.width)
            self.base = total * (1.0 / (self.rows * held))
        moved = block - self.base
        if mask is not None:
            moved = jnp.where(mask, moved, 0.0)
        self.first = self.first + jnp.sum(moved, axis=0, keepdims=True)
        self.second = self.second + jnp.sum(moved * moved, axis=0, keepdims=True)

    def settle(self, gain, shift):
        off = folded(self.first, self.width) * (1.0 / self.voxels)
        variance = folded(self.second, self.width) * (1.0 / self.voxels) - off * off
        self.center = self.base + off
        self.factor = lax.rsqrt(jnp.maximum(variance, 0.0) + epsilon) * gain
        self.shift = shift

    def give(self, block, mask):
        scaled = (block - self.center) * self.factor + self.shift
        scaled = jnp.maximum(scaled, leak_slope * scaled)
        return (scaled if mask is None else jnp.where(mask, scaled, 0.0)).astype(bf16)


def section_kernel(
    sizes,
    corners_hbm,
    counts_hbm,
    features_ref,
    taps_one_hbm,
    gain_one_hbm,
    shift_one_hbm,
    taps_two_hbm,
    gain_two_hbm,
    shift_two_hbm,
    head_hbm,
    bias_hbm,
    *rest,
):
    slots, edge, chunk, parts = sizes
    out_refs = rest[: len(parts)]
    (
        pad_one,
        pad_two,
        band_one,
        band_two,
        hidden,
        outcome,
        corners_ref,
        counts_ref,
        taps_one_ref,
        gain_one_ref,
        shift_one_ref,
        taps_two_ref,
        gain_two_ref,
        shift_two_ref,
        head_ref,
        bias_ref,
        selects,
        sems,
    ) = rest[len(parts) :]
    in_width = taps_one_ref.shape[1]
    classes, width = head_ref.shape
    area = edge * edge
    stride = area + edge
    count = hidden.shape[0]
    voxels = float(area * edge)
    data = edge * in_width
    lanes = edge * classes

    copies = []
    for at, (source, target) in enumerate(
        [
            (taps_one_hbm, taps_one_ref),
            (taps_two_hbm, taps_two_ref),
            (gain_one_hbm, gain_one_ref),
            (shift_one_hbm, shift_one_ref),
            (gain_two_hbm, gain_two_ref),
            (shift_two_hbm, shift_two_ref),
            (head_hbm, head_ref),
            (bias_hbm, bias_ref),
            (corners_hbm, corners_ref),
            (counts_hbm, counts_ref),
        ]
        + [
            (
                features_ref.at[slot],
                pad_one.at[pl.ds(edge + slot * stride, area), pl.ds(128, data)],
            )
            for slot in range(slots)
        ]
    ):
        copy = pltpu.make_async_copy(source, target, sems.at[at])
        copy.start()
        copies.append(copy)
    for pad in (pad_one, pad_two):
        for slot in range(slots + 1):
            pad[slot * stride : slot * stride + edge, :] = jnp.zeros((edge, pad.shape[1]), bf16)
    pad_one[:, :128] = jnp.zeros((pad_one.shape[0], 128), bf16)
    pad_one[:, 128 + data :] = jnp.zeros((pad_one.shape[0], 128), bf16)

    center, spread = (edge - 1) / 2.0, edge / 4.0

    def profile(offset):
        return jnp.exp(-((offset.astype(f32) - center) ** 2) / (2.0 * spread * spread))

    row_at = iota((area, 128), 0)
    lane_at = iota((1, lanes), 1)
    gauss = profile(row_at // edge) * profile(row_at % edge)
    gauss = jnp.concatenate([gauss] * (lanes // 128), axis=1) * profile(lane_at // classes)

    row = iota((chunk * edge, area), 0)
    source = iota((chunk * edge, area), 1)
    turn = (row % edge - source // edge) & (edge - 1)
    code = turn + edge * (source % edge - row // edge)
    across = iota((count, 128), 0) % edge
    tile_index = lax.axis_index("tiles")
    sub_index = lax.axis_index("sub")
    position = lax.axis_index("folds") * lax.axis_size("sub") + sub_index

    for copy in copies[:-slots]:
        copy.wait()
    build_first(taps_one_ref, band_one, in_width, width)
    gain_one, shift_one = tiled_row(gain_one_ref, 128), tiled_row(shift_one_ref, 128)
    gain_two, shift_two = tiled_row(gain_two_ref, 128), tiled_row(shift_two_ref, 128)

    half = edge // 2
    head_row = lax.dot_general(
        head_ref[...],
        tile_matrix(classes, half * classes),
        (((0,), (0,)), ((), ())),
        preferred_element_type=f32,
    )
    block = (half * width, half * classes)
    head_block = jnp.where(
        iota(block, 0) // width == iota(block, 1) // classes,
        jnp.concatenate([head_row] * half, axis=0),
        0.0,
    ).astype(bf16)
    bias = tiled_row(bias_ref, lanes)

    mark = iota((edge, lanes), 0)
    notes = jnp.zeros((edge, lanes), f32)
    for slot in range(slots):
        depth = corners_ref[slot, 0] - tile_index * TZ
        notes = jnp.where(mark == 2 * slot, depth.astype(f32), notes)
        notes = jnp.where(mark == 2 * slot + 1, corners_ref[slot, 2].astype(f32), notes)
    for (_, low_row, high_row, noted), out_ref in zip(parts, out_refs):
        if noted:
            out_ref[slots * edge * (high_row - low_row) :, :] = notes.astype(bf16)

    for copy in copies[-slots:]:
        copy.wait()
    low = iota((count, 128), 1) < 64
    spot = iota((area, 128), 1)
    pairs = edge // 4 + 1
    masks = [None] * pairs
    masks[0] = spot >= width
    masks[-1] = spot < width
    norms = [Norm(width, area, voxels) for _ in range(slots)]
    for pair in range(pairs):
        even = banded(pad_one, 256 * pair, count, edge, band_one[0])
        if pair < pairs - 1:
            odd = banded(pad_one, 256 * pair + 128, count, edge, band_one[1])
            here = jnp.where(low, even[:, :128], odd[:, :128])
            before = jnp.where(low, odd[:, :128], even[:, :128])
            after = even[:, 128:] + odd[:, 128:]
        else:
            here = jnp.where(low, even[:, :128], 0.0)
            before = jnp.where(low, 0.0, even[:, :128])
            after = even[:, 128:]
        before = pltpu.roll(before, 64, 1)
        block = join_across(before, here, after, across, edge)
        hidden[:, pair * 128 : (pair + 1) * 128] = block
        for slot, norm in enumerate(norms):
            norm.take(block[slot * stride : slot * stride + area], masks[pair], 3)
        if pair < 3:
            build_second(taps_two_ref, band_two, width, pair)
    for norm in norms:
        norm.settle(gain_one, shift_one)

    def refresh(pair):
        for slot, norm in enumerate(norms):
            at = slot * stride
            block = hidden[at : at + area, pair * 128 : (pair + 1) * 128]
            pad_two[at + edge : at + edge + area, pair * 128 : (pair + 1) * 128] = norm.give(
                block, masks[pair]
            )

    def prepare(slot):
        depth = corners_ref[slot, 0] - tile_index * TZ
        alive = slot < counts_ref[sub_index, tile_index]
        start = 0
        for peer, low_row, high_row, _ in parts:
            wanted = depth + edge * ((position ^ peer) * chunk - corners_ref[slot, 1])
            wanted = jnp.where(alive, wanted, far)
            select = (code[low_row * edge : high_row * edge] == wanted).astype(f32).astype(bf16)
            selects[slot, start : start + select.shape[0], :] = select
            start += select.shape[0]

    quads = edge // 4
    seconds = [Norm(width, area, voxels) for _ in range(slots)]
    refresh(0)
    for quad in range(quads):
        refresh(quad + 1)
        three = banded(pad_two, 128 * quad, count, edge, band_two[...])
        block = join_across(three[:, :128], three[:, 128:256], three[:, 256:], across, edge)
        outcome[:, quad * 128 : (quad + 1) * 128] = block
        for slot, norm in enumerate(seconds):
            norm.take(block[slot * stride : slot * stride + area], None, 4)
        if quad < slots:
            prepare(quad)
    for slot in range(quads, slots):
        prepare(slot)
    for norm in seconds:
        norm.settle(gain_two, shift_two)

    for slot, norm in enumerate(seconds):
        at = slot * stride
        logits = []
        for side in range(2):
            normed = [
                norm.give(outcome[at : at + area, quad * 128 : (quad + 1) * 128], None)
                for quad in range(side * quads // 2, (side + 1) * quads // 2)
            ]
            logits.append(
                jnp.dot(
                    jnp.concatenate(normed, axis=1), head_block, preferred_element_type=f32
                )
            )
        weighted = (jnp.concatenate(logits, axis=1) + bias) * gauss
        lane_start = corners_ref[slot, 2] * classes
        weighted = pltpu.roll(weighted, lane_start % lanes, 1).astype(bf16)
        placed = jnp.dot(selects[slot], weighted, preferred_element_type=f32).astype(bf16)
        start = 0
        for (_, low_row, high_row, _), out_ref in zip(parts, out_refs):
            size = (high_row - low_row) * edge
            out_ref[slot * size : (slot + 1) * size, :] = placed[start : start + size]
            start += size


def gather_kernel(sizes, spilled, *rest):
    slots, edge, chunk, parts, first, last, classes = sizes
    part_refs = rest[: len(parts)]
    out_ref = rest[len(parts)]
    lanes = edge * classes
    blocks = -(-VY * classes // lanes)

    depth_at = iota((edge, lanes), 0)
    lane_at = iota((edge, lanes), 1)
    groups = []
    for (peer, low_row, high_row, noted), part_ref in zip(parts, part_refs):
        if not noted or any(group[0] == peer % 2 for group in groups):
            continue
        notes = part_ref[slots * edge * (high_row - low_row) :, :].astype(f32).astype(jnp.int32)
        for slot in range(slots):
            depth = notes[2 * slot : 2 * slot + 1]
            start = notes[2 * slot + 1 : 2 * slot + 2] * classes
            keep = depth_at < depth if spilled else depth_at >= depth
            inside = []
            for block in range(blocks):
                lane = lane_at + block * lanes
                inside.append(keep & (lane >= start) & (lane < start + lanes))
            groups.append((peer % 2, slot, inside))

    for across in range(first, last):
        total = [jnp.zeros((edge, lanes), f32) for _ in range(blocks)]
        for parity, slot, inside in groups:
            piece = None
            for (peer, low_row, high_row, _), part_ref in zip(parts, part_refs):
                if peer % 2 == parity and low_row <= across < high_row:
                    at = (slot * (high_row - low_row) + across - low_row) * edge
                    part = part_ref[at : at + edge, :].astype(f32)
                    piece = part if piece is None else piece + part
            for block in range(blocks):
                total[block] = total[block] + jnp.where(inside[block], piece, 0.0)
        total = jnp.concatenate(total, axis=1)[:, : VY * classes]
        out_ref[across - first] = total.astype(out_ref.dtype)


def join_kernel(halves, own_ref, *rest):
    out_ref, total, sems = rest[-3:]
    tile_index = lax.axis_index("tiles")
    from_even = (tile_index % 2 == 1).astype(f32)
    from_odd = ((tile_index % 2 == 0) & (tile_index > 0)).astype(f32)
    copies = []
    for at, (low_row, high_row) in enumerate(halves):
        even_ref, odd_ref = rest[2 * at : 2 * at + 2]
        for row in range(low_row, high_row):
            total[row] = (
                own_ref[row]
                + even_ref[row - low_row].astype(f32) * from_even
                + odd_ref[row - low_row].astype(f32) * from_odd
            )
            copy = pltpu.make_async_copy(total.at[row], out_ref.at[row], sems.at[row])
            copy.start()
            copies.append(copy)
    for copy in copies:
        copy.wait()


vmem = pl.BlockSpec(memory_space=pltpu.VMEM)
hbm = pl.BlockSpec(memory_space=pltpu.HBM)
limits = pltpu.CompilerParams(vmem_limit_bytes=vmem_bytes)
ample = pltpu.CompilerParams(vmem_limit_bytes=60000000)


def on_device(
    features,
    conv_first,
    gain_first,
    shift_first,
    conv_second,
    gain_second,
    shift_second,
    head_weight,
    head_bias,
    corners,
    counts,
):
    _, slots, edge, _, data = features.shape
    in_width, width = conv_first.shape[-2:]
    classes = head_bias.shape[1]
    peers = lax.axis_size("folds") * lax.axis_size("sub")
    tiles = lax.axis_size("tiles")
    chunk = VX // peers
    area = edge * edge
    lanes = edge * classes
    padded = slots * (area + edge) + edge
    middle = chunk // 2
    halves = ((0, middle), (middle, chunk))
    parts = [(0, 0, chunk, True)]
    for low_row, high_row in halves:
        parts += [
            (peer, low_row, high_row, peer == peers - 1)
            for peer in [*range(2, peers), 1]
        ]
    rows = [
        slots * edge * (high_row - low_row) + (edge if noted else 0)
        for _, low_row, high_row, noted in parts
    ]
    pieces = pl.pallas_call(
        functools.partial(section_kernel, (slots, edge, chunk, parts)),
        out_shape=[pltpu.VMEM((count, lanes), bf16) for count in rows],
        in_specs=[hbm] * 11,
        out_specs=[vmem] * len(parts),
        scratch_shapes=[
            pltpu.VMEM((padded, data + 256), bf16),
            pltpu.VMEM((padded, edge * width + 128), bf16),
            pltpu.VMEM((2, 768, 256), bf16),
            pltpu.VMEM((768, 384), bf16),
            pltpu.VMEM((padded - 2 * edge, edge * width + 128), f32),
            pltpu.VMEM((padded - 2 * edge, edge * width), f32),
            pltpu.SMEM(corners.shape, jnp.int32),
            pltpu.SMEM(counts.shape[::-1], jnp.int32),
            pltpu.VMEM((27 * width, in_width), bf16),
            pltpu.VMEM((1, width), f32),
            pltpu.VMEM((1, width), f32),
            pltpu.VMEM((27 * width, width), bf16),
            pltpu.VMEM((1, width), f32),
            pltpu.VMEM((1, width), f32),
            pltpu.VMEM((classes, width), bf16),
            pltpu.VMEM((1, classes), f32),
            pltpu.VMEM((slots, VX * edge, area), bf16),
            pltpu.SemaphoreType.DMA((10 + slots,)),
        ],
        compiler_params=ample,
        name="section",
    )(
        corners,
        counts.T,
        features.reshape(slots, area, data),
        jnp.swapaxes(conv_first, 4, 5).reshape(27 * width, in_width),
        gain_first,
        shift_first,
        conv_second.reshape(27 * width, width),
        gain_second,
        shift_second,
        head_weight[0].T,
        head_bias,
    )
    arrived = []
    for (peer, _, _, _), piece in zip(parts, pieces):
        pairs = [(i, i ^ peer) for i in range(peers)]
        arrived.append(lax.ppermute(piece, ("folds", "sub"), pairs) if peer else piece)

    def gather(first, last, spilled, kind, name):
        chosen = [
            (part, piece)
            for part, piece in zip(parts, arrived)
            if part[1] < last and first < part[2]
        ]
        return pl.pallas_call(
            functools.partial(
                gather_kernel,
                (slots, edge, chunk, [part for part, _ in chosen], first, last, classes),
                spilled,
            ),
            out_shape=pltpu.VMEM((last - first, TZ, VY * classes), kind),
            in_specs=[vmem] * len(chosen),
            out_specs=vmem,
            compiler_params=limits,
            cost_estimate=pl.CostEstimate(
                flops=500000000, bytes_accessed=2000000, transcendentals=0
            ),
            name=name,
        )(*[piece for _, piece in chosen])

    even = [(tile, tile ^ 1) for tile in range(tiles)]
    odd = []
    for tile in range(tiles):
        for i in range(peers):
            if 0 < tile < tiles - 1:
                target = (tile + 1 if tile % 2 else tile - 1) * peers + i
            else:
                target = tile * peers + (i ^ 1)
            odd.append((tile * peers + i, target))
    from_below = []
    for first, last in halves:
        spill = gather(first, last, True, bf16, f"spill_{first}")
        from_below.append(lax.ppermute(spill, "tiles", even))
        from_below.append(lax.ppermute(spill, ("tiles", "folds", "sub"), odd))
    own = gather(0, chunk, False, f32, "own")
    joined = pl.pallas_call(
        functools.partial(join_kernel, halves),
        out_shape=jax.ShapeDtypeStruct((chunk, TZ, VY * classes), f32),
        in_specs=[vmem] * (1 + 2 * len(halves)),
        out_specs=hbm,
        scratch_shapes=[
            pltpu.VMEM((chunk, TZ, VY * classes), f32),
            pltpu.SemaphoreType.DMA((chunk,)),
        ],
        compiler_params=limits,
        name="join",
    )(own, *from_below)
    return jnp.transpose(joined, (1, 0, 2))


def solution(mesh):
    placed = (
        P("folds", ("groups", "tiles", "sub"), None, None, None),
        P("folds", None, None, None, None, None),
        P("folds", None),
        P("folds", None),
        P("folds", None, None, None, None, None),
        P("folds", None),
        P("folds", None),
        P("folds", None, None),
        P("folds", None),
        P(("groups", "tiles", "sub"), None),
        P("groups", None),
    )
    return jax.shard_map(
        on_device,
        mesh=mesh,
        in_specs=placed,
        out_specs=P(("groups", "tiles"), ("folds", "sub"), None),
        check_vma=False,
    )
```

```python
import functools

import jax
import jax.numpy as jnp
from jax import lax
from jax.experimental import pallas as pl
from jax.experimental.pallas import tpu as pltpu
from jax.sharding import PartitionSpec as P

TZ = 16
VX = 40
VY = 40

epsilon = 1e-05
leak_slope = 0.01
far = 1 << 20
bf16 = jnp.bfloat16
f32 = jnp.float32
vmem_bytes = 24 << 20


def iota(shape, dim):
    return lax.broadcasted_iota(jnp.int32, shape, dim)


def tile_matrix(width, lanes):
    return (iota((width, lanes), 1) % width == iota((width, lanes), 0)).astype(bf16)


def tiled_row(ref, lanes):
    width = ref.shape[1]
    row = jnp.concatenate([ref[...], jnp.zeros((1, lanes - width), f32)], axis=1)
    row = jnp.broadcast_to(row, (8, lanes))
    reach = width
    while reach < lanes:
        row = row + pltpu.roll(row, reach, 1)
        reach *= 2
    return row[0:1]


def lane_bands(parts, places):
    total = None
    for place, part in enumerate(parts):
        if part is not None:
            total = part if total is None else jnp.where(places == place, part, total)
    if total is None:
        return None
    if any(part is None for part in parts):
        empty = None
        for place, part in enumerate(parts):
            if part is None:
                here = places == place
                empty = here if empty is None else empty | here
        total = jnp.where(empty, 0.0, total)
    return total


def build_first(taps_ref, band_ref, in_width, width):
    spread = tile_matrix(width, 128)
    places = iota((in_width, 128), 1) // width
    zero = jnp.zeros((in_width, 128), bf16)
    orders = (((1, 0), (2, None)), ((0, 1), (None, 2)))
    for dz in range(3):
        tiled = {}
        for dx in range(3):
            for dy in range(3):
                at = ((dz * 3 + dx) * 3 + dy) * width
                tiled[dx, dy] = lax.dot_general(
                    taps_ref[at : at + width],
                    spread,
                    (((0,), (0,)), ((), ())),
                    preferred_element_type=f32,
                )
        for variant in range(2):
            for yi in range(4):
                for side in range(2):
                    parts = []
                    for dx in orders[variant][side]:
                        for yo in range(2):
                            parts.append(None if dx is None else tiled.get((dx, yi - yo)))
                    block = lane_bands(parts, places)
                    at = dz * 256 + yi * in_width
                    band_ref[variant, at : at + in_width, side * 128 : (side + 1) * 128] = zero if block is None else block.astype(bf16)


def build_second(taps_ref, band_ref, width, dz):
    spread = tile_matrix(width, 128)
    places = iota((width, 128), 1) // width
    zero = jnp.zeros((width, 128), bf16)
    at = dz * 9 * width
    tiled = jnp.dot(taps_ref[at : at + 9 * width], spread, preferred_element_type=f32)
    for dx in range(3):
        taps = {dy: tiled[(dx * 3 + dy) * width : (dx * 3 + dy + 1) * width] for dy in range(3)}
        for yi in range(8):
            block = lane_bands([taps.get(yi - yo) for yo in range(4)], places)
            at = dz * 256 + yi * width
            band_ref[at : at + width, dx * 128 : (dx + 1) * 128] = (
                zero if block is None else block.astype(bf16)
            )


def banded(pad_ref, lane, count, edge, band):
    view = [pad_ref[dz * edge : dz * edge + count, lane : lane + 256] for dz in range(3)]
    return jnp.dot(jnp.concatenate(view, axis=1), band, preferred_element_type=f32)


def join_across(before, here, after, across, edge):
    rows = here.shape[0]
    before = jnp.where(across == 0, 0.0, pltpu.roll(before, 1, 0))
    after = jnp.where(across == edge - 1, 0.0, pltpu.roll(after, rows - 1, 0))
    return here + before + after


def folded(row, width):
    row = jnp.broadcast_to(row, (8, 128))
    reach = width
    while reach < 128:
        row = row + pltpu.roll(row, reach, 1)
        reach *= 2
    return row[0:1]


class Norm:
    def __init__(self, width, rows, voxels):
        self.width, self.rows, self.voxels = width, rows, voxels
        self.base = None
        self.first = self.second = 0.0

    def take(self, block, mask, held):
        kept = block if mask is None else jnp.where(mask, block, 0.0)
        if self.base is None:
            total = folded(jnp.sum(kept, axis=0, keepdims=True), self.width)
            self.base = total * (1.0 / (self.rows * held))
        moved = block - self.base
        if mask is not None:
            moved = jnp.where(mask, moved, 0.0)
        self.first = self.first + jnp.sum(moved, axis=0, keepdims=True)
        self.second = self.second + jnp.sum(moved * moved, axis=0, keepdims=True)

    def settle(self, gain, shift):
        off = folded(self.first, self.width) * (1.0 / self.voxels)
        variance = folded(self.second, self.width) * (1.0 / self.voxels) - off * off
        self.center = self.base + off
        self.factor = lax.rsqrt(jnp.maximum(variance, 0.0) + epsilon) * gain
        self.shift = shift

    def give(self, block, mask):
        scaled = (block - self.center) * self.factor + self.shift
        scaled = jnp.maximum(scaled, leak_slope * scaled)
        return (scaled if mask is None else jnp.where(mask, scaled, 0.0)).astype(bf16)


def first_kernel(
    sizes,
    corners_hbm,
    counts_hbm,
    features_ref,
    taps_one_hbm,
    gain_one_hbm,
    shift_one_hbm,
    taps_two_hbm,
    gain_two_hbm,
    shift_two_hbm,
    head_hbm,
    bias_hbm,
    *rest,
):
    slots, edge, chunk, peers, parts = sizes
    out_refs = rest[: len(parts)]
    (
        weighted_ref,
        next_ref,
        band_two,
        rows_ref,
        head_block_ref,
        gauss_ref,
        code_ref,
        info_ref,
        turn_ref,
        notes_ref,
        pad_one,
        pad_two,
        band_one,
        hidden,
        outcome,
        corners_ref,
        counts_ref,
        taps_one_ref,
        gain_one_ref,
        shift_one_ref,
        taps_two_ref,
        gain_two_ref,
        shift_two_ref,
        head_ref,
        bias_ref,
        sems,
    ) = rest[len(parts) :]
    in_width = taps_one_ref.shape[1]
    classes, width = head_ref.shape
    area = edge * edge
    stride = area + edge
    count = hidden.shape[0]
    voxels = float(area * edge)
    data = edge * in_width
    lanes = edge * classes

    copies = []
    for at, (source, target) in enumerate(
        [
            (taps_one_hbm, taps_one_ref),
            (taps_two_hbm, taps_two_ref),
            (gain_one_hbm, gain_one_ref),
            (shift_one_hbm, shift_one_ref),
            (gain_two_hbm, gain_two_ref),
            (shift_two_hbm, shift_two_ref),
            (head_hbm, head_ref),
            (bias_hbm, bias_ref),
            (corners_hbm, corners_ref),
            (counts_hbm, counts_ref),
        ]
        + [
            (
                features_ref.at[slot],
                pad_one.at[pl.ds(edge + slot * stride, area), pl.ds(128, data)],
            )
            for slot in range(slots)
        ]
    ):
        copy = pltpu.make_async_copy(source, target, sems.at[at])
        copy.start()
        copies.append(copy)
    for slot in range(slots + 1):
        at = slot * stride
        pad_one[at : at + edge, :] = jnp.zeros((edge, pad_one.shape[1]), bf16)
    pads = [pad_two] + [next_ref.at[slot - 1] for slot in range(1, slots)]
    for pad in pads:
        pad[:edge, :] = jnp.zeros((edge, pad.shape[1]), bf16)
        pad[edge + area :, :] = jnp.zeros((edge, pad.shape[1]), bf16)
    pad_one[:, :128] = jnp.zeros((pad_one.shape[0], 128), bf16)
    pad_one[:, 128 + data :] = jnp.zeros((pad_one.shape[0], 128), bf16)

    center, spread = (edge - 1) / 2.0, edge / 4.0

    def profile(offset):
        return jnp.exp(-((offset.astype(f32) - center) ** 2) / (2.0 * spread * spread))

    row_at = iota((area, 128), 0)
    lane_at = iota((1, lanes), 1)
    gauss = profile(row_at // edge) * profile(row_at % edge)
    gauss = jnp.concatenate([gauss] * (lanes // 128), axis=1) * profile(lane_at // classes)
    gauss_ref[...] = gauss

    row = iota((chunk * edge, area), 0)
    source = iota((chunk * edge, area), 1)
    turn = (row % edge - source // edge) & (edge - 1)
    code = turn + edge * (source % edge - row // edge)
    code_ref[...] = code
    across = iota((count, 128), 0) % edge
    tile_index = lax.axis_index("tiles")
    sub_index = lax.axis_index("sub")
    position = lax.axis_index("folds") * lax.axis_size("sub") + sub_index

    for copy in copies[:-slots]:
        copy.wait()
    build_first(taps_one_ref, band_one, in_width, width)
    gain_one, shift_one = tiled_row(gain_one_ref, 128), tiled_row(shift_one_ref, 128)
    gain_two, shift_two = tiled_row(gain_two_ref, 128), tiled_row(shift_two_ref, 128)

    half = edge // 2
    head_row = lax.dot_general(
        head_ref[...],
        tile_matrix(classes, half * classes),
        (((0,), (0,)), ((), ())),
        preferred_element_type=f32,
    )
    block = (half * width, half * classes)
    head_block = jnp.where(
        iota(block, 0) // width == iota(block, 1) // classes,
        jnp.concatenate([head_row] * half, axis=0),
        0.0,
    ).astype(bf16)
    head_block_ref[...] = head_block
    bias = tiled_row(bias_ref, lanes)
    rows_ref[0:1, :128] = gain_two
    rows_ref[1:2, :128] = shift_two
    rows_ref[2:3, :] = bias

    mark = iota((edge, lanes), 0)
    notes = jnp.zeros((edge, lanes), f32)
    for slot in range(slots):
        depth = corners_ref[slot, 0] - tile_index * TZ
        notes = jnp.where(mark == 2 * slot, depth.astype(f32), notes)
        notes = jnp.where(mark == 2 * slot + 1, corners_ref[slot, 2].astype(f32), notes)
    notes_ref[...] = notes.astype(bf16)
    line = iota(info_ref.shape, 0)
    info = jnp.full(info_ref.shape, far, jnp.int32)
    for slot in range(slots):
        depth = corners_ref[slot, 0] - tile_index * TZ
        alive = slot < counts_ref[sub_index, tile_index]
        for peer in range(peers):
            wanted = depth + edge * ((position ^ peer) * chunk - corners_ref[slot, 1])
            wanted = jnp.where(alive, wanted, far)
            info = jnp.where(line == slot * peers + peer, wanted, info)
    info_ref[...] = info
    ahead = (iota((lanes, lanes), 1) - iota((lanes, lanes), 0)) & (lanes - 1)
    for slot in range(1, slots):
        lane_start = (corners_ref[slot, 2] * classes) & (lanes - 1)
        turn_ref[slot - 1] = (ahead == lane_start).astype(f32).astype(bf16)

    for copy in copies[-slots:]:
        copy.wait()
    low = iota((count, 128), 1) < 64
    spot = iota((area, 128), 1)
    pairs = edge // 4 + 1
    masks = [None] * pairs
    masks[0] = spot >= width
    masks[-1] = spot < width
    norms = [Norm(width, area, voxels) for _ in range(slots)]
    for pair in range(pairs):
        even = banded(pad_one, 256 * pair, count, edge, band_one[0])
        if pair < pairs - 1:
            odd = banded(pad_one, 256 * pair + 128, count, edge, band_one[1])
            here = jnp.where(low, even[:, :128], odd[:, :128])
            before = jnp.where(low, odd[:, :128], even[:, :128])
            after = even[:, 128:] + odd[:, 128:]
        else:
            here = jnp.where(low, even[:, :128], 0.0)
            before = jnp.where(low, 0.0, even[:, :128])
            after = even[:, 128:]
        before = pltpu.roll(before, 64, 1)
        block = join_across(before, here, after, across, edge)
        hidden[:, pair * 128 : (pair + 1) * 128] = block
        for slot, norm in enumerate(norms):
            norm.take(block[slot * stride : slot * stride + area], masks[pair], 3)
        if pair < 3:
            build_second(taps_two_ref, band_two, width, pair)
    for norm in norms:
        norm.settle(gain_one, shift_one)

    for pair in range(pairs):
        for slot, norm in enumerate(norms):
            at = slot * stride
            block = hidden[at : at + area, pair * 128 : (pair + 1) * 128]
            pads[slot][edge : edge + area, pair * 128 : (pair + 1) * 128] = norm.give(
                block, masks[pair]
            )
    weighted = second_half(
        pad_two, band_two, outcome, gain_two, shift_two, head_block, bias, gauss, edge, width
    )
    lane_start = corners_ref[0, 2] * classes
    weighted = pltpu.roll(weighted, lane_start % lanes, 1).astype(bf16)
    weighted_ref[...] = weighted
    place(weighted, 0, parts, out_refs, info, code, edge, peers)


def second_half(
    pad_two, band_two, outcome, gain_two, shift_two, head_block, bias, gauss, edge, width
):
    area = outcome.shape[0]
    quads = edge // 4
    across = iota((area, 128), 0) % edge
    norm = Norm(width, area, float(area * edge))
    for quad in range(quads):
        three = banded(pad_two, 128 * quad, area, edge, band_two[...])
        block = join_across(three[:, :128], three[:, 128:256], three[:, 256:], across, edge)
        outcome[:, quad * 128 : (quad + 1) * 128] = block
        norm.take(block, None, 4)
    norm.settle(gain_two, shift_two)
    logits = []
    for side in range(2):
        normed = [
            norm.give(outcome[:, quad * 128 : (quad + 1) * 128], None)
            for quad in range(side * quads // 2, (side + 1) * quads // 2)
        ]
        logits.append(
            jnp.dot(jnp.concatenate(normed, axis=1), head_block, preferred_element_type=f32)
        )
    return (jnp.concatenate(logits, axis=1) + bias) * gauss


def place(weighted, slot, parts, out_refs, info, code, edge, peers):
    chosen = [
        (part, out_ref) for part, out_ref in zip(parts, out_refs) if part[4] <= slot < part[5]
    ]
    selects = []
    for (peer, low_row, high_row, _, _, _), _ in chosen:
        line = slot * peers + peer
        wanted = info[line : line + 1, :]
        select = code[low_row * edge : high_row * edge, :] == wanted
        selects.append(select.astype(f32).astype(bf16))
    placed = jnp.dot(jnp.concatenate(selects, axis=0), weighted, preferred_element_type=f32)
    placed = placed.astype(bf16)
    start = 0
    for (_, low_row, high_row, _, first, _), out_ref in chosen:
        size = (high_row - low_row) * edge
        at = (slot - first) * size
        out_ref[at : at + size, :] = placed[start : start + size]
        start += size


def next_kernel(
    sizes,
    weighted_ref,
    next_ref,
    band_two,
    rows_ref,
    head_block_ref,
    gauss_ref,
    code_ref,
    info_ref,
    turn_ref,
    notes_ref,
    *rest,
):
    slots, edge, width, peers, parts = sizes
    out_refs = rest[: len(parts)]
    outcome = rest[len(parts)]
    code, info = code_ref[...], info_ref[...]
    place(weighted_ref[...], 0, parts, out_refs, info, code, edge, peers)
    for slot in range(1, slots):
        weighted = second_half(
            next_ref.at[slot - 1],
            band_two,
            outcome,
            rows_ref[0:1, :128],
            rows_ref[1:2, :128],
            head_block_ref[...],
            rows_ref[2:3, :],
            gauss_ref[...],
            edge,
            width,
        ).astype(bf16)
        weighted = jnp.dot(weighted, turn_ref[slot - 1], preferred_element_type=f32)
        place(weighted.astype(bf16), slot, parts, out_refs, info, code, edge, peers)
    for (_, low_row, high_row, noted, first, last), out_ref in zip(parts, out_refs):
        if noted:
            out_ref[(last - first) * edge * (high_row - low_row) :, :] = notes_ref[...]


def gather_kernel(sizes, spilled, *rest):
    slots, edge, chunk, parts, first, last, classes = sizes
    part_refs = rest[: len(parts)]
    out_ref = rest[len(parts)]
    lanes = edge * classes
    blocks = -(-VY * classes // lanes)

    depth_at = iota((edge, lanes), 0)
    lane_at = iota((edge, lanes), 1)
    groups = []
    for (peer, low_row, high_row, noted, _, _), part_ref in zip(parts, part_refs):
        if not noted or any(group[0] == peer % 2 for group in groups):
            continue
        notes = part_ref[-edge:, :].astype(f32).astype(jnp.int32)
        for slot in range(slots):
            depth = notes[2 * slot : 2 * slot + 1]
            start = notes[2 * slot + 1 : 2 * slot + 2] * classes
            keep = depth_at < depth if spilled else depth_at >= depth
            inside = []
            for block in range(blocks):
                lane = lane_at + block * lanes
                inside.append(keep & (lane >= start) & (lane < start + lanes))
            groups.append((peer % 2, slot, inside))

    for across in range(first, last):
        total = [jnp.zeros((edge, lanes), f32) for _ in range(blocks)]
        for parity, slot, inside in groups:
            piece = None
            for (peer, low_row, high_row, _, low, high), part_ref in zip(parts, part_refs):
                if peer % 2 == parity and low_row <= across < high_row and low <= slot < high:
                    at = ((slot - low) * (high_row - low_row) + across - low_row) * edge
                    part = part_ref[at : at + edge, :].astype(f32)
                    piece = part if piece is None else piece + part
            for block in range(blocks):
                total[block] = total[block] + jnp.where(inside[block], piece, 0.0)
        total = jnp.concatenate(total, axis=1)[:, : VY * classes]
        out_ref[across - first] = total.astype(out_ref.dtype)


def join_kernel(halves, own_ref, *rest):
    out_ref, total, sems = rest[-3:]
    tile_index = lax.axis_index("tiles")
    from_even = (tile_index % 2 == 1).astype(f32)
    from_odd = ((tile_index % 2 == 0) & (tile_index > 0)).astype(f32)
    copies = []
    for at, (low_row, high_row) in enumerate(halves):
        odd_ref, even_ref = rest[2 * at : 2 * at + 2]
        for row in range(low_row, high_row):
            total[row] = (
                own_ref[row]
                + even_ref[row - low_row].astype(f32) * from_even
                + odd_ref[row - low_row].astype(f32) * from_odd
            )
            copy = pltpu.make_async_copy(total.at[row], out_ref.at[row], sems.at[row])
            copy.start()
            copies.append(copy)
    for copy in copies:
        copy.wait()


vmem = pl.BlockSpec(memory_space=pltpu.VMEM)
hbm = pl.BlockSpec(memory_space=pltpu.HBM)
limits = pltpu.CompilerParams(vmem_limit_bytes=vmem_bytes)
ample = pltpu.CompilerParams(vmem_limit_bytes=58000000)


def on_device(
    features,
    conv_first,
    gain_first,
    shift_first,
    conv_second,
    gain_second,
    shift_second,
    head_weight,
    head_bias,
    corners,
    counts,
):
    _, slots, edge, _, data = features.shape
    in_width, width = conv_first.shape[-2:]
    classes = head_bias.shape[1]
    peers = lax.axis_size("folds") * lax.axis_size("sub")
    tiles = lax.axis_size("tiles")
    chunk = VX // peers
    area = edge * edge
    lanes = edge * classes
    padded = slots * (area + edge) + edge
    middle = chunk // 2
    halves = ((0, middle), (middle, chunk))
    far_peers = range(2, peers)
    first_parts = [(peer, 0, chunk, False, 0, 1) for peer in far_peers]
    next_parts = [(0, 0, chunk, True, 0, slots)]
    for low_row, high_row in halves:
        next_parts += [
            (peer, low_row, high_row, peer == peers - 1, 1, slots) for peer in far_peers
        ]
        next_parts.append((1, low_row, high_row, False, 0, slots))

    def shapes(parts):
        return [
            pltpu.VMEM(
                ((last - first) * edge * (high_row - low_row) + (edge if noted else 0), lanes),
                bf16,
            )
            for _, low_row, high_row, noted, first, last in parts
        ]

    work = pl.CostEstimate(flops=5000000000, bytes_accessed=3000000, transcendentals=0)
    handed = [
        pltpu.VMEM((area, lanes), bf16),
        pltpu.VMEM((slots - 1, area + 2 * edge, edge * width + 128), bf16),
        pltpu.VMEM((768, 384), bf16),
        pltpu.VMEM((8, lanes), f32),
        pltpu.VMEM((edge // 2 * width, edge // 2 * classes), bf16),
        pltpu.VMEM((area, lanes), f32),
        pltpu.VMEM((chunk * edge, area), jnp.int32),
        pltpu.VMEM((-(-slots * peers // 8) * 8, area), jnp.int32),
        pltpu.VMEM((slots - 1, lanes, lanes), bf16),
        pltpu.VMEM((edge, lanes), bf16),
    ]
    outs = shapes(first_parts) + handed
    results = pl.pallas_call(
        functools.partial(first_kernel, (slots, edge, chunk, peers, first_parts)),
        out_shape=outs,
        in_specs=[hbm] * 11,
        out_specs=[vmem] * len(outs),
        scratch_shapes=[
            pltpu.VMEM((padded, data + 256), bf16),
            pltpu.VMEM((area + 2 * edge, edge * width + 128), bf16),
            pltpu.VMEM((2, 768, 256), bf16),
            pltpu.VMEM((padded - 2 * edge, edge * width + 128), f32),
            pltpu.VMEM((area, edge * width), f32),
            pltpu.SMEM(corners.shape, jnp.int32),
            pltpu.SMEM(counts.shape[::-1], jnp.int32),
            pltpu.VMEM((27 * width, in_width), bf16),
            pltpu.VMEM((1, width), f32),
            pltpu.VMEM((1, width), f32),
            pltpu.VMEM((27 * width, width), bf16),
            pltpu.VMEM((1, width), f32),
            pltpu.VMEM((1, width), f32),
            pltpu.VMEM((classes, width), bf16),
            pltpu.VMEM((1, classes), f32),
            pltpu.SemaphoreType.DMA((10 + slots,)),
        ],
        compiler_params=ample,
        cost_estimate=work,
        name="section",
    )(
        corners,
        counts.T,
        features.reshape(slots, area, data),
        jnp.swapaxes(conv_first, 4, 5).reshape(27 * width, in_width),
        gain_first,
        shift_first,
        conv_second.reshape(27 * width, width),
        gain_second,
        shift_second,
        head_weight[0].T,
        head_bias,
    )
    first_pieces, results = results[: len(first_parts)], results[len(first_parts) :]
    next_pieces = pl.pallas_call(
        functools.partial(next_kernel, (slots, edge, width, peers, next_parts)),
        out_shape=shapes(next_parts),
        in_specs=[vmem] * len(handed),
        out_specs=[vmem] * len(next_parts),
        scratch_shapes=[pltpu.VMEM((area, edge * width), f32)],
        compiler_params=limits,
        cost_estimate=work,
        name="rest",
    )(*results)

    def exchange(peer, piece):
        pairs = [(i, i ^ peer) for i in range(peers)]
        return lax.ppermute(piece, ("folds", "sub"), pairs) if peer else piece

    parts = first_parts + next_parts
    early = [exchange(part[0], piece) for part, piece in zip(first_parts, first_pieces)]
    cores = [at for at, part in enumerate(next_parts) if part[0] == 1]
    next_pieces = list(next_pieces)
    early, next_pieces[cores[-1]] = lax.optimization_barrier((early, next_pieces[cores[-1]]))
    arrived = early + [exchange(part[0], piece) for part, piece in zip(next_parts, next_pieces)]

    def gather(first, last, spilled, kind, name):
        chosen = [
            (part, piece)
            for part, piece in zip(parts, arrived)
            if part[1] < last and first < part[2]
        ]
        return pl.pallas_call(
            functools.partial(
                gather_kernel,
                (slots, edge, chunk, [part for part, _ in chosen], first, last, classes),
                spilled,
            ),
            out_shape=pltpu.VMEM((last - first, TZ, VY * classes), kind),
            in_specs=[vmem] * len(chosen),
            out_specs=vmem,
            compiler_params=limits,
            cost_estimate=pl.CostEstimate(
                flops=500000000, bytes_accessed=2000000, transcendentals=0
            ),
            name=name,
        )(*[piece for _, piece in chosen])

    even = [(tile, tile ^ 1) for tile in range(tiles)]
    odd = []
    for tile in range(tiles):
        for i in range(peers):
            if 0 < tile < tiles - 1:
                target = (tile + 1 if tile % 2 else tile - 1) * peers + i
            else:
                target = tile * peers + (i ^ 1)
            odd.append((tile * peers + i, target))
    from_below = []
    for first, last in halves:
        spill = gather(first, last, True, bf16, f"spill_{first}")
        from_below.append(lax.ppermute(spill, ("tiles", "folds", "sub"), odd))
        from_below.append(lax.ppermute(spill, "tiles", even))
    own = gather(0, chunk, False, f32, "own")
    joined = pl.pallas_call(
        functools.partial(join_kernel, halves),
        out_shape=jax.ShapeDtypeStruct((chunk, TZ, VY * classes), f32),
        in_specs=[vmem] * (1 + 2 * len(halves)),
        out_specs=hbm,
        scratch_shapes=[
            pltpu.VMEM((chunk, TZ, VY * classes), f32),
            pltpu.SemaphoreType.DMA((chunk,)),
        ],
        compiler_params=limits,
        name="join",
    )(own, *from_below)
    return jnp.transpose(joined, (1, 0, 2))


def solution(mesh):
    placed = (
        P("folds", ("groups", "tiles", "sub"), None, None, None),
        P("folds", None, None, None, None, None),
        P("folds", None),
        P("folds", None),
        P("folds", None, None, None, None, None),
        P("folds", None),
        P("folds", None),
        P("folds", None, None),
        P("folds", None),
        P(("groups", "tiles", "sub"), None),
        P("groups", None),
    )
    return jax.shard_map(
        on_device,
        mesh=mesh,
        in_specs=placed,
        out_specs=P(("groups", "tiles"), ("folds", "sub"), None),
        check_vma=False,
    )
```

```python
import functools

import jax
import jax.numpy as jnp
from jax import lax
from jax.experimental import pallas as pl
from jax.experimental.pallas import tpu as pltpu
from jax.sharding import PartitionSpec as P

TZ = 16
VX = 40
VY = 40

epsilon = 1e-05
leak_slope = 0.01
far = 1 << 20
bf16 = jnp.bfloat16
f32 = jnp.float32
vmem_bytes = 48 << 20


def iota(shape, dim):
    return lax.broadcasted_iota(jnp.int32, shape, dim)


def tile_matrix(width, lanes):
    return (iota((width, lanes), 1) % width == iota((width, lanes), 0)).astype(bf16)


def tiled_row(ref, lanes):
    width = ref.shape[1]
    row = jnp.concatenate([ref[...], jnp.zeros((1, lanes - width), f32)], axis=1)
    row = jnp.broadcast_to(row, (8, lanes))
    reach = width
    while reach < lanes:
        row = row + pltpu.roll(row, reach, 1)
        reach *= 2
    return row[0:1]


def lane_bands(parts, places):
    total = None
    for place, part in enumerate(parts):
        if part is not None:
            total = part if total is None else jnp.where(places == place, part, total)
    if total is None:
        return None
    if any(part is None for part in parts):
        empty = None
        for place, part in enumerate(parts):
            if part is None:
                here = places == place
                empty = here if empty is None else empty | here
        total = jnp.where(empty, 0.0, total)
    return total


def build_first(taps_ref, band_ref, in_width, width):
    spread = tile_matrix(width, 128)
    places = iota((in_width, 128), 1) // width
    zero = jnp.zeros((in_width, 128), bf16)
    orders = (((1, 0), (2, None)), ((0, 1), (None, 2)))
    for dz in range(3):
        tiled = {}
        for dx in range(3):
            for dy in range(3):
                at = ((dz * 3 + dx) * 3 + dy) * width
                tiled[dx, dy] = lax.dot_general(
                    taps_ref[at : at + width],
                    spread,
                    (((0,), (0,)), ((), ())),
                    preferred_element_type=f32,
                )
        for variant in range(2):
            for yi in range(4):
                for side in range(2):
                    parts = []
                    for dx in orders[variant][side]:
                        for yo in range(2):
                            parts.append(None if dx is None else tiled.get((dx, yi - yo)))
                    block = lane_bands(parts, places)
                    at = dz * 256 + yi * in_width
                    band_ref[variant, at : at + in_width, side * 128 : (side + 1) * 128] = zero if block is None else block.astype(bf16)


def build_second(taps_ref, band_ref, width, dz):
    spread = tile_matrix(width, 128)
    places = iota((width, 128), 1) // width
    zero = jnp.zeros((width, 128), bf16)
    at = dz * 9 * width
    tiled = jnp.dot(taps_ref[at : at + 9 * width], spread, preferred_element_type=f32)
    for dx in range(3):
        taps = {dy: tiled[(dx * 3 + dy) * width : (dx * 3 + dy + 1) * width] for dy in range(3)}
        for yi in range(8):
            block = lane_bands([taps.get(yi - yo) for yo in range(4)], places)
            at = dz * 256 + yi * width
            band_ref[at : at + width, dx * 128 : (dx + 1) * 128] = (
                zero if block is None else block.astype(bf16)
            )


def banded(pad_ref, lane, count, edge, band):
    view = [pad_ref[dz * edge : dz * edge + count, lane : lane + 256] for dz in range(3)]
    return jnp.dot(jnp.concatenate(view, axis=1), band, preferred_element_type=f32)


def join_across(before, here, after, across, edge):
    rows = here.shape[0]
    before = jnp.where(across == 0, 0.0, pltpu.roll(before, 1, 0))
    after = jnp.where(across == edge - 1, 0.0, pltpu.roll(after, rows - 1, 0))
    return here + before + after


def folded(row, width):
    row = jnp.broadcast_to(row, (8, 128))
    reach = width
    while reach < 128:
        row = row + pltpu.roll(row, reach, 1)
        reach *= 2
    return row[0:1]


class Norm:
    def __init__(self, width, rows, voxels):
        self.width, self.rows, self.voxels = width, rows, voxels
        self.base = None
        self.first = self.second = 0.0

    def take(self, block, mask, held):
        kept = block if mask is None else jnp.where(mask, block, 0.0)
        if self.base is None:
            total = folded(jnp.sum(kept, axis=0, keepdims=True), self.width)
            self.base = total * (1.0 / (self.rows * held))
        moved = block - self.base
        if mask is not None:
            moved = jnp.where(mask, moved, 0.0)
        self.first = self.first + jnp.sum(moved, axis=0, keepdims=True)
        self.second = self.second + jnp.sum(moved * moved, axis=0, keepdims=True)

    def settle(self, gain, shift):
        off = folded(self.first, self.width) * (1.0 / self.voxels)
        variance = folded(self.second, self.width) * (1.0 / self.voxels) - off * off
        self.center = self.base + off
        self.factor = lax.rsqrt(jnp.maximum(variance, 0.0) + epsilon) * gain
        self.shift = shift

    def give(self, block, mask):
        scaled = (block - self.center) * self.factor + self.shift
        scaled = jnp.maximum(scaled, leak_slope * scaled)
        return (scaled if mask is None else jnp.where(mask, scaled, 0.0)).astype(bf16)


def section_kernel(
    sizes,
    corners_hbm,
    counts_hbm,
    features_ref,
    taps_one_hbm,
    gain_one_hbm,
    shift_one_hbm,
    taps_two_hbm,
    gain_two_hbm,
    shift_two_hbm,
    head_hbm,
    bias_hbm,
    *rest,
):
    slots, edge, chunk, parts = sizes
    out_refs = rest[: len(parts)]
    (
        pad_one,
        pad_two,
        band_one,
        band_two,
        hidden,
        outcome,
        corners_ref,
        counts_ref,
        taps_one_ref,
        gain_one_ref,
        shift_one_ref,
        taps_two_ref,
        gain_two_ref,
        shift_two_ref,
        head_ref,
        bias_ref,
        selects,
        sems,
    ) = rest[len(parts) :]
    in_width = taps_one_ref.shape[1]
    classes, width = head_ref.shape
    area = edge * edge
    stride = area + edge
    count = hidden.shape[0]
    voxels = float(area * edge)
    data = edge * in_width
    lanes = edge * classes

    copies = []
    for at, (source, target) in enumerate(
        [
            (taps_one_hbm, taps_one_ref),
            (taps_two_hbm, taps_two_ref),
            (gain_one_hbm, gain_one_ref),
            (shift_one_hbm, shift_one_ref),
            (gain_two_hbm, gain_two_ref),
            (shift_two_hbm, shift_two_ref),
            (head_hbm, head_ref),
            (bias_hbm, bias_ref),
            (corners_hbm, corners_ref),
            (counts_hbm, counts_ref),
        ]
        + [
            (
                features_ref.at[slot],
                pad_one.at[pl.ds(edge + slot * stride, area), pl.ds(128, data)],
            )
            for slot in range(slots)
        ]
    ):
        copy = pltpu.make_async_copy(source, target, sems.at[at])
        copy.start()
        copies.append(copy)
    for pad in (pad_one, pad_two):
        for slot in range(slots + 1):
            pad[slot * stride : slot * stride + edge, :] = jnp.zeros((edge, pad.shape[1]), bf16)
    pad_one[:, :128] = jnp.zeros((pad_one.shape[0], 128), bf16)
    pad_one[:, 128 + data :] = jnp.zeros((pad_one.shape[0], 128), bf16)

    center, spread = (edge - 1) / 2.0, edge / 4.0

    def profile(offset):
        return jnp.exp(-((offset.astype(f32) - center) ** 2) / (2.0 * spread * spread))

    row_at = iota((area, 128), 0)
    lane_at = iota((1, lanes), 1)
    gauss = profile(row_at // edge) * profile(row_at % edge)
    gauss = jnp.concatenate([gauss] * (lanes // 128), axis=1) * profile(lane_at // classes)

    row = iota((chunk * edge, area), 0)
    source = iota((chunk * edge, area), 1)
    turn = (row % edge - source // edge) & (edge - 1)
    code = turn + edge * (source % edge - row // edge)
    across = iota((count, 128), 0) % edge
    tile_index = lax.axis_index("tiles")
    sub_index = lax.axis_index("sub")
    position = lax.axis_index("folds") * lax.axis_size("sub") + sub_index

    for copy in copies[:-slots]:
        copy.wait()
    build_first(taps_one_ref, band_one, in_width, width)
    gain_one, shift_one = tiled_row(gain_one_ref, 128), tiled_row(shift_one_ref, 128)
    gain_two, shift_two = tiled_row(gain_two_ref, 128), tiled_row(shift_two_ref, 128)

    half = edge // 2
    head_row = lax.dot_general(
        head_ref[...],
        tile_matrix(classes, half * classes),
        (((0,), (0,)), ((), ())),
        preferred_element_type=f32,
    )
    block = (half * width, half * classes)
    head_block = jnp.where(
        iota(block, 0) // width == iota(block, 1) // classes,
        jnp.concatenate([head_row] * half, axis=0),
        0.0,
    ).astype(bf16)
    bias = tiled_row(bias_ref, lanes)

    mark = iota((edge, lanes), 0)
    notes = jnp.zeros((edge, lanes), f32)
    for slot in range(slots):
        depth = corners_ref[slot, 0] - tile_index * TZ
        notes = jnp.where(mark == 2 * slot, depth.astype(f32), notes)
        notes = jnp.where(mark == 2 * slot + 1, corners_ref[slot, 2].astype(f32), notes)
    for (_, low_row, high_row, noted), out_ref in zip(parts, out_refs):
        if noted:
            out_ref[slots * edge * (high_row - low_row) :, :] = notes.astype(bf16)

    for copy in copies[-slots:]:
        copy.wait()
    low = iota((count, 128), 1) < 64
    spot = iota((area, 128), 1)
    pairs = edge // 4 + 1
    masks = [None] * pairs
    masks[0] = spot >= width
    masks[-1] = spot < width
    norms = [Norm(width, area, voxels) for _ in range(slots)]
    for pair in range(pairs):
        even = banded(pad_one, 256 * pair, count, edge, band_one[0])
        if pair < pairs - 1:
            odd = banded(pad_one, 256 * pair + 128, count, edge, band_one[1])
            here = jnp.where(low, even[:, :128], odd[:, :128])
            before = jnp.where(low, odd[:, :128], even[:, :128])
            after = even[:, 128:] + odd[:, 128:]
        else:
            here = jnp.where(low, even[:, :128], 0.0)
            before = jnp.where(low, 0.0, even[:, :128])
            after = even[:, 128:]
        before = pltpu.roll(before, 64, 1)
        block = join_across(before, here, after, across, edge)
        hidden[:, pair * 128 : (pair + 1) * 128] = block
        for slot, norm in enumerate(norms):
            norm.take(block[slot * stride : slot * stride + area], masks[pair], 3)
        if pair < 3:
            build_second(taps_two_ref, band_two, width, pair)
    for norm in norms:
        norm.settle(gain_one, shift_one)

    def refresh(pair):
        for slot, norm in enumerate(norms):
            at = slot * stride
            block = hidden[at : at + area, pair * 128 : (pair + 1) * 128]
            pad_two[at + edge : at + edge + area, pair * 128 : (pair + 1) * 128] = norm.give(
                block, masks[pair]
            )

    def prepare(slot):
        depth = corners_ref[slot, 0] - tile_index * TZ
        alive = slot < counts_ref[sub_index, tile_index]
        start = 0
        for peer, low_row, high_row, _ in parts:
            wanted = depth + edge * ((position ^ peer) * chunk - corners_ref[slot, 1])
            wanted = jnp.where(alive, wanted, far)
            select = (code[low_row * edge : high_row * edge] == wanted).astype(f32).astype(bf16)
            selects[slot, start : start + select.shape[0], :] = select
            start += select.shape[0]

    quads = edge // 4
    seconds = [Norm(width, area, voxels) for _ in range(slots)]
    refresh(0)
    for quad in range(quads):
        refresh(quad + 1)
        three = banded(pad_two, 128 * quad, count, edge, band_two[...])
        block = join_across(three[:, :128], three[:, 128:256], three[:, 256:], across, edge)
        outcome[:, quad * 128 : (quad + 1) * 128] = block
        for slot, norm in enumerate(seconds):
            norm.take(block[slot * stride : slot * stride + area], None, 4)
        if quad < slots:
            prepare(quad)
    for slot in range(quads, slots):
        prepare(slot)
    for norm in seconds:
        norm.settle(gain_two, shift_two)

    for slot, norm in enumerate(seconds):
        at = slot * stride
        logits = []
        for side in range(2):
            normed = [
                norm.give(outcome[at : at + area, quad * 128 : (quad + 1) * 128], None)
                for quad in range(side * quads // 2, (side + 1) * quads // 2)
            ]
            logits.append(
                jnp.dot(
                    jnp.concatenate(normed, axis=1), head_block, preferred_element_type=f32
                )
            )
        weighted = (jnp.concatenate(logits, axis=1) + bias) * gauss
        lane_start = corners_ref[slot, 2] * classes
        weighted = pltpu.roll(weighted, lane_start % lanes, 1).astype(bf16)
        placed = jnp.dot(selects[slot], weighted, preferred_element_type=f32).astype(bf16)
        start = 0
        for (_, low_row, high_row, _), out_ref in zip(parts, out_refs):
            size = (high_row - low_row) * edge
            out_ref[slot * size : (slot + 1) * size, :] = placed[start : start + size]
            start += size


def gather_kernel(sizes, spilled, *rest):
    slots, edge, chunk, parts, first, last, classes = sizes
    part_refs = rest[: len(parts)]
    out_ref = rest[len(parts)]
    lanes = edge * classes
    blocks = -(-VY * classes // lanes)

    depth_at = iota((edge, lanes), 0)
    lane_at = iota((edge, lanes), 1)
    groups = []
    for (peer, low_row, high_row, noted), part_ref in zip(parts, part_refs):
        if not noted or any(group[0] == peer % 2 for group in groups):
            continue
        notes = part_ref[slots * edge * (high_row - low_row) :, :].astype(f32).astype(jnp.int32)
        for slot in range(slots):
            depth = notes[2 * slot : 2 * slot + 1]
            start = notes[2 * slot + 1 : 2 * slot + 2] * classes
            keep = depth_at < depth if spilled else depth_at >= depth
            inside = []
            for block in range(blocks):
                lane = lane_at + block * lanes
                inside.append(keep & (lane >= start) & (lane < start + lanes))
            groups.append((peer % 2, slot, inside))

    for across in range(first, last):
        total = [jnp.zeros((edge, lanes), f32) for _ in range(blocks)]
        for parity, slot, inside in groups:
            piece = None
            for (peer, low_row, high_row, _), part_ref in zip(parts, part_refs):
                if peer % 2 == parity and low_row <= across < high_row:
                    at = (slot * (high_row - low_row) + across - low_row) * edge
                    part = part_ref[at : at + edge, :].astype(f32)
                    piece = part if piece is None else piece + part
            for block in range(blocks):
                total[block] = total[block] + jnp.where(inside[block], piece, 0.0)
        total = jnp.concatenate(total, axis=1)[:, : VY * classes]
        out_ref[across - first] = total.astype(out_ref.dtype)


def join_kernel(halves, own_ref, *rest):
    out_ref, total, sems = rest[-3:]
    tile_index = lax.axis_index("tiles")
    from_even = (tile_index % 2 == 1).astype(f32)
    from_odd = ((tile_index % 2 == 0) & (tile_index > 0)).astype(f32)
    copies = []
    for at, (low_row, high_row) in enumerate(halves):
        even_ref, odd_ref = rest[2 * at : 2 * at + 2]
        for row in range(low_row, high_row):
            total[row] = (
                own_ref[row]
                + even_ref[row - low_row].astype(f32) * from_even
                + odd_ref[row - low_row].astype(f32) * from_odd
            )
            copy = pltpu.make_async_copy(total.at[row], out_ref.at[row], sems.at[row])
            copy.start()
            copies.append(copy)
    for copy in copies:
        copy.wait()


vmem = pl.BlockSpec(memory_space=pltpu.VMEM)
hbm = pl.BlockSpec(memory_space=pltpu.HBM)
limits = pltpu.CompilerParams(vmem_limit_bytes=vmem_bytes)
ample = pltpu.CompilerParams(vmem_limit_bytes=60000000)


def on_device(
    features,
    conv_first,
    gain_first,
    shift_first,
    conv_second,
    gain_second,
    shift_second,
    head_weight,
    head_bias,
    corners,
    counts,
):
    _, slots, edge, _, data = features.shape
    in_width, width = conv_first.shape[-2:]
    classes = head_bias.shape[1]
    peers = lax.axis_size("folds") * lax.axis_size("sub")
    tiles = lax.axis_size("tiles")
    chunk = VX // peers
    area = edge * edge
    lanes = edge * classes
    padded = slots * (area + edge) + edge
    middle = chunk // 3
    halves = ((0, middle), (middle, chunk))
    parts = [(0, 0, chunk, True)]
    for low_row, high_row in halves:
        parts += [
            (peer, low_row, high_row, peer == peers - 1)
            for peer in [*range(2, peers), 1]
        ]
    rows = [
        slots * edge * (high_row - low_row) + (edge if noted else 0)
        for _, low_row, high_row, noted in parts
    ]
    pieces = pl.pallas_call(
        functools.partial(section_kernel, (slots, edge, chunk, parts)),
        out_shape=[pltpu.VMEM((count, lanes), bf16) for count in rows],
        in_specs=[hbm] * 11,
        out_specs=[vmem] * len(parts),
        scratch_shapes=[
            pltpu.VMEM((padded, data + 256), bf16),
            pltpu.VMEM((padded, edge * width + 128), bf16),
            pltpu.VMEM((2, 768, 256), bf16),
            pltpu.VMEM((768, 384), bf16),
            pltpu.VMEM((padded - 2 * edge, edge * width + 128), f32),
            pltpu.VMEM((padded - 2 * edge, edge * width), f32),
            pltpu.SMEM(corners.shape, jnp.int32),
            pltpu.SMEM(counts.shape[::-1], jnp.int32),
            pltpu.VMEM((27 * width, in_width), bf16),
            pltpu.VMEM((1, width), f32),
            pltpu.VMEM((1, width), f32),
            pltpu.VMEM((27 * width, width), bf16),
            pltpu.VMEM((1, width), f32),
            pltpu.VMEM((1, width), f32),
            pltpu.VMEM((classes, width), bf16),
            pltpu.VMEM((1, classes), f32),
            pltpu.VMEM((slots, VX * edge, area), bf16),
            pltpu.SemaphoreType.DMA((10 + slots,)),
        ],
        compiler_params=ample,
        name="section",
    )(
        corners,
        counts.T,
        features.reshape(slots, area, data),
        jnp.swapaxes(conv_first, 4, 5).reshape(27 * width, in_width),
        gain_first,
        shift_first,
        conv_second.reshape(27 * width, width),
        gain_second,
        shift_second,
        head_weight[0].T,
        head_bias,
    )
    arrived = []
    for (peer, _, _, _), piece in zip(parts, pieces):
        pairs = [(i, i ^ peer) for i in range(peers)]
        arrived.append(lax.ppermute(piece, ("folds", "sub"), pairs) if peer else piece)

    def gather(first, last, spilled, kind, name):
        chosen = [
            (part, piece)
            for part, piece in zip(parts, arrived)
            if part[1] < last and first < part[2]
        ]
        return pl.pallas_call(
            functools.partial(
                gather_kernel,
                (slots, edge, chunk, [part for part, _ in chosen], first, last, classes),
                spilled,
            ),
            out_shape=pltpu.VMEM((last - first, TZ, VY * classes), kind),
            in_specs=[vmem] * len(chosen),
            out_specs=vmem,
            compiler_params=limits,
            cost_estimate=pl.CostEstimate(
                flops=500000000, bytes_accessed=2000000, transcendentals=0
            ),
            name=name,
        )(*[piece for _, piece in chosen])

    even = [(tile, tile ^ 1) for tile in range(tiles)]
    odd = []
    for tile in range(tiles):
        for i in range(peers):
            if 0 < tile < tiles - 1:
                target = (tile + 1 if tile % 2 else tile - 1) * peers + i
            else:
                target = tile * peers + (i ^ 1)
            odd.append((tile * peers + i, target))
    from_below = []
    for first, last in halves:
        spill = gather(first, last, True, bf16, f"spill_{first}")
        from_below.append(lax.ppermute(spill, "tiles", even))
        from_below.append(lax.ppermute(spill, ("tiles", "folds", "sub"), odd))
    own = gather(0, chunk, False, f32, "own")
    joined = pl.pallas_call(
        functools.partial(join_kernel, halves),
        out_shape=jax.ShapeDtypeStruct((chunk, TZ, VY * classes), f32),
        in_specs=[vmem] * (1 + 2 * len(halves)),
        out_specs=hbm,
        scratch_shapes=[
            pltpu.VMEM((chunk, TZ, VY * classes), f32),
            pltpu.SemaphoreType.DMA((chunk,)),
        ],
        compiler_params=limits,
        name="join",
    )(own, *from_below)
    return jnp.transpose(joined, (1, 0, 2))


def solution(mesh):
    placed = (
        P("folds", ("groups", "tiles", "sub"), None, None, None),
        P("folds", None, None, None, None, None),
        P("folds", None),
        P("folds", None),
        P("folds", None, None, None, None, None),
        P("folds", None),
        P("folds", None),
        P("folds", None, None),
        P("folds", None),
        P(("groups", "tiles", "sub"), None),
        P("groups", None),
    )
    return jax.shard_map(
        on_device,
        mesh=mesh,
        in_specs=placed,
        out_specs=P(("groups", "tiles"), ("folds", "sub"), None),
        check_vma=False,
    )
```

```python
import functools

import jax
import jax.numpy as jnp
from jax import lax
from jax.experimental import pallas as pl
from jax.experimental.pallas import tpu as pltpu
from jax.sharding import PartitionSpec as P

TZ = 16
VX = 40
VY = 40

epsilon = 1e-05
leak_slope = 0.01
far = 1 << 20
bf16 = jnp.bfloat16
f32 = jnp.float32
vmem_bytes = 48 << 20


def iota(shape, dim):
    return lax.broadcasted_iota(jnp.int32, shape, dim)


def tile_matrix(width, lanes):
    return (iota((width, lanes), 1) % width == iota((width, lanes), 0)).astype(bf16)


def tiled_row(ref, lanes):
    width = ref.shape[1]
    row = jnp.concatenate([ref[...], jnp.zeros((1, lanes - width), f32)], axis=1)
    row = jnp.broadcast_to(row, (8, lanes))
    reach = width
    while reach < lanes:
        row = row + pltpu.roll(row, reach, 1)
        reach *= 2
    return row[0:1]


def lane_bands(parts, places):
    total = None
    for place, part in enumerate(parts):
        if part is not None:
            total = part if total is None else jnp.where(places == place, part, total)
    if total is None:
        return None
    if any(part is None for part in parts):
        empty = None
        for place, part in enumerate(parts):
            if part is None:
                here = places == place
                empty = here if empty is None else empty | here
        total = jnp.where(empty, 0.0, total)
    return total


def build_first(taps_ref, band_ref, in_width, width):
    spread = tile_matrix(width, 128)
    places = iota((in_width, 128), 1) // width
    zero = jnp.zeros((in_width, 128), bf16)
    orders = (((1, 0), (2, None)), ((0, 1), (None, 2)))
    for dz in range(3):
        tiled = {}
        for dx in range(3):
            for dy in range(3):
                at = ((dz * 3 + dx) * 3 + dy) * width
                tiled[dx, dy] = lax.dot_general(
                    taps_ref[at : at + width],
                    spread,
                    (((0,), (0,)), ((), ())),
                    preferred_element_type=f32,
                )
        for variant in range(2):
            for yi in range(4):
                for side in range(2):
                    parts = []
                    for dx in orders[variant][side]:
                        for yo in range(2):
                            parts.append(None if dx is None else tiled.get((dx, yi - yo)))
                    block = lane_bands(parts, places)
                    at = dz * 256 + yi * in_width
                    band_ref[variant, at : at + in_width, side * 128 : (side + 1) * 128] = zero if block is None else block.astype(bf16)


def build_second(taps_ref, band_ref, width, dz):
    spread = tile_matrix(width, 128)
    places = iota((width, 128), 1) // width
    zero = jnp.zeros((width, 128), bf16)
    at = dz * 9 * width
    tiled = jnp.dot(taps_ref[at : at + 9 * width], spread, preferred_element_type=f32)
    for dx in range(3):
        taps = {dy: tiled[(dx * 3 + dy) * width : (dx * 3 + dy + 1) * width] for dy in range(3)}
        for yi in range(8):
            block = lane_bands([taps.get(yi - yo) for yo in range(4)], places)
            at = dz * 256 + yi * width
            band_ref[at : at + width, dx * 128 : (dx + 1) * 128] = (
                zero if block is None else block.astype(bf16)
            )


def banded(pad_ref, lane, count, edge, band):
    view = [pad_ref[dz * edge : dz * edge + count, lane : lane + 256] for dz in range(3)]
    return jnp.dot(jnp.concatenate(view, axis=1), band, preferred_element_type=f32)


def join_across(before, here, after, across, edge):
    rows = here.shape[0]
    before = jnp.where(across == 0, 0.0, pltpu.roll(before, 1, 0))
    after = jnp.where(across == edge - 1, 0.0, pltpu.roll(after, rows - 1, 0))
    return here + before + after


def folded(row, width):
    row = jnp.broadcast_to(row, (8, 128))
    reach = width
    while reach < 128:
        row = row + pltpu.roll(row, reach, 1)
        reach *= 2
    return row[0:1]


class Norm:
    def __init__(self, width, rows, voxels):
        self.width, self.rows, self.voxels = width, rows, voxels
        self.base = None
        self.first = self.second = 0.0

    def take(self, block, mask, held):
        kept = block if mask is None else jnp.where(mask, block, 0.0)
        if self.base is None:
            total = folded(jnp.sum(kept, axis=0, keepdims=True), self.width)
            self.base = total * (1.0 / (self.rows * held))
        moved = block - self.base
        if mask is not None:
            moved = jnp.where(mask, moved, 0.0)
        self.first = self.first + jnp.sum(moved, axis=0, keepdims=True)
        self.second = self.second + jnp.sum(moved * moved, axis=0, keepdims=True)

    def settle(self, gain, shift):
        off = folded(self.first, self.width) * (1.0 / self.voxels)
        variance = folded(self.second, self.width) * (1.0 / self.voxels) - off * off
        self.center = self.base + off
        self.factor = lax.rsqrt(jnp.maximum(variance, 0.0) + epsilon) * gain
        self.shift = shift

    def give(self, block, mask):
        scaled = (block - self.center) * self.factor + self.shift
        scaled = jnp.maximum(scaled, leak_slope * scaled)
        return (scaled if mask is None else jnp.where(mask, scaled, 0.0)).astype(bf16)


def section_kernel(
    sizes,
    corners_hbm,
    counts_hbm,
    features_ref,
    taps_one_hbm,
    gain_one_hbm,
    shift_one_hbm,
    taps_two_hbm,
    gain_two_hbm,
    shift_two_hbm,
    head_hbm,
    bias_hbm,
    *rest,
):
    slots, edge, chunk, parts = sizes
    out_refs = rest[: len(parts)]
    (
        pad_one,
        pad_two,
        band_one,
        band_two,
        hidden,
        outcome,
        corners_ref,
        counts_ref,
        taps_one_ref,
        gain_one_ref,
        shift_one_ref,
        taps_two_ref,
        gain_two_ref,
        shift_two_ref,
        head_ref,
        bias_ref,
        selects,
        sems,
    ) = rest[len(parts) :]
    in_width = taps_one_ref.shape[1]
    classes, width = head_ref.shape
    area = edge * edge
    stride = area + edge
    count = hidden.shape[0]
    voxels = float(area * edge)
    data = edge * in_width
    lanes = edge * classes

    copies = []
    for at, (source, target) in enumerate(
        [
            (taps_one_hbm, taps_one_ref),
            (taps_two_hbm, taps_two_ref),
            (gain_one_hbm, gain_one_ref),
            (shift_one_hbm, shift_one_ref),
            (gain_two_hbm, gain_two_ref),
            (shift_two_hbm, shift_two_ref),
            (head_hbm, head_ref),
            (bias_hbm, bias_ref),
            (corners_hbm, corners_ref),
            (counts_hbm, counts_ref),
        ]
        + [
            (
                features_ref.at[slot],
                pad_one.at[pl.ds(edge + slot * stride, area), pl.ds(128, data)],
            )
            for slot in range(slots)
        ]
    ):
        copy = pltpu.make_async_copy(source, target, sems.at[at])
        copy.start()
        copies.append(copy)
    for pad in (pad_one, pad_two):
        for slot in range(slots + 1):
            pad[slot * stride : slot * stride + edge, :] = jnp.zeros((edge, pad.shape[1]), bf16)
    pad_one[:, :128] = jnp.zeros((pad_one.shape[0], 128), bf16)
    pad_one[:, 128 + data :] = jnp.zeros((pad_one.shape[0], 128), bf16)

    center, spread = (edge - 1) / 2.0, edge / 4.0

    def profile(offset):
        return jnp.exp(-((offset.astype(f32) - center) ** 2) / (2.0 * spread * spread))

    row_at = iota((area, 128), 0)
    lane_at = iota((1, lanes), 1)
    gauss = profile(row_at // edge) * profile(row_at % edge)
    gauss = jnp.concatenate([gauss] * (lanes // 128), axis=1) * profile(lane_at // classes)

    row = iota((chunk * edge, area), 0)
    source = iota((chunk * edge, area), 1)
    turn = (row % edge - source // edge) & (edge - 1)
    code = turn + edge * (source % edge - row // edge)
    across = iota((count, 128), 0) % edge
    tile_index = lax.axis_index("tiles")
    sub_index = lax.axis_index("sub")
    position = lax.axis_index("folds") * lax.axis_size("sub") + sub_index

    for copy in copies[:-slots]:
        copy.wait()
    build_first(taps_one_ref, band_one, in_width, width)
    gain_one, shift_one = tiled_row(gain_one_ref, 128), tiled_row(shift_one_ref, 128)
    gain_two, shift_two = tiled_row(gain_two_ref, 128), tiled_row(shift_two_ref, 128)

    half = edge // 2
    head_row = lax.dot_general(
        head_ref[...],
        tile_matrix(classes, half * classes),
        (((0,), (0,)), ((), ())),
        preferred_element_type=f32,
    )
    block = (half * width, half * classes)
    head_block = jnp.where(
        iota(block, 0) // width == iota(block, 1) // classes,
        jnp.concatenate([head_row] * half, axis=0),
        0.0,
    ).astype(bf16)
    bias = tiled_row(bias_ref, lanes)

    mark = iota((edge, lanes), 0)
    notes = jnp.zeros((edge, lanes), f32)
    for slot in range(slots):
        depth = corners_ref[slot, 0] - tile_index * TZ
        notes = jnp.where(mark == 2 * slot, depth.astype(f32), notes)
        notes = jnp.where(mark == 2 * slot + 1, corners_ref[slot, 2].astype(f32), notes)
    for (_, low_row, high_row, noted), out_ref in zip(parts, out_refs):
        if noted:
            out_ref[slots * edge * (high_row - low_row) :, :] = notes.astype(bf16)

    for copy in copies[-slots:]:
        copy.wait()
    low = iota((count, 128), 1) < 64
    spot = iota((area, 128), 1)
    pairs = edge // 4 + 1
    masks = [None] * pairs
    masks[0] = spot >= width
    masks[-1] = spot < width
    norms = [Norm(width, area, voxels) for _ in range(slots)]
    for pair in range(pairs):
        even = banded(pad_one, 256 * pair, count, edge, band_one[0])
        if pair < pairs - 1:
            odd = banded(pad_one, 256 * pair + 128, count, edge, band_one[1])
            here = jnp.where(low, even[:, :128], odd[:, :128])
            before = jnp.where(low, odd[:, :128], even[:, :128])
            after = even[:, 128:] + odd[:, 128:]
        else:
            here = jnp.where(low, even[:, :128], 0.0)
            before = jnp.where(low, 0.0, even[:, :128])
            after = even[:, 128:]
        before = pltpu.roll(before, 64, 1)
        block = join_across(before, here, after, across, edge)
        hidden[:, pair * 128 : (pair + 1) * 128] = block
        for slot, norm in enumerate(norms):
            norm.take(block[slot * stride : slot * stride + area], masks[pair], 3)
        if pair < 3:
            build_second(taps_two_ref, band_two, width, pair)
    for norm in norms:
        norm.settle(gain_one, shift_one)

    def refresh(pair):
        for slot, norm in enumerate(norms):
            at = slot * stride
            block = hidden[at : at + area, pair * 128 : (pair + 1) * 128]
            pad_two[at + edge : at + edge + area, pair * 128 : (pair + 1) * 128] = norm.give(
                block, masks[pair]
            )

    def prepare(slot):
        depth = corners_ref[slot, 0] - tile_index * TZ
        alive = slot < counts_ref[sub_index, tile_index]
        start = 0
        for peer, low_row, high_row, _ in parts:
            wanted = depth + edge * ((position ^ peer) * chunk - corners_ref[slot, 1])
            wanted = jnp.where(alive, wanted, far)
            select = (code[low_row * edge : high_row * edge] == wanted).astype(f32).astype(bf16)
            selects[slot, start : start + select.shape[0], :] = select
            start += select.shape[0]

    quads = edge // 4
    seconds = [Norm(width, area, voxels) for _ in range(slots)]
    refresh(0)
    for quad in range(quads):
        refresh(quad + 1)
        three = banded(pad_two, 128 * quad, count, edge, band_two[...])
        block = join_across(three[:, :128], three[:, 128:256], three[:, 256:], across, edge)
        outcome[:, quad * 128 : (quad + 1) * 128] = block
        for slot, norm in enumerate(seconds):
            norm.take(block[slot * stride : slot * stride + area], None, 4)
        if quad < slots:
            prepare(quad)
    for slot in range(quads, slots):
        prepare(slot)
    for norm in seconds:
        norm.settle(gain_two, shift_two)

    for slot, norm in enumerate(seconds):
        at = slot * stride
        logits = []
        for side in range(2):
            normed = [
                norm.give(outcome[at : at + area, quad * 128 : (quad + 1) * 128], None)
                for quad in range(side * quads // 2, (side + 1) * quads // 2)
            ]
            logits.append(
                jnp.dot(
                    jnp.concatenate(normed, axis=1), head_block, preferred_element_type=f32
                )
            )
        weighted = (jnp.concatenate(logits, axis=1) + bias) * gauss
        lane_start = corners_ref[slot, 2] * classes
        weighted = pltpu.roll(weighted, lane_start % lanes, 1).astype(bf16)
        placed = jnp.dot(selects[slot], weighted, preferred_element_type=f32).astype(bf16)
        start = 0
        for (_, low_row, high_row, _), out_ref in zip(parts, out_refs):
            size = (high_row - low_row) * edge
            out_ref[slot * size : (slot + 1) * size, :] = placed[start : start + size]
            start += size


def gather_kernel(sizes, spilled, *rest):
    slots, edge, chunk, parts, first, last, classes = sizes
    part_refs = rest[: len(parts)]
    out_ref = rest[len(parts)]
    lanes = edge * classes
    blocks = -(-VY * classes // lanes)

    depth_at = iota((edge, lanes), 0)
    lane_at = iota((edge, lanes), 1)
    groups = []
    for (peer, low_row, high_row, noted), part_ref in zip(parts, part_refs):
        if not noted or any(group[0] == peer % 2 for group in groups):
            continue
        notes = part_ref[slots * edge * (high_row - low_row) :, :].astype(f32).astype(jnp.int32)
        for slot in range(slots):
            depth = notes[2 * slot : 2 * slot + 1]
            start = notes[2 * slot + 1 : 2 * slot + 2] * classes
            keep = depth_at < depth if spilled else depth_at >= depth
            inside = []
            for block in range(blocks):
                lane = lane_at + block * lanes
                inside.append(keep & (lane >= start) & (lane < start + lanes))
            groups.append((peer % 2, slot, inside))

    for across in range(first, last):
        total = [jnp.zeros((edge, lanes), f32) for _ in range(blocks)]
        for parity, slot, inside in groups:
            piece = None
            for (peer, low_row, high_row, _), part_ref in zip(parts, part_refs):
                if peer % 2 == parity and low_row <= across < high_row:
                    at = (slot * (high_row - low_row) + across - low_row) * edge
                    part = part_ref[at : at + edge, :].astype(f32)
                    piece = part if piece is None else piece + part
            for block in range(blocks):
                total[block] = total[block] + jnp.where(inside[block], piece, 0.0)
        total = jnp.concatenate(total, axis=1)[:, : VY * classes]
        out_ref[across - first] = total.astype(out_ref.dtype)


def join_kernel(low_row, own_ref, odd_ref, even_ref, *rest):
    out_ref, total, sems = rest[-3:]
    tile_index = lax.axis_index("tiles")
    from_even = (tile_index % 2 == 1).astype(f32)
    from_odd = ((tile_index % 2 == 0) & (tile_index > 0)).astype(f32)
    copies = []
    for row in range(even_ref.shape[0]):
        total[row] = (
            own_ref[low_row + row]
            + even_ref[row].astype(f32) * from_even
            + odd_ref[row].astype(f32) * from_odd
        )
        copy = pltpu.make_async_copy(total.at[row], out_ref.at[low_row + row], sems.at[row])
        copy.start()
        copies.append(copy)
    for copy in copies:
        copy.wait()


vmem = pl.BlockSpec(memory_space=pltpu.VMEM)
hbm = pl.BlockSpec(memory_space=pltpu.HBM)
limits = pltpu.CompilerParams(vmem_limit_bytes=vmem_bytes)
ample = pltpu.CompilerParams(vmem_limit_bytes=60000000)


def on_device(
    features,
    conv_first,
    gain_first,
    shift_first,
    conv_second,
    gain_second,
    shift_second,
    head_weight,
    head_bias,
    corners,
    counts,
):
    _, slots, edge, _, data = features.shape
    in_width, width = conv_first.shape[-2:]
    classes = head_bias.shape[1]
    peers = lax.axis_size("folds") * lax.axis_size("sub")
    tiles = lax.axis_size("tiles")
    chunk = VX // peers
    area = edge * edge
    lanes = edge * classes
    padded = slots * (area + edge) + edge
    middle = chunk * 2 // 5
    halves = ((0, middle), (middle, chunk))
    parts = [(0, 0, chunk, True)]
    for low_row, high_row in halves:
        parts += [
            (peer, low_row, high_row, peer == peers - 1)
            for peer in [*range(2, peers), 1]
        ]
    rows = [
        slots * edge * (high_row - low_row) + (edge if noted else 0)
        for _, low_row, high_row, noted in parts
    ]
    pieces = pl.pallas_call(
        functools.partial(section_kernel, (slots, edge, chunk, parts)),
        out_shape=[pltpu.VMEM((count, lanes), bf16) for count in rows],
        in_specs=[hbm] * 11,
        out_specs=[vmem] * len(parts),
        scratch_shapes=[
            pltpu.VMEM((padded, data + 256), bf16),
            pltpu.VMEM((padded, edge * width + 128), bf16),
            pltpu.VMEM((2, 768, 256), bf16),
            pltpu.VMEM((768, 384), bf16),
            pltpu.VMEM((padded - 2 * edge, edge * width + 128), f32),
            pltpu.VMEM((padded - 2 * edge, edge * width), f32),
            pltpu.SMEM(corners.shape, jnp.int32),
            pltpu.SMEM(counts.shape[::-1], jnp.int32),
            pltpu.VMEM((27 * width, in_width), bf16),
            pltpu.VMEM((1, width), f32),
            pltpu.VMEM((1, width), f32),
            pltpu.VMEM((27 * width, width), bf16),
            pltpu.VMEM((1, width), f32),
            pltpu.VMEM((1, width), f32),
            pltpu.VMEM((classes, width), bf16),
            pltpu.VMEM((1, classes), f32),
            pltpu.VMEM((slots, VX * edge, area), bf16),
            pltpu.SemaphoreType.DMA((10 + slots,)),
        ],
        compiler_params=ample,
        name="section",
    )(
        corners,
        counts.T,
        features.reshape(slots, area, data),
        jnp.swapaxes(conv_first, 4, 5).reshape(27 * width, in_width),
        gain_first,
        shift_first,
        conv_second.reshape(27 * width, width),
        gain_second,
        shift_second,
        head_weight[0].T,
        head_bias,
    )
    arrived = []
    for (peer, _, _, _), piece in zip(parts, pieces):
        pairs = [(i, i ^ peer) for i in range(peers)]
        arrived.append(lax.ppermute(piece, ("folds", "sub"), pairs) if peer else piece)

    def gather(first, last, spilled, kind, name):
        chosen = [
            (part, piece)
            for part, piece in zip(parts, arrived)
            if part[1] < last and first < part[2]
        ]
        return pl.pallas_call(
            functools.partial(
                gather_kernel,
                (slots, edge, chunk, [part for part, _ in chosen], first, last, classes),
                spilled,
            ),
            out_shape=pltpu.VMEM((last - first, TZ, VY * classes), kind),
            in_specs=[vmem] * len(chosen),
            out_specs=vmem,
            compiler_params=limits,
            cost_estimate=pl.CostEstimate(
                flops=500000000, bytes_accessed=2000000, transcendentals=0
            ),
            name=name,
        )(*[piece for _, piece in chosen])

    even = [(tile, tile ^ 1) for tile in range(tiles)]
    odd = []
    for tile in range(tiles):
        for i in range(peers):
            if 0 < tile < tiles - 1:
                target = (tile + 1 if tile % 2 else tile - 1) * peers + i
            else:
                target = tile * peers + (i ^ 1)
            odd.append((tile * peers + i, target))
    from_below = []
    for first, last in halves:
        spill = gather(first, last, True, bf16, f"spill_{first}")
        from_below.append(lax.ppermute(spill, ("tiles", "folds", "sub"), odd))
        from_below.append(lax.ppermute(spill, "tiles", even))
    own = gather(0, chunk, False, f32, "own")
    joined = None
    for at in (1, 0):
        low_row, high_row = halves[at]
        joined = pl.pallas_call(
            functools.partial(join_kernel, low_row),
            out_shape=jax.ShapeDtypeStruct((chunk, TZ, VY * classes), f32),
            in_specs=[vmem] * 3 + ([] if joined is None else [hbm]),
            out_specs=hbm,
            input_output_aliases={} if joined is None else {3: 0},
            scratch_shapes=[
                pltpu.VMEM((high_row - low_row, TZ, VY * classes), f32),
                pltpu.SemaphoreType.DMA((high_row - low_row,)),
            ],
            compiler_params=limits,
            name=f"join_{low_row}",
        )(own, *from_below[2 * at : 2 * at + 2], *([] if joined is None else [joined]))
    return jnp.transpose(joined, (1, 0, 2))


def solution(mesh):
    placed = (
        P("folds", ("groups", "tiles", "sub"), None, None, None),
        P("folds", None, None, None, None, None),
        P("folds", None),
        P("folds", None),
        P("folds", None, None, None, None, None),
        P("folds", None),
        P("folds", None),
        P("folds", None, None),
        P("folds", None),
        P(("groups", "tiles", "sub"), None),
        P("groups", None),
    )
    return jax.shard_map(
        on_device,
        mesh=mesh,
        in_specs=placed,
        out_specs=P(("groups", "tiles"), ("folds", "sub"), None),
        check_vma=False,
    )
```

```python
import functools

import jax
import jax.numpy as jnp
from jax import lax
from jax.experimental import pallas as pl
from jax.experimental.pallas import tpu as pltpu
from jax.sharding import PartitionSpec as P

TZ = 16
VX = 40
VY = 40

epsilon = 1e-05
leak_slope = 0.01
far = 1 << 20
bf16 = jnp.bfloat16
f32 = jnp.float32
vmem_bytes = 48 << 20


def iota(shape, dim):
    return lax.broadcasted_iota(jnp.int32, shape, dim)


def tile_matrix(width, lanes):
    return (iota((width, lanes), 1) % width == iota((width, lanes), 0)).astype(bf16)


def tiled_row(ref, lanes):
    width = ref.shape[1]
    row = jnp.concatenate([ref[...], jnp.zeros((1, lanes - width), f32)], axis=1)
    row = jnp.broadcast_to(row, (8, lanes))
    reach = width
    while reach < lanes:
        row = row + pltpu.roll(row, reach, 1)
        reach *= 2
    return row[0:1]


def lane_bands(parts, places):
    total = None
    for place, part in enumerate(parts):
        if part is not None:
            total = part if total is None else jnp.where(places == place, part, total)
    if total is None:
        return None
    if any(part is None for part in parts):
        empty = None
        for place, part in enumerate(parts):
            if part is None:
                here = places == place
                empty = here if empty is None else empty | here
        total = jnp.where(empty, 0.0, total)
    return total


def build_first(taps_ref, band_ref, in_width, width):
    spread = tile_matrix(width, 128)
    places = iota((in_width, 128), 1) // width
    zero = jnp.zeros((in_width, 128), bf16)
    orders = (((1, 0), (2, None)), ((0, 1), (None, 2)))
    for dz in range(3):
        tiled = {}
        for dx in range(3):
            for dy in range(3):
                at = ((dz * 3 + dx) * 3 + dy) * width
                tiled[dx, dy] = lax.dot_general(
                    taps_ref[at : at + width],
                    spread,
                    (((0,), (0,)), ((), ())),
                    preferred_element_type=f32,
                )
        for variant in range(2):
            for yi in range(4):
                for side in range(2):
                    parts = []
                    for dx in orders[variant][side]:
                        for yo in range(2):
                            parts.append(None if dx is None else tiled.get((dx, yi - yo)))
                    block = lane_bands(parts, places)
                    at = dz * 256 + yi * in_width
                    band_ref[variant, at : at + in_width, side * 128 : (side + 1) * 128] = zero if block is None else block.astype(bf16)


def build_second(taps_ref, band_ref, width, dz):
    spread = tile_matrix(width, 128)
    places = iota((width, 128), 1) // width
    zero = jnp.zeros((width, 128), bf16)
    at = dz * 9 * width
    tiled = jnp.dot(taps_ref[at : at + 9 * width], spread, preferred_element_type=f32)
    for dx in range(3):
        taps = {dy: tiled[(dx * 3 + dy) * width : (dx * 3 + dy + 1) * width] for dy in range(3)}
        for yi in range(8):
            block = lane_bands([taps.get(yi - yo) for yo in range(4)], places)
            at = dz * 256 + yi * width
            band_ref[at : at + width, dx * 128 : (dx + 1) * 128] = (
                zero if block is None else block.astype(bf16)
            )


def banded(pad_ref, lane, count, edge, band):
    view = [pad_ref[dz * edge : dz * edge + count, lane : lane + 256] for dz in range(3)]
    return jnp.dot(jnp.concatenate(view, axis=1), band, preferred_element_type=f32)


def join_across(before, here, after, across, edge):
    rows = here.shape[0]
    before = jnp.where(across == 0, 0.0, pltpu.roll(before, 1, 0))
    after = jnp.where(across == edge - 1, 0.0, pltpu.roll(after, rows - 1, 0))
    return here + before + after


def folded(row, width):
    row = jnp.broadcast_to(row, (8, 128))
    reach = width
    while reach < 128:
        row = row + pltpu.roll(row, reach, 1)
        reach *= 2
    return row[0:1]


class Norm:
    def __init__(self, width, rows, voxels):
        self.width, self.rows, self.voxels = width, rows, voxels
        self.base = None
        self.first = self.second = 0.0

    def take(self, block, mask, held):
        kept = block if mask is None else jnp.where(mask, block, 0.0)
        if self.base is None:
            total = folded(jnp.sum(kept, axis=0, keepdims=True), self.width)
            self.base = total * (1.0 / (self.rows * held))
        moved = block - self.base
        if mask is not None:
            moved = jnp.where(mask, moved, 0.0)
        self.first = self.first + jnp.sum(moved, axis=0, keepdims=True)
        self.second = self.second + jnp.sum(moved * moved, axis=0, keepdims=True)

    def settle(self, gain, shift):
        off = folded(self.first, self.width) * (1.0 / self.voxels)
        variance = folded(self.second, self.width) * (1.0 / self.voxels) - off * off
        self.center = self.base + off
        self.factor = lax.rsqrt(jnp.maximum(variance, 0.0) + epsilon) * gain
        self.shift = shift

    def give(self, block, mask):
        scaled = (block - self.center) * self.factor + self.shift
        scaled = jnp.maximum(scaled, leak_slope * scaled)
        return (scaled if mask is None else jnp.where(mask, scaled, 0.0)).astype(bf16)


def section_kernel(
    sizes,
    corners_hbm,
    counts_hbm,
    features_ref,
    taps_one_hbm,
    gain_one_hbm,
    shift_one_hbm,
    taps_two_hbm,
    gain_two_hbm,
    shift_two_hbm,
    head_hbm,
    bias_hbm,
    *rest,
):
    slots, edge, chunk, parts = sizes
    out_refs = rest[: len(parts)]
    (
        pad_one,
        pad_two,
        band_one,
        band_two,
        hidden,
        outcome,
        corners_ref,
        counts_ref,
        taps_one_ref,
        gain_one_ref,
        shift_one_ref,
        taps_two_ref,
        gain_two_ref,
        shift_two_ref,
        head_ref,
        bias_ref,
        selects,
        sems,
    ) = rest[len(parts) :]
    in_width = taps_one_ref.shape[1]
    classes, width = head_ref.shape
    area = edge * edge
    stride = area + edge
    count = hidden.shape[0]
    voxels = float(area * edge)
    data = edge * in_width
    lanes = edge * classes

    copies = []
    for at, (source, target) in enumerate(
        [
            (taps_one_hbm, taps_one_ref),
            (taps_two_hbm, taps_two_ref),
            (gain_one_hbm, gain_one_ref),
            (shift_one_hbm, shift_one_ref),
            (gain_two_hbm, gain_two_ref),
            (shift_two_hbm, shift_two_ref),
            (head_hbm, head_ref),
            (bias_hbm, bias_ref),
            (corners_hbm, corners_ref),
            (counts_hbm, counts_ref),
        ]
        + [
            (
                features_ref.at[slot],
                pad_one.at[pl.ds(edge + slot * stride, area), pl.ds(128, data)],
            )
            for slot in range(slots)
        ]
    ):
        copy = pltpu.make_async_copy(source, target, sems.at[at])
        copy.start()
        copies.append(copy)
    for pad in (pad_one, pad_two):
        for slot in range(slots + 1):
            pad[slot * stride : slot * stride + edge, :] = jnp.zeros((edge, pad.shape[1]), bf16)
    pad_one[:, :128] = jnp.zeros((pad_one.shape[0], 128), bf16)
    pad_one[:, 128 + data :] = jnp.zeros((pad_one.shape[0], 128), bf16)

    center, spread = (edge - 1) / 2.0, edge / 4.0

    def profile(offset):
        return jnp.exp(-((offset.astype(f32) - center) ** 2) / (2.0 * spread * spread))

    row_at = iota((area, 128), 0)
    lane_at = iota((1, lanes), 1)
    gauss = profile(row_at // edge) * profile(row_at % edge)
    gauss = jnp.concatenate([gauss] * (lanes // 128), axis=1) * profile(lane_at // classes)

    row = iota((chunk * edge, area), 0)
    source = iota((chunk * edge, area), 1)
    turn = (row % edge - source // edge) & (edge - 1)
    code = turn + edge * (source % edge - row // edge)
    across = iota((count, 128), 0) % edge
    tile_index = lax.axis_index("tiles")
    sub_index = lax.axis_index("sub")
    position = lax.axis_index("folds") * lax.axis_size("sub") + sub_index

    for copy in copies[:-slots]:
        copy.wait()
    build_first(taps_one_ref, band_one, in_width, width)
    gain_one, shift_one = tiled_row(gain_one_ref, 128), tiled_row(shift_one_ref, 128)
    gain_two, shift_two = tiled_row(gain_two_ref, 128), tiled_row(shift_two_ref, 128)

    half = edge // 2
    head_row = lax.dot_general(
        head_ref[...],
        tile_matrix(classes, half * classes),
        (((0,), (0,)), ((), ())),
        preferred_element_type=f32,
    )
    block = (half * width, half * classes)
    head_block = jnp.where(
        iota(block, 0) // width == iota(block, 1) // classes,
        jnp.concatenate([head_row] * half, axis=0),
        0.0,
    ).astype(bf16)
    bias = tiled_row(bias_ref, lanes)

    mark = iota((edge, lanes), 0)
    notes = jnp.zeros((edge, lanes), f32)
    for slot in range(slots):
        depth = corners_ref[slot, 0] - tile_index * TZ
        notes = jnp.where(mark == 2 * slot, depth.astype(f32), notes)
        notes = jnp.where(mark == 2 * slot + 1, corners_ref[slot, 2].astype(f32), notes)
    for (_, low_row, high_row, noted), out_ref in zip(parts, out_refs):
        if noted:
            out_ref[slots * edge * (high_row - low_row) :, :] = notes.astype(bf16)

    for copy in copies[-slots:]:
        copy.wait()
    low = iota((count, 128), 1) < 64
    spot = iota((area, 128), 1)
    pairs = edge // 4 + 1
    masks = [None] * pairs
    masks[0] = spot >= width
    masks[-1] = spot < width
    norms = [Norm(width, area, voxels) for _ in range(slots)]
    for pair in range(pairs):
        even = banded(pad_one, 256 * pair, count, edge, band_one[0])
        if pair < pairs - 1:
            odd = banded(pad_one, 256 * pair + 128, count, edge, band_one[1])
            here = jnp.where(low, even[:, :128], odd[:, :128])
            before = jnp.where(low, odd[:, :128], even[:, :128])
            after = even[:, 128:] + odd[:, 128:]
        else:
            here = jnp.where(low, even[:, :128], 0.0)
            before = jnp.where(low, 0.0, even[:, :128])
            after = even[:, 128:]
        before = pltpu.roll(before, 64, 1)
        block = join_across(before, here, after, across, edge)
        hidden[:, pair * 128 : (pair + 1) * 128] = block
        for slot, norm in enumerate(norms):
            norm.take(block[slot * stride : slot * stride + area], masks[pair], 3)
        if pair < 3:
            build_second(taps_two_ref, band_two, width, pair)
    for norm in norms:
        norm.settle(gain_one, shift_one)

    def refresh(pair):
        for slot, norm in enumerate(norms):
            at = slot * stride
            block = hidden[at : at + area, pair * 128 : (pair + 1) * 128]
            pad_two[at + edge : at + edge + area, pair * 128 : (pair + 1) * 128] = norm.give(
                block, masks[pair]
            )

    def prepare(slot):
        depth = corners_ref[slot, 0] - tile_index * TZ
        alive = slot < counts_ref[sub_index, tile_index]
        start = 0
        for peer, low_row, high_row, _ in parts:
            wanted = depth + edge * ((position ^ peer) * chunk - corners_ref[slot, 1])
            wanted = jnp.where(alive, wanted, far)
            select = (code[low_row * edge : high_row * edge] == wanted).astype(f32).astype(bf16)
            selects[slot, start : start + select.shape[0], :] = select
            start += select.shape[0]

    quads = edge // 4
    seconds = [Norm(width, area, voxels) for _ in range(slots)]
    refresh(0)
    for quad in range(quads):
        refresh(quad + 1)
        three = banded(pad_two, 128 * quad, count, edge, band_two[...])
        block = join_across(three[:, :128], three[:, 128:256], three[:, 256:], across, edge)
        outcome[:, quad * 128 : (quad + 1) * 128] = block
        for slot, norm in enumerate(seconds):
            norm.take(block[slot * stride : slot * stride + area], None, 4)
        if quad < slots:
            prepare(quad)
    for slot in range(quads, slots):
        prepare(slot)
    for norm in seconds:
        norm.settle(gain_two, shift_two)

    for slot, norm in enumerate(seconds):
        at = slot * stride
        logits = []
        for side in range(2):
            normed = [
                norm.give(outcome[at : at + area, quad * 128 : (quad + 1) * 128], None)
                for quad in range(side * quads // 2, (side + 1) * quads // 2)
            ]
            logits.append(
                jnp.dot(
                    jnp.concatenate(normed, axis=1), head_block, preferred_element_type=f32
                )
            )
        weighted = (jnp.concatenate(logits, axis=1) + bias) * gauss
        lane_start = corners_ref[slot, 2] * classes
        weighted = pltpu.roll(weighted, lane_start % lanes, 1).astype(bf16)
        placed = jnp.dot(selects[slot], weighted, preferred_element_type=f32).astype(bf16)
        start = 0
        for (_, low_row, high_row, _), out_ref in zip(parts, out_refs):
            size = (high_row - low_row) * edge
            out_ref[slot * size : (slot + 1) * size, :] = placed[start : start + size]
            start += size


def gather_kernel(sizes, spilled, *rest):
    slots, edge, chunk, parts, first, last, classes = sizes
    part_refs = rest[: len(parts)]
    out_ref = rest[len(parts)]
    lanes = edge * classes
    blocks = -(-VY * classes // lanes)

    depth_at = iota((edge, lanes), 0)
    lane_at = iota((edge, lanes), 1)
    groups = []
    for (peer, low_row, high_row, noted), part_ref in zip(parts, part_refs):
        if not noted or any(group[0] == peer % 2 for group in groups):
            continue
        notes = part_ref[slots * edge * (high_row - low_row) :, :].astype(f32).astype(jnp.int32)
        for slot in range(slots):
            depth = notes[2 * slot : 2 * slot + 1]
            start = notes[2 * slot + 1 : 2 * slot + 2] * classes
            keep = depth_at < depth if spilled else depth_at >= depth
            inside = []
            for block in range(blocks):
                lane = lane_at + block * lanes
                inside.append(keep & (lane >= start) & (lane < start + lanes))
            groups.append((peer % 2, slot, inside))

    for across in range(first, last):
        total = [jnp.zeros((edge, lanes), f32) for _ in range(blocks)]
        for parity, slot, inside in groups:
            piece = None
            for (peer, low_row, high_row, _), part_ref in zip(parts, part_refs):
                if peer % 2 == parity and low_row <= across < high_row:
                    at = (slot * (high_row - low_row) + across - low_row) * edge
                    part = part_ref[at : at + edge, :].astype(f32)
                    piece = part if piece is None else piece + part
            for block in range(blocks):
                total[block] = total[block] + jnp.where(inside[block], piece, 0.0)
        total = jnp.concatenate(total, axis=1)[:, : VY * classes]
        out_ref[across - first] = total.astype(out_ref.dtype)


def join_kernel(low_row, count, own_ref, *rest):
    arrived = rest[:count]
    out_ref, total, sems = rest[-3:]
    tile_index = lax.axis_index("tiles")
    if count == 1:
        shares = [(tile_index > 0).astype(f32)]
    else:
        shares = [
            ((tile_index % 2 == 0) & (tile_index > 0)).astype(f32),
            (tile_index % 2 == 1).astype(f32),
        ]
    copies = []
    for row in range(total.shape[0]):
        value = own_ref[low_row + row]
        for share, part_ref in zip(shares, arrived):
            value = value + part_ref[row].astype(f32) * share
        total[row] = value
        copy = pltpu.make_async_copy(total.at[row], out_ref.at[low_row + row], sems.at[row])
        copy.start()
        copies.append(copy)
    for copy in copies:
        copy.wait()


vmem = pl.BlockSpec(memory_space=pltpu.VMEM)
hbm = pl.BlockSpec(memory_space=pltpu.HBM)
limits = pltpu.CompilerParams(vmem_limit_bytes=vmem_bytes)
ample = pltpu.CompilerParams(vmem_limit_bytes=60000000)


def on_device(
    features,
    conv_first,
    gain_first,
    shift_first,
    conv_second,
    gain_second,
    shift_second,
    head_weight,
    head_bias,
    corners,
    counts,
):
    _, slots, edge, _, data = features.shape
    in_width, width = conv_first.shape[-2:]
    classes = head_bias.shape[1]
    peers = lax.axis_size("folds") * lax.axis_size("sub")
    tiles = lax.axis_size("tiles")
    chunk = VX // peers
    area = edge * edge
    lanes = edge * classes
    padded = slots * (area + edge) + edge
    middle = chunk * 2 // 5
    halves = ((0, middle), (middle, chunk))
    parts = [(0, 0, chunk, True)]
    for low_row, high_row in halves:
        parts += [
            (peer, low_row, high_row, peer == peers - 1)
            for peer in [*range(2, peers), 1]
        ]
    rows = [
        slots * edge * (high_row - low_row) + (edge if noted else 0)
        for _, low_row, high_row, noted in parts
    ]
    pieces = pl.pallas_call(
        functools.partial(section_kernel, (slots, edge, chunk, parts)),
        out_shape=[pltpu.VMEM((count, lanes), bf16) for count in rows],
        in_specs=[hbm] * 11,
        out_specs=[vmem] * len(parts),
        scratch_shapes=[
            pltpu.VMEM((padded, data + 256), bf16),
            pltpu.VMEM((padded, edge * width + 128), bf16),
            pltpu.VMEM((2, 768, 256), bf16),
            pltpu.VMEM((768, 384), bf16),
            pltpu.VMEM((padded - 2 * edge, edge * width + 128), f32),
            pltpu.VMEM((padded - 2 * edge, edge * width), f32),
            pltpu.SMEM(corners.shape, jnp.int32),
            pltpu.SMEM(counts.shape[::-1], jnp.int32),
            pltpu.VMEM((27 * width, in_width), bf16),
            pltpu.VMEM((1, width), f32),
            pltpu.VMEM((1, width), f32),
            pltpu.VMEM((27 * width, width), bf16),
            pltpu.VMEM((1, width), f32),
            pltpu.VMEM((1, width), f32),
            pltpu.VMEM((classes, width), bf16),
            pltpu.VMEM((1, classes), f32),
            pltpu.VMEM((slots, VX * edge, area), bf16),
            pltpu.SemaphoreType.DMA((10 + slots,)),
        ],
        compiler_params=ample,
        name="section",
    )(
        corners,
        counts.T,
        features.reshape(slots, area, data),
        jnp.swapaxes(conv_first, 4, 5).reshape(27 * width, in_width),
        gain_first,
        shift_first,
        conv_second.reshape(27 * width, width),
        gain_second,
        shift_second,
        head_weight[0].T,
        head_bias,
    )
    arrived = []
    for (peer, _, _, _), piece in zip(parts, pieces):
        pairs = [(i, i ^ peer) for i in range(peers)]
        arrived.append(lax.ppermute(piece, ("folds", "sub"), pairs) if peer else piece)

    def gather(first, last, spilled, kind, name):
        chosen = [
            (part, piece)
            for part, piece in zip(parts, arrived)
            if part[1] < last and first < part[2]
        ]
        return pl.pallas_call(
            functools.partial(
                gather_kernel,
                (slots, edge, chunk, [part for part, _ in chosen], first, last, classes),
                spilled,
            ),
            out_shape=pltpu.VMEM((last - first, TZ, VY * classes), kind),
            in_specs=[vmem] * len(chosen),
            out_specs=vmem,
            compiler_params=limits,
            cost_estimate=pl.CostEstimate(
                flops=500000000, bytes_accessed=2000000, transcendentals=0
            ),
            name=name,
        )(*[piece for _, piece in chosen])

    even = [(tile, tile ^ 1) for tile in range(tiles)]
    odd = []
    for tile in range(tiles):
        for i in range(peers):
            if 0 < tile < tiles - 1:
                target = (tile + 1 if tile % 2 else tile - 1) * peers + i
            else:
                target = tile * peers + (i ^ 1)
            odd.append((tile * peers + i, target))
    from_below = []
    for first, last in halves:
        spill = gather(first, last, True, bf16, f"spill_{first}")
        if first > 0:
            cycle = [(tile, (tile + 1) % tiles) for tile in range(tiles)]
            from_below.append([lax.ppermute(spill, "tiles", cycle)])
        else:
            from_below.append(
                [
                    lax.ppermute(spill, ("tiles", "folds", "sub"), odd),
                    lax.ppermute(spill, "tiles", even),
                ]
            )
    own = gather(0, chunk, False, f32, "own")
    joined = None
    for at in (1, 0):
        low_row, high_row = halves[at]
        count = len(from_below[at])
        joined = pl.pallas_call(
            functools.partial(join_kernel, low_row, count),
            out_shape=jax.ShapeDtypeStruct((chunk, TZ, VY * classes), f32),
            in_specs=[vmem] * (1 + count) + ([] if joined is None else [hbm]),
            out_specs=hbm,
            input_output_aliases={} if joined is None else {1 + count: 0},
            scratch_shapes=[
                pltpu.VMEM((high_row - low_row, TZ, VY * classes), f32),
                pltpu.SemaphoreType.DMA((high_row - low_row,)),
            ],
            compiler_params=limits,
            name=f"join_{low_row}",
        )(own, *from_below[at], *([] if joined is None else [joined]))
    return jnp.transpose(joined, (1, 0, 2))


def solution(mesh):
    placed = (
        P("folds", ("groups", "tiles", "sub"), None, None, None),
        P("folds", None, None, None, None, None),
        P("folds", None),
        P("folds", None),
        P("folds", None, None, None, None, None),
        P("folds", None),
        P("folds", None),
        P("folds", None, None),
        P("folds", None),
        P(("groups", "tiles", "sub"), None),
        P("groups", None),
    )
    return jax.shard_map(
        on_device,
        mesh=mesh,
        in_specs=placed,
        out_specs=P(("groups", "tiles"), ("folds", "sub"), None),
        check_vma=False,
    )
```

```python
import functools

import jax
import jax.numpy as jnp
from jax import lax
from jax.experimental import pallas as pl
from jax.experimental.pallas import tpu as pltpu
from jax.sharding import PartitionSpec as P

TZ = 16
VX = 40
VY = 40

epsilon = 1e-05
leak_slope = 0.01
far = 1 << 20
bf16 = jnp.bfloat16
f32 = jnp.float32
vmem_bytes = 48 << 20


def iota(shape, dim):
    return lax.broadcasted_iota(jnp.int32, shape, dim)


def tile_matrix(width, lanes):
    return (iota((width, lanes), 1) % width == iota((width, lanes), 0)).astype(bf16)


def tiled_row(ref, lanes):
    width = ref.shape[1]
    row = jnp.concatenate([ref[...], jnp.zeros((1, lanes - width), f32)], axis=1)
    row = jnp.broadcast_to(row, (8, lanes))
    reach = width
    while reach < lanes:
        row = row + pltpu.roll(row, reach, 1)
        reach *= 2
    return row[0:1]


def lane_bands(parts, places):
    total = None
    for place, part in enumerate(parts):
        if part is not None:
            total = part if total is None else jnp.where(places == place, part, total)
    if total is None:
        return None
    if any(part is None for part in parts):
        empty = None
        for place, part in enumerate(parts):
            if part is None:
                here = places == place
                empty = here if empty is None else empty | here
        total = jnp.where(empty, 0.0, total)
    return total


def build_pairs(taps_ref, band_ref, in_width, width, swapped, dz):
    spread = tile_matrix(width, 128)
    places = iota((in_width, 128), 1) // width
    zero = jnp.zeros((in_width, 128), bf16)
    orders = (((1, 0), (2, None)), ((0, 1), (None, 2)))
    tiled = {}
    if swapped:
        for tap in range(9):
            at = (dz * 9 + tap) * width
            tiled[divmod(tap, 3)] = lax.dot_general(
                taps_ref[at : at + width],
                spread,
                (((0,), (0,)), ((), ())),
                preferred_element_type=f32,
            )
    else:
        at = dz * 9 * in_width
        wide = jnp.dot(taps_ref[at : at + 9 * in_width], spread, preferred_element_type=f32)
        for tap in range(9):
            tiled[divmod(tap, 3)] = wide[tap * in_width : (tap + 1) * in_width]
    for variant in range(2):
        for yi in range(4):
            for side in range(2):
                parts = []
                for dx in orders[variant][side]:
                    for yo in range(2):
                        parts.append(None if dx is None else tiled.get((dx, yi - yo)))
                block = lane_bands(parts, places)
                at = (dz * 4 + yi) * in_width
                band_ref[variant, at : at + in_width, side * 128 : (side + 1) * 128] = (
                    zero if block is None else block.astype(bf16)
                )


def banded(pad_ref, lane, count, edge, band):
    depth = band.shape[0] // 3
    view = [pad_ref[dz * edge : dz * edge + count, lane : lane + depth] for dz in range(3)]
    return jnp.dot(jnp.concatenate(view, axis=1), band, preferred_element_type=f32)


def join_pair(even, odd, low, across, edge):
    if odd is None:
        here = jnp.where(low, even[:, :128], 0.0)
        before = jnp.where(low, 0.0, even[:, :128])
        after = even[:, 128:]
    else:
        here = jnp.where(low, even[:, :128], odd[:, :128])
        before = jnp.where(low, odd[:, :128], even[:, :128])
        after = even[:, 128:] + odd[:, 128:]
    return join_across(pltpu.roll(before, 64, 1), here, after, across, edge)


def join_across(before, here, after, across, edge):
    rows = here.shape[0]
    before = jnp.where(across == 0, 0.0, pltpu.roll(before, 1, 0))
    after = jnp.where(across == edge - 1, 0.0, pltpu.roll(after, rows - 1, 0))
    return here + before + after


def folded(row, width):
    row = jnp.broadcast_to(row, (8, 128))
    reach = width
    while reach < 128:
        row = row + pltpu.roll(row, reach, 1)
        reach *= 2
    return row[0:1]


class Norm:
    def __init__(self, width, rows, voxels):
        self.width, self.rows, self.voxels = width, rows, voxels
        self.base = None
        self.first = self.second = 0.0

    def take(self, block, mask, held):
        kept = block if mask is None else jnp.where(mask, block, 0.0)
        if self.base is None:
            total = folded(jnp.sum(kept, axis=0, keepdims=True), self.width)
            self.base = total * (1.0 / (self.rows * held))
        moved = block - self.base
        if mask is not None:
            moved = jnp.where(mask, moved, 0.0)
        self.first = self.first + jnp.sum(moved, axis=0, keepdims=True)
        self.second = self.second + jnp.sum(moved * moved, axis=0, keepdims=True)

    def settle(self, gain, shift):
        off = folded(self.first, self.width) * (1.0 / self.voxels)
        variance = folded(self.second, self.width) * (1.0 / self.voxels) - off * off
        self.center = self.base + off
        self.factor = lax.rsqrt(jnp.maximum(variance, 0.0) + epsilon) * gain
        self.shift = shift

    def give(self, block, mask):
        scaled = (block - self.center) * self.factor + self.shift
        scaled = jnp.maximum(scaled, leak_slope * scaled)
        return scaled if mask is None else jnp.where(mask, scaled, 0.0)


def section_kernel(
    sizes,
    corners_hbm,
    counts_hbm,
    features_ref,
    taps_one_hbm,
    gain_one_hbm,
    shift_one_hbm,
    taps_two_hbm,
    gain_two_hbm,
    shift_two_hbm,
    head_hbm,
    bias_hbm,
    *rest,
):
    slots, edge, chunk, parts = sizes
    out_refs = rest[: len(parts)]
    (
        pad_one,
        pad_two,
        pad_turned,
        band_one,
        band_two,
        hidden,
        outcome,
        corners_ref,
        counts_ref,
        taps_one_ref,
        gain_one_ref,
        shift_one_ref,
        taps_two_ref,
        gain_two_ref,
        shift_two_ref,
        head_ref,
        bias_ref,
        selects,
        sems,
    ) = rest[len(parts) :]
    in_width = taps_one_ref.shape[1]
    classes, width = head_ref.shape
    area = edge * edge
    stride = area + edge
    count = hidden.shape[0]
    voxels = float(area * edge)
    data = edge * in_width
    lanes = edge * classes

    copies = []
    for at, (source, target) in enumerate(
        [
            (taps_one_hbm, taps_one_ref),
            (taps_two_hbm, taps_two_ref),
            (gain_one_hbm, gain_one_ref),
            (shift_one_hbm, shift_one_ref),
            (gain_two_hbm, gain_two_ref),
            (shift_two_hbm, shift_two_ref),
            (head_hbm, head_ref),
            (bias_hbm, bias_ref),
            (corners_hbm, corners_ref),
            (counts_hbm, counts_ref),
        ]
        + [
            (
                features_ref.at[slot],
                pad_one.at[pl.ds(edge + slot * stride, area), pl.ds(128, data)],
            )
            for slot in range(slots)
        ]
    ):
        copy = pltpu.make_async_copy(source, target, sems.at[at])
        copy.start()
        copies.append(copy)
    for pad in (pad_one, pad_two, pad_turned):
        for slot in range(slots + 1):
            pad[slot * stride : slot * stride + edge, :] = jnp.zeros((edge, pad.shape[1]), bf16)
    pad_one[:, :128] = jnp.zeros((pad_one.shape[0], 128), bf16)
    pad_one[:, 128 + data :] = jnp.zeros((pad_one.shape[0], 128), bf16)

    center, spread = (edge - 1) / 2.0, edge / 4.0

    def profile(offset):
        return jnp.exp(-((offset.astype(f32) - center) ** 2) / (2.0 * spread * spread))

    row_at = iota((area, 128), 0)
    lane_at = iota((1, lanes), 1)
    gauss = profile(row_at // edge) * profile(row_at % edge)
    gauss = jnp.concatenate([gauss] * (lanes // 128), axis=1) * profile(lane_at // classes)

    row = iota((chunk * edge, area), 0)
    source = iota((chunk * edge, area), 1)
    turn = (row % edge - source // edge) & (edge - 1)
    code = turn + edge * (source % edge - row // edge)
    across = iota((count, 128), 0) % edge
    tile_index = lax.axis_index("tiles")
    sub_index = lax.axis_index("sub")
    position = lax.axis_index("folds") * lax.axis_size("sub") + sub_index

    for copy in copies[:-slots]:
        copy.wait()
    for dz in range(3):
        build_pairs(taps_one_ref, band_one, in_width, width, True, dz)
    gain_one, shift_one = tiled_row(gain_one_ref, 128), tiled_row(shift_one_ref, 128)
    gain_two, shift_two = tiled_row(gain_two_ref, 128), tiled_row(shift_two_ref, 128)

    half = edge // 2
    head_row = lax.dot_general(
        head_ref[...],
        tile_matrix(classes, half * classes),
        (((0,), (0,)), ((), ())),
        preferred_element_type=f32,
    )
    block = (half * width, half * classes)
    head_block = jnp.where(
        iota(block, 0) // width == iota(block, 1) // classes,
        jnp.concatenate([head_row] * half, axis=0),
        0.0,
    ).astype(bf16)
    bias = tiled_row(bias_ref, lanes)

    mark = iota((edge, lanes), 0)
    notes = jnp.zeros((edge, lanes), f32)
    for slot in range(slots):
        depth = corners_ref[slot, 0] - tile_index * TZ
        notes = jnp.where(mark == 2 * slot, depth.astype(f32), notes)
        notes = jnp.where(mark == 2 * slot + 1, corners_ref[slot, 2].astype(f32), notes)
    for (_, low_row, high_row, noted), out_ref in zip(parts, out_refs):
        if noted:
            out_ref[slots * edge * (high_row - low_row) :, :] = notes.astype(bf16)

    for copy in copies[-slots:]:
        copy.wait()
    low = iota((count, 128), 1) < 64
    spot = iota((area, 128), 1)
    pairs = edge // 4 + 1
    masks = [None] * pairs
    masks[0] = spot >= width
    masks[-1] = spot < width
    norms = [Norm(width, area, voxels) for _ in range(slots)]
    for pair in range(pairs):
        even = banded(pad_one, 256 * pair, count, edge, band_one[0])
        odd = None
        if pair < pairs - 1:
            odd = banded(pad_one, 256 * pair + 128, count, edge, band_one[1])
        block = join_pair(even, odd, low, across, edge)
        hidden[:, pair * 128 : (pair + 1) * 128] = block
        for slot, norm in enumerate(norms):
            norm.take(block[slot * stride : slot * stride + area], masks[pair], 3)
        if pair < 3:
            build_pairs(taps_two_ref, band_two, width, width, False, pair)
    for norm in norms:
        norm.settle(gain_one, shift_one)

    fresh = {}
    near = spot < 64

    def refresh(pair):
        for slot, norm in enumerate(norms):
            at = slot * stride
            block = norm.give(hidden[at : at + area, pair * 128 : (pair + 1) * 128], masks[pair])
            rows_at = pl.ds(at + edge, area)
            pad_two[rows_at, pair * 128 : (pair + 1) * 128] = block.astype(bf16)
            if pair > 0:
                turned = pltpu.roll(jnp.where(near, block, fresh[slot]), 64, 1)
                pad_turned[rows_at, (pair - 1) * 128 : pair * 128] = turned.astype(bf16)
            fresh[slot] = block

    def prepare(slot):
        depth = corners_ref[slot, 0] - tile_index * TZ
        alive = slot < counts_ref[sub_index, tile_index]
        start = 0
        for peer, low_row, high_row, _ in parts:
            wanted = depth + edge * ((position ^ peer) * chunk - corners_ref[slot, 1])
            wanted = jnp.where(alive, wanted, far)
            select = (code[low_row * edge : high_row * edge] == wanted).astype(f32).astype(bf16)
            selects[slot, start : start + select.shape[0], :] = select
            start += select.shape[0]

    quads = edge // 4
    seconds = [Norm(width, area, voxels) for _ in range(slots)]
    refresh(0)
    for quad in range(quads):
        refresh(quad + 1)
        even = banded(pad_two, 128 * quad, count, edge, band_two[0])
        odd = banded(pad_turned, 128 * quad, count, edge, band_two[1])
        block = join_pair(even, odd, low, across, edge)
        outcome[:, quad * 128 : (quad + 1) * 128] = block
        for slot, norm in enumerate(seconds):
            norm.take(block[slot * stride : slot * stride + area], None, 4)
        if quad < slots:
            prepare(quad)
    for slot in range(quads, slots):
        prepare(slot)
    for norm in seconds:
        norm.settle(gain_two, shift_two)

    for slot, norm in enumerate(seconds):
        at = slot * stride
        logits = []
        for side in range(2):
            normed = [
                norm.give(outcome[at : at + area, quad * 128 : (quad + 1) * 128], None).astype(
                    bf16
                )
                for quad in range(side * quads // 2, (side + 1) * quads // 2)
            ]
            logits.append(
                jnp.dot(
                    jnp.concatenate(normed, axis=1), head_block, preferred_element_type=f32
                )
            )
        weighted = (jnp.concatenate(logits, axis=1) + bias) * gauss
        lane_start = corners_ref[slot, 2] * classes
        weighted = pltpu.roll(weighted, lane_start % lanes, 1).astype(bf16)
        placed = jnp.dot(selects[slot], weighted, preferred_element_type=f32).astype(bf16)
        start = 0
        for (_, low_row, high_row, _), out_ref in zip(parts, out_refs):
            size = (high_row - low_row) * edge
            out_ref[slot * size : (slot + 1) * size, :] = placed[start : start + size]
            start += size


def gather_kernel(sizes, spilled, *rest):
    slots, edge, chunk, parts, first, last, classes = sizes
    part_refs = rest[: len(parts)]
    out_ref = rest[len(parts)]
    lanes = edge * classes
    blocks = -(-VY * classes // lanes)

    depth_at = iota((edge, lanes), 0)
    lane_at = iota((edge, lanes), 1)
    groups = []
    for (peer, low_row, high_row, noted), part_ref in zip(parts, part_refs):
        if not noted or any(group[0] == peer % 2 for group in groups):
            continue
        notes = part_ref[slots * edge * (high_row - low_row) :, :].astype(f32).astype(jnp.int32)
        for slot in range(slots):
            depth = notes[2 * slot : 2 * slot + 1]
            start = notes[2 * slot + 1 : 2 * slot + 2] * classes
            keep = depth_at < depth if spilled else depth_at >= depth
            inside = []
            for block in range(blocks):
                lane = lane_at + block * lanes
                inside.append(keep & (lane >= start) & (lane < start + lanes))
            groups.append((peer % 2, slot, inside))

    for across in range(first, last):
        total = [jnp.zeros((edge, lanes), f32) for _ in range(blocks)]
        for parity, slot, inside in groups:
            piece = None
            for (peer, low_row, high_row, _), part_ref in zip(parts, part_refs):
                if peer % 2 == parity and low_row <= across < high_row:
                    at = (slot * (high_row - low_row) + across - low_row) * edge
                    part = part_ref[at : at + edge, :].astype(f32)
                    piece = part if piece is None else piece + part
            for block in range(blocks):
                total[block] = total[block] + jnp.where(inside[block], piece, 0.0)
        total = jnp.concatenate(total, axis=1)[:, : VY * classes]
        out_ref[across - first] = total.astype(out_ref.dtype)


def join_kernel(low_row, own_ref, odd_ref, even_ref, *rest):
    out_ref, total, sems = rest[-3:]
    tile_index = lax.axis_index("tiles")
    from_even = (tile_index % 2 == 1).astype(f32)
    from_odd = ((tile_index % 2 == 0) & (tile_index > 0)).astype(f32)
    copies = []
    for row in range(even_ref.shape[0]):
        total[row] = (
            own_ref[low_row + row]
            + even_ref[row].astype(f32) * from_even
            + odd_ref[row].astype(f32) * from_odd
        )
        copy = pltpu.make_async_copy(total.at[row], out_ref.at[low_row + row], sems.at[row])
        copy.start()
        copies.append(copy)
    for copy in copies:
        copy.wait()


vmem = pl.BlockSpec(memory_space=pltpu.VMEM)
hbm = pl.BlockSpec(memory_space=pltpu.HBM)
limits = pltpu.CompilerParams(vmem_limit_bytes=vmem_bytes)
ample = pltpu.CompilerParams(vmem_limit_bytes=60000000)


def on_device(
    features,
    conv_first,
    gain_first,
    shift_first,
    conv_second,
    gain_second,
    shift_second,
    head_weight,
    head_bias,
    corners,
    counts,
):
    _, slots, edge, _, data = features.shape
    in_width, width = conv_first.shape[-2:]
    classes = head_bias.shape[1]
    peers = lax.axis_size("folds") * lax.axis_size("sub")
    tiles = lax.axis_size("tiles")
    chunk = VX // peers
    area = edge * edge
    lanes = edge * classes
    padded = slots * (area + edge) + edge
    middle = chunk * 2 // 5
    halves = ((0, middle), (middle, chunk))
    parts = [(0, 0, chunk, True)]
    for low_row, high_row in halves:
        parts += [
            (peer, low_row, high_row, peer == peers - 1)
            for peer in [*range(2, peers), 1]
        ]
    rows = [
        slots * edge * (high_row - low_row) + (edge if noted else 0)
        for _, low_row, high_row, noted in parts
    ]
    pieces = pl.pallas_call(
        functools.partial(section_kernel, (slots, edge, chunk, parts)),
        out_shape=[pltpu.VMEM((count, lanes), bf16) for count in rows],
        in_specs=[hbm] * 11,
        out_specs=[vmem] * len(parts),
        scratch_shapes=[
            pltpu.VMEM((padded, data + 256), bf16),
            pltpu.VMEM((padded, edge * width + 128), bf16),
            pltpu.VMEM((padded, edge * width), bf16),
            pltpu.VMEM((2, 768, 256), bf16),
            pltpu.VMEM((2, 384, 256), bf16),
            pltpu.VMEM((padded - 2 * edge, edge * width + 128), f32),
            pltpu.VMEM((padded - 2 * edge, edge * width), f32),
            pltpu.SMEM(corners.shape, jnp.int32),
            pltpu.SMEM(counts.shape[::-1], jnp.int32),
            pltpu.VMEM((27 * width, in_width), bf16),
            pltpu.VMEM((1, width), f32),
            pltpu.VMEM((1, width), f32),
            pltpu.VMEM((27 * width, width), bf16),
            pltpu.VMEM((1, width), f32),
            pltpu.VMEM((1, width), f32),
            pltpu.VMEM((classes, width), bf16),
            pltpu.VMEM((1, classes), f32),
            pltpu.VMEM((slots, VX * edge, area), bf16),
            pltpu.SemaphoreType.DMA((10 + slots,)),
        ],
        compiler_params=ample,
        name="section",
    )(
        corners,
        counts.T,
        features.reshape(slots, area, data),
        jnp.swapaxes(conv_first, 4, 5).reshape(27 * width, in_width),
        gain_first,
        shift_first,
        conv_second.reshape(27 * width, width),
        gain_second,
        shift_second,
        head_weight[0].T,
        head_bias,
    )
    arrived = []
    for (peer, _, _, _), piece in zip(parts, pieces):
        pairs = [(i, i ^ peer) for i in range(peers)]
        arrived.append(lax.ppermute(piece, ("folds", "sub"), pairs) if peer else piece)

    def gather(first, last, spilled, kind, name):
        chosen = [
            (part, piece)
            for part, piece in zip(parts, arrived)
            if part[1] < last and first < part[2]
        ]
        return pl.pallas_call(
            functools.partial(
                gather_kernel,
                (slots, edge, chunk, [part for part, _ in chosen], first, last, classes),
                spilled,
            ),
            out_shape=pltpu.VMEM((last - first, TZ, VY * classes), kind),
            in_specs=[vmem] * len(chosen),
            out_specs=vmem,
            compiler_params=limits,
            cost_estimate=pl.CostEstimate(
                flops=500000000, bytes_accessed=2000000, transcendentals=0
            ),
            name=name,
        )(*[piece for _, piece in chosen])

    even = [(tile, tile ^ 1) for tile in range(tiles)]
    odd = []
    for tile in range(tiles):
        for i in range(peers):
            if 0 < tile < tiles - 1:
                target = (tile + 1 if tile % 2 else tile - 1) * peers + i
            else:
                target = tile * peers + (i ^ 1)
            odd.append((tile * peers + i, target))
    from_below = []
    for first, last in halves:
        spill = gather(first, last, True, bf16, f"spill_{first}")
        from_below.append(lax.ppermute(spill, ("tiles", "folds", "sub"), odd))
        from_below.append(lax.ppermute(spill, "tiles", even))
    own = gather(0, chunk, False, f32, "own")
    joined = None
    for at in (1, 0):
        low_row, high_row = halves[at]
        joined = pl.pallas_call(
            functools.partial(join_kernel, low_row),
            out_shape=jax.ShapeDtypeStruct((chunk, TZ, VY * classes), f32),
            in_specs=[vmem] * 3 + ([] if joined is None else [hbm]),
            out_specs=hbm,
            input_output_aliases={} if joined is None else {3: 0},
            scratch_shapes=[
                pltpu.VMEM((high_row - low_row, TZ, VY * classes), f32),
                pltpu.SemaphoreType.DMA((high_row - low_row,)),
            ],
            compiler_params=limits,
            name=f"join_{low_row}",
        )(own, *from_below[2 * at : 2 * at + 2], *([] if joined is None else [joined]))
    return jnp.transpose(joined, (1, 0, 2))


def solution(mesh):
    placed = (
        P("folds", ("groups", "tiles", "sub"), None, None, None),
        P("folds", None, None, None, None, None),
        P("folds", None),
        P("folds", None),
        P("folds", None, None, None, None, None),
        P("folds", None),
        P("folds", None),
        P("folds", None, None),
        P("folds", None),
        P(("groups", "tiles", "sub"), None),
        P("groups", None),
    )
    return jax.shard_map(
        on_device,
        mesh=mesh,
        in_specs=placed,
        out_specs=P(("groups", "tiles"), ("folds", "sub"), None),
        check_vma=False,
    )
```

```python
import functools

import jax
import jax.numpy as jnp
from jax import lax
from jax.experimental import pallas as pl
from jax.experimental.pallas import tpu as pltpu
from jax.sharding import PartitionSpec as P

TZ = 16
VX = 40
VY = 40

epsilon = 1e-05
leak_slope = 0.01
far = 1 << 20
bf16 = jnp.bfloat16
f32 = jnp.float32
vmem_bytes = 48 << 20


def iota(shape, dim):
    return lax.broadcasted_iota(jnp.int32, shape, dim)


def tile_matrix(width, lanes):
    return (iota((width, lanes), 1) % width == iota((width, lanes), 0)).astype(bf16)


def tiled_row(ref, lanes):
    width = ref.shape[1]
    row = jnp.concatenate([ref[...], jnp.zeros((1, lanes - width), f32)], axis=1)
    row = jnp.broadcast_to(row, (8, lanes))
    reach = width
    while reach < lanes:
        row = row + pltpu.roll(row, reach, 1)
        reach *= 2
    return row[0:1]


def lane_bands(parts, places):
    total = None
    for place, part in enumerate(parts):
        if part is not None:
            total = part if total is None else jnp.where(places == place, part, total)
    if total is None:
        return None
    if any(part is None for part in parts):
        empty = None
        for place, part in enumerate(parts):
            if part is None:
                here = places == place
                empty = here if empty is None else empty | here
        total = jnp.where(empty, 0.0, total)
    return total


def build_pairs(taps_ref, band_ref, in_width, width, swapped, dz):
    spread = tile_matrix(width, 128)
    places = iota((in_width, 128), 1) // width
    zero = jnp.zeros((in_width, 128), bf16)
    orders = (((1, 0), (2, None)), ((0, 1), (None, 2)))
    tiled = {}
    if swapped:
        for tap in range(9):
            at = (dz * 9 + tap) * width
            tiled[divmod(tap, 3)] = lax.dot_general(
                taps_ref[at : at + width],
                spread,
                (((0,), (0,)), ((), ())),
                preferred_element_type=f32,
            )
    else:
        at = dz * 9 * in_width
        wide = jnp.dot(taps_ref[at : at + 9 * in_width], spread, preferred_element_type=f32)
        for tap in range(9):
            tiled[divmod(tap, 3)] = wide[tap * in_width : (tap + 1) * in_width]
    for variant in range(2):
        for yi in range(4):
            for side in range(2):
                parts = []
                for dx in orders[variant][side]:
                    for yo in range(2):
                        parts.append(None if dx is None else tiled.get((dx, yi - yo)))
                block = lane_bands(parts, places)
                at = (dz * 4 + yi) * in_width
                band_ref[variant, at : at + in_width, side * 128 : (side + 1) * 128] = (
                    zero if block is None else block.astype(bf16)
                )


def banded(pad_ref, lane, count, edge, band):
    depth = band.shape[0] // 3
    view = [pad_ref[dz * edge : dz * edge + count, lane : lane + depth] for dz in range(3)]
    return jnp.dot(jnp.concatenate(view, axis=1), band, preferred_element_type=f32)


def join_pair(even, odd, low, across, edge):
    if odd is None:
        here = jnp.where(low, even[:, :128], 0.0)
        before = jnp.where(low, 0.0, even[:, :128])
        after = even[:, 128:]
    else:
        here = jnp.where(low, even[:, :128], odd[:, :128])
        before = jnp.where(low, odd[:, :128], even[:, :128])
        after = even[:, 128:] + odd[:, 128:]
    return join_across(pltpu.roll(before, 64, 1), here, after, across, edge)


def join_across(before, here, after, across, edge):
    rows = here.shape[0]
    before = jnp.where(across == 0, 0.0, pltpu.roll(before, 1, 0))
    after = jnp.where(across == edge - 1, 0.0, pltpu.roll(after, rows - 1, 0))
    return here + before + after


def folded(row, width):
    row = jnp.broadcast_to(row, (8, 128))
    reach = width
    while reach < 128:
        row = row + pltpu.roll(row, reach, 1)
        reach *= 2
    return row[0:1]


class Norm:
    def __init__(self, width, rows, voxels):
        self.width, self.rows, self.voxels = width, rows, voxels
        self.base = None
        self.first = self.second = 0.0

    def take(self, block, mask, held):
        kept = block if mask is None else jnp.where(mask, block, 0.0)
        if self.base is None:
            total = folded(jnp.sum(kept, axis=0, keepdims=True), self.width)
            self.base = total * (1.0 / (self.rows * held))
        moved = block - self.base
        if mask is not None:
            moved = jnp.where(mask, moved, 0.0)
        self.first = self.first + jnp.sum(moved, axis=0, keepdims=True)
        self.second = self.second + jnp.sum(moved * moved, axis=0, keepdims=True)

    def settle(self, gain, shift):
        off = folded(self.first, self.width) * (1.0 / self.voxels)
        variance = folded(self.second, self.width) * (1.0 / self.voxels) - off * off
        self.center = self.base + off
        self.factor = lax.rsqrt(jnp.maximum(variance, 0.0) + epsilon) * gain
        self.shift = shift

    def give(self, block, mask):
        scaled = (block - self.center) * self.factor + self.shift
        scaled = jnp.maximum(scaled, leak_slope * scaled)
        return scaled if mask is None else jnp.where(mask, scaled, 0.0)


def section_kernel(
    sizes,
    corners_hbm,
    counts_hbm,
    features_ref,
    taps_one_hbm,
    gain_one_hbm,
    shift_one_hbm,
    taps_two_hbm,
    gain_two_hbm,
    shift_two_hbm,
    head_hbm,
    bias_hbm,
    *rest,
):
    slots, edge, chunk, parts = sizes
    out_refs = rest[: len(parts)]
    (
        pad_one,
        pad_two,
        pad_turned,
        band_one,
        band_two,
        hidden,
        outcome,
        corners_ref,
        counts_ref,
        taps_one_ref,
        gain_one_ref,
        shift_one_ref,
        taps_two_ref,
        gain_two_ref,
        shift_two_ref,
        head_ref,
        bias_ref,
        selects,
        sems,
    ) = rest[len(parts) :]
    in_width = taps_one_ref.shape[1]
    classes, width = head_ref.shape
    area = edge * edge
    stride = area + edge
    count = hidden.shape[0]
    voxels = float(area * edge)
    data = edge * in_width
    lanes = edge * classes

    copies = []
    for at, (source, target) in enumerate(
        [
            (taps_one_hbm, taps_one_ref),
            (taps_two_hbm, taps_two_ref),
            (gain_one_hbm, gain_one_ref),
            (shift_one_hbm, shift_one_ref),
            (gain_two_hbm, gain_two_ref),
            (shift_two_hbm, shift_two_ref),
            (head_hbm, head_ref),
            (bias_hbm, bias_ref),
            (corners_hbm, corners_ref),
            (counts_hbm, counts_ref),
        ]
        + [
            (
                features_ref.at[slot],
                pad_one.at[pl.ds(edge + slot * stride, area), pl.ds(128, data)],
            )
            for slot in range(slots)
        ]
    ):
        copy = pltpu.make_async_copy(source, target, sems.at[at])
        copy.start()
        copies.append(copy)
    for pad in (pad_one, pad_two, pad_turned):
        for slot in range(slots + 1):
            pad[slot * stride : slot * stride + edge, :] = jnp.zeros((edge, pad.shape[1]), bf16)
    pad_one[:, :128] = jnp.zeros((pad_one.shape[0], 128), bf16)
    pad_one[:, 128 + data :] = jnp.zeros((pad_one.shape[0], 128), bf16)

    center, spread = (edge - 1) / 2.0, edge / 4.0

    def profile(offset):
        return jnp.exp(-((offset.astype(f32) - center) ** 2) / (2.0 * spread * spread))

    row_at = iota((area, 128), 0)
    lane_at = iota((1, lanes), 1)
    gauss = profile(row_at // edge) * profile(row_at % edge)
    gauss = jnp.concatenate([gauss] * (lanes // 128), axis=1) * profile(lane_at // classes)

    row = iota((chunk * edge, area), 0)
    source = iota((chunk * edge, area), 1)
    turn = (row % edge - source // edge) & (edge - 1)
    code = turn + edge * (source % edge - row // edge)
    across = iota((count, 128), 0) % edge
    tile_index = lax.axis_index("tiles")
    sub_index = lax.axis_index("sub")
    position = lax.axis_index("folds") * lax.axis_size("sub") + sub_index

    for copy in copies[:-slots]:
        copy.wait()
    for dz in range(3):
        build_pairs(taps_one_ref, band_one, in_width, width, True, dz)
    gain_one, shift_one = tiled_row(gain_one_ref, 128), tiled_row(shift_one_ref, 128)
    gain_two, shift_two = tiled_row(gain_two_ref, 128), tiled_row(shift_two_ref, 128)

    half = edge // 2
    head_row = lax.dot_general(
        head_ref[...],
        tile_matrix(classes, half * classes),
        (((0,), (0,)), ((), ())),
        preferred_element_type=f32,
    )
    block = (half * width, half * classes)
    head_block = jnp.where(
        iota(block, 0) // width == iota(block, 1) // classes,
        jnp.concatenate([head_row] * half, axis=0),
        0.0,
    ).astype(bf16)
    bias = tiled_row(bias_ref, lanes)

    mark = iota((edge, lanes), 0)
    notes = jnp.zeros((edge, lanes), f32)
    for slot in range(slots):
        depth = corners_ref[slot, 0] - tile_index * TZ
        notes = jnp.where(mark == 2 * slot, depth.astype(f32), notes)
        notes = jnp.where(mark == 2 * slot + 1, corners_ref[slot, 2].astype(f32), notes)
    for (_, low_row, high_row, noted), out_ref in zip(parts, out_refs):
        if noted:
            out_ref[slots * edge * (high_row - low_row) :, :] = notes.astype(bf16)

    for copy in copies[-slots:]:
        copy.wait()
    low = iota((count, 128), 1) < 64
    spot = iota((area, 128), 1)
    pairs = edge // 4 + 1
    masks = [None] * pairs
    masks[0] = spot >= width
    masks[-1] = spot < width
    norms = [Norm(width, area, voxels) for _ in range(slots)]
    for pair in range(pairs):
        even = banded(pad_one, 256 * pair, count, edge, band_one[0])
        odd = None
        if pair < pairs - 1:
            odd = banded(pad_one, 256 * pair + 128, count, edge, band_one[1])
        block = join_pair(even, odd, low, across, edge)
        hidden[:, pair * 128 : (pair + 1) * 128] = block
        for slot, norm in enumerate(norms):
            norm.take(block[slot * stride : slot * stride + area], masks[pair], 3)
        if pair < 3:
            build_pairs(taps_two_ref, band_two, width, width, False, pair)
    for norm in norms:
        norm.settle(gain_one, shift_one)

    fresh = {}
    near = spot < 64

    def refresh(pair):
        for slot, norm in enumerate(norms):
            at = slot * stride
            block = norm.give(hidden[at : at + area, pair * 128 : (pair + 1) * 128], masks[pair])
            rows_at = pl.ds(at + edge, area)
            pad_two[rows_at, pair * 128 : (pair + 1) * 128] = block.astype(bf16)
            if pair > 0:
                turned = pltpu.roll(jnp.where(near, block, fresh[slot]), 64, 1)
                pad_turned[rows_at, (pair - 1) * 128 : pair * 128] = turned.astype(bf16)
            fresh[slot] = block

    def prepare(slot):
        depth = corners_ref[slot, 0] - tile_index * TZ
        alive = slot < counts_ref[sub_index, tile_index]
        start = 0
        for peer, low_row, high_row, _ in parts:
            wanted = depth + edge * ((position ^ peer) * chunk - corners_ref[slot, 1])
            wanted = jnp.where(alive, wanted, far)
            select = (code[low_row * edge : high_row * edge] == wanted).astype(f32).astype(bf16)
            selects[slot, start : start + select.shape[0], :] = select
            start += select.shape[0]

    quads = edge // 4
    seconds = [Norm(width, area, voxels) for _ in range(slots)]
    refresh(0)
    for quad in range(quads):
        refresh(quad + 1)
        even = banded(pad_two, 128 * quad, count, edge, band_two[0])
        odd = banded(pad_turned, 128 * quad, count, edge, band_two[1])
        block = join_pair(even, odd, low, across, edge)
        outcome[:, quad * 128 : (quad + 1) * 128] = block
        for slot, norm in enumerate(seconds):
            norm.take(block[slot * stride : slot * stride + area], None, 4)
        if quad < slots:
            prepare(quad)
    for slot in range(quads, slots):
        prepare(slot)
    for norm in seconds:
        norm.settle(gain_two, shift_two)

    for slot, norm in enumerate(seconds):
        at = slot * stride
        logits = []
        for side in range(2):
            normed = [
                norm.give(outcome[at : at + area, quad * 128 : (quad + 1) * 128], None).astype(
                    bf16
                )
                for quad in range(side * quads // 2, (side + 1) * quads // 2)
            ]
            logits.append(
                jnp.dot(
                    jnp.concatenate(normed, axis=1), head_block, preferred_element_type=f32
                )
            )
        weighted = (jnp.concatenate(logits, axis=1) + bias) * gauss
        lane_start = corners_ref[slot, 2] * classes
        weighted = pltpu.roll(weighted, lane_start % lanes, 1).astype(bf16)
        placed = jnp.dot(selects[slot], weighted, preferred_element_type=f32).astype(bf16)
        start = 0
        for (_, low_row, high_row, _), out_ref in zip(parts, out_refs):
            size = (high_row - low_row) * edge
            out_ref[slot * size : (slot + 1) * size, :] = placed[start : start + size]
            start += size


def gather_kernel(sizes, spilled, *rest):
    slots, edge, chunk, parts, first, last, classes = sizes
    part_refs = rest[: len(parts)]
    out_ref = rest[len(parts)]
    lanes = edge * classes
    blocks = -(-VY * classes // lanes)

    depth_at = iota((edge, lanes), 0)
    lane_at = iota((edge, lanes), 1)
    groups = []
    for (peer, low_row, high_row, noted), part_ref in zip(parts, part_refs):
        if not noted or any(group[0] == peer % 2 for group in groups):
            continue
        notes = part_ref[slots * edge * (high_row - low_row) :, :].astype(f32).astype(jnp.int32)
        for slot in range(slots):
            depth = notes[2 * slot : 2 * slot + 1]
            start = notes[2 * slot + 1 : 2 * slot + 2] * classes
            keep = depth_at < depth if spilled else depth_at >= depth
            inside = []
            for block in range(blocks):
                lane = lane_at + block * lanes
                inside.append(keep & (lane >= start) & (lane < start + lanes))
            groups.append((peer % 2, slot, inside))

    for across in range(first, last):
        total = [jnp.zeros((edge, lanes), f32) for _ in range(blocks)]
        for parity, slot, inside in groups:
            piece = None
            for (peer, low_row, high_row, _), part_ref in zip(parts, part_refs):
                if peer % 2 == parity and low_row <= across < high_row:
                    at = (slot * (high_row - low_row) + across - low_row) * edge
                    part = part_ref[at : at + edge, :].astype(f32)
                    piece = part if piece is None else piece + part
            for block in range(blocks):
                total[block] = total[block] + jnp.where(inside[block], piece, 0.0)
        total = jnp.concatenate(total, axis=1)[:, : VY * classes]
        out_ref[across - first] = total.astype(out_ref.dtype)


def join_kernel(low_row, own_ref, odd_ref, even_ref, *rest):
    out_ref, total, sems = rest[-3:]
    tile_index = lax.axis_index("tiles")
    from_even = (tile_index % 2 == 1).astype(f32)
    from_odd = ((tile_index % 2 == 0) & (tile_index > 0)).astype(f32)
    copies = []
    for row in range(even_ref.shape[0]):
        total[row] = (
            own_ref[low_row + row]
            + even_ref[row].astype(f32) * from_even
            + odd_ref[row].astype(f32) * from_odd
        )
        copy = pltpu.make_async_copy(total.at[row], out_ref.at[low_row + row], sems.at[row])
        copy.start()
        copies.append(copy)
    for copy in copies:
        copy.wait()


vmem = pl.BlockSpec(memory_space=pltpu.VMEM)
hbm = pl.BlockSpec(memory_space=pltpu.HBM)
limits = pltpu.CompilerParams(vmem_limit_bytes=vmem_bytes)
ample = pltpu.CompilerParams(vmem_limit_bytes=60000000)


def on_device(
    features,
    conv_first,
    gain_first,
    shift_first,
    conv_second,
    gain_second,
    shift_second,
    head_weight,
    head_bias,
    corners,
    counts,
):
    _, slots, edge, _, data = features.shape
    in_width, width = conv_first.shape[-2:]
    classes = head_bias.shape[1]
    peers = lax.axis_size("folds") * lax.axis_size("sub")
    tiles = lax.axis_size("tiles")
    chunk = VX // peers
    area = edge * edge
    lanes = edge * classes
    padded = slots * (area + edge) + edge
    middle = chunk * 2 // 5
    halves = ((0, middle), (middle, chunk))
    parts = [(0, 0, chunk, True)]
    for low_row, high_row in halves:
        parts += [
            (peer, low_row, high_row, peer == 1 and low_row > 0)
            for peer in [*range(2, peers), 1]
        ]
    rows = [
        slots * edge * (high_row - low_row) + (edge if noted else 0)
        for _, low_row, high_row, noted in parts
    ]
    pieces = pl.pallas_call(
        functools.partial(section_kernel, (slots, edge, chunk, parts)),
        out_shape=[pltpu.VMEM((count, lanes), bf16) for count in rows],
        in_specs=[hbm] * 11,
        out_specs=[vmem] * len(parts),
        scratch_shapes=[
            pltpu.VMEM((padded, data + 256), bf16),
            pltpu.VMEM((padded, edge * width + 128), bf16),
            pltpu.VMEM((padded, edge * width), bf16),
            pltpu.VMEM((2, 768, 256), bf16),
            pltpu.VMEM((2, 384, 256), bf16),
            pltpu.VMEM((padded - 2 * edge, edge * width + 128), f32),
            pltpu.VMEM((padded - 2 * edge, edge * width), f32),
            pltpu.SMEM(corners.shape, jnp.int32),
            pltpu.SMEM(counts.shape[::-1], jnp.int32),
            pltpu.VMEM((27 * width, in_width), bf16),
            pltpu.VMEM((1, width), f32),
            pltpu.VMEM((1, width), f32),
            pltpu.VMEM((27 * width, width), bf16),
            pltpu.VMEM((1, width), f32),
            pltpu.VMEM((1, width), f32),
            pltpu.VMEM((classes, width), bf16),
            pltpu.VMEM((1, classes), f32),
            pltpu.VMEM((slots, VX * edge, area), bf16),
            pltpu.SemaphoreType.DMA((10 + slots,)),
        ],
        compiler_params=ample,
        name="section",
    )(
        corners,
        counts.T,
        features.reshape(slots, area, data),
        jnp.swapaxes(conv_first, 4, 5).reshape(27 * width, in_width),
        gain_first,
        shift_first,
        conv_second.reshape(27 * width, width),
        gain_second,
        shift_second,
        head_weight[0].T,
        head_bias,
    )
    arrived = []
    for (peer, _, _, _), piece in zip(parts, pieces):
        pairs = [(i, i ^ peer) for i in range(peers)]
        arrived.append(lax.ppermute(piece, ("folds", "sub"), pairs) if peer else piece)

    def gather(first, last, spilled, kind, name):
        chosen = [
            (part, piece)
            for part, piece in zip(parts, arrived)
            if part[3] or (part[1] < last and first < part[2])
        ]
        return pl.pallas_call(
            functools.partial(
                gather_kernel,
                (slots, edge, chunk, [part for part, _ in chosen], first, last, classes),
                spilled,
            ),
            out_shape=pltpu.VMEM((last - first, TZ, VY * classes), kind),
            in_specs=[vmem] * len(chosen),
            out_specs=vmem,
            compiler_params=limits,
            cost_estimate=pl.CostEstimate(
                flops=500000000, bytes_accessed=2000000, transcendentals=0
            ),
            name=name,
        )(*[piece for _, piece in chosen])

    even = [(tile, tile ^ 1) for tile in range(tiles)]
    odd = []
    for tile in range(tiles):
        for i in range(peers):
            if 0 < tile < tiles - 1:
                target = (tile + 1 if tile % 2 else tile - 1) * peers + i
            else:
                target = tile * peers + (i ^ 1)
            odd.append((tile * peers + i, target))
    from_below = []
    for first, last in halves:
        spill = gather(first, last, True, bf16, f"spill_{first}")
        from_below.append(lax.ppermute(spill, ("tiles", "folds", "sub"), odd))
        from_below.append(lax.ppermute(spill, "tiles", even))
    own = gather(0, chunk, False, f32, "own")
    joined = None
    for at in (1, 0):
        low_row, high_row = halves[at]
        joined = pl.pallas_call(
            functools.partial(join_kernel, low_row),
            out_shape=jax.ShapeDtypeStruct((chunk, TZ, VY * classes), f32),
            in_specs=[vmem] * 3 + ([] if joined is None else [hbm]),
            out_specs=hbm,
            input_output_aliases={} if joined is None else {3: 0},
            scratch_shapes=[
                pltpu.VMEM((high_row - low_row, TZ, VY * classes), f32),
                pltpu.SemaphoreType.DMA((high_row - low_row,)),
            ],
            compiler_params=limits,
            name=f"join_{low_row}",
        )(own, *from_below[2 * at : 2 * at + 2], *([] if joined is None else [joined]))
    return jnp.transpose(joined, (1, 0, 2))


def solution(mesh):
    placed = (
        P("folds", ("groups", "tiles", "sub"), None, None, None),
        P("folds", None, None, None, None, None),
        P("folds", None),
        P("folds", None),
        P("folds", None, None, None, None, None),
        P("folds", None),
        P("folds", None),
        P("folds", None, None),
        P("folds", None),
        P(("groups", "tiles", "sub"), None),
        P("groups", None),
    )
    return jax.shard_map(
        on_device,
        mesh=mesh,
        in_specs=placed,
        out_specs=P(("groups", "tiles"), ("folds", "sub"), None),
        check_vma=False,
    )
```

```python
import functools

import jax
import jax.numpy as jnp
from jax import lax
from jax.experimental import pallas as pl
from jax.experimental.pallas import tpu as pltpu
from jax.sharding import PartitionSpec as P

TZ = 16
VX = 40
VY = 40

epsilon = 1e-05
leak_slope = 0.01
far = 1 << 20
bf16 = jnp.bfloat16
f32 = jnp.float32
vmem_bytes = 48 << 20


def iota(shape, dim):
    return lax.broadcasted_iota(jnp.int32, shape, dim)


def tile_matrix(width, lanes):
    return (iota((width, lanes), 1) % width == iota((width, lanes), 0)).astype(bf16)


def tiled_row(ref, lanes):
    width = ref.shape[1]
    row = jnp.concatenate([ref[...], jnp.zeros((1, lanes - width), f32)], axis=1)
    row = jnp.broadcast_to(row, (8, lanes))
    reach = width
    while reach < lanes:
        row = row + pltpu.roll(row, reach, 1)
        reach *= 2
    return row[0:1]


def lane_bands(parts, places):
    total = None
    for place, part in enumerate(parts):
        if part is not None:
            total = part if total is None else jnp.where(places == place, part, total)
    if total is None:
        return None
    if any(part is None for part in parts):
        empty = None
        for place, part in enumerate(parts):
            if part is None:
                here = places == place
                empty = here if empty is None else empty | here
        total = jnp.where(empty, 0.0, total)
    return total


def build_pairs(taps_ref, band_ref, in_width, width, swapped, dz):
    spread = tile_matrix(width, 128)
    places = iota((in_width, 128), 1) // width
    zero = jnp.zeros((in_width, 128), bf16)
    orders = (((1, 0), (2, None)), ((0, 1), (None, 2)))
    tiled = {}
    if swapped:
        for tap in range(9):
            at = (dz * 9 + tap) * width
            tiled[divmod(tap, 3)] = lax.dot_general(
                taps_ref[at : at + width],
                spread,
                (((0,), (0,)), ((), ())),
                preferred_element_type=f32,
            )
    else:
        at = dz * 9 * in_width
        wide = jnp.dot(taps_ref[at : at + 9 * in_width], spread, preferred_element_type=f32)
        for tap in range(9):
            tiled[divmod(tap, 3)] = wide[tap * in_width : (tap + 1) * in_width]
    for variant in range(2):
        for yi in range(4):
            for side in range(2):
                parts = []
                for dx in orders[variant][side]:
                    for yo in range(2):
                        parts.append(None if dx is None else tiled.get((dx, yi - yo)))
                block = lane_bands(parts, places)
                at = (dz * 4 + yi) * in_width
                band_ref[variant, at : at + in_width, side * 128 : (side + 1) * 128] = (
                    zero if block is None else block.astype(bf16)
                )


def banded(pad_ref, lane, count, edge, band):
    depth = band.shape[0] // 3
    view = [pad_ref[dz * edge : dz * edge + count, lane : lane + depth] for dz in range(3)]
    return jnp.dot(jnp.concatenate(view, axis=1), band, preferred_element_type=f32)


def join_pair(even, odd, low, across, edge):
    if odd is None:
        here = jnp.where(low, even[:, :128], 0.0)
        before = jnp.where(low, 0.0, even[:, :128])
        after = even[:, 128:]
    else:
        here = jnp.where(low, even[:, :128], odd[:, :128])
        before = jnp.where(low, odd[:, :128], even[:, :128])
        after = even[:, 128:] + odd[:, 128:]
    return join_across(pltpu.roll(before, 64, 1), here, after, across, edge)


def join_across(before, here, after, across, edge):
    rows = here.shape[0]
    before = jnp.where(across == 0, 0.0, pltpu.roll(before, 1, 0))
    after = jnp.where(across == edge - 1, 0.0, pltpu.roll(after, rows - 1, 0))
    return here + before + after


def folded(row, width):
    row = jnp.broadcast_to(row, (8, 128))
    reach = width
    while reach < 128:
        row = row + pltpu.roll(row, reach, 1)
        reach *= 2
    return row[0:1]


class Norm:
    def __init__(self, width, rows, voxels):
        self.width, self.rows, self.voxels = width, rows, voxels
        self.base = None
        self.first = self.second = 0.0

    def take(self, block, mask, held):
        kept = block if mask is None else jnp.where(mask, block, 0.0)
        if self.base is None:
            total = folded(jnp.sum(kept, axis=0, keepdims=True), self.width)
            self.base = total * (1.0 / (self.rows * held))
        moved = block - self.base
        if mask is not None:
            moved = jnp.where(mask, moved, 0.0)
        self.first = self.first + jnp.sum(moved, axis=0, keepdims=True)
        self.second = self.second + jnp.sum(moved * moved, axis=0, keepdims=True)

    def settle(self, gain, shift):
        off = folded(self.first, self.width) * (1.0 / self.voxels)
        variance = folded(self.second, self.width) * (1.0 / self.voxels) - off * off
        self.center = self.base + off
        self.factor = lax.rsqrt(jnp.maximum(variance, 0.0) + epsilon) * gain
        self.shift = shift

    def give(self, block, mask):
        scaled = (block - self.center) * self.factor + self.shift
        scaled = jnp.maximum(scaled, leak_slope * scaled)
        return scaled if mask is None else jnp.where(mask, scaled, 0.0)


def section_kernel(
    sizes,
    corners_hbm,
    counts_hbm,
    features_ref,
    taps_one_hbm,
    gain_one_hbm,
    shift_one_hbm,
    taps_two_hbm,
    gain_two_hbm,
    shift_two_hbm,
    head_hbm,
    bias_hbm,
    *rest,
):
    slots, edge, chunk, parts = sizes
    out_refs = rest[: len(parts)]
    (
        pad_one,
        pad_two,
        pad_turned,
        band_one,
        band_two,
        hidden,
        outcome,
        corners_ref,
        counts_ref,
        taps_one_ref,
        gain_one_ref,
        shift_one_ref,
        taps_two_ref,
        gain_two_ref,
        shift_two_ref,
        head_ref,
        bias_ref,
        selects,
        sems,
    ) = rest[len(parts) :]
    in_width = taps_one_ref.shape[1]
    classes, width = head_ref.shape
    area = edge * edge
    stride = area + edge
    count = hidden.shape[0]
    voxels = float(area * edge)
    data = edge * in_width
    lanes = edge * classes

    copies = []
    for at, (source, target) in enumerate(
        [
            (taps_one_hbm, taps_one_ref),
            (taps_two_hbm, taps_two_ref),
            (gain_one_hbm, gain_one_ref),
            (shift_one_hbm, shift_one_ref),
            (gain_two_hbm, gain_two_ref),
            (shift_two_hbm, shift_two_ref),
            (head_hbm, head_ref),
            (bias_hbm, bias_ref),
            (corners_hbm, corners_ref),
            (counts_hbm, counts_ref),
        ]
        + [
            (
                features_ref.at[slot],
                pad_one.at[pl.ds(edge + slot * stride, area), pl.ds(128, data)],
            )
            for slot in range(slots)
        ]
    ):
        copy = pltpu.make_async_copy(source, target, sems.at[at])
        copy.start()
        copies.append(copy)
    for pad in (pad_one, pad_two, pad_turned):
        for slot in range(slots + 1):
            pad[slot * stride : slot * stride + edge, :] = jnp.zeros((edge, pad.shape[1]), bf16)
    pad_one[:, :128] = jnp.zeros((pad_one.shape[0], 128), bf16)
    pad_one[:, 128 + data :] = jnp.zeros((pad_one.shape[0], 128), bf16)

    center, spread = (edge - 1) / 2.0, edge / 4.0

    def profile(offset):
        return jnp.exp(-((offset.astype(f32) - center) ** 2) / (2.0 * spread * spread))

    row_at = iota((area, 128), 0)
    lane_at = iota((1, lanes), 1)
    gauss = profile(row_at // edge) * profile(row_at % edge)
    gauss = jnp.concatenate([gauss] * (lanes // 128), axis=1) * profile(lane_at // classes)

    row = iota((chunk * edge, area), 0)
    source = iota((chunk * edge, area), 1)
    turn = (row % edge - source // edge) & (edge - 1)
    code = turn + edge * (source % edge - row // edge)
    across = iota((count, 128), 0) % edge
    tile_index = lax.axis_index("tiles")
    sub_index = lax.axis_index("sub")
    position = lax.axis_index("folds") * lax.axis_size("sub") + sub_index

    for copy in copies[:-slots]:
        copy.wait()
    for dz in range(3):
        build_pairs(taps_one_ref, band_one, in_width, width, True, dz)
    gain_one, shift_one = tiled_row(gain_one_ref, 128), tiled_row(shift_one_ref, 128)
    gain_two, shift_two = tiled_row(gain_two_ref, 128), tiled_row(shift_two_ref, 128)

    half = edge // 2
    head_row = lax.dot_general(
        head_ref[...],
        tile_matrix(classes, half * classes),
        (((0,), (0,)), ((), ())),
        preferred_element_type=f32,
    )
    block = (half * width, half * classes)
    head_block = jnp.where(
        iota(block, 0) // width == iota(block, 1) // classes,
        jnp.concatenate([head_row] * half, axis=0),
        0.0,
    ).astype(bf16)
    bias = tiled_row(bias_ref, lanes)

    mark = iota((edge, lanes), 0)
    notes = jnp.zeros((edge, lanes), f32)
    for slot in range(slots):
        depth = corners_ref[slot, 0] - tile_index * TZ
        notes = jnp.where(mark == 2 * slot, depth.astype(f32), notes)
        notes = jnp.where(mark == 2 * slot + 1, corners_ref[slot, 2].astype(f32), notes)
    for (_, low_row, high_row, noted), out_ref in zip(parts, out_refs):
        if noted:
            out_ref[slots * edge * (high_row - low_row) :, :] = notes.astype(bf16)

    for copy in copies[-slots:]:
        copy.wait()
    low = iota((count, 128), 1) < 64
    spot = iota((area, 128), 1)
    pairs = edge // 4 + 1
    masks = [None] * pairs
    masks[0] = spot >= width
    masks[-1] = spot < width
    norms = [Norm(width, area, voxels) for _ in range(slots)]
    for pair in range(pairs):
        even = banded(pad_one, 256 * pair, count, edge, band_one[0])
        odd = None
        if pair < pairs - 1:
            odd = banded(pad_one, 256 * pair + 128, count, edge, band_one[1])
        block = join_pair(even, odd, low, across, edge)
        hidden[:, pair * 128 : (pair + 1) * 128] = block
        for slot, norm in enumerate(norms):
            norm.take(block[slot * stride : slot * stride + area], masks[pair], 3)
        if pair < 3:
            build_pairs(taps_two_ref, band_two, width, width, False, pair)
    for norm in norms:
        norm.settle(gain_one, shift_one)

    fresh = {}
    near = spot < 64

    def refresh(pair):
        for slot, norm in enumerate(norms):
            at = slot * stride
            block = norm.give(hidden[at : at + area, pair * 128 : (pair + 1) * 128], masks[pair])
            rows_at = pl.ds(at + edge, area)
            pad_two[rows_at, pair * 128 : (pair + 1) * 128] = block.astype(bf16)
            if pair > 0:
                turned = pltpu.roll(jnp.where(near, block, fresh[slot]), 64, 1)
                pad_turned[rows_at, (pair - 1) * 128 : pair * 128] = turned.astype(bf16)
            fresh[slot] = block

    def prepare(slot):
        depth = corners_ref[slot, 0] - tile_index * TZ
        alive = slot < counts_ref[sub_index, tile_index]
        start = 0
        for peer, low_row, high_row, _ in parts:
            wanted = depth + edge * ((position ^ peer) * chunk - corners_ref[slot, 1])
            wanted = jnp.where(alive, wanted, far)
            select = (code[low_row * edge : high_row * edge] == wanted).astype(f32).astype(bf16)
            selects[slot, start : start + select.shape[0], :] = select
            start += select.shape[0]

    quads = edge // 4
    seconds = [Norm(width, area, voxels) for _ in range(slots)]
    refresh(0)
    for quad in range(quads):
        refresh(quad + 1)
        even = banded(pad_two, 128 * quad, count, edge, band_two[0])
        odd = banded(pad_turned, 128 * quad, count, edge, band_two[1])
        block = join_pair(even, odd, low, across, edge)
        outcome[:, quad * 128 : (quad + 1) * 128] = block
        for slot, norm in enumerate(seconds):
            norm.take(block[slot * stride : slot * stride + area], None, 4)
        if quad < slots:
            prepare(quad)
    for slot in range(quads, slots):
        prepare(slot)
    for norm in seconds:
        norm.settle(gain_two, shift_two)

    for slot, norm in enumerate(seconds):
        at = slot * stride
        logits = []
        for side in range(2):
            normed = [
                norm.give(outcome[at : at + area, quad * 128 : (quad + 1) * 128], None).astype(
                    bf16
                )
                for quad in range(side * quads // 2, (side + 1) * quads // 2)
            ]
            logits.append(
                jnp.dot(
                    jnp.concatenate(normed, axis=1), head_block, preferred_element_type=f32
                )
            )
        weighted = (jnp.concatenate(logits, axis=1) + bias) * gauss
        lane_start = corners_ref[slot, 2] * classes
        weighted = pltpu.roll(weighted, lane_start % lanes, 1).astype(bf16)
        placed = jnp.dot(selects[slot], weighted, preferred_element_type=f32).astype(bf16)
        start = 0
        for (_, low_row, high_row, _), out_ref in zip(parts, out_refs):
            size = (high_row - low_row) * edge
            out_ref[slot * size : (slot + 1) * size, :] = placed[start : start + size]
            start += size


def gather_kernel(sizes, spilled, *rest):
    slots, edge, chunk, parts, first, last, classes = sizes
    part_refs = rest[: len(parts)]
    out_ref = rest[len(parts)]
    lanes = edge * classes
    blocks = -(-VY * classes // lanes)

    depth_at = iota((edge, lanes), 0)
    lane_at = iota((edge, lanes), 1)
    groups = []
    for (peer, low_row, high_row, noted), part_ref in zip(parts, part_refs):
        if not noted or any(group[0] == peer % 2 for group in groups):
            continue
        notes = part_ref[slots * edge * (high_row - low_row) :, :].astype(f32).astype(jnp.int32)
        for slot in range(slots):
            depth = notes[2 * slot : 2 * slot + 1]
            start = notes[2 * slot + 1 : 2 * slot + 2] * classes
            keep = depth_at < depth if spilled else depth_at >= depth
            inside = []
            for block in range(blocks):
                lane = lane_at + block * lanes
                inside.append(keep & (lane >= start) & (lane < start + lanes))
            groups.append((peer % 2, slot, inside))

    for across in range(first, last):
        total = [jnp.zeros((edge, lanes), f32) for _ in range(blocks)]
        for parity, slot, inside in groups:
            piece = None
            for (peer, low_row, high_row, _), part_ref in zip(parts, part_refs):
                if peer % 2 == parity and low_row <= across < high_row:
                    at = (slot * (high_row - low_row) + across - low_row) * edge
                    part = part_ref[at : at + edge, :].astype(f32)
                    piece = part if piece is None else piece + part
            for block in range(blocks):
                total[block] = total[block] + jnp.where(inside[block], piece, 0.0)
        total = jnp.concatenate(total, axis=1)[:, : VY * classes]
        out_ref[across - first] = total.astype(out_ref.dtype)


def join_kernel(low_row, own_ref, *rest):
    odd_ref, even_ref = rest[1::-1] if low_row > 0 else rest[:2]
    out_ref, total, sems = rest[-3:]
    tile_index = lax.axis_index("tiles")
    from_even = (tile_index % 2 == 1).astype(f32)
    from_odd = ((tile_index % 2 == 0) & (tile_index > 0)).astype(f32)
    copies = []
    for row in range(even_ref.shape[0]):
        total[row] = (
            own_ref[low_row + row]
            + even_ref[row].astype(f32) * from_even
            + odd_ref[row].astype(f32) * from_odd
        )
        copy = pltpu.make_async_copy(total.at[row], out_ref.at[low_row + row], sems.at[row])
        copy.start()
        copies.append(copy)
    for copy in copies:
        copy.wait()


vmem = pl.BlockSpec(memory_space=pltpu.VMEM)
hbm = pl.BlockSpec(memory_space=pltpu.HBM)
limits = pltpu.CompilerParams(vmem_limit_bytes=vmem_bytes)
ample = pltpu.CompilerParams(vmem_limit_bytes=60000000)


def on_device(
    features,
    conv_first,
    gain_first,
    shift_first,
    conv_second,
    gain_second,
    shift_second,
    head_weight,
    head_bias,
    corners,
    counts,
):
    _, slots, edge, _, data = features.shape
    in_width, width = conv_first.shape[-2:]
    classes = head_bias.shape[1]
    peers = lax.axis_size("folds") * lax.axis_size("sub")
    tiles = lax.axis_size("tiles")
    chunk = VX // peers
    area = edge * edge
    lanes = edge * classes
    padded = slots * (area + edge) + edge
    middle = chunk * 2 // 5
    halves = ((0, middle), (middle, chunk))
    parts = [(0, 0, chunk, True)]
    for low_row, high_row in halves:
        parts += [
            (peer, low_row, high_row, peer == 1 and low_row > 0)
            for peer in [*range(2, peers), 1]
        ]
    rows = [
        slots * edge * (high_row - low_row) + (edge if noted else 0)
        for _, low_row, high_row, noted in parts
    ]
    pieces = pl.pallas_call(
        functools.partial(section_kernel, (slots, edge, chunk, parts)),
        out_shape=[pltpu.VMEM((count, lanes), bf16) for count in rows],
        in_specs=[hbm] * 11,
        out_specs=[vmem] * len(parts),
        scratch_shapes=[
            pltpu.VMEM((padded, data + 256), bf16),
            pltpu.VMEM((padded, edge * width + 128), bf16),
            pltpu.VMEM((padded, edge * width), bf16),
            pltpu.VMEM((2, 768, 256), bf16),
            pltpu.VMEM((2, 384, 256), bf16),
            pltpu.VMEM((padded - 2 * edge, edge * width + 128), f32),
            pltpu.VMEM((padded - 2 * edge, edge * width), f32),
            pltpu.SMEM(corners.shape, jnp.int32),
            pltpu.SMEM(counts.shape[::-1], jnp.int32),
            pltpu.VMEM((27 * width, in_width), bf16),
            pltpu.VMEM((1, width), f32),
            pltpu.VMEM((1, width), f32),
            pltpu.VMEM((27 * width, width), bf16),
            pltpu.VMEM((1, width), f32),
            pltpu.VMEM((1, width), f32),
            pltpu.VMEM((classes, width), bf16),
            pltpu.VMEM((1, classes), f32),
            pltpu.VMEM((slots, VX * edge, area), bf16),
            pltpu.SemaphoreType.DMA((10 + slots,)),
        ],
        compiler_params=ample,
        name="section",
    )(
        corners,
        counts.T,
        features.reshape(slots, area, data),
        jnp.swapaxes(conv_first, 4, 5).reshape(27 * width, in_width),
        gain_first,
        shift_first,
        conv_second.reshape(27 * width, width),
        gain_second,
        shift_second,
        head_weight[0].T,
        head_bias,
    )
    arrived = []
    for (peer, _, _, _), piece in zip(parts, pieces):
        pairs = [(i, i ^ peer) for i in range(peers)]
        arrived.append(lax.ppermute(piece, ("folds", "sub"), pairs) if peer else piece)

    def gather(first, last, spilled, kind, name):
        chosen = [
            (part, piece)
            for part, piece in zip(parts, arrived)
            if part[3] or (part[1] < last and first < part[2])
        ]
        return pl.pallas_call(
            functools.partial(
                gather_kernel,
                (slots, edge, chunk, [part for part, _ in chosen], first, last, classes),
                spilled,
            ),
            out_shape=pltpu.VMEM((last - first, TZ, VY * classes), kind),
            in_specs=[vmem] * len(chosen),
            out_specs=vmem,
            compiler_params=limits,
            cost_estimate=pl.CostEstimate(
                flops=500000000, bytes_accessed=2000000, transcendentals=0
            ),
            name=name,
        )(*[piece for _, piece in chosen])

    even = [(tile, tile ^ 1) for tile in range(tiles)]
    odd = []
    for tile in range(tiles):
        for i in range(peers):
            if 0 < tile < tiles - 1:
                target = (tile + 1 if tile % 2 else tile - 1) * peers + i
            else:
                target = tile * peers + (i ^ 1)
            odd.append((tile * peers + i, target))
    from_below = []
    for first, last in halves:
        spill = gather(first, last, True, bf16, f"spill_{first}")
        swaps = [
            lax.ppermute(spill, ("tiles", "folds", "sub"), odd),
            lax.ppermute(spill, "tiles", even),
        ]
        from_below += swaps[::-1] if first > 0 else swaps
    own = gather(0, chunk, False, f32, "own")
    joined = None
    for at in (1, 0):
        low_row, high_row = halves[at]
        joined = pl.pallas_call(
            functools.partial(join_kernel, low_row),
            out_shape=jax.ShapeDtypeStruct((chunk, TZ, VY * classes), f32),
            in_specs=[vmem] * 3 + ([] if joined is None else [hbm]),
            out_specs=hbm,
            input_output_aliases={} if joined is None else {3: 0},
            scratch_shapes=[
                pltpu.VMEM((high_row - low_row, TZ, VY * classes), f32),
                pltpu.SemaphoreType.DMA((high_row - low_row,)),
            ],
            compiler_params=limits,
            name=f"join_{low_row}",
        )(own, *from_below[2 * at : 2 * at + 2], *([] if joined is None else [joined]))
    return jnp.transpose(joined, (1, 0, 2))


def solution(mesh):
    placed = (
        P("folds", ("groups", "tiles", "sub"), None, None, None),
        P("folds", None, None, None, None, None),
        P("folds", None),
        P("folds", None),
        P("folds", None, None, None, None, None),
        P("folds", None),
        P("folds", None),
        P("folds", None, None),
        P("folds", None),
        P(("groups", "tiles", "sub"), None),
        P("groups", None),
    )
    return jax.shard_map(
        on_device,
        mesh=mesh,
        in_specs=placed,
        out_specs=P(("groups", "tiles"), ("folds", "sub"), None),
        check_vma=False,
    )
```

```python
import functools

import jax
import jax.numpy as jnp
from jax import lax
from jax.experimental import pallas as pl
from jax.experimental.pallas import tpu as pltpu
from jax.sharding import PartitionSpec as P

TZ = 16
VX = 40
VY = 40

epsilon = 1e-05
leak_slope = 0.01
far = 1 << 20
bf16 = jnp.bfloat16
f32 = jnp.float32
vmem_bytes = 48 << 20


def iota(shape, dim):
    return lax.broadcasted_iota(jnp.int32, shape, dim)


def tile_matrix(width, lanes):
    return (iota((width, lanes), 1) % width == iota((width, lanes), 0)).astype(bf16)


def tiled_row(ref, lanes):
    width = ref.shape[1]
    row = jnp.concatenate([ref[...], jnp.zeros((1, lanes - width), f32)], axis=1)
    row = jnp.broadcast_to(row, (8, lanes))
    reach = width
    while reach < lanes:
        row = row + pltpu.roll(row, reach, 1)
        reach *= 2
    return row[0:1]


def lane_bands(parts, places):
    total = None
    for place, part in enumerate(parts):
        if part is not None:
            total = part if total is None else jnp.where(places == place, part, total)
    if total is None:
        return None
    if any(part is None for part in parts):
        empty = None
        for place, part in enumerate(parts):
            if part is None:
                here = places == place
                empty = here if empty is None else empty | here
        total = jnp.where(empty, 0.0, total)
    return total


OUTER = ({2: 0, 3: 1}, {0: 1, 1: 2})


def build_pairs(taps_ref, band_ref, in_width, width, swapped, dz):
    spread = tile_matrix(width, 128)
    places = iota((in_width, 128), 1) // width
    zero = jnp.zeros((in_width, 128), bf16)
    orders = (((1, 0), (2, None)), ((0, 1), (None, 2)))
    tiled = {}
    if swapped:
        for tap in range(9):
            at = (dz * 9 + tap) * width
            tiled[divmod(tap, 3)] = lax.dot_general(
                taps_ref[at : at + width],
                spread,
                (((0,), (0,)), ((), ())),
                preferred_element_type=f32,
            )
    else:
        at = dz * 9 * in_width
        wide = jnp.dot(taps_ref[at : at + 9 * in_width], spread, preferred_element_type=f32)
        for tap in range(9):
            tiled[divmod(tap, 3)] = wide[tap * in_width : (tap + 1) * in_width]
    for variant in range(band_ref.shape[0]):
        for yi in range(4):
            for side in range(2):
                parts = []
                for dx in orders[variant % 2][side]:
                    for yo in range(2):
                        dy = OUTER[yo].get(yi) if variant == 2 else yi - yo
                        parts.append(None if dx is None else tiled.get((dx, dy)))
                block = lane_bands(parts, places)
                at = (dz * 4 + yi) * in_width
                band_ref[variant, at : at + in_width, side * 128 : (side + 1) * 128] = (
                    zero if block is None else block.astype(bf16)
                )


def banded(pad_ref, starts, count, edge, band):
    depth = band.shape[0] // (3 * len(starts))
    view = [
        pad_ref[dz * edge : dz * edge + count, lane : lane + depth]
        for dz in range(3)
        for lane in starts
    ]
    return jnp.dot(jnp.concatenate(view, axis=1), band, preferred_element_type=f32)


def join_pair(even, odd, low, across, edge):
    if odd is None:
        here = jnp.where(low, even[:, :128], 0.0)
        before = jnp.where(low, 0.0, even[:, :128])
        after = even[:, 128:]
    else:
        here = jnp.where(low, even[:, :128], odd[:, :128])
        before = jnp.where(low, odd[:, :128], even[:, :128])
        after = even[:, 128:] + odd[:, 128:]
    return join_across(pltpu.roll(before, 64, 1), here, after, across, edge)


def join_across(before, here, after, across, edge):
    rows = here.shape[0]
    before = jnp.where(across == 0, 0.0, pltpu.roll(before, 1, 0))
    after = jnp.where(across == edge - 1, 0.0, pltpu.roll(after, rows - 1, 0))
    return here + before + after


def folded(row, width):
    row = jnp.broadcast_to(row, (8, 128))
    reach = width
    while reach < 128:
        row = row + pltpu.roll(row, reach, 1)
        reach *= 2
    return row[0:1]


class Norm:
    def __init__(self, width, rows, voxels):
        self.width, self.rows, self.voxels = width, rows, voxels
        self.base = None
        self.first = self.second = 0.0

    def take(self, block, mask, held):
        kept = block if mask is None else jnp.where(mask, block, 0.0)
        if self.base is None:
            total = folded(jnp.sum(kept, axis=0, keepdims=True), self.width)
            self.base = total * (1.0 / (self.rows * held))
        moved = block - self.base
        if mask is not None:
            moved = jnp.where(mask, moved, 0.0)
        self.first = self.first + jnp.sum(moved, axis=0, keepdims=True)
        self.second = self.second + jnp.sum(moved * moved, axis=0, keepdims=True)

    def settle(self, gain, shift):
        off = folded(self.first, self.width) * (1.0 / self.voxels)
        variance = folded(self.second, self.width) * (1.0 / self.voxels) - off * off
        self.center = self.base + off
        self.factor = lax.rsqrt(jnp.maximum(variance, 0.0) + epsilon) * gain
        self.shift = shift

    def give(self, block, mask):
        scaled = (block - self.center) * self.factor + self.shift
        scaled = jnp.maximum(scaled, leak_slope * scaled)
        return scaled if mask is None else jnp.where(mask, scaled, 0.0)


def section_kernel(
    sizes,
    corners_hbm,
    counts_hbm,
    features_ref,
    taps_one_hbm,
    gain_one_hbm,
    shift_one_hbm,
    taps_two_hbm,
    gain_two_hbm,
    shift_two_hbm,
    head_hbm,
    bias_hbm,
    *rest,
):
    slots, edge, chunk, parts = sizes
    out_refs = rest[: len(parts)]
    (
        pad_one,
        pad_two,
        pad_turned,
        band_one,
        band_two,
        hidden,
        outcome,
        corners_ref,
        counts_ref,
        taps_one_ref,
        gain_one_ref,
        shift_one_ref,
        taps_two_ref,
        gain_two_ref,
        shift_two_ref,
        head_ref,
        bias_ref,
        selects,
        sems,
    ) = rest[len(parts) :]
    in_width = taps_one_ref.shape[1]
    classes, width = head_ref.shape
    area = edge * edge
    stride = area + edge
    count = hidden.shape[0]
    voxels = float(area * edge)
    data = edge * in_width
    lanes = edge * classes

    copies = []
    for at, (source, target) in enumerate(
        [
            (taps_one_hbm, taps_one_ref),
            (taps_two_hbm, taps_two_ref),
            (gain_one_hbm, gain_one_ref),
            (shift_one_hbm, shift_one_ref),
            (gain_two_hbm, gain_two_ref),
            (shift_two_hbm, shift_two_ref),
            (head_hbm, head_ref),
            (bias_hbm, bias_ref),
            (corners_hbm, corners_ref),
            (counts_hbm, counts_ref),
        ]
        + [
            (
                features_ref.at[slot],
                pad_one.at[pl.ds(edge + slot * stride, area), pl.ds(128, data)],
            )
            for slot in range(slots)
        ]
    ):
        copy = pltpu.make_async_copy(source, target, sems.at[at])
        copy.start()
        copies.append(copy)
    for pad in (pad_one, pad_two, pad_turned):
        for slot in range(slots + 1):
            pad[slot * stride : slot * stride + edge, :] = jnp.zeros((edge, pad.shape[1]), bf16)
    center, spread = (edge - 1) / 2.0, edge / 4.0

    def profile(offset):
        return jnp.exp(-((offset.astype(f32) - center) ** 2) / (2.0 * spread * spread))

    row_at = iota((area, 128), 0)
    lane_at = iota((1, lanes), 1)
    gauss = profile(row_at // edge) * profile(row_at % edge)
    gauss = jnp.concatenate([gauss] * (lanes // 128), axis=1) * profile(lane_at // classes)

    row = iota((chunk * edge, area), 0)
    source = iota((chunk * edge, area), 1)
    turn = (row % edge - source // edge) & (edge - 1)
    code = turn + edge * (source % edge - row // edge)
    across = iota((count, 128), 0) % edge
    tile_index = lax.axis_index("tiles")
    sub_index = lax.axis_index("sub")
    position = lax.axis_index("folds") * lax.axis_size("sub") + sub_index

    for copy in copies[:-slots]:
        copy.wait()
    for dz in range(3):
        build_pairs(taps_one_ref, band_one, in_width, width, True, dz)
    gain_one, shift_one = tiled_row(gain_one_ref, 128), tiled_row(shift_one_ref, 128)
    gain_two, shift_two = tiled_row(gain_two_ref, 128), tiled_row(shift_two_ref, 128)

    half = edge // 2
    head_row = lax.dot_general(
        head_ref[...],
        tile_matrix(classes, half * classes),
        (((0,), (0,)), ((), ())),
        preferred_element_type=f32,
    )
    block = (half * width, half * classes)
    head_block = jnp.where(
        iota(block, 0) // width == iota(block, 1) // classes,
        jnp.concatenate([head_row] * half, axis=0),
        0.0,
    ).astype(bf16)
    bias = tiled_row(bias_ref, lanes)

    mark = iota((edge, lanes), 0)
    notes = jnp.zeros((edge, lanes), f32)
    for slot in range(slots):
        depth = corners_ref[slot, 0] - tile_index * TZ
        notes = jnp.where(mark == 2 * slot, depth.astype(f32), notes)
        notes = jnp.where(mark == 2 * slot + 1, corners_ref[slot, 2].astype(f32), notes)
    for (_, low_row, high_row, noted), out_ref in zip(parts, out_refs):
        if noted:
            out_ref[slots * edge * (high_row - low_row) :, :] = notes.astype(bf16)

    for copy in copies[-slots:]:
        copy.wait()
    low = iota((count, 128), 1) < 64
    spot = iota((area, 128), 1)
    pairs = edge // 4 + 1
    masks = [None] * pairs
    masks[0] = spot >= width
    masks[-1] = spot < width
    norms = [Norm(width, area, voxels) for _ in range(slots)]
    outer = banded(pad_one, [128, data], count, edge, band_one[2])
    for pair in range(pairs):
        if 0 < pair < pairs - 1:
            even = banded(pad_one, [256 * pair], count, edge, band_one[0])
        else:
            even = outer
        odd = None
        if pair < pairs - 1:
            odd = banded(pad_one, [256 * pair + 128], count, edge, band_one[1])
        block = join_pair(even, odd, low, across, edge)
        hidden[:, pair * 128 : (pair + 1) * 128] = block
        for slot, norm in enumerate(norms):
            norm.take(block[slot * stride : slot * stride + area], masks[pair], 3)
        if pair < 3:
            build_pairs(taps_two_ref, band_two, width, width, False, pair)
    for norm in norms:
        norm.settle(gain_one, shift_one)

    fresh = {}
    near = spot < 64

    def refresh(pair):
        for slot, norm in enumerate(norms):
            at = slot * stride
            block = norm.give(hidden[at : at + area, pair * 128 : (pair + 1) * 128], masks[pair])
            rows_at = pl.ds(at + edge, area)
            pad_two[rows_at, pair * 128 : (pair + 1) * 128] = block.astype(bf16)
            if pair > 0:
                turned = pltpu.roll(jnp.where(near, block, fresh[slot]), 64, 1)
                pad_turned[rows_at, (pair - 1) * 128 : pair * 128] = turned.astype(bf16)
            fresh[slot] = block

    def prepare(slot):
        depth = corners_ref[slot, 0] - tile_index * TZ
        alive = slot < counts_ref[sub_index, tile_index]
        start = 0
        for peer, low_row, high_row, _ in parts:
            wanted = depth + edge * ((position ^ peer) * chunk - corners_ref[slot, 1])
            wanted = jnp.where(alive, wanted, far)
            select = (code[low_row * edge : high_row * edge] == wanted).astype(f32).astype(bf16)
            selects[slot, start : start + select.shape[0], :] = select
            start += select.shape[0]

    quads = edge // 4
    seconds = [Norm(width, area, voxels) for _ in range(slots)]
    refresh(0)
    for quad in range(quads):
        refresh(quad + 1)
        even = banded(pad_two, [128 * quad], count, edge, band_two[0])
        odd = banded(pad_turned, [128 * quad], count, edge, band_two[1])
        block = join_pair(even, odd, low, across, edge)
        outcome[:, quad * 128 : (quad + 1) * 128] = block
        for slot, norm in enumerate(seconds):
            norm.take(block[slot * stride : slot * stride + area], None, 4)
        if quad < slots:
            prepare(quad)
    for slot in range(quads, slots):
        prepare(slot)
    for norm in seconds:
        norm.settle(gain_two, shift_two)

    for slot, norm in enumerate(seconds):
        at = slot * stride
        logits = []
        for side in range(2):
            normed = [
                norm.give(outcome[at : at + area, quad * 128 : (quad + 1) * 128], None).astype(
                    bf16
                )
                for quad in range(side * quads // 2, (side + 1) * quads // 2)
            ]
            logits.append(
                jnp.dot(
                    jnp.concatenate(normed, axis=1), head_block, preferred_element_type=f32
                )
            )
        weighted = (jnp.concatenate(logits, axis=1) + bias) * gauss
        lane_start = corners_ref[slot, 2] * classes
        weighted = pltpu.roll(weighted, lane_start % lanes, 1).astype(bf16)
        placed = jnp.dot(selects[slot], weighted, preferred_element_type=f32).astype(bf16)
        start = 0
        for (_, low_row, high_row, _), out_ref in zip(parts, out_refs):
            size = (high_row - low_row) * edge
            out_ref[slot * size : (slot + 1) * size, :] = placed[start : start + size]
            start += size


def gather_kernel(sizes, spilled, *rest):
    slots, edge, chunk, parts, first, last, classes = sizes
    part_refs = rest[: len(parts)]
    out_ref = rest[len(parts)]
    lanes = edge * classes
    blocks = -(-VY * classes // lanes)

    depth_at = iota((edge, lanes), 0)
    lane_at = iota((edge, lanes), 1)
    groups = []
    for (peer, low_row, high_row, noted), part_ref in zip(parts, part_refs):
        if not noted or any(group[0] == peer % 2 for group in groups):
            continue
        notes = part_ref[slots * edge * (high_row - low_row) :, :].astype(f32).astype(jnp.int32)
        for slot in range(slots):
            depth = notes[2 * slot : 2 * slot + 1]
            start = notes[2 * slot + 1 : 2 * slot + 2] * classes
            keep = depth_at < depth if spilled else depth_at >= depth
            inside = []
            for block in range(blocks):
                lane = lane_at + block * lanes
                inside.append(keep & (lane >= start) & (lane < start + lanes))
            groups.append((peer % 2, slot, inside))

    for across in range(first, last):
        total = [jnp.zeros((edge, lanes), f32) for _ in range(blocks)]
        for parity, slot, inside in groups:
            piece = None
            for (peer, low_row, high_row, _), part_ref in zip(parts, part_refs):
                if peer % 2 == parity and low_row <= across < high_row:
                    at = (slot * (high_row - low_row) + across - low_row) * edge
                    part = part_ref[at : at + edge, :].astype(f32)
                    piece = part if piece is None else piece + part
            for block in range(blocks):
                total[block] = total[block] + jnp.where(inside[block], piece, 0.0)
        total = jnp.concatenate(total, axis=1)[:, : VY * classes]
        out_ref[across - first] = total.astype(out_ref.dtype)


def join_kernel(low_row, own_ref, odd_ref, even_ref, *rest):
    out_ref, total, sems = rest[-3:]
    tile_index = lax.axis_index("tiles")
    from_even = (tile_index % 2 == 1).astype(f32)
    from_odd = ((tile_index % 2 == 0) & (tile_index > 0)).astype(f32)
    copies = []
    for row in range(even_ref.shape[0]):
        total[row] = (
            own_ref[low_row + row]
            + even_ref[row].astype(f32) * from_even
            + odd_ref[row].astype(f32) * from_odd
        )
        copy = pltpu.make_async_copy(total.at[row], out_ref.at[low_row + row], sems.at[row])
        copy.start()
        copies.append(copy)
    for copy in copies:
        copy.wait()


vmem = pl.BlockSpec(memory_space=pltpu.VMEM)
hbm = pl.BlockSpec(memory_space=pltpu.HBM)
limits = pltpu.CompilerParams(vmem_limit_bytes=vmem_bytes)
ample = pltpu.CompilerParams(vmem_limit_bytes=60000000)


def on_device(
    features,
    conv_first,
    gain_first,
    shift_first,
    conv_second,
    gain_second,
    shift_second,
    head_weight,
    head_bias,
    corners,
    counts,
):
    _, slots, edge, _, data = features.shape
    in_width, width = conv_first.shape[-2:]
    classes = head_bias.shape[1]
    peers = lax.axis_size("folds") * lax.axis_size("sub")
    tiles = lax.axis_size("tiles")
    chunk = VX // peers
    area = edge * edge
    lanes = edge * classes
    padded = slots * (area + edge) + edge
    middle = chunk * 2 // 5
    halves = ((0, middle), (middle, chunk))
    parts = [(0, 0, chunk, True)]
    for low_row, high_row in halves:
        parts += [
            (peer, low_row, high_row, peer == 1 and low_row > 0)
            for peer in [*range(2, peers), 1]
        ]
    rows = [
        slots * edge * (high_row - low_row) + (edge if noted else 0)
        for _, low_row, high_row, noted in parts
    ]
    pieces = pl.pallas_call(
        functools.partial(section_kernel, (slots, edge, chunk, parts)),
        out_shape=[pltpu.VMEM((count, lanes), bf16) for count in rows],
        in_specs=[hbm] * 11,
        out_specs=[vmem] * len(parts),
        scratch_shapes=[
            pltpu.VMEM((padded, data + 256), bf16),
            pltpu.VMEM((padded, edge * width + 128), bf16),
            pltpu.VMEM((padded, edge * width), bf16),
            pltpu.VMEM((3, 768, 256), bf16),
            pltpu.VMEM((2, 384, 256), bf16),
            pltpu.VMEM((padded - 2 * edge, edge * width + 128), f32),
            pltpu.VMEM((padded - 2 * edge, edge * width), f32),
            pltpu.SMEM(corners.shape, jnp.int32),
            pltpu.SMEM(counts.shape[::-1], jnp.int32),
            pltpu.VMEM((27 * width, in_width), bf16),
            pltpu.VMEM((1, width), f32),
            pltpu.VMEM((1, width), f32),
            pltpu.VMEM((27 * width, width), bf16),
            pltpu.VMEM((1, width), f32),
            pltpu.VMEM((1, width), f32),
            pltpu.VMEM((classes, width), bf16),
            pltpu.VMEM((1, classes), f32),
            pltpu.VMEM((slots, VX * edge, area), bf16),
            pltpu.SemaphoreType.DMA((10 + slots,)),
        ],
        compiler_params=ample,
        name="section",
    )(
        corners,
        counts.T,
        features.reshape(slots, area, data),
        jnp.swapaxes(conv_first, 4, 5).reshape(27 * width, in_width),
        gain_first,
        shift_first,
        conv_second.reshape(27 * width, width),
        gain_second,
        shift_second,
        head_weight[0].T,
        head_bias,
    )
    arrived = []
    for (peer, _, _, _), piece in zip(parts, pieces):
        pairs = [(i, i ^ peer) for i in range(peers)]
        arrived.append(lax.ppermute(piece, ("folds", "sub"), pairs) if peer else piece)

    def gather(first, last, spilled, kind, name):
        chosen = [
            (part, piece)
            for part, piece in zip(parts, arrived)
            if part[3] or (part[1] < last and first < part[2])
        ]
        return pl.pallas_call(
            functools.partial(
                gather_kernel,
                (slots, edge, chunk, [part for part, _ in chosen], first, last, classes),
                spilled,
            ),
            out_shape=pltpu.VMEM((last - first, TZ, VY * classes), kind),
            in_specs=[vmem] * len(chosen),
            out_specs=vmem,
            compiler_params=limits,
            cost_estimate=pl.CostEstimate(
                flops=500000000, bytes_accessed=2000000, transcendentals=0
            ),
            name=name,
        )(*[piece for _, piece in chosen])

    even = [(tile, tile ^ 1) for tile in range(tiles)]
    odd = []
    for tile in range(tiles):
        for i in range(peers):
            if 0 < tile < tiles - 1:
                target = (tile + 1 if tile % 2 else tile - 1) * peers + i
            else:
                target = tile * peers + (i ^ 1)
            odd.append((tile * peers + i, target))
    from_below = []
    for first, last in halves:
        spill = gather(first, last, True, bf16, f"spill_{first}")
        from_below.append(lax.ppermute(spill, ("tiles", "folds", "sub"), odd))
        from_below.append(lax.ppermute(spill, "tiles", even))
    own = gather(0, chunk, False, f32, "own")
    joined = None
    for at in (1, 0):
        low_row, high_row = halves[at]
        joined = pl.pallas_call(
            functools.partial(join_kernel, low_row),
            out_shape=jax.ShapeDtypeStruct((chunk, TZ, VY * classes), f32),
            in_specs=[vmem] * 3 + ([] if joined is None else [hbm]),
            out_specs=hbm,
            input_output_aliases={} if joined is None else {3: 0},
            scratch_shapes=[
                pltpu.VMEM((high_row - low_row, TZ, VY * classes), f32),
                pltpu.SemaphoreType.DMA((high_row - low_row,)),
            ],
            compiler_params=limits,
            name=f"join_{low_row}",
        )(own, *from_below[2 * at : 2 * at + 2], *([] if joined is None else [joined]))
    return jnp.transpose(joined, (1, 0, 2))


def solution(mesh):
    placed = (
        P("folds", ("groups", "tiles", "sub"), None, None, None),
        P("folds", None, None, None, None, None),
        P("folds", None),
        P("folds", None),
        P("folds", None, None, None, None, None),
        P("folds", None),
        P("folds", None),
        P("folds", None, None),
        P("folds", None),
        P(("groups", "tiles", "sub"), None),
        P("groups", None),
    )
    return jax.shard_map(
        on_device,
        mesh=mesh,
        in_specs=placed,
        out_specs=P(("groups", "tiles"), ("folds", "sub"), None),
        check_vma=False,
    )
```

```python
import functools

import jax
import jax.numpy as jnp
from jax import lax
from jax.experimental import pallas as pl
from jax.experimental.pallas import tpu as pltpu
from jax.sharding import PartitionSpec as P

TZ = 16
VX = 40
VY = 40

epsilon = 1e-05
leak_slope = 0.01
far = 1 << 20
bf16 = jnp.bfloat16
f32 = jnp.float32
vmem_bytes = 48 << 20


def iota(shape, dim):
    return lax.broadcasted_iota(jnp.int32, shape, dim)


def tile_matrix(width, lanes):
    return (iota((width, lanes), 1) % width == iota((width, lanes), 0)).astype(bf16)


def tiled_row(ref, lanes):
    width = ref.shape[1]
    row = jnp.concatenate([ref[...], jnp.zeros((1, lanes - width), f32)], axis=1)
    row = jnp.broadcast_to(row, (8, lanes))
    reach = width
    while reach < lanes:
        row = row + pltpu.roll(row, reach, 1)
        reach *= 2
    return row[0:1]


def lane_bands(parts, places):
    total = None
    for place, part in enumerate(parts):
        if part is not None:
            total = part if total is None else jnp.where(places == place, part, total)
    if total is None:
        return None
    if any(part is None for part in parts):
        empty = None
        for place, part in enumerate(parts):
            if part is None:
                here = places == place
                empty = here if empty is None else empty | here
        total = jnp.where(empty, 0.0, total)
    return total


OUTER = ({2: 0, 3: 1}, {0: 1, 1: 2})


def build_pairs(taps_ref, band_ref, in_width, width, swapped, dz):
    spread = tile_matrix(width, 128)
    places = iota((in_width, 128), 1) // width
    zero = jnp.zeros((in_width, 128), bf16)
    orders = (((1, 0), (2, None)), ((0, 1), (None, 2)))
    tiled = {}
    if swapped:
        for tap in range(9):
            at = (dz * 9 + tap) * width
            tiled[divmod(tap, 3)] = lax.dot_general(
                taps_ref[at : at + width],
                spread,
                (((0,), (0,)), ((), ())),
                preferred_element_type=f32,
            )
    else:
        at = dz * 9 * in_width
        wide = jnp.dot(taps_ref[at : at + 9 * in_width], spread, preferred_element_type=f32)
        for tap in range(9):
            tiled[divmod(tap, 3)] = wide[tap * in_width : (tap + 1) * in_width]
    for variant in range(band_ref.shape[0]):
        for yi in range(4):
            for side in range(2):
                parts = []
                for dx in orders[variant % 2][side]:
                    for yo in range(2):
                        dy = OUTER[yo].get(yi) if variant == 2 else yi - yo
                        parts.append(None if dx is None else tiled.get((dx, dy)))
                block = lane_bands(parts, places)
                at = (dz * 4 + yi) * in_width
                band_ref[variant, at : at + in_width, side * 128 : (side + 1) * 128] = (
                    zero if block is None else block.astype(bf16)
                )


def banded(pad_ref, starts, count, edge, band):
    depth = band.shape[0] // (3 * len(starts))
    view = [
        pad_ref[dz * edge : dz * edge + count, lane : lane + depth]
        for dz in range(3)
        for lane in starts
    ]
    return jnp.dot(jnp.concatenate(view, axis=1), band, preferred_element_type=f32)


def join_pair(even, odd, low, across, edge):
    if odd is None:
        here = jnp.where(low, even[:, :128], 0.0)
        before = jnp.where(low, 0.0, even[:, :128])
        after = even[:, 128:]
    else:
        here = jnp.where(low, even[:, :128], odd[:, :128])
        before = jnp.where(low, odd[:, :128], even[:, :128])
        after = even[:, 128:] + odd[:, 128:]
    return join_across(pltpu.roll(before, 64, 1), here, after, across, edge)


def join_across(before, here, after, across, edge):
    rows = here.shape[0]
    before = jnp.where(across == 0, 0.0, pltpu.roll(before, 1, 0))
    after = jnp.where(across == edge - 1, 0.0, pltpu.roll(after, rows - 1, 0))
    return here + before + after


def folded(row, width):
    row = jnp.broadcast_to(row, (8, 128))
    reach = width
    while reach < 128:
        row = row + pltpu.roll(row, reach, 1)
        reach *= 2
    return row[0:1]


class Norm:
    def __init__(self, width, rows, voxels):
        self.width, self.rows, self.voxels = width, rows, voxels
        self.base = None
        self.first = self.second = 0.0

    def take(self, block, mask, held):
        kept = block if mask is None else jnp.where(mask, block, 0.0)
        if self.base is None:
            total = folded(jnp.sum(kept, axis=0, keepdims=True), self.width)
            self.base = total * (1.0 / (self.rows * held))
        moved = block - self.base
        if mask is not None:
            moved = jnp.where(mask, moved, 0.0)
        self.first = self.first + jnp.sum(moved, axis=0, keepdims=True)
        self.second = self.second + jnp.sum(moved * moved, axis=0, keepdims=True)

    def settle(self, gain, shift):
        off = folded(self.first, self.width) * (1.0 / self.voxels)
        variance = folded(self.second, self.width) * (1.0 / self.voxels) - off * off
        self.center = self.base + off
        self.factor = lax.rsqrt(jnp.maximum(variance, 0.0) + epsilon) * gain
        self.shift = shift

    def give(self, block, mask):
        scaled = (block - self.center) * self.factor + self.shift
        scaled = jnp.maximum(scaled, leak_slope * scaled)
        return scaled if mask is None else jnp.where(mask, scaled, 0.0)


def section_kernel(
    sizes,
    corners_hbm,
    counts_hbm,
    features_ref,
    taps_one_hbm,
    gain_one_hbm,
    shift_one_hbm,
    taps_two_hbm,
    gain_two_hbm,
    shift_two_hbm,
    head_hbm,
    bias_hbm,
    *rest,
):
    slots, edge, chunk, parts = sizes
    out_refs = rest[: len(parts)]
    (
        pad_one,
        pad_two,
        pad_turned,
        band_one,
        band_two,
        hidden,
        outcome,
        corners_ref,
        counts_ref,
        taps_one_ref,
        gain_one_ref,
        shift_one_ref,
        taps_two_ref,
        gain_two_ref,
        shift_two_ref,
        head_ref,
        bias_ref,
        selects,
        sems,
    ) = rest[len(parts) :]
    in_width = taps_one_ref.shape[1]
    classes, width = head_ref.shape
    area = edge * edge
    stride = area + edge
    count = hidden.shape[0]
    voxels = float(area * edge)
    data = edge * in_width
    lanes = edge * classes

    copies = []
    for at, (source, target) in enumerate(
        [(taps_one_hbm, taps_one_ref)]
        + [
            (
                features_ref.at[slot],
                pad_one.at[pl.ds(edge + slot * stride, area), pl.ds(128, data)],
            )
            for slot in range(slots)
        ]
        + [
            (taps_two_hbm, taps_two_ref),
            (corners_hbm, corners_ref),
            (counts_hbm, counts_ref),
            (gain_one_hbm, gain_one_ref),
            (shift_one_hbm, shift_one_ref),
            (gain_two_hbm, gain_two_ref),
            (shift_two_hbm, shift_two_ref),
            (head_hbm, head_ref),
            (bias_hbm, bias_ref),
        ]
    ):
        copy = pltpu.make_async_copy(source, target, sems.at[at])
        copy.start()
        copies.append(copy)
    for pad in (pad_one, pad_two, pad_turned):
        for slot in range(slots + 1):
            pad[slot * stride : slot * stride + edge, :] = jnp.zeros((edge, pad.shape[1]), bf16)
    center, spread = (edge - 1) / 2.0, edge / 4.0

    def profile(offset):
        return jnp.exp(-((offset.astype(f32) - center) ** 2) / (2.0 * spread * spread))

    row_at = iota((area, 128), 0)
    lane_at = iota((1, lanes), 1)
    gauss = profile(row_at // edge) * profile(row_at % edge)
    gauss = jnp.concatenate([gauss] * (lanes // 128), axis=1) * profile(lane_at // classes)

    row = iota((chunk * edge, area), 0)
    source = iota((chunk * edge, area), 1)
    turn = (row % edge - source // edge) & (edge - 1)
    code = turn + edge * (source % edge - row // edge)
    across = iota((count, 128), 0) % edge
    tile_index = lax.axis_index("tiles")
    sub_index = lax.axis_index("sub")
    position = lax.axis_index("folds") * lax.axis_size("sub") + sub_index

    copies[0].wait()
    for dz in range(3):
        build_pairs(taps_one_ref, band_one, in_width, width, True, dz)
    for copy in copies[1 : 1 + slots]:
        copy.wait()
    low = iota((count, 128), 1) < 64
    spot = iota((area, 128), 1)
    pairs = edge // 4 + 1
    masks = [None] * pairs
    masks[0] = spot >= width
    masks[-1] = spot < width
    norms = [Norm(width, area, voxels) for _ in range(slots)]
    outer = banded(pad_one, [128, data], count, edge, band_one[2])
    for copy in copies[1 + slots :]:
        copy.wait()
    gain_one, shift_one = tiled_row(gain_one_ref, 128), tiled_row(shift_one_ref, 128)
    gain_two, shift_two = tiled_row(gain_two_ref, 128), tiled_row(shift_two_ref, 128)

    half = edge // 2
    head_row = lax.dot_general(
        head_ref[...],
        tile_matrix(classes, half * classes),
        (((0,), (0,)), ((), ())),
        preferred_element_type=f32,
    )
    block = (half * width, half * classes)
    head_block = jnp.where(
        iota(block, 0) // width == iota(block, 1) // classes,
        jnp.concatenate([head_row] * half, axis=0),
        0.0,
    ).astype(bf16)
    bias = tiled_row(bias_ref, lanes)

    mark = iota((edge, lanes), 0)
    notes = jnp.zeros((edge, lanes), f32)
    for slot in range(slots):
        depth = corners_ref[slot, 0] - tile_index * TZ
        notes = jnp.where(mark == 2 * slot, depth.astype(f32), notes)
        notes = jnp.where(mark == 2 * slot + 1, corners_ref[slot, 2].astype(f32), notes)
    for (_, low_row, high_row, noted), out_ref in zip(parts, out_refs):
        if noted:
            out_ref[slots * edge * (high_row - low_row) :, :] = notes.astype(bf16)

    for pair in range(pairs):
        if 0 < pair < pairs - 1:
            even = banded(pad_one, [256 * pair], count, edge, band_one[0])
        else:
            even = outer
        odd = None
        if pair < pairs - 1:
            odd = banded(pad_one, [256 * pair + 128], count, edge, band_one[1])
        block = join_pair(even, odd, low, across, edge)
        hidden[:, pair * 128 : (pair + 1) * 128] = block
        for slot, norm in enumerate(norms):
            norm.take(block[slot * stride : slot * stride + area], masks[pair], 3)
        if pair < 3:
            build_pairs(taps_two_ref, band_two, width, width, False, pair)
    for norm in norms:
        norm.settle(gain_one, shift_one)

    fresh = {}
    near = spot < 64

    def refresh(pair):
        for slot, norm in enumerate(norms):
            at = slot * stride
            block = norm.give(hidden[at : at + area, pair * 128 : (pair + 1) * 128], masks[pair])
            rows_at = pl.ds(at + edge, area)
            pad_two[rows_at, pair * 128 : (pair + 1) * 128] = block.astype(bf16)
            if pair > 0:
                turned = pltpu.roll(jnp.where(near, block, fresh[slot]), 64, 1)
                pad_turned[rows_at, (pair - 1) * 128 : pair * 128] = turned.astype(bf16)
            fresh[slot] = block

    def prepare(slot):
        depth = corners_ref[slot, 0] - tile_index * TZ
        alive = slot < counts_ref[sub_index, tile_index]
        start = 0
        for peer, low_row, high_row, _ in parts:
            wanted = depth + edge * ((position ^ peer) * chunk - corners_ref[slot, 1])
            wanted = jnp.where(alive, wanted, far)
            select = (code[low_row * edge : high_row * edge] == wanted).astype(f32).astype(bf16)
            selects[slot, start : start + select.shape[0], :] = select
            start += select.shape[0]

    quads = edge // 4
    seconds = [Norm(width, area, voxels) for _ in range(slots)]
    refresh(0)
    for quad in range(quads):
        refresh(quad + 1)
        even = banded(pad_two, [128 * quad], count, edge, band_two[0])
        odd = banded(pad_turned, [128 * quad], count, edge, band_two[1])
        block = join_pair(even, odd, low, across, edge)
        outcome[:, quad * 128 : (quad + 1) * 128] = block
        for slot, norm in enumerate(seconds):
            norm.take(block[slot * stride : slot * stride + area], None, 4)
        if quad < slots:
            prepare(quad)
    for slot in range(quads, slots):
        prepare(slot)
    for norm in seconds:
        norm.settle(gain_two, shift_two)

    for slot, norm in enumerate(seconds):
        at = slot * stride
        logits = []
        for side in range(2):
            normed = [
                norm.give(outcome[at : at + area, quad * 128 : (quad + 1) * 128], None).astype(
                    bf16
                )
                for quad in range(side * quads // 2, (side + 1) * quads // 2)
            ]
            logits.append(
                jnp.dot(
                    jnp.concatenate(normed, axis=1), head_block, preferred_element_type=f32
                )
            )
        weighted = (jnp.concatenate(logits, axis=1) + bias) * gauss
        lane_start = corners_ref[slot, 2] * classes
        weighted = pltpu.roll(weighted, lane_start % lanes, 1).astype(bf16)
        placed = jnp.dot(selects[slot], weighted, preferred_element_type=f32).astype(bf16)
        start = 0
        for (_, low_row, high_row, _), out_ref in zip(parts, out_refs):
            size = (high_row - low_row) * edge
            out_ref[slot * size : (slot + 1) * size, :] = placed[start : start + size]
            start += size


def gather_kernel(sizes, spilled, *rest):
    slots, edge, chunk, parts, first, last, classes = sizes
    part_refs = rest[: len(parts)]
    out_ref = rest[len(parts)]
    lanes = edge * classes
    blocks = -(-VY * classes // lanes)

    depth_at = iota((edge, lanes), 0)
    lane_at = iota((edge, lanes), 1)
    groups = []
    for (peer, low_row, high_row, noted), part_ref in zip(parts, part_refs):
        if not noted or any(group[0] == peer % 2 for group in groups):
            continue
        notes = part_ref[slots * edge * (high_row - low_row) :, :].astype(f32).astype(jnp.int32)
        for slot in range(slots):
            depth = notes[2 * slot : 2 * slot + 1]
            start = notes[2 * slot + 1 : 2 * slot + 2] * classes
            keep = depth_at < depth if spilled else depth_at >= depth
            inside = []
            for block in range(blocks):
                lane = lane_at + block * lanes
                inside.append(keep & (lane >= start) & (lane < start + lanes))
            groups.append((peer % 2, slot, inside))

    for across in range(first, last):
        total = [jnp.zeros((edge, lanes), f32) for _ in range(blocks)]
        for parity, slot, inside in groups:
            piece = None
            for (peer, low_row, high_row, _), part_ref in zip(parts, part_refs):
                if peer % 2 == parity and low_row <= across < high_row:
                    at = (slot * (high_row - low_row) + across - low_row) * edge
                    part = part_ref[at : at + edge, :].astype(f32)
                    piece = part if piece is None else piece + part
            for block in range(blocks):
                total[block] = total[block] + jnp.where(inside[block], piece, 0.0)
        total = jnp.concatenate(total, axis=1)[:, : VY * classes]
        out_ref[across - first] = total.astype(out_ref.dtype)


def join_kernel(low_row, own_ref, odd_ref, even_ref, *rest):
    out_ref, total, sems = rest[-3:]
    tile_index = lax.axis_index("tiles")
    from_even = (tile_index % 2 == 1).astype(f32)
    from_odd = ((tile_index % 2 == 0) & (tile_index > 0)).astype(f32)
    copies = []
    for row in range(even_ref.shape[0]):
        total[row] = (
            own_ref[low_row + row]
            + even_ref[row].astype(f32) * from_even
            + odd_ref[row].astype(f32) * from_odd
        )
        copy = pltpu.make_async_copy(total.at[row], out_ref.at[low_row + row], sems.at[row])
        copy.start()
        copies.append(copy)
    for copy in copies:
        copy.wait()


vmem = pl.BlockSpec(memory_space=pltpu.VMEM)
hbm = pl.BlockSpec(memory_space=pltpu.HBM)
limits = pltpu.CompilerParams(vmem_limit_bytes=vmem_bytes)
ample = pltpu.CompilerParams(vmem_limit_bytes=60000000)


def on_device(
    features,
    conv_first,
    gain_first,
    shift_first,
    conv_second,
    gain_second,
    shift_second,
    head_weight,
    head_bias,
    corners,
    counts,
):
    _, slots, edge, _, data = features.shape
    in_width, width = conv_first.shape[-2:]
    classes = head_bias.shape[1]
    peers = lax.axis_size("folds") * lax.axis_size("sub")
    tiles = lax.axis_size("tiles")
    chunk = VX // peers
    area = edge * edge
    lanes = edge * classes
    padded = slots * (area + edge) + edge
    middle = chunk * 2 // 5
    halves = ((0, middle), (middle, chunk))
    parts = [(0, 0, chunk, True)]
    for low_row, high_row in halves:
        parts += [
            (peer, low_row, high_row, peer == 1 and low_row > 0)
            for peer in [*range(2, peers), 1]
        ]
    rows = [
        slots * edge * (high_row - low_row) + (edge if noted else 0)
        for _, low_row, high_row, noted in parts
    ]
    pieces = pl.pallas_call(
        functools.partial(section_kernel, (slots, edge, chunk, parts)),
        out_shape=[pltpu.VMEM((count, lanes), bf16) for count in rows],
        in_specs=[hbm] * 11,
        out_specs=[vmem] * len(parts),
        scratch_shapes=[
            pltpu.VMEM((padded, data + 256), bf16),
            pltpu.VMEM((padded, edge * width + 128), bf16),
            pltpu.VMEM((padded, edge * width), bf16),
            pltpu.VMEM((3, 768, 256), bf16),
            pltpu.VMEM((2, 384, 256), bf16),
            pltpu.VMEM((padded - 2 * edge, edge * width + 128), f32),
            pltpu.VMEM((padded - 2 * edge, edge * width), f32),
            pltpu.SMEM(corners.shape, jnp.int32),
            pltpu.SMEM(counts.shape[::-1], jnp.int32),
            pltpu.VMEM((27 * width, in_width), bf16),
            pltpu.VMEM((1, width), f32),
            pltpu.VMEM((1, width), f32),
            pltpu.VMEM((27 * width, width), bf16),
            pltpu.VMEM((1, width), f32),
            pltpu.VMEM((1, width), f32),
            pltpu.VMEM((classes, width), bf16),
            pltpu.VMEM((1, classes), f32),
            pltpu.VMEM((slots, VX * edge, area), bf16),
            pltpu.SemaphoreType.DMA((10 + slots,)),
        ],
        compiler_params=ample,
        name="section",
    )(
        corners,
        counts.T,
        features.reshape(slots, area, data),
        jnp.swapaxes(conv_first, 4, 5).reshape(27 * width, in_width),
        gain_first,
        shift_first,
        conv_second.reshape(27 * width, width),
        gain_second,
        shift_second,
        head_weight[0].T,
        head_bias,
    )
    arrived = []
    for (peer, _, _, _), piece in zip(parts, pieces):
        pairs = [(i, i ^ peer) for i in range(peers)]
        arrived.append(lax.ppermute(piece, ("folds", "sub"), pairs) if peer else piece)

    def gather(first, last, spilled, kind, name):
        chosen = [
            (part, piece)
            for part, piece in zip(parts, arrived)
            if part[3] or (part[1] < last and first < part[2])
        ]
        return pl.pallas_call(
            functools.partial(
                gather_kernel,
                (slots, edge, chunk, [part for part, _ in chosen], first, last, classes),
                spilled,
            ),
            out_shape=pltpu.VMEM((last - first, TZ, VY * classes), kind),
            in_specs=[vmem] * len(chosen),
            out_specs=vmem,
            compiler_params=limits,
            cost_estimate=pl.CostEstimate(
                flops=500000000, bytes_accessed=2000000, transcendentals=0
            ),
            name=name,
        )(*[piece for _, piece in chosen])

    even = [(tile, tile ^ 1) for tile in range(tiles)]
    odd = []
    for tile in range(tiles):
        for i in range(peers):
            if 0 < tile < tiles - 1:
                target = (tile + 1 if tile % 2 else tile - 1) * peers + i
            else:
                target = tile * peers + (i ^ 1)
            odd.append((tile * peers + i, target))
    from_below = []
    for first, last in halves:
        spill = gather(first, last, True, bf16, f"spill_{first}")
        from_below.append(lax.ppermute(spill, ("tiles", "folds", "sub"), odd))
        from_below.append(lax.ppermute(spill, "tiles", even))
    own = gather(0, chunk, False, f32, "own")
    joined = None
    for at in (1, 0):
        low_row, high_row = halves[at]
        joined = pl.pallas_call(
            functools.partial(join_kernel, low_row),
            out_shape=jax.ShapeDtypeStruct((chunk, TZ, VY * classes), f32),
            in_specs=[vmem] * 3 + ([] if joined is None else [hbm]),
            out_specs=hbm,
            input_output_aliases={} if joined is None else {3: 0},
            scratch_shapes=[
                pltpu.VMEM((high_row - low_row, TZ, VY * classes), f32),
                pltpu.SemaphoreType.DMA((high_row - low_row,)),
            ],
            compiler_params=limits,
            name=f"join_{low_row}",
        )(own, *from_below[2 * at : 2 * at + 2], *([] if joined is None else [joined]))
    return jnp.transpose(joined, (1, 0, 2))


def solution(mesh):
    placed = (
        P("folds", ("groups", "tiles", "sub"), None, None, None),
        P("folds", None, None, None, None, None),
        P("folds", None),
        P("folds", None),
        P("folds", None, None, None, None, None),
        P("folds", None),
        P("folds", None),
        P("folds", None, None),
        P("folds", None),
        P(("groups", "tiles", "sub"), None),
        P("groups", None),
    )
    return jax.shard_map(
        on_device,
        mesh=mesh,
        in_specs=placed,
        out_specs=P(("groups", "tiles"), ("folds", "sub"), None),
        check_vma=False,
    )
```

```python
import functools

import jax
import jax.numpy as jnp
from jax import lax
from jax.experimental import pallas as pl
from jax.experimental.pallas import tpu as pltpu
from jax.sharding import PartitionSpec as P

TZ = 16
VX = 40
VY = 40

epsilon = 1e-05
leak_slope = 0.01
far = 1 << 20
bf16 = jnp.bfloat16
f32 = jnp.float32
vmem_bytes = 48 << 20


def iota(shape, dim):
    return lax.broadcasted_iota(jnp.int32, shape, dim)


def tile_matrix(width, lanes):
    return (iota((width, lanes), 1) % width == iota((width, lanes), 0)).astype(bf16)


def tiled_row(ref, lanes):
    width = ref.shape[1]
    row = jnp.concatenate([ref[...], jnp.zeros((1, lanes - width), f32)], axis=1)
    row = jnp.broadcast_to(row, (8, lanes))
    reach = width
    while reach < lanes:
        row = row + pltpu.roll(row, reach, 1)
        reach *= 2
    return row[0:1]


def lane_bands(parts, places):
    total = None
    for place, part in enumerate(parts):
        if part is not None:
            total = part if total is None else jnp.where(places == place, part, total)
    if total is None:
        return None
    if any(part is None for part in parts):
        empty = None
        for place, part in enumerate(parts):
            if part is None:
                here = places == place
                empty = here if empty is None else empty | here
        total = jnp.where(empty, 0.0, total)
    return total


OUTER = ({2: 0, 3: 1}, {0: 1, 1: 2})


def build_pairs(taps_ref, band_ref, in_width, width, swapped, dz):
    spread = tile_matrix(width, 128)
    places = iota((in_width, 128), 1) // width
    zero = jnp.zeros((in_width, 128), bf16)
    orders = (((1, 0), (2, None)), ((0, 1), (None, 2)))
    tiled = {}
    if swapped:
        for tap in range(9):
            at = (dz * 9 + tap) * width
            tiled[divmod(tap, 3)] = lax.dot_general(
                taps_ref[at : at + width],
                spread,
                (((0,), (0,)), ((), ())),
                preferred_element_type=f32,
            )
    else:
        at = dz * 9 * in_width
        wide = jnp.dot(taps_ref[at : at + 9 * in_width], spread, preferred_element_type=f32)
        for tap in range(9):
            tiled[divmod(tap, 3)] = wide[tap * in_width : (tap + 1) * in_width]
    for variant in range(band_ref.shape[0]):
        for yi in range(4):
            for side in range(2):
                parts = []
                for dx in orders[variant % 2][side]:
                    for yo in range(2):
                        dy = OUTER[yo].get(yi) if variant == 2 else yi - yo
                        parts.append(None if dx is None else tiled.get((dx, dy)))
                block = lane_bands(parts, places)
                at = (dz * 4 + yi) * in_width
                band_ref[variant, at : at + in_width, side * 128 : (side + 1) * 128] = (
                    zero if block is None else block.astype(bf16)
                )


def banded(pad_ref, starts, count, edge, band):
    depth = band.shape[0] // (3 * len(starts))
    view = [
        pad_ref[dz * edge : dz * edge + count, lane : lane + depth]
        for dz in range(3)
        for lane in starts
    ]
    return jnp.dot(jnp.concatenate(view, axis=1), band, preferred_element_type=f32)


def join_pair(even, odd, low, across, edge):
    if odd is None:
        here = jnp.where(low, even[:, :128], 0.0)
        before = jnp.where(low, 0.0, even[:, :128])
        after = even[:, 128:]
    else:
        here = jnp.where(low, even[:, :128], odd[:, :128])
        before = jnp.where(low, odd[:, :128], even[:, :128])
        after = even[:, 128:] + odd[:, 128:]
    return join_across(pltpu.roll(before, 64, 1), here, after, across, edge)


def join_across(before, here, after, across, edge):
    rows = here.shape[0]
    before = jnp.where(across == 0, 0.0, pltpu.roll(before, 1, 0))
    after = jnp.where(across == edge - 1, 0.0, pltpu.roll(after, rows - 1, 0))
    return here + before + after


def folded(row, width):
    row = jnp.broadcast_to(row, (8, 128))
    reach = width
    while reach < 128:
        row = row + pltpu.roll(row, reach, 1)
        reach *= 2
    return row[0:1]


class Norm:
    def __init__(self, width, rows, voxels):
        self.width, self.rows, self.voxels = width, rows, voxels
        self.base = None
        self.first = self.second = 0.0

    def take(self, block, mask, held):
        kept = block if mask is None else jnp.where(mask, block, 0.0)
        if self.base is None:
            total = folded(jnp.sum(kept, axis=0, keepdims=True), self.width)
            self.base = total * (1.0 / (self.rows * held))
        moved = block - self.base
        if mask is not None:
            moved = jnp.where(mask, moved, 0.0)
        self.first = self.first + jnp.sum(moved, axis=0, keepdims=True)
        self.second = self.second + jnp.sum(moved * moved, axis=0, keepdims=True)

    def settle(self, gain, shift):
        off = folded(self.first, self.width) * (1.0 / self.voxels)
        variance = folded(self.second, self.width) * (1.0 / self.voxels) - off * off
        self.center = self.base + off
        self.factor = lax.rsqrt(jnp.maximum(variance, 0.0) + epsilon) * gain
        self.shift = shift

    def give(self, block, mask):
        scaled = (block - self.center) * self.factor + self.shift
        scaled = jnp.maximum(scaled, leak_slope * scaled)
        return scaled if mask is None else jnp.where(mask, scaled, 0.0)


def section_kernel(
    sizes,
    corners_hbm,
    counts_hbm,
    features_ref,
    taps_one_hbm,
    gain_one_hbm,
    shift_one_hbm,
    taps_two_hbm,
    gain_two_hbm,
    shift_two_hbm,
    head_hbm,
    bias_hbm,
    *rest,
):
    slots, edge, chunk, parts = sizes
    out_refs = rest[: len(parts)]
    (
        pad_one,
        pad_two,
        pad_turned,
        band_one,
        band_two,
        hidden,
        outcome,
        corners_ref,
        counts_ref,
        taps_one_ref,
        gain_one_ref,
        shift_one_ref,
        taps_two_ref,
        gain_two_ref,
        shift_two_ref,
        head_ref,
        bias_ref,
        selects,
        sems,
    ) = rest[len(parts) :]
    in_width = taps_one_ref.shape[1]
    classes, width = head_ref.shape
    area = edge * edge
    stride = area + edge
    count = hidden.shape[0]
    voxels = float(area * edge)
    data = edge * in_width
    lanes = edge * classes

    copies = []
    for at, (source, target) in enumerate(
        [
            (taps_one_hbm, taps_one_ref),
            (taps_two_hbm, taps_two_ref),
            (gain_one_hbm, gain_one_ref),
            (shift_one_hbm, shift_one_ref),
            (gain_two_hbm, gain_two_ref),
            (shift_two_hbm, shift_two_ref),
            (head_hbm, head_ref),
            (bias_hbm, bias_ref),
            (corners_hbm, corners_ref),
            (counts_hbm, counts_ref),
        ]
        + [
            (
                features_ref.at[slot],
                pad_one.at[pl.ds(edge + slot * stride, area), pl.ds(128, data)],
            )
            for slot in range(slots)
        ]
    ):
        copy = pltpu.make_async_copy(source, target, sems.at[at])
        copy.start()
        copies.append(copy)
    for pad in (pad_one, pad_two, pad_turned):
        for slot in range(slots + 1):
            pad[slot * stride : slot * stride + edge, :] = jnp.zeros((edge, pad.shape[1]), bf16)
    center, spread = (edge - 1) / 2.0, edge / 4.0

    def profile(offset):
        return jnp.exp(-((offset.astype(f32) - center) ** 2) / (2.0 * spread * spread))

    row_at = iota((area, 128), 0)
    lane_at = iota((1, lanes), 1)
    gauss = profile(row_at // edge) * profile(row_at % edge)
    gauss = jnp.concatenate([gauss] * (lanes // 128), axis=1) * profile(lane_at // classes)

    row = iota((chunk * edge, area), 0)
    source = iota((chunk * edge, area), 1)
    turn = (row % edge - source // edge) & (edge - 1)
    code = turn + edge * (source % edge - row // edge)
    across = iota((count, 128), 0) % edge
    tile_index = lax.axis_index("tiles")
    sub_index = lax.axis_index("sub")
    position = lax.axis_index("folds") * lax.axis_size("sub") + sub_index

    copies[0].wait()
    for dz in range(3):
        build_pairs(taps_one_ref, band_one, in_width, width, True, dz)
    for copy in copies[1:-slots]:
        copy.wait()
    gain_one, shift_one = tiled_row(gain_one_ref, 128), tiled_row(shift_one_ref, 128)
    gain_two, shift_two = tiled_row(gain_two_ref, 128), tiled_row(shift_two_ref, 128)

    half = edge // 2
    head_row = lax.dot_general(
        head_ref[...],
        tile_matrix(classes, half * classes),
        (((0,), (0,)), ((), ())),
        preferred_element_type=f32,
    )
    block = (half * width, half * classes)
    head_block = jnp.where(
        iota(block, 0) // width == iota(block, 1) // classes,
        jnp.concatenate([head_row] * half, axis=0),
        0.0,
    ).astype(bf16)
    bias = tiled_row(bias_ref, lanes)

    mark = iota((edge, lanes), 0)
    notes = jnp.zeros((edge, lanes), f32)
    for slot in range(slots):
        depth = corners_ref[slot, 0] - tile_index * TZ
        notes = jnp.where(mark == 2 * slot, depth.astype(f32), notes)
        notes = jnp.where(mark == 2 * slot + 1, corners_ref[slot, 2].astype(f32), notes)
    for (_, low_row, high_row, noted), out_ref in zip(parts, out_refs):
        if noted:
            out_ref[slots * edge * (high_row - low_row) :, :] = notes.astype(bf16)

    for copy in copies[-slots:]:
        copy.wait()
    low = iota((count, 128), 1) < 64
    spot = iota((area, 128), 1)
    pairs = edge // 4 + 1
    masks = [None] * pairs
    masks[0] = spot >= width
    masks[-1] = spot < width
    norms = [Norm(width, area, voxels) for _ in range(slots)]
    outer = banded(pad_one, [128, data], count, edge, band_one[2])
    for pair in range(pairs):
        if 0 < pair < pairs - 1:
            even = banded(pad_one, [256 * pair], count, edge, band_one[0])
        else:
            even = outer
        odd = None
        if pair < pairs - 1:
            odd = banded(pad_one, [256 * pair + 128], count, edge, band_one[1])
        block = join_pair(even, odd, low, across, edge)
        hidden[:, pair * 128 : (pair + 1) * 128] = block
        for slot, norm in enumerate(norms):
            norm.take(block[slot * stride : slot * stride + area], masks[pair], 3)
        if pair < 3:
            build_pairs(taps_two_ref, band_two, width, width, False, pair)
    for norm in norms:
        norm.settle(gain_one, shift_one)

    fresh = {}
    near = spot < 64

    def refresh(pair):
        for slot, norm in enumerate(norms):
            at = slot * stride
            block = norm.give(hidden[at : at + area, pair * 128 : (pair + 1) * 128], masks[pair])
            rows_at = pl.ds(at + edge, area)
            pad_two[rows_at, pair * 128 : (pair + 1) * 128] = block.astype(bf16)
            if pair > 0:
                turned = pltpu.roll(jnp.where(near, block, fresh[slot]), 64, 1)
                pad_turned[rows_at, (pair - 1) * 128 : pair * 128] = turned.astype(bf16)
            fresh[slot] = block

    def prepare(slot):
        depth = corners_ref[slot, 0] - tile_index * TZ
        alive = slot < counts_ref[sub_index, tile_index]
        start = 0
        for peer, low_row, high_row, _ in parts:
            wanted = depth + edge * ((position ^ peer) * chunk - corners_ref[slot, 1])
            wanted = jnp.where(alive, wanted, far)
            select = (code[low_row * edge : high_row * edge] == wanted).astype(f32).astype(bf16)
            selects[slot, start : start + select.shape[0], :] = select
            start += select.shape[0]

    quads = edge // 4
    seconds = [Norm(width, area, voxels) for _ in range(slots)]
    refresh(0)
    for quad in range(quads):
        refresh(quad + 1)
        even = banded(pad_two, [128 * quad], count, edge, band_two[0])
        odd = banded(pad_turned, [128 * quad], count, edge, band_two[1])
        block = join_pair(even, odd, low, across, edge)
        outcome[:, quad * 128 : (quad + 1) * 128] = block
        for slot, norm in enumerate(seconds):
            norm.take(block[slot * stride : slot * stride + area], None, 4)
        if quad < slots:
            prepare(quad)
    for slot in range(quads, slots):
        prepare(slot)
    for norm in seconds:
        norm.settle(gain_two, shift_two)

    normed = []
    for slot, norm in enumerate(seconds):
        at = slot * stride
        for side in range(2):
            blocks = [
                norm.give(outcome[at : at + area, quad * 128 : (quad + 1) * 128], None).astype(
                    bf16
                )
                for quad in range(side * quads // 2, (side + 1) * quads // 2)
            ]
            normed.append(jnp.concatenate(blocks, axis=1))
    logits = [jnp.dot(block, head_block, preferred_element_type=f32) for block in normed]
    weighted = []
    for slot in range(slots):
        value = jnp.concatenate(logits[2 * slot : 2 * slot + 2], axis=1)
        value = (value + bias) * gauss
        lane_start = corners_ref[slot, 2] * classes
        weighted.append(pltpu.roll(value, lane_start % lanes, 1).astype(bf16))
    placed = [
        jnp.dot(selects[slot], weighted[slot], preferred_element_type=f32).astype(bf16)
        for slot in range(slots)
    ]
    for slot in range(slots):
        start = 0
        for (_, low_row, high_row, _), out_ref in zip(parts, out_refs):
            size = (high_row - low_row) * edge
            out_ref[slot * size : (slot + 1) * size, :] = placed[slot][start : start + size]
            start += size


def gather_kernel(sizes, spilled, *rest):
    slots, edge, chunk, parts, first, last, classes = sizes
    part_refs = rest[: len(parts)]
    out_ref = rest[len(parts)]
    lanes = edge * classes
    blocks = -(-VY * classes // lanes)

    depth_at = iota((edge, lanes), 0)
    lane_at = iota((edge, lanes), 1)
    groups = []
    for (peer, low_row, high_row, noted), part_ref in zip(parts, part_refs):
        if not noted or any(group[0] == peer % 2 for group in groups):
            continue
        notes = part_ref[slots * edge * (high_row - low_row) :, :].astype(f32).astype(jnp.int32)
        for slot in range(slots):
            depth = notes[2 * slot : 2 * slot + 1]
            start = notes[2 * slot + 1 : 2 * slot + 2] * classes
            keep = depth_at < depth if spilled else depth_at >= depth
            inside = []
            for block in range(blocks):
                lane = lane_at + block * lanes
                inside.append(keep & (lane >= start) & (lane < start + lanes))
            groups.append((peer % 2, slot, inside))

    for across in range(first, last):
        total = [jnp.zeros((edge, lanes), f32) for _ in range(blocks)]
        for parity, slot, inside in groups:
            piece = None
            for (peer, low_row, high_row, _), part_ref in zip(parts, part_refs):
                if peer % 2 == parity and low_row <= across < high_row:
                    at = (slot * (high_row - low_row) + across - low_row) * edge
                    part = part_ref[at : at + edge, :].astype(f32)
                    piece = part if piece is None else piece + part
            for block in range(blocks):
                total[block] = total[block] + jnp.where(inside[block], piece, 0.0)
        total = jnp.concatenate(total, axis=1)[:, : VY * classes]
        out_ref[across - first] = total.astype(out_ref.dtype)


def join_kernel(low_row, own_ref, odd_ref, even_ref, *rest):
    out_ref, total, sems = rest[-3:]
    tile_index = lax.axis_index("tiles")
    from_even = (tile_index % 2 == 1).astype(f32)
    from_odd = ((tile_index % 2 == 0) & (tile_index > 0)).astype(f32)
    copies = []
    for row in range(even_ref.shape[0]):
        total[row] = (
            own_ref[low_row + row]
            + even_ref[row].astype(f32) * from_even
            + odd_ref[row].astype(f32) * from_odd
        )
        copy = pltpu.make_async_copy(total.at[row], out_ref.at[low_row + row], sems.at[row])
        copy.start()
        copies.append(copy)
    for copy in copies:
        copy.wait()


vmem = pl.BlockSpec(memory_space=pltpu.VMEM)
hbm = pl.BlockSpec(memory_space=pltpu.HBM)
limits = pltpu.CompilerParams(vmem_limit_bytes=vmem_bytes)
ample = pltpu.CompilerParams(vmem_limit_bytes=60000000)


def on_device(
    features,
    conv_first,
    gain_first,
    shift_first,
    conv_second,
    gain_second,
    shift_second,
    head_weight,
    head_bias,
    corners,
    counts,
):
    _, slots, edge, _, data = features.shape
    in_width, width = conv_first.shape[-2:]
    classes = head_bias.shape[1]
    peers = lax.axis_size("folds") * lax.axis_size("sub")
    tiles = lax.axis_size("tiles")
    chunk = VX // peers
    area = edge * edge
    lanes = edge * classes
    padded = slots * (area + edge) + edge
    middle = chunk * 2 // 5
    halves = ((0, middle), (middle, chunk))
    parts = [(0, 0, chunk, True)]
    for low_row, high_row in halves:
        parts += [
            (peer, low_row, high_row, peer == 1 and low_row > 0)
            for peer in [*range(2, peers), 1]
        ]
    rows = [
        slots * edge * (high_row - low_row) + (edge if noted else 0)
        for _, low_row, high_row, noted in parts
    ]
    pieces = pl.pallas_call(
        functools.partial(section_kernel, (slots, edge, chunk, parts)),
        out_shape=[pltpu.VMEM((count, lanes), bf16) for count in rows],
        in_specs=[hbm] * 11,
        out_specs=[vmem] * len(parts),
        scratch_shapes=[
            pltpu.VMEM((padded, data + 256), bf16),
            pltpu.VMEM((padded, edge * width + 128), bf16),
            pltpu.VMEM((padded, edge * width), bf16),
            pltpu.VMEM((3, 768, 256), bf16),
            pltpu.VMEM((2, 384, 256), bf16),
            pltpu.VMEM((padded - 2 * edge, edge * width + 128), f32),
            pltpu.VMEM((padded - 2 * edge, edge * width), f32),
            pltpu.SMEM(corners.shape, jnp.int32),
            pltpu.SMEM(counts.shape[::-1], jnp.int32),
            pltpu.VMEM((27 * width, in_width), bf16),
            pltpu.VMEM((1, width), f32),
            pltpu.VMEM((1, width), f32),
            pltpu.VMEM((27 * width, width), bf16),
            pltpu.VMEM((1, width), f32),
            pltpu.VMEM((1, width), f32),
            pltpu.VMEM((classes, width), bf16),
            pltpu.VMEM((1, classes), f32),
            pltpu.VMEM((slots, VX * edge, area), bf16),
            pltpu.SemaphoreType.DMA((10 + slots,)),
        ],
        compiler_params=ample,
        name="section",
    )(
        corners,
        counts.T,
        features.reshape(slots, area, data),
        jnp.swapaxes(conv_first, 4, 5).reshape(27 * width, in_width),
        gain_first,
        shift_first,
        conv_second.reshape(27 * width, width),
        gain_second,
        shift_second,
        head_weight[0].T,
        head_bias,
    )
    arrived = []
    for (peer, _, _, _), piece in zip(parts, pieces):
        pairs = [(i, i ^ peer) for i in range(peers)]
        arrived.append(lax.ppermute(piece, ("folds", "sub"), pairs) if peer else piece)

    def gather(first, last, spilled, kind, name):
        chosen = [
            (part, piece)
            for part, piece in zip(parts, arrived)
            if part[3] or (part[1] < last and first < part[2])
        ]
        return pl.pallas_call(
            functools.partial(
                gather_kernel,
                (slots, edge, chunk, [part for part, _ in chosen], first, last, classes),
                spilled,
            ),
            out_shape=pltpu.VMEM((last - first, TZ, VY * classes), kind),
            in_specs=[vmem] * len(chosen),
            out_specs=vmem,
            compiler_params=limits,
            cost_estimate=pl.CostEstimate(
                flops=500000000, bytes_accessed=2000000, transcendentals=0
            ),
            name=name,
        )(*[piece for _, piece in chosen])

    even = [(tile, tile ^ 1) for tile in range(tiles)]
    odd = []
    for tile in range(tiles):
        for i in range(peers):
            if 0 < tile < tiles - 1:
                target = (tile + 1 if tile % 2 else tile - 1) * peers + i
            else:
                target = tile * peers + (i ^ 1)
            odd.append((tile * peers + i, target))
    from_below = []
    for first, last in halves:
        spill = gather(first, last, True, bf16, f"spill_{first}")
        from_below.append(lax.ppermute(spill, ("tiles", "folds", "sub"), odd))
        from_below.append(lax.ppermute(spill, "tiles", even))
    own = gather(0, chunk, False, f32, "own")
    joined = None
    for at in (1, 0):
        low_row, high_row = halves[at]
        joined = pl.pallas_call(
            functools.partial(join_kernel, low_row),
            out_shape=jax.ShapeDtypeStruct((chunk, TZ, VY * classes), f32),
            in_specs=[vmem] * 3 + ([] if joined is None else [hbm]),
            out_specs=hbm,
            input_output_aliases={} if joined is None else {3: 0},
            scratch_shapes=[
                pltpu.VMEM((high_row - low_row, TZ, VY * classes), f32),
                pltpu.SemaphoreType.DMA((high_row - low_row,)),
            ],
            compiler_params=limits,
            name=f"join_{low_row}",
        )(own, *from_below[2 * at : 2 * at + 2], *([] if joined is None else [joined]))
    return jnp.transpose(joined, (1, 0, 2))


def solution(mesh):
    placed = (
        P("folds", ("groups", "tiles", "sub"), None, None, None),
        P("folds", None, None, None, None, None),
        P("folds", None),
        P("folds", None),
        P("folds", None, None, None, None, None),
        P("folds", None),
        P("folds", None),
        P("folds", None, None),
        P("folds", None),
        P(("groups", "tiles", "sub"), None),
        P("groups", None),
    )
    return jax.shard_map(
        on_device,
        mesh=mesh,
        in_specs=placed,
        out_specs=P(("groups", "tiles"), ("folds", "sub"), None),
        check_vma=False,
    )
```

```python
import functools

import jax
import jax.numpy as jnp
from jax import lax
from jax.experimental import pallas as pl
from jax.experimental.pallas import tpu as pltpu
from jax.sharding import PartitionSpec as P

TZ = 16
VX = 40
VY = 40

epsilon = 1e-05
leak_slope = 0.01
far = 1 << 20
bf16 = jnp.bfloat16
f32 = jnp.float32
vmem_bytes = 48 << 20


def iota(shape, dim):
    return lax.broadcasted_iota(jnp.int32, shape, dim)


def tile_matrix(width, lanes):
    return (iota((width, lanes), 1) % width == iota((width, lanes), 0)).astype(bf16)


def tiled_row(ref, lanes):
    width = ref.shape[1]
    row = jnp.concatenate([ref[...], jnp.zeros((1, lanes - width), f32)], axis=1)
    row = jnp.broadcast_to(row, (8, lanes))
    reach = width
    while reach < lanes:
        row = row + pltpu.roll(row, reach, 1)
        reach *= 2
    return row[0:1]


def lane_bands(parts, places):
    total = None
    for place, part in enumerate(parts):
        if part is not None:
            total = part if total is None else jnp.where(places == place, part, total)
    if total is None:
        return None
    if any(part is None for part in parts):
        empty = None
        for place, part in enumerate(parts):
            if part is None:
                here = places == place
                empty = here if empty is None else empty | here
        total = jnp.where(empty, 0.0, total)
    return total


OUTER = ({2: 0, 3: 1}, {0: 1, 1: 2})


def build_pairs(taps_ref, band_ref, in_width, width, swapped, dz):
    spread = tile_matrix(width, 128)
    places = iota((in_width, 128), 1) // width
    zero = jnp.zeros((in_width, 128), bf16)
    orders = (((1, 0), (2, None)), ((0, 1), (None, 2)))
    tiled = {}
    if swapped:
        for tap in range(9):
            at = (dz * 9 + tap) * width
            tiled[divmod(tap, 3)] = lax.dot_general(
                taps_ref[at : at + width],
                spread,
                (((0,), (0,)), ((), ())),
                preferred_element_type=f32,
            )
    else:
        at = dz * 9 * in_width
        wide = jnp.dot(taps_ref[at : at + 9 * in_width], spread, preferred_element_type=f32)
        for tap in range(9):
            tiled[divmod(tap, 3)] = wide[tap * in_width : (tap + 1) * in_width]
    for variant in range(band_ref.shape[0]):
        for yi in range(4):
            for side in range(2):
                parts = []
                for dx in orders[variant % 2][side]:
                    for yo in range(2):
                        dy = OUTER[yo].get(yi) if variant == 2 else yi - yo
                        parts.append(None if dx is None else tiled.get((dx, dy)))
                block = lane_bands(parts, places)
                at = (dz * 4 + yi) * in_width
                band_ref[variant, at : at + in_width, side * 128 : (side + 1) * 128] = (
                    zero if block is None else block.astype(bf16)
                )


def banded(pad_ref, starts, count, edge, band):
    depth = band.shape[0] // (3 * len(starts))
    view = [
        pad_ref[dz * edge : dz * edge + count, lane : lane + depth]
        for dz in range(3)
        for lane in starts
    ]
    return jnp.dot(jnp.concatenate(view, axis=1), band, preferred_element_type=f32)


def join_pair(even, odd, low, edge):
    if odd is None:
        here = jnp.where(low, even[:, :128], 0.0)
        before = jnp.where(low, 0.0, even[:, :128])
        after = even[:, 128:]
    else:
        here = jnp.where(low, even[:, :128], odd[:, :128])
        before = jnp.where(low, odd[:, :128], even[:, :128])
        after = even[:, 128:] + odd[:, 128:]
    return join_across(pltpu.roll(before, 64, 1), here, after, edge)


def join_across(before, here, after, edge):
    rows = here.shape[0]
    row = iota((edge, 128), 0)
    inside = [(row != 0).astype(f32), (row != edge - 1).astype(f32)]
    sides = [pltpu.roll(before, 1, 0), pltpu.roll(after, rows - 1, 0)]
    lines = here.reshape(rows // edge, edge, 128)
    for side, keep in zip(sides, inside):
        lines = lines + side.reshape(rows // edge, edge, 128) * keep[None]
    return lines.reshape(rows, 128)


def folded(row, width):
    row = jnp.broadcast_to(row, (8, 128))
    reach = width
    while reach < 128:
        row = row + pltpu.roll(row, reach, 1)
        reach *= 2
    return row[0:1]


class Norm:
    def __init__(self, width, rows, voxels):
        self.width, self.rows, self.voxels = width, rows, voxels
        self.base = None
        self.first = self.second = 0.0

    def take(self, block, mask, held):
        kept = block if mask is None else jnp.where(mask, block, 0.0)
        if self.base is None:
            total = folded(jnp.sum(kept, axis=0, keepdims=True), self.width)
            self.base = total * (1.0 / (self.rows * held))
        moved = block - self.base
        if mask is not None:
            moved = jnp.where(mask, moved, 0.0)
        self.first = self.first + jnp.sum(moved, axis=0, keepdims=True)
        self.second = self.second + jnp.sum(moved * moved, axis=0, keepdims=True)

    def settle(self, gain, shift):
        off = folded(self.first, self.width) * (1.0 / self.voxels)
        variance = folded(self.second, self.width) * (1.0 / self.voxels) - off * off
        self.center = self.base + off
        self.factor = lax.rsqrt(jnp.maximum(variance, 0.0) + epsilon) * gain
        self.shift = shift - self.center * self.factor

    def give(self, block, mask):
        scaled = block * self.factor + self.shift
        scaled = jnp.maximum(scaled, leak_slope * scaled)
        return scaled if mask is None else jnp.where(mask, scaled, 0.0)


def section_kernel(
    sizes,
    corners_hbm,
    counts_hbm,
    features_ref,
    taps_one_hbm,
    gain_one_hbm,
    shift_one_hbm,
    taps_two_hbm,
    gain_two_hbm,
    shift_two_hbm,
    head_hbm,
    bias_hbm,
    *rest,
):
    slots, edge, chunk, parts = sizes
    out_refs = rest[: len(parts)]
    (
        pad_one,
        pad_two,
        pad_turned,
        band_one,
        band_two,
        hidden,
        outcome,
        corners_ref,
        counts_ref,
        taps_one_ref,
        gain_one_ref,
        shift_one_ref,
        taps_two_ref,
        gain_two_ref,
        shift_two_ref,
        head_ref,
        bias_ref,
        selects,
        sems,
    ) = rest[len(parts) :]
    in_width = taps_one_ref.shape[1]
    classes, width = head_ref.shape
    area = edge * edge
    stride = area + edge
    count = hidden.shape[0]
    voxels = float(area * edge)
    data = edge * in_width
    lanes = edge * classes

    copies = []
    for at, (source, target) in enumerate(
        [
            (taps_one_hbm, taps_one_ref),
            (taps_two_hbm, taps_two_ref),
            (gain_one_hbm, gain_one_ref),
            (shift_one_hbm, shift_one_ref),
            (gain_two_hbm, gain_two_ref),
            (shift_two_hbm, shift_two_ref),
            (head_hbm, head_ref),
            (bias_hbm, bias_ref),
            (corners_hbm, corners_ref),
            (counts_hbm, counts_ref),
        ]
        + [
            (
                features_ref.at[slot],
                pad_one.at[pl.ds(edge + slot * stride, area), pl.ds(128, data)],
            )
            for slot in range(slots)
        ]
    ):
        copy = pltpu.make_async_copy(source, target, sems.at[at])
        copy.start()
        copies.append(copy)
    for pad in (pad_one, pad_two, pad_turned):
        for slot in range(slots + 1):
            pad[slot * stride : slot * stride + edge, :] = jnp.zeros((edge, pad.shape[1]), bf16)
    center, spread = (edge - 1) / 2.0, edge / 4.0

    def profile(offset):
        return jnp.exp(-((offset.astype(f32) - center) ** 2) / (2.0 * spread * spread))

    row_at = iota((area, 128), 0)
    lane_at = iota((1, lanes), 1)
    gauss = profile(row_at // edge) * profile(row_at % edge)
    gauss = jnp.concatenate([gauss] * (lanes // 128), axis=1) * profile(lane_at // classes)

    row = iota((chunk * edge, area), 0)
    source = iota((chunk * edge, area), 1)
    turn = (row % edge - source // edge) & (edge - 1)
    code = turn + edge * (source % edge - row // edge)
    tile_index = lax.axis_index("tiles")
    sub_index = lax.axis_index("sub")
    position = lax.axis_index("folds") * lax.axis_size("sub") + sub_index

    copies[0].wait()
    for dz in range(3):
        build_pairs(taps_one_ref, band_one, in_width, width, True, dz)
    for copy in copies[1:-slots]:
        copy.wait()
    gain_one, shift_one = tiled_row(gain_one_ref, 128), tiled_row(shift_one_ref, 128)
    gain_two, shift_two = tiled_row(gain_two_ref, 128), tiled_row(shift_two_ref, 128)

    half = edge // 2
    head_row = lax.dot_general(
        head_ref[...],
        tile_matrix(classes, half * classes),
        (((0,), (0,)), ((), ())),
        preferred_element_type=f32,
    )
    block = (half * width, half * classes)
    head_block = jnp.where(
        iota(block, 0) // width == iota(block, 1) // classes,
        jnp.concatenate([head_row] * half, axis=0),
        0.0,
    ).astype(bf16)
    bias = tiled_row(bias_ref, lanes)

    mark = iota((edge, lanes), 0)
    notes = jnp.zeros((edge, lanes), f32)
    for slot in range(slots):
        depth = corners_ref[slot, 0] - tile_index * TZ
        notes = jnp.where(mark == 2 * slot, depth.astype(f32), notes)
        notes = jnp.where(mark == 2 * slot + 1, corners_ref[slot, 2].astype(f32), notes)
    for (_, low_row, high_row, noted), out_ref in zip(parts, out_refs):
        if noted:
            out_ref[slots * edge * (high_row - low_row) :, :] = notes.astype(bf16)

    for copy in copies[-slots:]:
        copy.wait()
    low = iota((count, 128), 1) < 64
    spot = iota((area, 128), 1)
    pairs = edge // 4 + 1
    masks = [None] * pairs
    masks[0] = spot >= width
    masks[-1] = spot < width
    norms = [Norm(width, area, voxels) for _ in range(slots)]
    outer = banded(pad_one, [128, data], count, edge, band_one[2])
    for pair in range(pairs):
        if 0 < pair < pairs - 1:
            even = banded(pad_one, [256 * pair], count, edge, band_one[0])
        else:
            even = outer
        odd = None
        if pair < pairs - 1:
            odd = banded(pad_one, [256 * pair + 128], count, edge, band_one[1])
        block = join_pair(even, odd, low, edge)
        hidden[:, pair * 128 : (pair + 1) * 128] = block
        for slot, norm in enumerate(norms):
            norm.take(block[slot * stride : slot * stride + area], masks[pair], 3)
        if pair < 3:
            build_pairs(taps_two_ref, band_two, width, width, False, pair)
    for norm in norms:
        norm.settle(gain_one, shift_one)

    fresh = {}
    near = spot < 64

    def refresh(pair):
        for slot, norm in enumerate(norms):
            at = slot * stride
            block = norm.give(hidden[at : at + area, pair * 128 : (pair + 1) * 128], masks[pair])
            rows_at = pl.ds(at + edge, area)
            pad_two[rows_at, pair * 128 : (pair + 1) * 128] = block.astype(bf16)
            if pair > 0:
                turned = pltpu.roll(jnp.where(near, block, fresh[slot]), 64, 1)
                pad_turned[rows_at, (pair - 1) * 128 : pair * 128] = turned.astype(bf16)
            fresh[slot] = block

    def prepare(slot):
        depth = corners_ref[slot, 0] - tile_index * TZ
        alive = slot < counts_ref[sub_index, tile_index]
        start = 0
        for peer, low_row, high_row, _ in parts:
            wanted = depth + edge * ((position ^ peer) * chunk - corners_ref[slot, 1])
            wanted = jnp.where(alive, wanted, far)
            select = (code[low_row * edge : high_row * edge] == wanted).astype(f32).astype(bf16)
            selects[slot, start : start + select.shape[0], :] = select
            start += select.shape[0]

    quads = edge // 4
    seconds = [Norm(width, area, voxels) for _ in range(slots)]
    refresh(0)
    for quad in range(quads):
        refresh(quad + 1)
        even = banded(pad_two, [128 * quad], count, edge, band_two[0])
        odd = banded(pad_turned, [128 * quad], count, edge, band_two[1])
        block = join_pair(even, odd, low, edge)
        outcome[:, quad * 128 : (quad + 1) * 128] = block
        for slot, norm in enumerate(seconds):
            norm.take(block[slot * stride : slot * stride + area], None, 4)
        if quad < slots:
            prepare(quad)
    for slot in range(quads, slots):
        prepare(slot)
    for norm in seconds:
        norm.settle(gain_two, shift_two)

    normed = []
    for slot, norm in enumerate(seconds):
        at = slot * stride
        for side in range(2):
            blocks = [
                norm.give(outcome[at : at + area, quad * 128 : (quad + 1) * 128], None).astype(
                    bf16
                )
                for quad in range(side * quads // 2, (side + 1) * quads // 2)
            ]
            normed.append(jnp.concatenate(blocks, axis=1))
    logits = [jnp.dot(block, head_block, preferred_element_type=f32) for block in normed]
    weighted = []
    for slot in range(slots):
        value = jnp.concatenate(logits[2 * slot : 2 * slot + 2], axis=1)
        value = (value + bias) * gauss
        lane_start = corners_ref[slot, 2] * classes
        weighted.append(pltpu.roll(value, lane_start % lanes, 1).astype(bf16))
    placed = [
        jnp.dot(selects[slot], weighted[slot], preferred_element_type=f32).astype(bf16)
        for slot in range(slots)
    ]
    for slot in range(slots):
        start = 0
        for (_, low_row, high_row, _), out_ref in zip(parts, out_refs):
            size = (high_row - low_row) * edge
            out_ref[slot * size : (slot + 1) * size, :] = placed[slot][start : start + size]
            start += size


def gather_kernel(sizes, spilled, *rest):
    slots, edge, chunk, parts, first, last, classes = sizes
    part_refs = rest[: len(parts)]
    out_ref = rest[len(parts)]
    lanes = edge * classes
    blocks = -(-VY * classes // lanes)

    depth_at = iota((edge, lanes), 0)
    lane_at = iota((edge, lanes), 1)
    groups = []
    for (peer, low_row, high_row, noted), part_ref in zip(parts, part_refs):
        if not noted or any(group[0] == peer % 2 for group in groups):
            continue
        notes = part_ref[slots * edge * (high_row - low_row) :, :].astype(f32).astype(jnp.int32)
        for slot in range(slots):
            depth = notes[2 * slot : 2 * slot + 1]
            start = notes[2 * slot + 1 : 2 * slot + 2] * classes
            keep = depth_at < depth if spilled else depth_at >= depth
            inside = []
            for block in range(blocks):
                lane = lane_at + block * lanes
                inside.append(keep & (lane >= start) & (lane < start + lanes))
            groups.append((peer % 2, slot, inside))

    for across in range(first, last):
        total = [jnp.zeros((edge, lanes), f32) for _ in range(blocks)]
        for parity, slot, inside in groups:
            piece = None
            for (peer, low_row, high_row, _), part_ref in zip(parts, part_refs):
                if peer % 2 == parity and low_row <= across < high_row:
                    at = (slot * (high_row - low_row) + across - low_row) * edge
                    part = part_ref[at : at + edge, :].astype(f32)
                    piece = part if piece is None else piece + part
            for block in range(blocks):
                total[block] = total[block] + jnp.where(inside[block], piece, 0.0)
        total = jnp.concatenate(total, axis=1)[:, : VY * classes]
        out_ref[across - first] = total.astype(out_ref.dtype)


def join_kernel(low_row, own_ref, odd_ref, even_ref, *rest):
    out_ref, total, sems = rest[-3:]
    tile_index = lax.axis_index("tiles")
    from_even = (tile_index % 2 == 1).astype(f32)
    from_odd = ((tile_index % 2 == 0) & (tile_index > 0)).astype(f32)
    copies = []
    for row in range(even_ref.shape[0]):
        total[row] = (
            own_ref[low_row + row]
            + even_ref[row].astype(f32) * from_even
            + odd_ref[row].astype(f32) * from_odd
        )
        copy = pltpu.make_async_copy(total.at[row], out_ref.at[low_row + row], sems.at[row])
        copy.start()
        copies.append(copy)
    for copy in copies:
        copy.wait()


vmem = pl.BlockSpec(memory_space=pltpu.VMEM)
hbm = pl.BlockSpec(memory_space=pltpu.HBM)
limits = pltpu.CompilerParams(vmem_limit_bytes=vmem_bytes)
ample = pltpu.CompilerParams(vmem_limit_bytes=60000000)


def on_device(
    features,
    conv_first,
    gain_first,
    shift_first,
    conv_second,
    gain_second,
    shift_second,
    head_weight,
    head_bias,
    corners,
    counts,
):
    _, slots, edge, _, data = features.shape
    in_width, width = conv_first.shape[-2:]
    classes = head_bias.shape[1]
    peers = lax.axis_size("folds") * lax.axis_size("sub")
    tiles = lax.axis_size("tiles")
    chunk = VX // peers
    area = edge * edge
    lanes = edge * classes
    padded = slots * (area + edge) + edge
    middle = chunk * 2 // 5
    halves = ((0, middle), (middle, chunk))
    parts = [(0, 0, chunk, True)]
    for low_row, high_row in halves:
        parts += [
            (peer, low_row, high_row, peer == 1 and low_row > 0)
            for peer in [*range(2, peers), 1]
        ]
    rows = [
        slots * edge * (high_row - low_row) + (edge if noted else 0)
        for _, low_row, high_row, noted in parts
    ]
    pieces = pl.pallas_call(
        functools.partial(section_kernel, (slots, edge, chunk, parts)),
        out_shape=[pltpu.VMEM((count, lanes), bf16) for count in rows],
        in_specs=[hbm] * 11,
        out_specs=[vmem] * len(parts),
        scratch_shapes=[
            pltpu.VMEM((padded, data + 256), bf16),
            pltpu.VMEM((padded, edge * width + 128), bf16),
            pltpu.VMEM((padded, edge * width), bf16),
            pltpu.VMEM((3, 768, 256), bf16),
            pltpu.VMEM((2, 384, 256), bf16),
            pltpu.VMEM((padded - 2 * edge, edge * width + 128), f32),
            pltpu.VMEM((padded - 2 * edge, edge * width), f32),
            pltpu.SMEM(corners.shape, jnp.int32),
            pltpu.SMEM(counts.shape[::-1], jnp.int32),
            pltpu.VMEM((27 * width, in_width), bf16),
            pltpu.VMEM((1, width), f32),
            pltpu.VMEM((1, width), f32),
            pltpu.VMEM((27 * width, width), bf16),
            pltpu.VMEM((1, width), f32),
            pltpu.VMEM((1, width), f32),
            pltpu.VMEM((classes, width), bf16),
            pltpu.VMEM((1, classes), f32),
            pltpu.VMEM((slots, VX * edge, area), bf16),
            pltpu.SemaphoreType.DMA((10 + slots,)),
        ],
        compiler_params=ample,
        name="section",
    )(
        corners,
        counts.T,
        features.reshape(slots, area, data),
        jnp.swapaxes(conv_first, 4, 5).reshape(27 * width, in_width),
        gain_first,
        shift_first,
        conv_second.reshape(27 * width, width),
        gain_second,
        shift_second,
        head_weight[0].T,
        head_bias,
    )
    arrived = []
    for (peer, _, _, _), piece in zip(parts, pieces):
        pairs = [(i, i ^ peer) for i in range(peers)]
        arrived.append(lax.ppermute(piece, ("folds", "sub"), pairs) if peer else piece)

    def gather(first, last, spilled, kind, name):
        chosen = [
            (part, piece)
            for part, piece in zip(parts, arrived)
            if part[3] or (part[1] < last and first < part[2])
        ]
        return pl.pallas_call(
            functools.partial(
                gather_kernel,
                (slots, edge, chunk, [part for part, _ in chosen], first, last, classes),
                spilled,
            ),
            out_shape=pltpu.VMEM((last - first, TZ, VY * classes), kind),
            in_specs=[vmem] * len(chosen),
            out_specs=vmem,
            compiler_params=limits,
            cost_estimate=pl.CostEstimate(
                flops=500000000, bytes_accessed=2000000, transcendentals=0
            ),
            name=name,
        )(*[piece for _, piece in chosen])

    even = [(tile, tile ^ 1) for tile in range(tiles)]
    odd = []
    for tile in range(tiles):
        for i in range(peers):
            if 0 < tile < tiles - 1:
                target = (tile + 1 if tile % 2 else tile - 1) * peers + i
            else:
                target = tile * peers + (i ^ 1)
            odd.append((tile * peers + i, target))
    from_below = []
    for first, last in halves:
        spill = gather(first, last, True, bf16, f"spill_{first}")
        from_below.append(lax.ppermute(spill, ("tiles", "folds", "sub"), odd))
        from_below.append(lax.ppermute(spill, "tiles", even))
    own = gather(0, chunk, False, f32, "own")
    joined = None
    for at in (1, 0):
        low_row, high_row = halves[at]
        joined = pl.pallas_call(
            functools.partial(join_kernel, low_row),
            out_shape=jax.ShapeDtypeStruct((chunk, TZ, VY * classes), f32),
            in_specs=[vmem] * 3 + ([] if joined is None else [hbm]),
            out_specs=hbm,
            input_output_aliases={} if joined is None else {3: 0},
            scratch_shapes=[
                pltpu.VMEM((high_row - low_row, TZ, VY * classes), f32),
                pltpu.SemaphoreType.DMA((high_row - low_row,)),
            ],
            compiler_params=limits,
            name=f"join_{low_row}",
        )(own, *from_below[2 * at : 2 * at + 2], *([] if joined is None else [joined]))
    return jnp.transpose(joined, (1, 0, 2))


def solution(mesh):
    placed = (
        P("folds", ("groups", "tiles", "sub"), None, None, None),
        P("folds", None, None, None, None, None),
        P("folds", None),
        P("folds", None),
        P("folds", None, None, None, None, None),
        P("folds", None),
        P("folds", None),
        P("folds", None, None),
        P("folds", None),
        P(("groups", "tiles", "sub"), None),
        P("groups", None),
    )
    return jax.shard_map(
        on_device,
        mesh=mesh,
        in_specs=placed,
        out_specs=P(("groups", "tiles"), ("folds", "sub"), None),
        check_vma=False,
    )
```

```python
import functools

import jax
import jax.numpy as jnp
from jax import lax
from jax.experimental import pallas as pl
from jax.experimental.pallas import tpu as pltpu
from jax.sharding import PartitionSpec as P

TZ = 16
VX = 40
VY = 40

epsilon = 1e-05
leak_slope = 0.01
far = 1 << 20
bf16 = jnp.bfloat16
f32 = jnp.float32
vmem_bytes = 48 << 20


def iota(shape, dim):
    return lax.broadcasted_iota(jnp.int32, shape, dim)


def tile_matrix(width, lanes):
    return (iota((width, lanes), 1) % width == iota((width, lanes), 0)).astype(bf16)


def tiled_row(ref, lanes):
    width = ref.shape[1]
    row = jnp.concatenate([ref[...], jnp.zeros((1, lanes - width), f32)], axis=1)
    row = jnp.broadcast_to(row, (8, lanes))
    reach = width
    while reach < lanes:
        row = row + pltpu.roll(row, reach, 1)
        reach *= 2
    return row[0:1]


def lane_bands(parts, places):
    total = None
    for place, part in enumerate(parts):
        if part is not None:
            total = part if total is None else jnp.where(places == place, part, total)
    if total is None:
        return None
    if any(part is None for part in parts):
        empty = None
        for place, part in enumerate(parts):
            if part is None:
                here = places == place
                empty = here if empty is None else empty | here
        total = jnp.where(empty, 0.0, total)
    return total


OUTER = ({2: 0, 3: 1}, {0: 1, 1: 2})


def build_pairs(taps_ref, band_ref, in_width, width, swapped, dz, variants, tiled):
    spread = tile_matrix(width, 128)
    places = iota((in_width, 128), 1) // width
    zero = jnp.zeros((in_width, 128), bf16)
    orders = (((1, 0), (2, None)), ((0, 1), (None, 2)))
    if tiled:
        pass
    elif swapped:
        for tap in range(9):
            at = (dz * 9 + tap) * width
            tiled[divmod(tap, 3)] = lax.dot_general(
                taps_ref[at : at + width],
                spread,
                (((0,), (0,)), ((), ())),
                preferred_element_type=f32,
            )
    else:
        at = dz * 9 * in_width
        wide = jnp.dot(taps_ref[at : at + 9 * in_width], spread, preferred_element_type=f32)
        for tap in range(9):
            tiled[divmod(tap, 3)] = wide[tap * in_width : (tap + 1) * in_width]
    for variant in variants:
        for yi in range(4):
            for side in range(2):
                parts = []
                for dx in orders[variant % 2][side]:
                    for yo in range(2):
                        dy = OUTER[yo].get(yi) if variant == 2 else yi - yo
                        parts.append(None if dx is None else tiled.get((dx, dy)))
                block = lane_bands(parts, places)
                at = (dz * 4 + yi) * in_width
                band_ref[variant, at : at + in_width, side * 128 : (side + 1) * 128] = (
                    zero if block is None else block.astype(bf16)
                )


def banded(pad_ref, starts, count, edge, band):
    depth = band.shape[0] // (3 * len(starts))
    view = [
        pad_ref[dz * edge : dz * edge + count, lane : lane + depth]
        for dz in range(3)
        for lane in starts
    ]
    return jnp.dot(jnp.concatenate(view, axis=1), band, preferred_element_type=f32)


def join_pair(even, odd, low, edge):
    if odd is None:
        here = jnp.where(low, even[:, :128], 0.0)
        before = jnp.where(low, 0.0, even[:, :128])
        after = even[:, 128:]
    else:
        here = jnp.where(low, even[:, :128], odd[:, :128])
        before = jnp.where(low, odd[:, :128], even[:, :128])
        after = even[:, 128:] + odd[:, 128:]
    return join_across(pltpu.roll(before, 64, 1), here, after, edge)


def join_across(before, here, after, edge):
    rows = here.shape[0]
    row = iota((edge, 128), 0)
    inside = [(row != 0).astype(f32), (row != edge - 1).astype(f32)]
    sides = [pltpu.roll(before, 1, 0), pltpu.roll(after, rows - 1, 0)]
    lines = here.reshape(rows // edge, edge, 128)
    for side, keep in zip(sides, inside):
        lines = lines + side.reshape(rows // edge, edge, 128) * keep[None]
    return lines.reshape(rows, 128)


def folded(row, width):
    row = jnp.broadcast_to(row, (8, 128))
    reach = width
    while reach < 128:
        row = row + pltpu.roll(row, reach, 1)
        reach *= 2
    return row[0:1]


class Norm:
    def __init__(self, width, rows, voxels):
        self.width, self.rows, self.voxels = width, rows, voxels
        self.base = None
        self.first = self.second = 0.0

    def take(self, block, mask, held):
        kept = block if mask is None else jnp.where(mask, block, 0.0)
        if self.base is None:
            total = folded(jnp.sum(kept, axis=0, keepdims=True), self.width)
            self.base = total * (1.0 / (self.rows * held))
        moved = block - self.base
        if mask is not None:
            moved = jnp.where(mask, moved, 0.0)
        self.first = self.first + jnp.sum(moved, axis=0, keepdims=True)
        self.second = self.second + jnp.sum(moved * moved, axis=0, keepdims=True)

    def settle(self, gain, shift):
        off = folded(self.first, self.width) * (1.0 / self.voxels)
        variance = folded(self.second, self.width) * (1.0 / self.voxels) - off * off
        self.center = self.base + off
        self.factor = lax.rsqrt(jnp.maximum(variance, 0.0) + epsilon) * gain
        self.shift = shift - self.center * self.factor

    def give(self, block, mask):
        scaled = block * self.factor + self.shift
        scaled = jnp.maximum(scaled, leak_slope * scaled)
        return scaled if mask is None else jnp.where(mask, scaled, 0.0)


def section_kernel(
    sizes,
    corners_hbm,
    counts_hbm,
    features_ref,
    taps_one_hbm,
    gain_one_hbm,
    shift_one_hbm,
    taps_two_hbm,
    gain_two_hbm,
    shift_two_hbm,
    head_hbm,
    bias_hbm,
    *rest,
):
    slots, edge, chunk, parts = sizes
    out_refs = rest[: len(parts)]
    (
        pad_one,
        pad_two,
        pad_turned,
        band_one,
        band_two,
        hidden,
        outcome,
        corners_ref,
        counts_ref,
        taps_one_ref,
        gain_one_ref,
        shift_one_ref,
        taps_two_ref,
        gain_two_ref,
        shift_two_ref,
        head_ref,
        bias_ref,
        selects,
        sems,
    ) = rest[len(parts) :]
    in_width = taps_one_ref.shape[1]
    classes, width = head_ref.shape
    area = edge * edge
    stride = area + edge
    count = hidden.shape[0]
    voxels = float(area * edge)
    data = edge * in_width
    lanes = edge * classes

    copies = []
    for at, (source, target) in enumerate(
        [
            (taps_one_hbm, taps_one_ref),
            (taps_two_hbm, taps_two_ref),
            (gain_one_hbm, gain_one_ref),
            (shift_one_hbm, shift_one_ref),
            (gain_two_hbm, gain_two_ref),
            (shift_two_hbm, shift_two_ref),
            (head_hbm, head_ref),
            (bias_hbm, bias_ref),
            (corners_hbm, corners_ref),
            (counts_hbm, counts_ref),
        ]
        + [
            (
                features_ref.at[slot],
                pad_one.at[pl.ds(edge + slot * stride, area), pl.ds(128, data)],
            )
            for slot in range(slots)
        ]
    ):
        copy = pltpu.make_async_copy(source, target, sems.at[at])
        copy.start()
        copies.append(copy)
    for pad in (pad_one, pad_two, pad_turned):
        for slot in range(slots + 1):
            pad[slot * stride : slot * stride + edge, :] = jnp.zeros((edge, pad.shape[1]), bf16)
    center, spread = (edge - 1) / 2.0, edge / 4.0

    def profile(offset):
        return jnp.exp(-((offset.astype(f32) - center) ** 2) / (2.0 * spread * spread))

    row_at = iota((area, 128), 0)
    lane_at = iota((1, lanes), 1)
    gauss = profile(row_at // edge) * profile(row_at % edge)
    gauss = jnp.concatenate([gauss] * (lanes // 128), axis=1) * profile(lane_at // classes)

    row = iota((chunk * edge, area), 0)
    source = iota((chunk * edge, area), 1)
    turn = (row % edge - source // edge) & (edge - 1)
    code = turn + edge * (source % edge - row // edge)
    tile_index = lax.axis_index("tiles")
    sub_index = lax.axis_index("sub")
    position = lax.axis_index("folds") * lax.axis_size("sub") + sub_index

    copies[0].wait()
    tiled = [{}, {}, {}]

    def build(variant):
        for dz in range(3):
            build_pairs(
                taps_one_ref, band_one, in_width, width, True, dz, (variant,), tiled[dz]
            )

    build(2)
    for copy in copies[1:-slots]:
        copy.wait()
    gain_one, shift_one = tiled_row(gain_one_ref, 128), tiled_row(shift_one_ref, 128)
    gain_two, shift_two = tiled_row(gain_two_ref, 128), tiled_row(shift_two_ref, 128)

    half = edge // 2
    head_row = lax.dot_general(
        head_ref[...],
        tile_matrix(classes, half * classes),
        (((0,), (0,)), ((), ())),
        preferred_element_type=f32,
    )
    block = (half * width, half * classes)
    head_block = jnp.where(
        iota(block, 0) // width == iota(block, 1) // classes,
        jnp.concatenate([head_row] * half, axis=0),
        0.0,
    ).astype(bf16)
    bias = tiled_row(bias_ref, lanes)

    mark = iota((edge, lanes), 0)
    notes = jnp.zeros((edge, lanes), f32)
    for slot in range(slots):
        depth = corners_ref[slot, 0] - tile_index * TZ
        notes = jnp.where(mark == 2 * slot, depth.astype(f32), notes)
        notes = jnp.where(mark == 2 * slot + 1, corners_ref[slot, 2].astype(f32), notes)
    for (_, low_row, high_row, noted), out_ref in zip(parts, out_refs):
        if noted:
            out_ref[slots * edge * (high_row - low_row) :, :] = notes.astype(bf16)

    for copy in copies[-slots:]:
        copy.wait()
    low = iota((count, 128), 1) < 64
    spot = iota((area, 128), 1)
    pairs = edge // 4 + 1
    masks = [None] * pairs
    masks[0] = spot >= width
    masks[-1] = spot < width
    norms = [Norm(width, area, voxels) for _ in range(slots)]
    outer = banded(pad_one, [128, data], count, edge, band_one[2])
    for pair in range(pairs):
        if pair < 2:
            build(1 - pair)
        if 0 < pair < pairs - 1:
            even = banded(pad_one, [256 * pair], count, edge, band_one[0])
        else:
            even = outer
        odd = None
        if pair < pairs - 1:
            odd = banded(pad_one, [256 * pair + 128], count, edge, band_one[1])
        block = join_pair(even, odd, low, edge)
        hidden[:, pair * 128 : (pair + 1) * 128] = block
        for slot, norm in enumerate(norms):
            norm.take(block[slot * stride : slot * stride + area], masks[pair], 3)
        if pair < 3:
            build_pairs(taps_two_ref, band_two, width, width, False, pair, (0, 1), {})
    for norm in norms:
        norm.settle(gain_one, shift_one)

    fresh = {}
    near = spot < 64

    def refresh(pair):
        for slot, norm in enumerate(norms):
            at = slot * stride
            block = norm.give(hidden[at : at + area, pair * 128 : (pair + 1) * 128], masks[pair])
            rows_at = pl.ds(at + edge, area)
            pad_two[rows_at, pair * 128 : (pair + 1) * 128] = block.astype(bf16)
            if pair > 0:
                turned = pltpu.roll(jnp.where(near, block, fresh[slot]), 64, 1)
                pad_turned[rows_at, (pair - 1) * 128 : pair * 128] = turned.astype(bf16)
            fresh[slot] = block

    def prepare(slot):
        depth = corners_ref[slot, 0] - tile_index * TZ
        alive = slot < counts_ref[sub_index, tile_index]
        start = 0
        for peer, low_row, high_row, _ in parts:
            wanted = depth + edge * ((position ^ peer) * chunk - corners_ref[slot, 1])
            wanted = jnp.where(alive, wanted, far)
            select = (code[low_row * edge : high_row * edge] == wanted).astype(f32).astype(bf16)
            selects[slot, start : start + select.shape[0], :] = select
            start += select.shape[0]

    quads = edge // 4
    seconds = [Norm(width, area, voxels) for _ in range(slots)]
    refresh(0)
    for quad in range(quads):
        refresh(quad + 1)
        even = banded(pad_two, [128 * quad], count, edge, band_two[0])
        odd = banded(pad_turned, [128 * quad], count, edge, band_two[1])
        block = join_pair(even, odd, low, edge)
        outcome[:, quad * 128 : (quad + 1) * 128] = block
        for slot, norm in enumerate(seconds):
            norm.take(block[slot * stride : slot * stride + area], None, 4)
        if quad < slots:
            prepare(quad)
    for slot in range(quads, slots):
        prepare(slot)
    for norm in seconds:
        norm.settle(gain_two, shift_two)

    normed = []
    for slot, norm in enumerate(seconds):
        at = slot * stride
        for side in range(2):
            blocks = [
                norm.give(outcome[at : at + area, quad * 128 : (quad + 1) * 128], None).astype(
                    bf16
                )
                for quad in range(side * quads // 2, (side + 1) * quads // 2)
            ]
            normed.append(jnp.concatenate(blocks, axis=1))
    logits = [jnp.dot(block, head_block, preferred_element_type=f32) for block in normed]
    weighted = []
    for slot in range(slots):
        value = jnp.concatenate(logits[2 * slot : 2 * slot + 2], axis=1)
        value = (value + bias) * gauss
        lane_start = corners_ref[slot, 2] * classes
        weighted.append(pltpu.roll(value, lane_start % lanes, 1).astype(bf16))
    placed = [
        jnp.dot(selects[slot], weighted[slot], preferred_element_type=f32).astype(bf16)
        for slot in range(slots)
    ]
    for slot in range(slots):
        start = 0
        for (_, low_row, high_row, _), out_ref in zip(parts, out_refs):
            size = (high_row - low_row) * edge
            out_ref[slot * size : (slot + 1) * size, :] = placed[slot][start : start + size]
            start += size


def gather_kernel(sizes, spilled, *rest):
    slots, edge, chunk, parts, first, last, classes = sizes
    part_refs = rest[: len(parts)]
    out_ref = rest[len(parts)]
    lanes = edge * classes
    blocks = -(-VY * classes // lanes)

    depth_at = iota((edge, lanes), 0)
    lane_at = iota((edge, lanes), 1)
    groups = []
    for (peer, low_row, high_row, noted), part_ref in zip(parts, part_refs):
        if not noted or any(group[0] == peer % 2 for group in groups):
            continue
        notes = part_ref[slots * edge * (high_row - low_row) :, :].astype(f32).astype(jnp.int32)
        for slot in range(slots):
            depth = notes[2 * slot : 2 * slot + 1]
            start = notes[2 * slot + 1 : 2 * slot + 2] * classes
            keep = depth_at < depth if spilled else depth_at >= depth
            inside = []
            for block in range(blocks):
                lane = lane_at + block * lanes
                inside.append(keep & (lane >= start) & (lane < start + lanes))
            groups.append((peer % 2, slot, inside))

    for across in range(first, last):
        total = [jnp.zeros((edge, lanes), f32) for _ in range(blocks)]
        for parity, slot, inside in groups:
            piece = None
            for (peer, low_row, high_row, _), part_ref in zip(parts, part_refs):
                if peer % 2 == parity and low_row <= across < high_row:
                    at = (slot * (high_row - low_row) + across - low_row) * edge
                    part = part_ref[at : at + edge, :].astype(f32)
                    piece = part if piece is None else piece + part
            for block in range(blocks):
                total[block] = total[block] + jnp.where(inside[block], piece, 0.0)
        total = jnp.concatenate(total, axis=1)[:, : VY * classes]
        out_ref[across - first] = total.astype(out_ref.dtype)


def join_kernel(low_row, own_ref, odd_ref, even_ref, *rest):
    out_ref, total, sems = rest[-3:]
    tile_index = lax.axis_index("tiles")
    from_even = (tile_index % 2 == 1).astype(f32)
    from_odd = ((tile_index % 2 == 0) & (tile_index > 0)).astype(f32)
    copies = []
    for row in range(even_ref.shape[0]):
        total[row] = (
            own_ref[low_row + row]
            + even_ref[row].astype(f32) * from_even
            + odd_ref[row].astype(f32) * from_odd
        )
        copy = pltpu.make_async_copy(total.at[row], out_ref.at[low_row + row], sems.at[row])
        copy.start()
        copies.append(copy)
    for copy in copies:
        copy.wait()


vmem = pl.BlockSpec(memory_space=pltpu.VMEM)
hbm = pl.BlockSpec(memory_space=pltpu.HBM)
limits = pltpu.CompilerParams(vmem_limit_bytes=vmem_bytes)
ample = pltpu.CompilerParams(vmem_limit_bytes=60000000)


def on_device(
    features,
    conv_first,
    gain_first,
    shift_first,
    conv_second,
    gain_second,
    shift_second,
    head_weight,
    head_bias,
    corners,
    counts,
):
    _, slots, edge, _, data = features.shape
    in_width, width = conv_first.shape[-2:]
    classes = head_bias.shape[1]
    peers = lax.axis_size("folds") * lax.axis_size("sub")
    tiles = lax.axis_size("tiles")
    chunk = VX // peers
    area = edge * edge
    lanes = edge * classes
    padded = slots * (area + edge) + edge
    middle = chunk * 2 // 5
    halves = ((0, middle), (middle, chunk))
    parts = [(0, 0, chunk, True)]
    for low_row, high_row in halves:
        parts += [
            (peer, low_row, high_row, peer == 1 and low_row > 0)
            for peer in [*range(2, peers), 1]
        ]
    rows = [
        slots * edge * (high_row - low_row) + (edge if noted else 0)
        for _, low_row, high_row, noted in parts
    ]
    pieces = pl.pallas_call(
        functools.partial(section_kernel, (slots, edge, chunk, parts)),
        out_shape=[pltpu.VMEM((count, lanes), bf16) for count in rows],
        in_specs=[hbm] * 11,
        out_specs=[vmem] * len(parts),
        scratch_shapes=[
            pltpu.VMEM((padded, data + 256), bf16),
            pltpu.VMEM((padded, edge * width + 128), bf16),
            pltpu.VMEM((padded, edge * width), bf16),
            pltpu.VMEM((3, 768, 256), bf16),
            pltpu.VMEM((2, 384, 256), bf16),
            pltpu.VMEM((padded - 2 * edge, edge * width + 128), f32),
            pltpu.VMEM((padded - 2 * edge, edge * width), f32),
            pltpu.SMEM(corners.shape, jnp.int32),
            pltpu.SMEM(counts.shape[::-1], jnp.int32),
            pltpu.VMEM((27 * width, in_width), bf16),
            pltpu.VMEM((1, width), f32),
            pltpu.VMEM((1, width), f32),
            pltpu.VMEM((27 * width, width), bf16),
            pltpu.VMEM((1, width), f32),
            pltpu.VMEM((1, width), f32),
            pltpu.VMEM((classes, width), bf16),
            pltpu.VMEM((1, classes), f32),
            pltpu.VMEM((slots, VX * edge, area), bf16),
            pltpu.SemaphoreType.DMA((10 + slots,)),
        ],
        compiler_params=ample,
        name="section",
    )(
        corners,
        counts.T,
        features.reshape(slots, area, data),
        jnp.swapaxes(conv_first, 4, 5).reshape(27 * width, in_width),
        gain_first,
        shift_first,
        conv_second.reshape(27 * width, width),
        gain_second,
        shift_second,
        head_weight[0].T,
        head_bias,
    )
    arrived = []
    for (peer, _, _, _), piece in zip(parts, pieces):
        pairs = [(i, i ^ peer) for i in range(peers)]
        arrived.append(lax.ppermute(piece, ("folds", "sub"), pairs) if peer else piece)

    def gather(first, last, spilled, kind, name):
        chosen = [
            (part, piece)
            for part, piece in zip(parts, arrived)
            if part[3] or (part[1] < last and first < part[2])
        ]
        return pl.pallas_call(
            functools.partial(
                gather_kernel,
                (slots, edge, chunk, [part for part, _ in chosen], first, last, classes),
                spilled,
            ),
            out_shape=pltpu.VMEM((last - first, TZ, VY * classes), kind),
            in_specs=[vmem] * len(chosen),
            out_specs=vmem,
            compiler_params=limits,
            cost_estimate=pl.CostEstimate(
                flops=500000000, bytes_accessed=2000000, transcendentals=0
            ),
            name=name,
        )(*[piece for _, piece in chosen])

    even = [(tile, tile ^ 1) for tile in range(tiles)]
    odd = []
    for tile in range(tiles):
        for i in range(peers):
            if 0 < tile < tiles - 1:
                target = (tile + 1 if tile % 2 else tile - 1) * peers + i
            else:
                target = tile * peers + (i ^ 1)
            odd.append((tile * peers + i, target))
    from_below = []
    for first, last in halves:
        spill = gather(first, last, True, bf16, f"spill_{first}")
        from_below.append(lax.ppermute(spill, ("tiles", "folds", "sub"), odd))
        from_below.append(lax.ppermute(spill, "tiles", even))
    own = gather(0, chunk, False, f32, "own")
    joined = None
    for at in (1, 0):
        low_row, high_row = halves[at]
        joined = pl.pallas_call(
            functools.partial(join_kernel, low_row),
            out_shape=jax.ShapeDtypeStruct((chunk, TZ, VY * classes), f32),
            in_specs=[vmem] * 3 + ([] if joined is None else [hbm]),
            out_specs=hbm,
            input_output_aliases={} if joined is None else {3: 0},
            scratch_shapes=[
                pltpu.VMEM((high_row - low_row, TZ, VY * classes), f32),
                pltpu.SemaphoreType.DMA((high_row - low_row,)),
            ],
            compiler_params=limits,
            name=f"join_{low_row}",
        )(own, *from_below[2 * at : 2 * at + 2], *([] if joined is None else [joined]))
    return jnp.transpose(joined, (1, 0, 2))


def solution(mesh):
    placed = (
        P("folds", ("groups", "tiles", "sub"), None, None, None),
        P("folds", None, None, None, None, None),
        P("folds", None),
        P("folds", None),
        P("folds", None, None, None, None, None),
        P("folds", None),
        P("folds", None),
        P("folds", None, None),
        P("folds", None),
        P(("groups", "tiles", "sub"), None),
        P("groups", None),
    )
    return jax.shard_map(
        on_device,
        mesh=mesh,
        in_specs=placed,
        out_specs=P(("groups", "tiles"), ("folds", "sub"), None),
        check_vma=False,
    )
```

```python
import functools

import jax
import jax.numpy as jnp
from jax import lax
from jax.experimental import pallas as pl
from jax.experimental.pallas import tpu as pltpu
from jax.sharding import PartitionSpec as P

TZ = 16
VX = 40
VY = 40

epsilon = 1e-05
leak_slope = 0.01
far = 1 << 20
bf16 = jnp.bfloat16
f32 = jnp.float32
vmem_bytes = 48 << 20


def iota(shape, dim):
    return lax.broadcasted_iota(jnp.int32, shape, dim)


def tile_matrix(width, lanes):
    return (iota((width, lanes), 1) % width == iota((width, lanes), 0)).astype(bf16)


def tiled_row(ref, lanes):
    width = ref.shape[1]
    row = jnp.concatenate([ref[...], jnp.zeros((1, lanes - width), f32)], axis=1)
    row = jnp.broadcast_to(row, (8, lanes))
    reach = width
    while reach < lanes:
        row = row + pltpu.roll(row, reach, 1)
        reach *= 2
    return row[0:1]


def lane_bands(parts, places):
    total = None
    for place, part in enumerate(parts):
        if part is not None:
            total = part if total is None else jnp.where(places == place, part, total)
    if total is None:
        return None
    if any(part is None for part in parts):
        empty = None
        for place, part in enumerate(parts):
            if part is None:
                here = places == place
                empty = here if empty is None else empty | here
        total = jnp.where(empty, 0.0, total)
    return total


OUTER = ({2: 0, 3: 1}, {0: 1, 1: 2})


def build_pairs(taps_ref, band_ref, in_width, width, swapped, dz):
    spread = tile_matrix(width, 128)
    places = iota((in_width, 128), 1) // width
    zero = jnp.zeros((in_width, 128), bf16)
    orders = (((1, 0), (2, None)), ((0, 1), (None, 2)))
    tiled = {}
    if swapped:
        for tap in range(9):
            at = (dz * 9 + tap) * width
            tiled[divmod(tap, 3)] = lax.dot_general(
                taps_ref[at : at + width],
                spread,
                (((0,), (0,)), ((), ())),
                preferred_element_type=f32,
            )
    else:
        at = dz * 9 * in_width
        wide = jnp.dot(taps_ref[at : at + 9 * in_width], spread, preferred_element_type=f32)
        for tap in range(9):
            tiled[divmod(tap, 3)] = wide[tap * in_width : (tap + 1) * in_width]
    for variant in range(band_ref.shape[0]):
        for yi in range(4):
            for side in range(2):
                parts = []
                for dx in orders[variant % 2][side]:
                    for yo in range(2):
                        dy = OUTER[yo].get(yi) if variant == 2 else yi - yo
                        parts.append(None if dx is None else tiled.get((dx, dy)))
                block = lane_bands(parts, places)
                at = (dz * 4 + yi) * in_width
                band_ref[variant, at : at + in_width, side * 128 : (side + 1) * 128] = (
                    zero if block is None else block.astype(bf16)
                )


def banded(pad_ref, starts, count, edge, band):
    depth = band.shape[0] // (3 * len(starts))
    view = [
        pad_ref[dz * edge : dz * edge + count, lane : lane + depth]
        for dz in range(3)
        for lane in starts
    ]
    return jnp.dot(jnp.concatenate(view, axis=1), band, preferred_element_type=f32)


def join_pair(even, odd, low, edge):
    if odd is None:
        here = jnp.where(low, even[:, :128], 0.0)
        before = jnp.where(low, 0.0, even[:, :128])
        after = even[:, 128:]
    else:
        here = jnp.where(low, even[:, :128], odd[:, :128])
        before = jnp.where(low, odd[:, :128], even[:, :128])
        after = even[:, 128:] + odd[:, 128:]
    return join_across(pltpu.roll(before, 64, 1), here, after, edge)


def join_across(before, here, after, edge):
    rows = here.shape[0]
    row = iota((edge, 128), 0)
    inside = [(row != 0).astype(f32), (row != edge - 1).astype(f32)]
    sides = [pltpu.roll(before, 1, 0), pltpu.roll(after, rows - 1, 0)]
    lines = here.reshape(rows // edge, edge, 128)
    for side, keep in zip(sides, inside):
        lines = lines + side.reshape(rows // edge, edge, 128) * keep[None]
    return lines.reshape(rows, 128)


def folded(row, width):
    row = jnp.broadcast_to(row, (8, 128))
    reach = width
    while reach < 128:
        row = row + pltpu.roll(row, reach, 1)
        reach *= 2
    return row[0:1]


class Norm:
    def __init__(self, width, rows, voxels):
        self.width, self.rows, self.voxels = width, rows, voxels
        self.base = None
        self.first = self.second = 0.0

    def take(self, block, mask, held):
        kept = block if mask is None else jnp.where(mask, block, 0.0)
        if self.base is None:
            total = folded(jnp.sum(kept, axis=0, keepdims=True), self.width)
            self.base = total * (1.0 / (self.rows * held))
        moved = block - self.base
        if mask is not None:
            moved = jnp.where(mask, moved, 0.0)
        self.first = self.first + jnp.sum(moved, axis=0, keepdims=True)
        self.second = self.second + jnp.sum(moved * moved, axis=0, keepdims=True)

    def settle(self, gain, shift):
        off = folded(self.first, self.width) * (1.0 / self.voxels)
        variance = folded(self.second, self.width) * (1.0 / self.voxels) - off * off
        self.center = self.base + off
        self.factor = lax.rsqrt(jnp.maximum(variance, 0.0) + epsilon) * gain
        self.shift = shift - self.center * self.factor

    def give(self, block, mask):
        scaled = block * self.factor + self.shift
        scaled = jnp.maximum(scaled, leak_slope * scaled)
        return scaled if mask is None else jnp.where(mask, scaled, 0.0)


def section_kernel(
    sizes,
    corners_hbm,
    counts_hbm,
    features_ref,
    taps_one_hbm,
    gain_one_hbm,
    shift_one_hbm,
    taps_two_hbm,
    gain_two_hbm,
    shift_two_hbm,
    head_hbm,
    bias_hbm,
    *rest,
):
    slots, edge, chunk, parts = sizes
    out_refs = rest[: len(parts)]
    (
        pad_one,
        pad_two,
        pad_turned,
        band_one,
        band_two,
        hidden,
        outcome,
        corners_ref,
        counts_ref,
        taps_one_ref,
        gain_one_ref,
        shift_one_ref,
        taps_two_ref,
        gain_two_ref,
        shift_two_ref,
        head_ref,
        bias_ref,
        selects,
        sems,
    ) = rest[len(parts) :]
    in_width = taps_one_ref.shape[1]
    classes, width = head_ref.shape
    area = edge * edge
    stride = area + edge
    count = hidden.shape[0]
    voxels = float(area * edge)
    data = edge * in_width
    lanes = edge * classes

    copies = []
    for at, (source, target) in enumerate(
        [
            (taps_one_hbm, taps_one_ref),
            (taps_two_hbm, taps_two_ref),
            (gain_one_hbm, gain_one_ref),
            (shift_one_hbm, shift_one_ref),
            (gain_two_hbm, gain_two_ref),
            (shift_two_hbm, shift_two_ref),
            (head_hbm, head_ref),
            (bias_hbm, bias_ref),
            (corners_hbm, corners_ref),
            (counts_hbm, counts_ref),
        ]
        + [
            (
                features_ref.at[slot],
                pad_one.at[pl.ds(edge + slot * stride, area), pl.ds(128, data)],
            )
            for slot in range(slots)
        ]
    ):
        copy = pltpu.make_async_copy(source, target, sems.at[at])
        copy.start()
        copies.append(copy)
    for pad in (pad_one, pad_two, pad_turned):
        for slot in range(slots + 1):
            pad[slot * stride : slot * stride + edge, :] = jnp.zeros((edge, pad.shape[1]), bf16)
    center, spread = (edge - 1) / 2.0, edge / 4.0

    def profile(offset):
        return jnp.exp(-((offset.astype(f32) - center) ** 2) / (2.0 * spread * spread))

    row_at = iota((area, 128), 0)
    lane_at = iota((1, lanes), 1)
    gauss = profile(row_at // edge) * profile(row_at % edge)
    gauss = jnp.concatenate([gauss] * (lanes // 128), axis=1) * profile(lane_at // classes)

    row = iota((chunk * edge, area), 0)
    source = iota((chunk * edge, area), 1)
    turn = (row % edge - source // edge) & (edge - 1)
    code = turn + edge * (source % edge - row // edge)
    tile_index = lax.axis_index("tiles")
    sub_index = lax.axis_index("sub")
    position = lax.axis_index("folds") * lax.axis_size("sub") + sub_index

    copies[0].wait()
    for dz in range(3):
        build_pairs(taps_one_ref, band_one, in_width, width, True, dz)
    for copy in copies[1:-slots]:
        copy.wait()
    gain_one, shift_one = tiled_row(gain_one_ref, 128), tiled_row(shift_one_ref, 128)
    gain_two, shift_two = tiled_row(gain_two_ref, 128), tiled_row(shift_two_ref, 128)

    half = edge // 2
    head_row = lax.dot_general(
        head_ref[...],
        tile_matrix(classes, half * classes),
        (((0,), (0,)), ((), ())),
        preferred_element_type=f32,
    )
    block = (half * width, half * classes)
    head_block = jnp.where(
        iota(block, 0) // width == iota(block, 1) // classes,
        jnp.concatenate([head_row] * half, axis=0),
        0.0,
    ).astype(bf16)
    bias = tiled_row(bias_ref, lanes)

    mark = iota((edge, lanes), 0)
    notes = jnp.zeros((edge, lanes), f32)
    for slot in range(slots):
        depth = corners_ref[slot, 0] - tile_index * TZ
        notes = jnp.where(mark == 2 * slot, depth.astype(f32), notes)
        notes = jnp.where(mark == 2 * slot + 1, corners_ref[slot, 2].astype(f32), notes)
    for (_, low_row, high_row, noted), out_ref in zip(parts, out_refs):
        if noted:
            out_ref[slots * edge * (high_row - low_row) :, :] = notes.astype(bf16)

    for copy in copies[-slots:]:
        copy.wait()
    low = iota((count, 128), 1) < 64
    spot = iota((area, 128), 1)
    pairs = edge // 4 + 1
    masks = [None] * pairs
    masks[0] = spot >= width
    masks[-1] = spot < width
    norms = [Norm(width, area, voxels) for _ in range(slots)]
    outer = banded(pad_one, [128, data], count, edge, band_one[2])
    for pair in range(pairs):
        if 0 < pair < pairs - 1:
            even = banded(pad_one, [256 * pair], count, edge, band_one[0])
        else:
            even = outer
        odd = None
        if pair < pairs - 1:
            odd = banded(pad_one, [256 * pair + 128], count, edge, band_one[1])
        block = join_pair(even, odd, low, edge)
        hidden[:, pair * 128 : (pair + 1) * 128] = block
        for slot, norm in enumerate(norms):
            norm.take(block[slot * stride : slot * stride + area], masks[pair], 3)
        if pair < 3:
            build_pairs(taps_two_ref, band_two, width, width, False, pair)
    for norm in norms:
        norm.settle(gain_one, shift_one)

    fresh = {}
    near = spot < 64

    def refresh(pair):
        for slot, norm in enumerate(norms):
            at = slot * stride
            block = norm.give(hidden[at : at + area, pair * 128 : (pair + 1) * 128], masks[pair])
            rows_at = pl.ds(at + edge, area)
            pad_two[rows_at, pair * 128 : (pair + 1) * 128] = block.astype(bf16)
            if pair > 0:
                turned = pltpu.roll(jnp.where(near, block, fresh[slot]), 64, 1)
                pad_turned[rows_at, (pair - 1) * 128 : pair * 128] = turned.astype(bf16)
            fresh[slot] = block

    def prepare(slot):
        depth = corners_ref[slot, 0] - tile_index * TZ
        alive = slot < counts_ref[sub_index, tile_index]
        start = 0
        for peer, low_row, high_row, _ in parts:
            wanted = depth + edge * ((position ^ peer) * chunk - corners_ref[slot, 1])
            wanted = jnp.where(alive, wanted, far)
            select = (code[low_row * edge : high_row * edge] == wanted).astype(f32).astype(bf16)
            selects[slot, start : start + select.shape[0], :] = select
            start += select.shape[0]

    quads = edge // 4
    seconds = [Norm(width, area, voxels) for _ in range(slots)]
    refresh(0)
    for quad in range(quads):
        refresh(quad + 1)
        even = banded(pad_two, [128 * quad], count, edge, band_two[0])
        odd = banded(pad_turned, [128 * quad], count, edge, band_two[1])
        block = join_pair(even, odd, low, edge)
        outcome[:, quad * 128 : (quad + 1) * 128] = block
        for slot, norm in enumerate(seconds):
            norm.take(block[slot * stride : slot * stride + area], None, 4)
        if quad < slots:
            prepare(quad)
    for slot in range(quads, slots):
        prepare(slot)
    for norm in seconds:
        norm.settle(gain_two, shift_two)

    normed = []
    for slot, norm in enumerate(seconds):
        at = slot * stride
        for side in range(2):
            blocks = [
                norm.give(outcome[at : at + area, quad * 128 : (quad + 1) * 128], None).astype(
                    bf16
                )
                for quad in range(side * quads // 2, (side + 1) * quads // 2)
            ]
            normed.append(jnp.concatenate(blocks, axis=1))
    logits = [jnp.dot(block, head_block, preferred_element_type=f32) for block in normed]
    weighted = []
    for slot in range(slots):
        value = jnp.concatenate(logits[2 * slot : 2 * slot + 2], axis=1)
        value = (value + bias) * gauss
        lane_start = corners_ref[slot, 2] * classes
        weighted.append(pltpu.roll(value, lane_start % lanes, 1).astype(bf16))
    placed = [
        jnp.dot(selects[slot], weighted[slot], preferred_element_type=f32).astype(bf16)
        for slot in range(slots)
    ]
    for slot in range(slots):
        start = 0
        for (_, low_row, high_row, _), out_ref in zip(parts, out_refs):
            size = (high_row - low_row) * edge
            out_ref[slot * size : (slot + 1) * size, :] = placed[slot][start : start + size]
            start += size


def gather_kernel(sizes, spilled, *rest):
    slots, edge, chunk, parts, first, last, classes = sizes
    part_refs = rest[: len(parts)]
    out_ref = rest[len(parts)]
    lanes = edge * classes
    blocks = -(-VY * classes // lanes)

    depth_at = iota((edge, lanes), 0)
    lane_at = iota((edge, lanes), 1)
    groups = []
    for (peer, low_row, high_row, noted), part_ref in zip(parts, part_refs):
        if not noted or any(group[0] == peer % 2 for group in groups):
            continue
        notes = part_ref[slots * edge * (high_row - low_row) :, :].astype(f32).astype(jnp.int32)
        for slot in range(slots):
            depth = notes[2 * slot : 2 * slot + 1]
            start = notes[2 * slot + 1 : 2 * slot + 2] * classes
            keep = depth_at < depth if spilled else depth_at >= depth
            inside = []
            for block in range(blocks):
                lane = lane_at + block * lanes
                inside.append(keep & (lane >= start) & (lane < start + lanes))
            groups.append((peer % 2, slot, inside))

    for across in range(first, last):
        total = [jnp.zeros((edge, lanes), f32) for _ in range(blocks)]
        for parity, slot, inside in groups:
            piece = None
            for (peer, low_row, high_row, _), part_ref in zip(parts, part_refs):
                if peer % 2 == parity and low_row <= across < high_row:
                    at = (slot * (high_row - low_row) + across - low_row) * edge
                    part = part_ref[at : at + edge, :].astype(f32)
                    piece = part if piece is None else piece + part
            for block in range(blocks):
                total[block] = total[block] + jnp.where(inside[block], piece, 0.0)
        total = jnp.concatenate(total, axis=1)[:, : VY * classes]
        out_ref[across - first] = total.astype(out_ref.dtype)


def join_kernel(low_row, own_ref, odd_ref, even_ref, *rest):
    out_ref, total, sems = rest[-3:]
    tile_index = lax.axis_index("tiles")
    from_even = (tile_index % 2 == 1).astype(f32)
    from_odd = ((tile_index % 2 == 0) & (tile_index > 0)).astype(f32)
    copies = []
    for row in range(even_ref.shape[0]):
        total[row] = (
            own_ref[low_row + row]
            + even_ref[row].astype(f32) * from_even
            + odd_ref[row].astype(f32) * from_odd
        )
        copy = pltpu.make_async_copy(total.at[row], out_ref.at[low_row + row], sems.at[row])
        copy.start()
        copies.append(copy)
    for copy in copies:
        copy.wait()


vmem = pl.BlockSpec(memory_space=pltpu.VMEM)
hbm = pl.BlockSpec(memory_space=pltpu.HBM)
limits = pltpu.CompilerParams(vmem_limit_bytes=vmem_bytes)
ample = pltpu.CompilerParams(vmem_limit_bytes=60000000)


def on_device(
    features,
    conv_first,
    gain_first,
    shift_first,
    conv_second,
    gain_second,
    shift_second,
    head_weight,
    head_bias,
    corners,
    counts,
):
    _, slots, edge, _, data = features.shape
    in_width, width = conv_first.shape[-2:]
    classes = head_bias.shape[1]
    peers = lax.axis_size("folds") * lax.axis_size("sub")
    tiles = lax.axis_size("tiles")
    chunk = VX // peers
    area = edge * edge
    lanes = edge * classes
    padded = slots * (area + edge) + edge
    middle = chunk // 2
    halves = ((0, middle), (middle, chunk))
    parts = [(0, 0, chunk, True)]
    for low_row, high_row in halves:
        parts += [
            (peer, low_row, high_row, peer == 1 and low_row > 0)
            for peer in [*range(2, peers), 1]
        ]
    rows = [
        slots * edge * (high_row - low_row) + (edge if noted else 0)
        for _, low_row, high_row, noted in parts
    ]
    pieces = pl.pallas_call(
        functools.partial(section_kernel, (slots, edge, chunk, parts)),
        out_shape=[pltpu.VMEM((count, lanes), bf16) for count in rows],
        in_specs=[hbm] * 11,
        out_specs=[vmem] * len(parts),
        scratch_shapes=[
            pltpu.VMEM((padded, data + 256), bf16),
            pltpu.VMEM((padded, edge * width + 128), bf16),
            pltpu.VMEM((padded, edge * width), bf16),
            pltpu.VMEM((3, 768, 256), bf16),
            pltpu.VMEM((2, 384, 256), bf16),
            pltpu.VMEM((padded - 2 * edge, edge * width + 128), f32),
            pltpu.VMEM((padded - 2 * edge, edge * width), f32),
            pltpu.SMEM(corners.shape, jnp.int32),
            pltpu.SMEM(counts.shape[::-1], jnp.int32),
            pltpu.VMEM((27 * width, in_width), bf16),
            pltpu.VMEM((1, width), f32),
            pltpu.VMEM((1, width), f32),
            pltpu.VMEM((27 * width, width), bf16),
            pltpu.VMEM((1, width), f32),
            pltpu.VMEM((1, width), f32),
            pltpu.VMEM((classes, width), bf16),
            pltpu.VMEM((1, classes), f32),
            pltpu.VMEM((slots, VX * edge, area), bf16),
            pltpu.SemaphoreType.DMA((10 + slots,)),
        ],
        compiler_params=ample,
        name="section",
    )(
        corners,
        counts.T,
        features.reshape(slots, area, data),
        jnp.swapaxes(conv_first, 4, 5).reshape(27 * width, in_width),
        gain_first,
        shift_first,
        conv_second.reshape(27 * width, width),
        gain_second,
        shift_second,
        head_weight[0].T,
        head_bias,
    )
    arrived = []
    for (peer, _, _, _), piece in zip(parts, pieces):
        pairs = [(i, i ^ peer) for i in range(peers)]
        arrived.append(lax.ppermute(piece, ("folds", "sub"), pairs) if peer else piece)

    def gather(first, last, spilled, kind, name):
        chosen = [
            (part, piece)
            for part, piece in zip(parts, arrived)
            if part[3] or (part[1] < last and first < part[2])
        ]
        return pl.pallas_call(
            functools.partial(
                gather_kernel,
                (slots, edge, chunk, [part for part, _ in chosen], first, last, classes),
                spilled,
            ),
            out_shape=pltpu.VMEM((last - first, TZ, VY * classes), kind),
            in_specs=[vmem] * len(chosen),
            out_specs=vmem,
            compiler_params=limits,
            cost_estimate=pl.CostEstimate(
                flops=500000000, bytes_accessed=2000000, transcendentals=0
            ),
            name=name,
        )(*[piece for _, piece in chosen])

    even = [(tile, tile ^ 1) for tile in range(tiles)]
    odd = []
    for tile in range(tiles):
        for i in range(peers):
            if 0 < tile < tiles - 1:
                target = (tile + 1 if tile % 2 else tile - 1) * peers + i
            else:
                target = tile * peers + (i ^ 1)
            odd.append((tile * peers + i, target))
    from_below = []
    for first, last in halves:
        spill = gather(first, last, True, bf16, f"spill_{first}")
        from_below.append(lax.ppermute(spill, ("tiles", "folds", "sub"), odd))
        from_below.append(lax.ppermute(spill, "tiles", even))
    own = gather(0, chunk, False, f32, "own")
    joined = None
    for at in (1, 0):
        low_row, high_row = halves[at]
        joined = pl.pallas_call(
            functools.partial(join_kernel, low_row),
            out_shape=jax.ShapeDtypeStruct((chunk, TZ, VY * classes), f32),
            in_specs=[vmem] * 3 + ([] if joined is None else [hbm]),
            out_specs=hbm,
            input_output_aliases={} if joined is None else {3: 0},
            scratch_shapes=[
                pltpu.VMEM((high_row - low_row, TZ, VY * classes), f32),
                pltpu.SemaphoreType.DMA((high_row - low_row,)),
            ],
            compiler_params=limits,
            name=f"join_{low_row}",
        )(own, *from_below[2 * at : 2 * at + 2], *([] if joined is None else [joined]))
    return jnp.transpose(joined, (1, 0, 2))


def solution(mesh):
    placed = (
        P("folds", ("groups", "tiles", "sub"), None, None, None),
        P("folds", None, None, None, None, None),
        P("folds", None),
        P("folds", None),
        P("folds", None, None, None, None, None),
        P("folds", None),
        P("folds", None),
        P("folds", None, None),
        P("folds", None),
        P(("groups", "tiles", "sub"), None),
        P("groups", None),
    )
    return jax.shard_map(
        on_device,
        mesh=mesh,
        in_specs=placed,
        out_specs=P(("groups", "tiles"), ("folds", "sub"), None),
        check_vma=False,
    )
```
